32 devices in a mesh: ctx: 8 (over z, x), tp: 4 (over y, core).
Axes of the slice: x: 2, y: 2, z: 4, core: 2. Of those that a mesh axis runs over, the one named last changes fastest.
Arguments:
- queries: bfloat16 [2048, 1024], P('ctx', 'tp'), may hold values from -6 to 6
- keys: bfloat16 [2048, 1024], P('ctx', 'tp'), may hold values from -6 to 6
- values: bfloat16 [2048, 1024], P('ctx', 'tp'), may hold values from -20 to 20, as said below
- gain: float32 [1024], P('tp'), may hold values from 0.25 to 1.75
- out_grad: bfloat16 [2048, 1024], P('ctx', 'tp'), may hold values from -6 to 6
Outputs:
- normed: bfloat16 [2048, 1024], P('ctx', 'tp')
- grad_queries: bfloat16 [2048, 1024], P('ctx', 'tp')
- grad_keys: bfloat16 [2048, 1024], P('ctx', 'tp')
- grad_values: bfloat16 [2048, 1024], P('ctx', 'tp')
The draws below stay inside these ranges and needn't reach their ends.
Inputs may be any that keep to these rules, and one draw needn't show every extreme that they name: values of order one, each head at its own scale.
All inputs are finite; a program needn't handle non-finite values.
Results may differ from the reference program's by a relative error of at most 0.0065.
Values sent between devices are 32-bit elements; how exact they have to be, the bound alone decides.
No kernel may reach another device: no remote copies, remote signals or barrier semaphores. Data moves between devices by JAX's collectives and lax.ppermute only.
A program may use at most 64 MiB of HBM per device.

```python
import jax
import jax.numpy as jnp
from jax import lax

HEAD = 128
TOK_DEV = 256
HEADS = 8
SEQ = 2048
N_CTX = 8


def draw_values(key, part):
    key = jax.random.fold_in(key, 5)
    jitter_key, main_key = jax.random.split(key)
    placing = (jnp.arange(HEADS, dtype=jnp.float32) + jax.random.uniform(jitter_key, (HEADS,), jnp.float32)) / HEADS
    scales = 10.0 ** (placing - 0.5)
    noise = jnp.clip(jax.random.normal(main_key, (SEQ, HEADS, HEAD), jnp.float32), -6.0, 6.0)
    return (noise * scales[None, :, None]).reshape(SEQ, HEADS * HEAD).astype(jnp.bfloat16)


def steps_of(own_key, shape, cuts, least, largest):
    loudness = 1.0
    for dim, blocks in cuts:
        heights = jax.random.uniform(jax.random.fold_in(jax.random.fold_in(own_key, 6), dim), (blocks,), jnp.float32, least / len(cuts), largest / len(cuts))
        loudness = loudness * jnp.repeat(jnp.exp(heights), shape[dim] // blocks).reshape((-1,) + (1,) * (len(shape) - 1 - dim))
    return loudness


def scatter_about(rng, dims, width, most, pieces=(), held_as=jnp.bfloat16):
    result = width * jax.random.normal(rng, dims, jnp.float32)
    if pieces:
        result = result * steps_of(rng, dims, pieces, -0.22, 0.18)
    return jnp.clip(result, -most, most).astype(held_as)


def setup_inputs(seed: int = 0) -> dict:
    streams_of = jax.random.split(jax.random.key(seed), 6)
    return {
        "queries": scatter_about(streams_of[0], (SEQ, HEADS * HEAD), 1.0, 6.0, ((0, 8), (1, 4))),
        "keys": scatter_about(streams_of[1], (SEQ, HEADS * HEAD), 1.0, 6.0, ((0, 8), (1, 4))),
        "values": draw_values(jax.random.fold_in(streams_of[5], 71), 0),
        "gain": jnp.clip(1.0 + 0.15 * jax.random.normal(streams_of[3], (HEADS * HEAD,), jnp.float32), 0.25, 1.75),
        "out_grad": scatter_about(streams_of[4], (SEQ, HEADS * HEAD), 1.0, 6.0, ((0, 8), (1, 4))),
    }


epsilon = 1e-06

def reference(queries, keys, values, gain, out_grad):
    blocks = N_CTX
    tokens = TOK_DEV
    factor = (HEAD * SEQ) ** (-0.5)
    features = HEADS * HEAD
    q_all = queries.reshape(blocks, tokens, HEADS, HEAD)
    k_all = keys.reshape(blocks, tokens, HEADS, HEAD)
    v_all = values.reshape(blocks, tokens, HEADS, HEAD)
    position = jnp.arange(tokens, dtype=jnp.int32)
    causal = position[:, None] >= position[None, :]

    def make_scores(q_blk, k_blk):
        raw = jnp.einsum('thd,shd->hts', q_blk.astype(jnp.float32), k_blk.astype(jnp.float32)) * factor
        return jnp.where(causal[None], raw, 0.0).astype(jnp.bfloat16)

    def forward(carry, blk):
        q_blk, k_blk, v_blk = blk
        prefix = carry.astype(jnp.bfloat16)
        scores = make_scores(q_blk, k_blk)
        attended = factor * jnp.einsum('thd,hde->the', q_blk.astype(jnp.float32), prefix.astype(jnp.float32))
        attended = attended + jnp.einsum('hts,she->the', scores.astype(jnp.float32), v_blk.astype(jnp.float32))
        states = jnp.einsum('thd,the->hde', k_blk.astype(jnp.float32), v_blk.astype(jnp.float32))
        return (carry + states, (attended, prefix))
    start = jnp.zeros((HEADS, HEAD, HEAD), jnp.float32)
    _, (attended, prefixes) = lax.scan(forward, start, (q_all, k_all, v_all))
    inv_rms = lax.rsqrt(lax.optimization_barrier(jnp.sum(attended * attended, axis=(2, 3))) / features + epsilon)
    gains = gain.astype(jnp.float32).reshape(HEADS, HEAD)
    normed = (attended * inv_rms[:, :, None, None] * gains).reshape(SEQ, features).astype(jnp.bfloat16)
    weighted = out_grad.astype(jnp.float32).reshape(blocks, tokens, HEADS, HEAD) * gains
    row_mean = lax.optimization_barrier(jnp.sum(weighted * attended, axis=(2, 3))) / features
    grad_attn = inv_rms[:, :, None, None] * (weighted - attended * (inv_rms * inv_rms * row_mean)[:, :, None, None])
    grad_attn = grad_attn.astype(jnp.bfloat16)

    def backward(carry, blk):
        q_blk, k_blk, v_blk, g_blk, prefix = blk
        suffix = carry.astype(jnp.bfloat16)
        qf = q_blk.astype(jnp.float32)
        kf = k_blk.astype(jnp.float32)
        vf = v_blk.astype(jnp.float32)
        gf = g_blk.astype(jnp.float32)
        pf = prefix.astype(jnp.float32)
        sf = suffix.astype(jnp.float32)
        scores = make_scores(q_blk, k_blk).astype(jnp.float32)
        raw = jnp.einsum('the,she->hts', gf, vf) * factor
        grad_scores = jnp.where(causal[None], raw, 0.0).astype(jnp.bfloat16).astype(jnp.float32)
        grad_q = factor * jnp.einsum('the,hde->thd', gf, pf) + jnp.einsum('hts,shd->thd', grad_scores, kf)
        grad_k = factor * jnp.einsum('the,hde->thd', vf, sf) + jnp.einsum('hts,thd->shd', grad_scores, qf)
        grad_v = factor * jnp.einsum('thd,hde->the', kf, sf) + jnp.einsum('hts,the->she', scores, gf)
        updates = jnp.einsum('thd,the->hde', qf, gf)
        return (carry + updates, (grad_q.astype(jnp.bfloat16), grad_k.astype(jnp.bfloat16), grad_v.astype(jnp.bfloat16)))
    _, (grad_q, grad_k, grad_v) = lax.scan(backward, start, (q_all, k_all, v_all, grad_attn, prefixes), reverse=True)
    return (normed, grad_q.reshape(SEQ, features), grad_k.reshape(SEQ, features), grad_v.reshape(SEQ, features))
```

```python
import functools

import jax
import jax.numpy as jnp
from jax import lax
from jax.experimental import pallas as pl
from jax.experimental.pallas import tpu as pltpu
from jax.sharding import PartitionSpec as P

HEAD = 128

epsilon = 1e-06
F32 = jnp.float32
BF16 = jnp.bfloat16

NN = (((1,), (0,)), ((), ()))
NT = (((1,), (1,)), ((), ()))
TN = (((0,), (0,)), ((), ()))


def dot(a, b, dims):
    return lax.dot_general(a, b, dims, preferred_element_type=F32)


def call(body, outs, *args, flops=1e7):
    moved = sum(a.size * a.dtype.itemsize for a in args)
    return pl.pallas_call(
        body,
        out_shape=outs,
        in_specs=[pl.BlockSpec(memory_space=pltpu.VMEM)] * len(args),
        out_specs=jax.tree.map(lambda _: pl.BlockSpec(memory_space=pltpu.VMEM), outs),
        compiler_params=pltpu.CompilerParams(vmem_limit_bytes=16 * 1024 * 1024),
        cost_estimate=pl.CostEstimate(flops=int(flops), bytes_accessed=int(moved), transcendentals=0),
    )(*args)


def head(h):
    return slice(h * HEAD, (h + 1) * HEAD)


def causal_mask(tokens):
    row = lax.broadcasted_iota(jnp.int32, (tokens, tokens), 0)
    col = lax.broadcasted_iota(jnp.int32, (tokens, tokens), 1)
    return row >= col


def states_body(heads, left, right, out):
    for h in range(heads):
        out[head(h), :] = dot(left[:, head(h)], right[:, head(h)], TN)


def scan_body(count, reverse, arrived, sums):
    running = jnp.zeros(arrived.shape[1:], F32)
    for place in range(count - 1, -1, -1) if reverse else range(count):
        sums[place] = running
        running = running + arrived[place]


def attend_body(heads, factor, q, k, v, og, gain, prefix, attended, scores, stats):
    causal = causal_mask(q.shape[0])
    power = 0.0
    inner = 0.0
    for h in range(heads):
        qh = q[:, head(h)]
        vh = v[:, head(h)]
        raw = dot(qh, k[:, head(h)], NT) * factor
        sc = jnp.where(causal, raw, 0.0).astype(BF16)
        scores[h] = sc
        att = factor * dot(qh, prefix[head(h), :].astype(BF16), NN) + dot(sc, vh, NN)
        attended[:, head(h)] = att
        weighted = og[:, head(h)].astype(F32) * gain[h : h + 1, :]
        power = power + att * att
        inner = inner + weighted * att
    stats[0:1, :] = jnp.sum(power.T, axis=0, keepdims=True)
    stats[1:2, :] = jnp.sum(inner.T, axis=0, keepdims=True)


def grad_body(heads, features, ways, attended, og, gain, q, *rest):
    stats, (normed, grad, updates) = rest[:ways], rest[ways:]
    total = stats[0][...]
    for other in stats[1:]:
        total = total + other[...]
    inv_rms = lax.rsqrt(total[0:1, :] / features + epsilon)
    bend = inv_rms * inv_rms * (total[1:2, :] / features)
    tokens = q.shape[0]
    inv_rms = jnp.broadcast_to(inv_rms, (HEAD, tokens)).T
    bend = jnp.broadcast_to(bend, (HEAD, tokens)).T
    for h in range(heads):
        att = attended[:, head(h)]
        gain_h = gain[h : h + 1, :]
        normed[:, head(h)] = (att * inv_rms * gain_h).astype(BF16)
        weighted = og[:, head(h)].astype(F32) * gain_h
        ga = (inv_rms * (weighted - att * bend)).astype(BF16)
        grad[:, head(h)] = ga
        updates[head(h), :] = dot(q[:, head(h)], ga, TN)


def local_body(heads, factor, ga, q, k, v, prefix, scores, gq, gk_part, gv_part):
    causal = causal_mask(q.shape[0])
    for h in range(heads):
        gah = ga[:, head(h)]
        raw = dot(gah, v[:, head(h)], NT) * factor
        gs = jnp.where(causal, raw, 0.0).astype(BF16)
        out = factor * dot(gah, prefix[head(h), :].astype(BF16), NT)
        gq[:, head(h)] = (out + dot(gs, k[:, head(h)], NN)).astype(BF16)
        gk_part[:, head(h)] = dot(gs, q[:, head(h)], TN)
        gv_part[:, head(h)] = dot(scores[h], gah, TN)


def final_body(heads, factor, k, v, suffix, gk_part, gv_part, gk, gv):
    for h in range(heads):
        suf = suffix[head(h), :].astype(BF16)
        gk[:, head(h)] = (factor * dot(v[:, head(h)], suf, NT) + gk_part[:, head(h)]).astype(BF16)
        gv[:, head(h)] = (factor * dot(k[:, head(h)], suf, NN) + gv_part[:, head(h)]).astype(BF16)


def carried_in(part, axis, reverse):
    count = lax.axis_size(axis)
    pieces = part.reshape(count, -1, part.shape[-1])
    arrived = lax.all_to_all(pieces, axis, 0, 0, tiled=True)
    sums = call(
        functools.partial(scan_body, count, reverse),
        jax.ShapeDtypeStruct(pieces.shape, F32),
        arrived,
    )
    return lax.all_to_all(sums, axis, 0, 0, tiled=True).reshape(part.shape)


def from_all(part, axis):
    count = lax.axis_size(axis)
    return [part] + [
        lax.ppermute(part, axis, [(i, (i + shift) % count) for i in range(count)])
        for shift in range(1, count)
    ]


def on_device(queries, keys, values, gain, out_grad):
    tokens, width = queries.shape
    heads = width // HEAD
    factor = (HEAD * tokens * lax.axis_size("ctx")) ** (-0.5)
    features = width * lax.axis_size("tp")
    gains = gain.reshape(heads, HEAD)
    sds = jax.ShapeDtypeStruct
    state = sds((width, HEAD), F32)
    wide = sds((tokens, width), F32)
    half = sds((tokens, width), BF16)

    states = call(functools.partial(states_body, heads), state, keys, values)
    prefix = carried_in(states, "ctx", False)
    attended, scores, stats = call(
        functools.partial(attend_body, heads, factor),
        (wide, sds((heads, tokens, tokens), BF16), sds((2, tokens), F32)),
        queries, keys, values, out_grad, gains, prefix,
    )
    every = from_all(stats, "tp")
    normed, grad_attn, updates = call(
        functools.partial(grad_body, heads, features, len(every)),
        (half, half, state),
        attended, out_grad, gains, queries, *every,
    )
    suffix = carried_in(updates, "ctx", True)
    grad_q, gk_part, gv_part = call(
        functools.partial(local_body, heads, factor),
        (half, wide, wide),
        grad_attn, queries, keys, values, prefix, scores,
    )
    grad_k, grad_v = call(
        functools.partial(final_body, heads, factor),
        (half, half),
        keys, values, suffix, gk_part, gv_part,
    )
    return normed, grad_q, grad_k, grad_v


def solution(mesh):
    placed = (P("ctx", "tp"), P("ctx", "tp"), P("ctx", "tp"), P("tp"), P("ctx", "tp"))
    return jax.shard_map(
        on_device,
        mesh=mesh,
        in_specs=placed,
        out_specs=(P("ctx", "tp"), P("ctx", "tp"), P("ctx", "tp"), P("ctx", "tp")),
        check_vma=False,
    )
```

```python
import functools

import jax
import jax.numpy as jnp
from jax import lax
from jax.experimental import pallas as pl
from jax.experimental.pallas import tpu as pltpu
from jax.sharding import PartitionSpec as P

HEAD = 128

epsilon = 1e-06
DIRECT = 16
F32 = jnp.float32
BF16 = jnp.bfloat16

NN = (((1,), (0,)), ((), ()))
NT = (((1,), (1,)), ((), ()))
TN = (((0,), (0,)), ((), ()))


def dot(a, b, dims):
    return lax.dot_general(a, b, dims, preferred_element_type=F32)


def call(body, outs, *args, scratch=(), flops=1e7):
    moved = sum(a.size * a.dtype.itemsize for a in args)
    return pl.pallas_call(
        body,
        out_shape=outs,
        in_specs=[pl.BlockSpec(memory_space=pltpu.VMEM)] * len(args),
        out_specs=jax.tree.map(lambda _: pl.BlockSpec(memory_space=pltpu.VMEM), outs),
        scratch_shapes=scratch,
        compiler_params=pltpu.CompilerParams(vmem_limit_bytes=16 * 1024 * 1024),
        cost_estimate=pl.CostEstimate(flops=int(flops), bytes_accessed=int(moved), transcendentals=0),
    )(*args)


def head(h):
    return slice(h * HEAD, (h + 1) * HEAD)


def causal_mask(tokens):
    row = lax.broadcasted_iota(jnp.int32, (tokens, tokens), 0)
    col = lax.broadcasted_iota(jnp.int32, (tokens, tokens), 1)
    return row >= col


def piece_at(scratch, count, place):
    rows = scratch.shape[0] // count
    return scratch.at[pl.ds(pl.multiple_of(place * rows, rows), rows), :]


def put_pieces(scratch, count, outs):
    if len(outs) == 1:
        outs[0][...] = scratch[...].reshape(outs[0].shape)
        return
    me = lax.axis_index("ctx")
    for r, out in enumerate(outs):
        out[...] = piece_at(scratch, count, lax.rem(me + r, count))[...]


def take_pieces(ins, scratch, count):
    if len(ins) == 1:
        scratch[...] = ins[0][...].reshape(scratch.shape)
        return
    me = lax.axis_index("ctx")
    for r, piece in enumerate(ins):
        piece_at(scratch, count, lax.rem(me + count - r, count))[...] = piece[...]


def states_body(heads, count, left, right, *rest):
    outs, scratch = rest[:-1], rest[-1]
    for h in range(heads):
        scratch[head(h), :] = dot(left[:, head(h)], right[:, head(h)], TN)
    put_pieces(scratch, count, outs)


def scan_body(count, reverse, *rest):
    many = len(rest) // 2
    arrived, outs, scratch = rest[:many], rest[many:-1], rest[-1]
    take_pieces(arrived, scratch, count)
    rows = scratch.shape[0] // count
    running = jnp.zeros((rows, scratch.shape[1]), F32)
    for place in range(count - 1, -1, -1) if reverse else range(count):
        own = slice(place * rows, (place + 1) * rows)
        here = scratch[own, :]
        scratch[own, :] = running
        running = running + here
    put_pieces(scratch, count, outs)


def attend_body(heads, factor, count, q, k, v, og, gain, *rest):
    pieces, (attended, scores, stats, prefix) = rest[:-4], rest[-4:]
    take_pieces(pieces, prefix, count)
    causal = causal_mask(q.shape[0])
    power = 0.0
    inner = 0.0
    for h in range(heads):
        qh = q[:, head(h)]
        vh = v[:, head(h)]
        raw = dot(qh, k[:, head(h)], NT) * factor
        sc = jnp.where(causal, raw, 0.0).astype(BF16)
        scores[h] = sc
        att = factor * dot(qh, prefix[head(h), :].astype(BF16), NN) + dot(sc, vh, NN)
        attended[:, head(h)] = att
        weighted = og[:, head(h)].astype(F32) * gain[h : h + 1, :]
        power = power + att * att
        inner = inner + weighted * att
    stats[0:1, :] = jnp.sum(power.T, axis=0, keepdims=True)
    stats[1:2, :] = jnp.sum(inner.T, axis=0, keepdims=True)


def grad_body(heads, features, ways, count, attended, og, gain, q, *rest):
    stats, normed, grad, outs, updates = rest[:ways], rest[ways], rest[ways + 1], rest[ways + 2 : -1], rest[-1]
    total = stats[0][...]
    for other in stats[1:]:
        total = total + other[...]
    inv_rms = lax.rsqrt(total[0:1, :] / features + epsilon)
    bend = inv_rms * inv_rms * (total[1:2, :] / features)
    tokens = q.shape[0]
    inv_rms = jnp.broadcast_to(inv_rms, (HEAD, tokens)).T
    bend = jnp.broadcast_to(bend, (HEAD, tokens)).T
    for h in range(heads):
        att = attended[:, head(h)]
        gain_h = gain[h : h + 1, :]
        normed[:, head(h)] = (att * inv_rms * gain_h).astype(BF16)
        weighted = og[:, head(h)].astype(F32) * gain_h
        ga = (inv_rms * (weighted - att * bend)).astype(BF16)
        grad[:, head(h)] = ga
        updates[head(h), :] = dot(q[:, head(h)], ga, TN)
    put_pieces(updates, count, outs)


def local_body(heads, factor, ga, q, k, v, prefix, scores, gq, gk_part, gv_part):
    causal = causal_mask(q.shape[0])
    for h in range(heads):
        gah = ga[:, head(h)]
        raw = dot(gah, v[:, head(h)], NT) * factor
        gs = jnp.where(causal, raw, 0.0).astype(BF16)
        out = factor * dot(gah, prefix[head(h), :].astype(BF16), NT)
        gq[:, head(h)] = (out + dot(gs, k[:, head(h)], NN)).astype(BF16)
        gk_part[:, head(h)] = dot(gs, q[:, head(h)], TN)
        gv_part[:, head(h)] = dot(scores[h], gah, TN)


def final_body(heads, factor, count, k, v, gk_part, gv_part, *rest):
    pieces, (gk, gv, suffix) = rest[:-3], rest[-3:]
    take_pieces(pieces, suffix, count)
    for h in range(heads):
        suf = suffix[head(h), :].astype(BF16)
        gk[:, head(h)] = (factor * dot(v[:, head(h)], suf, NT) + gk_part[:, head(h)]).astype(BF16)
        gv[:, head(h)] = (factor * dot(k[:, head(h)], suf, NN) + gv_part[:, head(h)]).astype(BF16)


def spread(pieces, axis):
    count = lax.axis_size(axis)
    if len(pieces) == 1:
        return [lax.all_to_all(pieces[0], axis, 0, 0, tiled=True)]
    return [pieces[0]] + [
        lax.ppermute(pieces[r], axis, [(i, (i + r) % count) for i in range(count)])
        for r in range(1, count)
    ]


def carried_in(pieces, axis, reverse, scratch):
    count = lax.axis_size(axis)
    outs = [jax.ShapeDtypeStruct(piece.shape, F32) for piece in pieces]
    body = functools.partial(scan_body, count, reverse)
    return spread(call(body, outs, *spread(pieces, axis), scratch=[scratch]), axis)


def from_all(part, axis):
    count = lax.axis_size(axis)
    return [part] + [
        lax.ppermute(part, axis, [(i, (i + shift) % count) for i in range(count)])
        for shift in range(1, count)
    ]


def on_device(queries, keys, values, gain, out_grad):
    tokens, width = queries.shape
    heads = width // HEAD
    factor = (HEAD * tokens * lax.axis_size("ctx")) ** (-0.5)
    features = width * lax.axis_size("tp")
    gains = gain.reshape(heads, HEAD)
    sds = jax.ShapeDtypeStruct
    wide = sds((tokens, width), F32)
    half = sds((tokens, width), BF16)
    count = lax.axis_size("ctx")
    rows = width // count
    if count <= DIRECT:
        pieces = [sds((rows, HEAD), F32)] * count
    else:
        pieces = [sds((count, rows, HEAD), F32)]
    state = pltpu.VMEM((width, HEAD), F32)

    states = call(
        functools.partial(states_body, heads, count), pieces, keys, values, scratch=[state]
    )
    prefix = carried_in(states, "ctx", False, state)
    attended, scores, stats, prefix = call(
        functools.partial(attend_body, heads, factor, count),
        (wide, sds((heads, tokens, tokens), BF16), sds((2, tokens), F32), sds((width, HEAD), F32)),
        queries, keys, values, out_grad, gains, *prefix,
    )
    every = from_all(stats, "tp")
    normed, grad_attn, *updates = call(
        functools.partial(grad_body, heads, features, len(every), count),
        (half, half, *pieces),
        attended, out_grad, gains, queries, *every,
        scratch=[state],
    )
    suffix = carried_in(updates, "ctx", True, state)
    grad_q, gk_part, gv_part = call(
        functools.partial(local_body, heads, factor),
        (half, wide, wide),
        grad_attn, queries, keys, values, prefix, scores,
    )
    grad_k, grad_v = call(
        functools.partial(final_body, heads, factor, count),
        (half, half),
        keys, values, gk_part, gv_part, *suffix,
        scratch=[state],
    )
    return normed, grad_q, grad_k, grad_v


def solution(mesh):
    placed = (P("ctx", "tp"), P("ctx", "tp"), P("ctx", "tp"), P("tp"), P("ctx", "tp"))
    return jax.shard_map(
        on_device,
        mesh=mesh,
        in_specs=placed,
        out_specs=(P("ctx", "tp"), P("ctx", "tp"), P("ctx", "tp"), P("ctx", "tp")),
        check_vma=False,
    )
```

```python
import functools

import jax
import jax.numpy as jnp
from jax import lax
from jax.experimental import pallas as pl
from jax.experimental.pallas import tpu as pltpu
from jax.sharding import PartitionSpec as P

HEAD = 128

epsilon = 1e-06
F32 = jnp.float32
BF16 = jnp.bfloat16

NN = (((1,), (0,)), ((), ()))
NT = (((1,), (1,)), ((), ()))
TN = (((0,), (0,)), ((), ()))


def dot(a, b, dims):
    return lax.dot_general(a, b, dims, preferred_element_type=F32)


VMEM = pl.BlockSpec(memory_space=pltpu.VMEM)
HBM = pl.BlockSpec(memory_space=pltpu.HBM)


def call(body, outs, *args, ins=None, dests=None, scratch=(), flops=1e7):
    moved = sum(a.size * a.dtype.itemsize for a in args)
    return pl.pallas_call(
        body,
        out_shape=outs,
        in_specs=ins or [VMEM] * len(args),
        out_specs=dests or jax.tree.map(lambda _: VMEM, outs),
        scratch_shapes=scratch,
        compiler_params=pltpu.CompilerParams(vmem_limit_bytes=16 * 1024 * 1024),
        cost_estimate=pl.CostEstimate(flops=int(flops), bytes_accessed=int(moved), transcendentals=0),
    )(*args)


def head(h):
    return slice(h * HEAD, (h + 1) * HEAD)


def causal_mask(tokens):
    row = lax.broadcasted_iota(jnp.int32, (tokens, tokens), 0)
    col = lax.broadcasted_iota(jnp.int32, (tokens, tokens), 1)
    return row >= col


def states_body(heads, *refs):
    many = (len(refs) - 2) // 2
    given, (out, *held), sems = refs[:many], refs[many:-1], refs[-1]
    copies = [pltpu.make_async_copy(a, b, sems.at[i]) for i, (a, b) in enumerate(zip(given, held))]
    for copy in copies:
        copy.start()
    copies[0].wait()
    copies[1].wait()
    left, right = held[0], held[1]
    for h in range(heads):
        out[head(h), :] = dot(left[:, head(h)], right[:, head(h)], TN)
    for copy in copies[2:]:
        copy.wait()


def scan_body(count, reverse, arrived, sums):
    running = jnp.zeros(arrived.shape[1:], F32)
    for place in range(count - 1, -1, -1) if reverse else range(count):
        sums[place] = running
        running = running + arrived[place]


def attend_body(heads, factor, q, k, v, og, gain, prefix, attended, scores, stats):
    causal = causal_mask(q.shape[0])
    power = 0.0
    inner = 0.0
    for h in range(heads):
        qh = q[:, head(h)]
        vh = v[:, head(h)]
        raw = dot(qh, k[:, head(h)], NT) * factor
        sc = jnp.where(causal, raw, 0.0).astype(BF16)
        scores[h] = sc
        att = factor * dot(qh, prefix[head(h), :].astype(BF16), NN) + dot(sc, vh, NN)
        attended[:, head(h)] = att
        weighted = og[:, head(h)].astype(F32) * gain[h : h + 1, :]
        power = power + att * att
        inner = inner + weighted * att
    power = jnp.sum(power.T, axis=0, keepdims=True)
    inner = jnp.sum(inner.T, axis=0, keepdims=True)
    for peer in range(stats.shape[0]):
        stats[peer, 0:1, :] = power
        stats[peer, 1:2, :] = inner


def grad_body(heads, features, attended, og, gain, q, stats, normed, grad, updates):
    total = jnp.sum(stats[...], axis=0)
    inv_rms = lax.rsqrt(total[0:1, :] / features + epsilon)
    bend = inv_rms * inv_rms * (total[1:2, :] / features)
    tokens = q.shape[0]
    inv_rms = jnp.broadcast_to(inv_rms, (HEAD, tokens)).T
    bend = jnp.broadcast_to(bend, (HEAD, tokens)).T
    for h in range(heads):
        att = attended[:, head(h)]
        gain_h = gain[h : h + 1, :]
        weighted = og[:, head(h)].astype(F32) * gain_h
        ga = (inv_rms * (weighted - att * bend)).astype(BF16)
        grad[:, head(h)] = ga
        updates[head(h), :] = dot(q[:, head(h)], ga, TN)
        normed[:, head(h)] = (att * inv_rms * gain_h).astype(BF16)


def final_body(heads, factor, ga, q, k, v, prefix, suffix, scores, normed, *rest):
    outs, (gq, gk, gv, sems) = rest[:4], rest[4:]
    sources = [normed, gq, gk, gv]
    copies = [pltpu.make_async_copy(a, b, sems.at[i]) for i, (a, b) in enumerate(zip(sources, outs))]
    copies[0].start()
    causal = causal_mask(q.shape[0])
    grads = []
    for h in range(heads):
        gah = ga[:, head(h)]
        raw = dot(gah, v[:, head(h)], NT) * factor
        gs = jnp.where(causal, raw, 0.0).astype(BF16)
        grads.append(gs)
        out = factor * dot(gah, prefix[head(h), :].astype(BF16), NT)
        gq[:, head(h)] = (out + dot(gs, k[:, head(h)], NN)).astype(BF16)
    copies[1].start()
    for h in range(heads):
        suf = suffix[head(h), :].astype(BF16)
        part = dot(grads[h], q[:, head(h)], TN)
        gk[:, head(h)] = (factor * dot(v[:, head(h)], suf, NT) + part).astype(BF16)
    copies[2].start()
    for h in range(heads):
        suf = suffix[head(h), :].astype(BF16)
        part = dot(scores[h], ga[:, head(h)], TN)
        gv[:, head(h)] = (factor * dot(k[:, head(h)], suf, NN) + part).astype(BF16)
    copies[3].start()
    for copy in copies:
        copy.wait()


def carried_in(part, axis, reverse):
    count = lax.axis_size(axis)
    pieces = part.reshape(count, -1, part.shape[-1])
    arrived = lax.all_to_all(pieces, axis, 0, 0, tiled=True)
    sums = call(
        functools.partial(scan_body, count, reverse),
        jax.ShapeDtypeStruct(pieces.shape, F32),
        arrived,
    )
    return lax.all_to_all(sums, axis, 0, 0, tiled=True).reshape(part.shape)


def on_device(queries, keys, values, gain, out_grad):
    tokens, width = queries.shape
    heads = width // HEAD
    factor = (HEAD * tokens * lax.axis_size("ctx")) ** (-0.5)
    features = width * lax.axis_size("tp")
    gains = gain.reshape(heads, HEAD)
    sds = jax.ShapeDtypeStruct
    state = sds((width, HEAD), F32)
    wide = sds((tokens, width), F32)
    half = sds((tokens, width), BF16)

    given = (keys, values, queries, out_grad, gains)
    states, keys, values, queries, out_grad, gains = call(
        functools.partial(states_body, heads),
        (state, *(pltpu.VMEM(a.shape, a.dtype) for a in given)),
        *(pltpu.with_memory_space_constraint(a, pltpu.HBM) for a in given),
        ins=[HBM] * len(given),
        scratch=[pltpu.SemaphoreType.DMA((len(given),))],
    )
    prefix = carried_in(states, "ctx", False)
    ways = lax.axis_size("tp")
    attended, scores, stats = call(
        functools.partial(attend_body, heads, factor),
        (wide, sds((heads, tokens, tokens), BF16), sds((ways, 2, tokens), F32)),
        queries, keys, values, out_grad, gains, prefix,
    )
    stats = lax.all_to_all(stats, "tp", 0, 0, tiled=True)
    normed, grad_attn, updates = call(
        functools.partial(grad_body, heads, features),
        (half, half, state),
        attended, out_grad, gains, queries, stats,
    )
    suffix = carried_in(updates, "ctx", True)
    held = pltpu.VMEM((tokens, width), BF16)
    return call(
        functools.partial(final_body, heads, factor),
        (half, half, half, half),
        grad_attn, queries, keys, values, prefix, suffix, scores, normed,
        dests=(HBM, HBM, HBM, HBM),
        scratch=[held, held, held, pltpu.SemaphoreType.DMA((4,))],
    )


def solution(mesh):
    placed = (P("ctx", "tp"), P("ctx", "tp"), P("ctx", "tp"), P("tp"), P("ctx", "tp"))
    return jax.shard_map(
        on_device,
        mesh=mesh,
        in_specs=placed,
        out_specs=(P("ctx", "tp"), P("ctx", "tp"), P("ctx", "tp"), P("ctx", "tp")),
        check_vma=False,
    )
```

```python
import functools

import jax
import jax.numpy as jnp
from jax import lax
from jax.experimental import pallas as pl
from jax.experimental.pallas import tpu as pltpu
from jax.sharding import PartitionSpec as P

HEAD = 128

epsilon = 1e-06
F32 = jnp.float32
BF16 = jnp.bfloat16

NN = (((1,), (0,)), ((), ()))
NT = (((1,), (1,)), ((), ()))
TN = (((0,), (0,)), ((), ()))


def dot(a, b, dims):
    return lax.dot_general(a, b, dims, preferred_element_type=F32)


VMEM = pl.BlockSpec(memory_space=pltpu.VMEM)
HBM = pl.BlockSpec(memory_space=pltpu.HBM)


def call(body, outs, *args, ins=None, dests=None, scratch=(), flops=1e7):
    moved = sum(a.size * a.dtype.itemsize for a in args)
    return pl.pallas_call(
        body,
        out_shape=outs,
        in_specs=ins or [VMEM] * len(args),
        out_specs=dests or jax.tree.map(lambda _: VMEM, outs),
        scratch_shapes=scratch,
        compiler_params=pltpu.CompilerParams(vmem_limit_bytes=16 * 1024 * 1024),
        cost_estimate=pl.CostEstimate(flops=int(flops), bytes_accessed=int(moved), transcendentals=0),
    )(*args)


def head(h):
    return slice(h * HEAD, (h + 1) * HEAD)


def causal_mask(tokens):
    row = lax.broadcasted_iota(jnp.int32, (tokens, tokens), 0)
    col = lax.broadcasted_iota(jnp.int32, (tokens, tokens), 1)
    return row >= col


def rows_of(scratch, parts, place):
    rows = scratch.shape[0] // parts
    return scratch.at[pl.ds(pl.multiple_of(place * rows, rows), rows), :]


def give(scratch, group, outs):
    if len(outs) == 1:
        outs[0][...] = scratch[...].reshape(outs[0].shape)
        return
    place = lax.rem(lax.axis_index("ctx"), group)
    for r, out in enumerate(outs):
        out[...] = rows_of(scratch, group, lax.bitwise_xor(place, r))[...]


def take(ins, scratch, group):
    if len(ins) == 1:
        scratch[...] = ins[0][...].reshape(scratch.shape)
        return
    place = lax.rem(lax.axis_index("ctx"), group)
    for r, piece in enumerate(ins):
        rows_of(scratch, group, lax.bitwise_xor(place, r))[...] = piece[...]


def running_sums(scratch, parts, reverse):
    rows = scratch.shape[0] // parts
    running = jnp.zeros((rows, scratch.shape[1]), F32)
    for place in range(parts - 1, -1, -1) if reverse else range(parts):
        own = slice(place * rows, (place + 1) * rows)
        here = scratch[own, :]
        scratch[own, :] = running
        running = running + here
    return running


def states_body(heads, group, many, *refs):
    given, held, outs = refs[:many], refs[many : 2 * many], refs[2 * many : -2]
    state, sems = refs[-2:]
    copies = [pltpu.make_async_copy(a, b, sems.at[i]) for i, (a, b) in enumerate(zip(given, held))]
    for copy in copies:
        copy.start()
    copies[0].wait()
    copies[1].wait()
    left, right = held[0], held[1]
    for h in range(heads):
        state[head(h), :] = dot(left[:, head(h)], right[:, head(h)], TN)
    give(state, group, outs)
    for copy in copies[2:]:
        copy.wait()


def scan_body(count, reverse, arrived, sums, scratch):
    take([arrived], scratch, count)
    running_sums(scratch, count, reverse)
    give(scratch, count, [sums])


def inner_body(group, reverse, *refs):
    arrived, (sums, total) = refs[:-2], refs[-2:]
    take(arrived, sums, group)
    total[...] = running_sums(sums, group, reverse)


def outer_body(group, reverse, sums, other, *outs):
    me = lax.axis_index("ctx")
    place = lax.rem(me, group)
    later = me < group if reverse else me >= group
    carried = jnp.where(later, other[...], 0.0)
    for r, out in enumerate(outs):
        out[...] = rows_of(sums, group, lax.bitwise_xor(place, r))[...] + carried


def attend_body(heads, factor, group, q, k, v, og, gain, *refs):
    pieces, (attended, scores, stats, prefix) = refs[:-4], refs[-4:]
    take(pieces, prefix, group)
    causal = causal_mask(q.shape[0])
    power = 0.0
    inner = 0.0
    for h in range(heads):
        qh = q[:, head(h)]
        vh = v[:, head(h)]
        raw = dot(qh, k[:, head(h)], NT) * factor
        sc = jnp.where(causal, raw, 0.0).astype(BF16)
        scores[h] = sc
        att = factor * dot(qh, prefix[head(h), :].astype(BF16), NN) + dot(sc, vh, NN)
        attended[:, head(h)] = att
        weighted = og[:, head(h)].astype(F32) * gain[h : h + 1, :]
        power = power + att * att
        inner = inner + weighted * att
    stats[0:1, :] = jnp.sum(power.T, axis=0, keepdims=True)
    stats[1:2, :] = jnp.sum(inner.T, axis=0, keepdims=True)


def grad_body(heads, features, group, ways, attended, og, gain, q, *refs):
    stats, (normed, grad), outs, updates = refs[:ways], refs[ways : ways + 2], refs[ways + 2 : -1], refs[-1]
    total = stats[0][...]
    for other in stats[1:]:
        total = total + other[...]
    inv_rms = lax.rsqrt(total[0:1, :] / features + epsilon)
    bend = inv_rms * inv_rms * (total[1:2, :] / features)
    tokens = q.shape[0]
    inv_rms = jnp.broadcast_to(inv_rms, (HEAD, tokens)).T
    bend = jnp.broadcast_to(bend, (HEAD, tokens)).T
    for h in range(heads):
        att = attended[:, head(h)]
        gain_h = gain[h : h + 1, :]
        weighted = og[:, head(h)].astype(F32) * gain_h
        ga = (inv_rms * (weighted - att * bend)).astype(BF16)
        grad[:, head(h)] = ga
        updates[head(h), :] = dot(q[:, head(h)], ga, TN)
        normed[:, head(h)] = (att * inv_rms * gain_h).astype(BF16)
    give(updates, group, outs)


def final_body(heads, factor, group, ga, q, k, v, prefix, scores, normed, *refs):
    pieces, outs, (suffix, gq, gk, gv, sems) = refs[:-9], refs[-9:-5], refs[-5:]
    sources = [normed, gq, gk, gv]
    copies = [pltpu.make_async_copy(a, b, sems.at[i]) for i, (a, b) in enumerate(zip(sources, outs))]
    copies[0].start()
    take(pieces, suffix, group)
    causal = causal_mask(q.shape[0])
    grads = []
    for h in range(heads):
        gah = ga[:, head(h)]
        raw = dot(gah, v[:, head(h)], NT) * factor
        gs = jnp.where(causal, raw, 0.0).astype(BF16)
        grads.append(gs)
        out = factor * dot(gah, prefix[head(h), :].astype(BF16), NT)
        gq[:, head(h)] = (out + dot(gs, k[:, head(h)], NN)).astype(BF16)
    copies[1].start()
    for h in range(heads):
        suf = suffix[head(h), :].astype(BF16)
        part = dot(grads[h], q[:, head(h)], TN)
        gk[:, head(h)] = (factor * dot(v[:, head(h)], suf, NT) + part).astype(BF16)
    copies[2].start()
    for h in range(heads):
        suf = suffix[head(h), :].astype(BF16)
        part = dot(scores[h], ga[:, head(h)], TN)
        gv[:, head(h)] = (factor * dot(k[:, head(h)], suf, NN) + part).astype(BF16)
    copies[3].start()
    for copy in copies:
        copy.wait()


def partners(part, axis, step):
    return lax.ppermute(part, axis, [(i, i ^ step) for i in range(lax.axis_size(axis))])


def carried_in(pieces, group, reverse, state):
    count = lax.axis_size("ctx")
    sds = jax.ShapeDtypeStruct
    if len(pieces) == 1:
        arrived = lax.all_to_all(pieces[0], "ctx", 0, 0, tiled=True)
        sums = call(
            functools.partial(scan_body, count, reverse),
            sds(arrived.shape, F32), arrived, scratch=[state],
        )
        return [lax.all_to_all(sums, "ctx", 0, 0, tiled=True)]
    arrived = [pieces[0]] + [partners(pieces[r], "ctx", r) for r in range(1, group)]
    rows, width = pieces[0].shape
    sums, total = call(
        functools.partial(inner_body, group, reverse),
        (sds((group * rows, width), F32), sds((rows, width), F32)), *arrived,
    )
    other = partners(total, "ctx", group)
    back = call(
        functools.partial(outer_body, group, reverse),
        [sds((rows, width), F32)] * group, sums, other,
    )
    return [back[0]] + [partners(back[r], "ctx", r) for r in range(1, group)]


def from_all(part, axis):
    count = lax.axis_size(axis)
    if count & (count - 1) == 0:
        return [part] + [partners(part, axis, step) for step in range(1, count)]
    return [part] + [
        lax.ppermute(part, axis, [(i, (i + step) % count) for i in range(count)])
        for step in range(1, count)
    ]


def on_device(queries, keys, values, gain, out_grad):
    tokens, width = queries.shape
    heads = width // HEAD
    count = lax.axis_size("ctx")
    factor = (HEAD * tokens * count) ** (-0.5)
    features = width * lax.axis_size("tp")
    gains = gain.reshape(heads, HEAD)
    sds = jax.ShapeDtypeStruct
    wide = sds((tokens, width), F32)
    half = sds((tokens, width), BF16)
    state = pltpu.VMEM((width, HEAD), F32)
    if count in (4, 8):
        group = count // 2
        pieces = [sds((width // group, HEAD), F32)] * group
    else:
        group = count
        pieces = [sds((count, width // count, HEAD), F32)]

    given = (keys, values, queries, out_grad, gains)
    keys, values, queries, out_grad, gains, *states = call(
        functools.partial(states_body, heads, group, len(given)),
        (*(pltpu.VMEM(a.shape, a.dtype) for a in given), *pieces),
        *(pltpu.with_memory_space_constraint(a, pltpu.HBM) for a in given),
        ins=[HBM] * len(given),
        scratch=[state, pltpu.SemaphoreType.DMA((len(given),))],
    )
    prefix = carried_in(states, group, False, state)
    attended, scores, stats, prefix = call(
        functools.partial(attend_body, heads, factor, group),
        (wide, sds((heads, tokens, tokens), BF16), sds((2, tokens), F32), sds((width, HEAD), F32)),
        queries, keys, values, out_grad, gains, *prefix,
    )
    every = from_all(stats, "tp")
    normed, grad_attn, *updates = call(
        functools.partial(grad_body, heads, features, group, len(every)),
        (half, half, *pieces),
        attended, out_grad, gains, queries, *every,
        scratch=[state],
    )
    suffix = carried_in(updates, group, True, state)
    held = pltpu.VMEM((tokens, width), BF16)
    return call(
        functools.partial(final_body, heads, factor, group),
        (half, half, half, half),
        grad_attn, queries, keys, values, prefix, scores, normed, *suffix,
        dests=(HBM, HBM, HBM, HBM),
        scratch=[state, held, held, held, pltpu.SemaphoreType.DMA((4,))],
    )


def solution(mesh):
    placed = (P("ctx", "tp"), P("ctx", "tp"), P("ctx", "tp"), P("tp"), P("ctx", "tp"))
    return jax.shard_map(
        on_device,
        mesh=mesh,
        in_specs=placed,
        out_specs=(P("ctx", "tp"), P("ctx", "tp"), P("ctx", "tp"), P("ctx", "tp")),
        check_vma=False,
    )
```

```python
import functools

import jax
import jax.numpy as jnp
from jax import lax
from jax.experimental import pallas as pl
from jax.experimental.pallas import tpu as pltpu
from jax.sharding import PartitionSpec as P

HEAD = 128

epsilon = 1e-06
F32 = jnp.float32
BF16 = jnp.bfloat16

NN = (((1,), (0,)), ((), ()))
NT = (((1,), (1,)), ((), ()))
TN = (((0,), (0,)), ((), ()))


def dot(a, b, dims):
    return lax.dot_general(a, b, dims, preferred_element_type=F32)


VMEM = pl.BlockSpec(memory_space=pltpu.VMEM)
HBM = pl.BlockSpec(memory_space=pltpu.HBM)


def call(body, outs, *args, ins=None, dests=None, scratch=(), flops=1e7):
    moved = sum(a.size * a.dtype.itemsize for a in args)
    return pl.pallas_call(
        body,
        out_shape=outs,
        in_specs=ins or [VMEM] * len(args),
        out_specs=dests or jax.tree.map(lambda _: VMEM, outs),
        scratch_shapes=scratch,
        compiler_params=pltpu.CompilerParams(vmem_limit_bytes=16 * 1024 * 1024),
        cost_estimate=pl.CostEstimate(flops=int(flops), bytes_accessed=int(moved), transcendentals=0),
    )(*args)


def head(h):
    return slice(h * HEAD, (h + 1) * HEAD)


def causal_mask(tokens):
    row = lax.broadcasted_iota(jnp.int32, (tokens, tokens), 0)
    col = lax.broadcasted_iota(jnp.int32, (tokens, tokens), 1)
    return row >= col


def rows_of(scratch, parts, place):
    rows = scratch.shape[0] // parts
    return scratch.at[pl.ds(pl.multiple_of(place * rows, rows), rows), :]


def partner(i, group):
    return (group - i) % group


def give(scratch, group, outs):
    if len(outs) == 1:
        outs[0][...] = scratch[...].reshape(outs[0].shape)
        return
    place = lax.rem(lax.axis_index("ctx"), group)
    for i, out in enumerate(outs):
        out[...] = rows_of(scratch, group, lax.bitwise_xor(place, partner(i, group)))[...]


def take(ins, scratch, group):
    if len(ins) == 1:
        scratch[...] = ins[0][...].reshape(scratch.shape)
        return
    place = lax.rem(lax.axis_index("ctx"), group)
    for i, piece in enumerate(ins):
        rows_of(scratch, group, lax.bitwise_xor(place, partner(i, group)))[...] = piece[...]


def running_sums(scratch, parts, reverse):
    rows = scratch.shape[0] // parts
    running = jnp.zeros((rows, scratch.shape[1]), F32)
    for place in range(parts - 1, -1, -1) if reverse else range(parts):
        own = slice(place * rows, (place + 1) * rows)
        here = scratch[own, :]
        scratch[own, :] = running
        running = running + here
    return running


def states_body(heads, group, many, *refs):
    given, held, outs = refs[:many], refs[many : 2 * many], refs[2 * many : -2]
    state, sems = refs[-2:]
    copies = [pltpu.make_async_copy(a, b, sems.at[i]) for i, (a, b) in enumerate(zip(given, held))]
    for copy in copies:
        copy.start()
    copies[0].wait()
    copies[1].wait()
    left, right = held[0], held[1]
    for h in range(heads):
        state[head(h), :] = dot(left[:, head(h)], right[:, head(h)], TN)
    give(state, group, outs)
    for copy in copies[2:]:
        copy.wait()


def scan_body(count, reverse, arrived, sums, scratch):
    take([arrived], scratch, count)
    running_sums(scratch, count, reverse)
    give(scratch, count, [sums])


def inner_body(group, reverse, *refs):
    arrived, (sums, total) = refs[:-2], refs[-2:]
    take(arrived, sums, group)
    total[...] = running_sums(sums, group, reverse)


def hand_back(sums, over, takes, outs):
    group = len(outs)
    place = lax.rem(lax.axis_index("ctx"), group)
    carried = jnp.where(takes, over[...], 0.0)
    for i, out in enumerate(outs):
        out[...] = rows_of(sums, group, lax.bitwise_xor(place, partner(i, group)))[...] + carried


def outer_body(group, sums, over, *outs):
    hand_back(sums, over, lax.axis_index("ctx") < group, outs)


def merge_body(group, *refs):
    arrived, (early, over), outs, sums = refs[:group], refs[group : group + 2], refs[group + 2 : -1], refs[-1]
    late = lax.axis_index("ctx") >= group
    take(arrived, sums, group)
    running_sums(sums, group, False)
    sums[...] = jnp.where(late, sums[...], early[...])
    hand_back(sums, over, late, outs)


def scores_body(heads, factor, q, k, v, scores, attended):
    causal = causal_mask(q.shape[0])
    for h in range(heads):
        raw = dot(q[:, head(h)], k[:, head(h)], NT) * factor
        sc = jnp.where(causal, raw, 0.0).astype(BF16)
        scores[h] = sc
        attended[:, head(h)] = dot(sc, v[:, head(h)], NN)


def attend_body(heads, factor, group, q, og, gain, local, *refs):
    pieces, (attended, stats, prefix) = refs[:-3], refs[-3:]
    take(pieces, prefix, group)
    power = 0.0
    inner = 0.0
    for h in range(heads):
        att = factor * dot(q[:, head(h)], prefix[head(h), :].astype(BF16), NN) + local[:, head(h)]
        attended[:, head(h)] = att
        weighted = og[:, head(h)].astype(F32) * gain[h : h + 1, :]
        power = power + att * att
        inner = inner + weighted * att
    stats[0:1, :] = jnp.sum(power.T, axis=0, keepdims=True)
    stats[1:2, :] = jnp.sum(inner.T, axis=0, keepdims=True)


def grad_body(heads, features, group, ways, attended, og, gain, q, *refs):
    stats, (normed, grad), outs, updates = refs[:ways], refs[ways : ways + 2], refs[ways + 2 : -1], refs[-1]
    total = stats[0][...]
    for other in stats[1:]:
        total = total + other[...]
    inv_rms = lax.rsqrt(total[0:1, :] / features + epsilon)
    bend = inv_rms * inv_rms * (total[1:2, :] / features)
    tokens = q.shape[0]
    inv_rms = jnp.broadcast_to(inv_rms, (HEAD, tokens)).T
    bend = jnp.broadcast_to(bend, (HEAD, tokens)).T
    for h in range(heads):
        att = attended[:, head(h)]
        gain_h = gain[h : h + 1, :]
        weighted = og[:, head(h)].astype(F32) * gain_h
        ga = (inv_rms * (weighted - att * bend)).astype(BF16)
        grad[:, head(h)] = ga
        updates[head(h), :] = dot(q[:, head(h)], ga, TN)
        normed[:, head(h)] = (att * inv_rms * gain_h).astype(BF16)
    give(updates, group, outs)


def local_body(heads, factor, ga, q, k, v, prefix, scores, normed, normed_out, gq, gk_part, gv_part):
    normed_out[...] = normed[...]
    causal = causal_mask(q.shape[0])
    for h in range(heads):
        gah = ga[:, head(h)]
        raw = dot(gah, v[:, head(h)], NT) * factor
        gs = jnp.where(causal, raw, 0.0).astype(BF16)
        out = factor * dot(gah, prefix[head(h), :].astype(BF16), NT)
        gq[:, head(h)] = (out + dot(gs, k[:, head(h)], NN)).astype(BF16)
        gk_part[:, head(h)] = dot(gs, q[:, head(h)], TN)
        gv_part[:, head(h)] = dot(scores[h], gah, TN)


def final_body(heads, factor, group, k, v, gk_part, gv_part, *refs):
    pieces, outs, (suffix, gk, gv, sems) = refs[:-6], refs[-6:-4], refs[-4:]
    copies = [pltpu.make_async_copy(a, b, sems.at[i]) for i, (a, b) in enumerate(zip((gk, gv), outs))]
    take(pieces, suffix, group)
    suf = [suffix[head(h), :].astype(BF16) for h in range(heads)]
    for h in range(heads):
        gk[:, head(h)] = (factor * dot(v[:, head(h)], suf[h], NT) + gk_part[:, head(h)]).astype(BF16)
    copies[0].start()
    for h in range(heads):
        gv[:, head(h)] = (factor * dot(k[:, head(h)], suf[h], NN) + gv_part[:, head(h)]).astype(BF16)
    copies[1].start()
    for copy in copies:
        copy.wait()


def exchange(pieces, members):
    group = len(pieces)
    return [pieces[0]] + [
        lax.ppermute(pieces[i], "ctx", [(j, j ^ partner(i, group)) for j in members])
        for i in range(1, group)
    ]


def shared_scan(pieces, reverse, state):
    count = lax.axis_size("ctx")
    arrived = lax.all_to_all(pieces[0], "ctx", 0, 0, tiled=True)
    sums = call(
        functools.partial(scan_body, count, reverse),
        jax.ShapeDtypeStruct(arrived.shape, F32), arrived, scratch=[state],
    )
    return [lax.all_to_all(sums, "ctx", 0, 0, tiled=True)]


def earlier_sums(pieces, state):
    group = len(pieces)
    if group == 1:
        return shared_scan(pieces, False, state)
    sds = jax.ShapeDtypeStruct
    early, late = range(group), range(group, 2 * group)
    rows, width = pieces[0].shape
    sums, total = call(
        functools.partial(inner_body, group, False),
        (sds((group * rows, width), F32), sds((rows, width), F32)), *exchange(pieces, early),
    )
    over = lax.ppermute(total, "ctx", [(i, i + group) for i in early])
    back = call(
        functools.partial(merge_body, group),
        [sds((rows, width), F32)] * group, *exchange(pieces, late), sums, over, scratch=[state],
    )
    return exchange(back, range(2 * group))


def later_sums(pieces, state):
    group = len(pieces)
    if group == 1:
        return shared_scan(pieces, True, state)
    sds = jax.ShapeDtypeStruct
    rows, width = pieces[0].shape
    sums, total = call(
        functools.partial(inner_body, group, True),
        (sds((group * rows, width), F32), sds((rows, width), F32)),
        *exchange(pieces, range(2 * group)),
    )
    over = lax.ppermute(total, "ctx", [(i + group, i) for i in range(group)])
    back = call(
        functools.partial(outer_body, group), [sds((rows, width), F32)] * group, sums, over,
    )
    return exchange(back, range(2 * group))


def from_all(part, axis):
    count = lax.axis_size(axis)
    even = count & (count - 1) == 0
    steps = [1, 3, 2] if count == 4 else range(1, count)
    return [part] + [
        lax.ppermute(part, axis, [(i, i ^ step if even else (i + step) % count) for i in range(count)])
        for step in steps
    ]


def on_device(queries, keys, values, gain, out_grad):
    tokens, width = queries.shape
    heads = width // HEAD
    count = lax.axis_size("ctx")
    factor = (HEAD * tokens * count) ** (-0.5)
    features = width * lax.axis_size("tp")
    gains = gain.reshape(heads, HEAD)
    sds = jax.ShapeDtypeStruct
    wide = sds((tokens, width), F32)
    half = sds((tokens, width), BF16)
    state = pltpu.VMEM((width, HEAD), F32)
    if count in (4, 8):
        group = count // 2
        pieces = [sds((width // group, HEAD), F32)] * group
    else:
        group = count
        pieces = [sds((count, width // count, HEAD), F32)]

    given = (keys, values, queries, out_grad, gains)
    keys, values, queries, out_grad, gains, *states = call(
        functools.partial(states_body, heads, group, len(given)),
        (*(pltpu.VMEM(a.shape, a.dtype) for a in given), *pieces),
        *(pltpu.with_memory_space_constraint(a, pltpu.HBM) for a in given),
        ins=[HBM] * len(given),
        scratch=[state, pltpu.SemaphoreType.DMA((len(given),))],
    )
    prefix = earlier_sums(states, state)
    pairs = heads * tokens * tokens * HEAD
    scores, local = call(
        functools.partial(scores_body, heads, factor),
        (sds((heads, tokens, tokens), BF16), wide),
        queries, keys, values,
        flops=4 * pairs,
    )
    attended, stats, prefix = call(
        functools.partial(attend_body, heads, factor, group),
        (wide, sds((2, tokens), F32), sds((width, HEAD), F32)),
        queries, out_grad, gains, local, *prefix,
    )
    every = from_all(stats, "tp")
    normed, grad_attn, *updates = call(
        functools.partial(grad_body, heads, features, group, len(every)),
        (pltpu.VMEM((tokens, width), BF16), half, *pieces),
        attended, out_grad, gains, queries, *every,
        scratch=[state],
    )
    suffix = later_sums(updates, state)
    normed, grad_q, gk_part, gv_part = call(
        functools.partial(local_body, heads, factor),
        (half, half, wide, wide),
        grad_attn, queries, keys, values, prefix, scores, normed,
        flops=9 * pairs,
    )
    held = pltpu.VMEM((tokens, width), BF16)
    grad_k, grad_v = call(
        functools.partial(final_body, heads, factor, group),
        (half, half),
        keys, values, gk_part, gv_part, *suffix,
        dests=(HBM, HBM),
        scratch=[state, held, held, pltpu.SemaphoreType.DMA((2,))],
    )
    return normed, grad_q, grad_k, grad_v


def solution(mesh):
    placed = (P("ctx", "tp"), P("ctx", "tp"), P("ctx", "tp"), P("tp"), P("ctx", "tp"))
    return jax.shard_map(
        on_device,
        mesh=mesh,
        in_specs=placed,
        out_specs=(P("ctx", "tp"), P("ctx", "tp"), P("ctx", "tp"), P("ctx", "tp")),
        check_vma=False,
    )
```

```python
import functools

import jax
import jax.numpy as jnp
from jax import lax
from jax.experimental import pallas as pl
from jax.experimental.pallas import tpu as pltpu
from jax.sharding import PartitionSpec as P

HEAD = 128

epsilon = 1e-06
F32 = jnp.float32
BF16 = jnp.bfloat16

NN = (((1,), (0,)), ((), ()))
NT = (((1,), (1,)), ((), ()))
TN = (((0,), (0,)), ((), ()))


def dot(a, b, dims):
    return lax.dot_general(a, b, dims, preferred_element_type=F32)


VMEM = pl.BlockSpec(memory_space=pltpu.VMEM)
HBM = pl.BlockSpec(memory_space=pltpu.HBM)


def call(body, outs, *args, ins=None, dests=None, scratch=(), flops=1e7):
    moved = sum(a.size * a.dtype.itemsize for a in args)
    return pl.pallas_call(
        body,
        out_shape=outs,
        in_specs=ins or [VMEM] * len(args),
        out_specs=dests or jax.tree.map(lambda _: VMEM, outs),
        scratch_shapes=scratch,
        compiler_params=pltpu.CompilerParams(vmem_limit_bytes=16 * 1024 * 1024),
        cost_estimate=pl.CostEstimate(flops=int(flops), bytes_accessed=int(moved), transcendentals=0),
    )(*args)


def head(h):
    return slice(h * HEAD, (h + 1) * HEAD)


def causal_mask(tokens):
    row = lax.broadcasted_iota(jnp.int32, (tokens, tokens), 0)
    col = lax.broadcasted_iota(jnp.int32, (tokens, tokens), 1)
    return row >= col


def rows_of(scratch, parts, place):
    rows = scratch.shape[0] // parts
    return scratch.at[pl.ds(pl.multiple_of(place * rows, rows), rows), :]


def partner(i, group):
    return (group - i) % group


def give(scratch, group, outs):
    if len(outs) == 1:
        outs[0][...] = scratch[...].reshape(outs[0].shape)
        return
    place = lax.rem(lax.axis_index("ctx"), group)
    for i, out in enumerate(outs):
        out[...] = rows_of(scratch, group, lax.bitwise_xor(place, partner(i, group)))[...]


def take(ins, scratch, group):
    if len(ins) == 1:
        scratch[...] = ins[0][...].reshape(scratch.shape)
        return
    place = lax.rem(lax.axis_index("ctx"), group)
    for i, piece in enumerate(ins):
        rows_of(scratch, group, lax.bitwise_xor(place, partner(i, group)))[...] = piece[...]


def running_sums(scratch, parts, reverse):
    rows = scratch.shape[0] // parts
    running = jnp.zeros((rows, scratch.shape[1]), F32)
    for place in range(parts - 1, -1, -1) if reverse else range(parts):
        own = slice(place * rows, (place + 1) * rows)
        here = scratch[own, :]
        scratch[own, :] = running
        running = running + here
    return running


def states_body(heads, group, many, *refs):
    given, held, outs = refs[:many], refs[many : 2 * many], refs[2 * many : -2]
    state, sems = refs[-2:]
    copies = [pltpu.make_async_copy(a, b, sems.at[i]) for i, (a, b) in enumerate(zip(given, held))]
    for copy in copies:
        copy.start()
    copies[0].wait()
    copies[1].wait()
    left, right = held[0], held[1]
    for h in range(heads):
        state[head(h), :] = dot(left[:, head(h)], right[:, head(h)], TN)
    give(state, group, outs)
    for copy in copies[2:]:
        copy.wait()


def scan_body(count, reverse, arrived, sums, scratch):
    take([arrived], scratch, count)
    running_sums(scratch, count, reverse)
    give(scratch, count, [sums])


def inner_body(group, reverse, *refs):
    arrived, (sums, total) = refs[:-2], refs[-2:]
    take(arrived, sums, group)
    total[...] = running_sums(sums, group, reverse)


def outer_body(group, reverse, sums, over, *outs):
    me = lax.axis_index("ctx")
    place = lax.rem(me, group)
    takes = me < group if reverse else me >= group
    carried = jnp.where(takes, over[...], 0.0)
    for i, out in enumerate(outs):
        out[...] = rows_of(sums, group, lax.bitwise_xor(place, partner(i, group)))[...] + carried


def scores_body(heads, factor, q, k, v, scores, attended):
    causal = causal_mask(q.shape[0])
    for h in range(heads):
        raw = dot(q[:, head(h)], k[:, head(h)], NT) * factor
        sc = jnp.where(causal, raw, 0.0).astype(BF16)
        scores[h] = sc
        attended[:, head(h)] = dot(sc, v[:, head(h)], NN)


def attend_body(heads, factor, group, q, og, gain, local, *refs):
    pieces, (attended, stats, prefix) = refs[:-3], refs[-3:]
    take(pieces, prefix, group)
    power = 0.0
    inner = 0.0
    for h in range(heads):
        att = factor * dot(q[:, head(h)], prefix[head(h), :].astype(BF16), NN) + local[:, head(h)]
        attended[:, head(h)] = att
        weighted = og[:, head(h)].astype(F32) * gain[h : h + 1, :]
        power = power + att * att
        inner = inner + weighted * att
    stats[0:1, :] = jnp.sum(power.T, axis=0, keepdims=True)
    stats[1:2, :] = jnp.sum(inner.T, axis=0, keepdims=True)


def grad_body(heads, features, group, ways, attended, og, gain, q, *refs):
    stats, (normed, grad), outs, updates = refs[:ways], refs[ways : ways + 2], refs[ways + 2 : -1], refs[-1]
    total = stats[0][...]
    for other in stats[1:]:
        total = total + other[...]
    inv_rms = lax.rsqrt(total[0:1, :] / features + epsilon)
    bend = inv_rms * inv_rms * (total[1:2, :] / features)
    tokens = q.shape[0]
    inv_rms = jnp.broadcast_to(inv_rms, (HEAD, tokens)).T
    bend = jnp.broadcast_to(bend, (HEAD, tokens)).T
    for h in range(heads):
        att = attended[:, head(h)]
        gain_h = gain[h : h + 1, :]
        weighted = og[:, head(h)].astype(F32) * gain_h
        ga = (inv_rms * (weighted - att * bend)).astype(BF16)
        grad[:, head(h)] = ga
        updates[head(h), :] = dot(q[:, head(h)], ga, TN)
        normed[:, head(h)] = (att * inv_rms * gain_h).astype(BF16)
    give(updates, group, outs)


def local_body(heads, factor, ga, q, k, v, prefix, scores, normed, normed_out, gq, gk_part, gv_part):
    normed_out[...] = normed[...]
    causal = causal_mask(q.shape[0])
    for h in range(heads):
        gah = ga[:, head(h)]
        raw = dot(gah, v[:, head(h)], NT) * factor
        gs = jnp.where(causal, raw, 0.0).astype(BF16)
        out = factor * dot(gah, prefix[head(h), :].astype(BF16), NT)
        gq[:, head(h)] = (out + dot(gs, k[:, head(h)], NN)).astype(BF16)
        gk_part[:, head(h)] = dot(gs, q[:, head(h)], TN)
        gv_part[:, head(h)] = dot(scores[h], gah, TN)


def final_body(heads, factor, group, k, v, gk_part, gv_part, *refs):
    pieces, outs, (suffix, gk, gv, sems) = refs[:-6], refs[-6:-4], refs[-4:]
    copies = [pltpu.make_async_copy(a, b, sems.at[i]) for i, (a, b) in enumerate(zip((gk, gv), outs))]
    take(pieces, suffix, group)
    suf = [suffix[head(h), :].astype(BF16) for h in range(heads)]
    for h in range(heads):
        gk[:, head(h)] = (factor * dot(v[:, head(h)], suf[h], NT) + gk_part[:, head(h)]).astype(BF16)
    copies[0].start()
    for h in range(heads):
        gv[:, head(h)] = (factor * dot(k[:, head(h)], suf[h], NN) + gv_part[:, head(h)]).astype(BF16)
    copies[1].start()
    for copy in copies:
        copy.wait()


def exchange(pieces):
    group = len(pieces)
    return [pieces[0]] + [
        lax.ppermute(pieces[i], "ctx", [(j, j ^ partner(i, group)) for j in range(2 * group)])
        for i in range(1, group)
    ]


def carried_in(pieces, reverse, state):
    group = len(pieces)
    count = lax.axis_size("ctx")
    sds = jax.ShapeDtypeStruct
    if group == 1:
        arrived = lax.all_to_all(pieces[0], "ctx", 0, 0, tiled=True)
        sums = call(
            functools.partial(scan_body, count, reverse),
            sds(arrived.shape, F32), arrived, scratch=[state],
        )
        return [lax.all_to_all(sums, "ctx", 0, 0, tiled=True)]
    rows, width = pieces[0].shape
    sums, total = call(
        functools.partial(inner_body, group, reverse),
        (sds((group * rows, width), F32), sds((rows, width), F32)), *exchange(pieces),
    )
    over = lax.ppermute(total, "ctx", [(j, j ^ group) for j in range(count)])
    back = call(
        functools.partial(outer_body, group, reverse),
        [sds((rows, width), F32)] * group, sums, over,
    )
    return exchange(back)


def from_all(part, axis):
    count = lax.axis_size(axis)
    even = count & (count - 1) == 0
    return [part] + [
        lax.ppermute(part, axis, [(i, i ^ step if even else (i + step) % count) for i in range(count)])
        for step in range(1, count)
    ]


def on_device(queries, keys, values, gain, out_grad):
    tokens, width = queries.shape
    heads = width // HEAD
    count = lax.axis_size("ctx")
    factor = (HEAD * tokens * count) ** (-0.5)
    features = width * lax.axis_size("tp")
    gains = gain.reshape(heads, HEAD)
    sds = jax.ShapeDtypeStruct
    wide = sds((tokens, width), F32)
    half = sds((tokens, width), BF16)
    state = pltpu.VMEM((width, HEAD), F32)
    if count in (4, 8):
        group = count // 2
        pieces = [sds((width // group, HEAD), F32)] * group
    else:
        group = count
        pieces = [sds((count, width // count, HEAD), F32)]

    given = (keys, values, queries, out_grad, gains)
    keys, values, queries, out_grad, gains, *states = call(
        functools.partial(states_body, heads, group, len(given)),
        (*(pltpu.VMEM(a.shape, a.dtype) for a in given), *pieces),
        *(pltpu.with_memory_space_constraint(a, pltpu.HBM) for a in given),
        ins=[HBM] * len(given),
        scratch=[state, pltpu.SemaphoreType.DMA((len(given),))],
    )
    prefix = carried_in(states, False, state)
    pairs = heads * tokens * tokens * HEAD
    scores, local = call(
        functools.partial(scores_body, heads, factor),
        (sds((heads, tokens, tokens), BF16), wide),
        queries, keys, values,
        flops=4 * pairs,
    )
    attended, stats, prefix = call(
        functools.partial(attend_body, heads, factor, group),
        (wide, sds((2, tokens), F32), sds((width, HEAD), F32)),
        queries, out_grad, gains, local, *prefix,
    )
    every = from_all(stats, "tp")
    normed, grad_attn, *updates = call(
        functools.partial(grad_body, heads, features, group, len(every)),
        (pltpu.VMEM((tokens, width), BF16), half, *pieces),
        attended, out_grad, gains, queries, *every,
        scratch=[state],
    )
    suffix = carried_in(updates, True, state)
    normed, grad_q, gk_part, gv_part = call(
        functools.partial(local_body, heads, factor),
        (half, half, wide, wide),
        grad_attn, queries, keys, values, prefix, scores, normed,
        flops=9 * pairs,
    )
    held = pltpu.VMEM((tokens, width), BF16)
    grad_k, grad_v = call(
        functools.partial(final_body, heads, factor, group),
        (half, half),
        keys, values, gk_part, gv_part, *suffix,
        dests=(HBM, HBM),
        scratch=[state, held, held, pltpu.SemaphoreType.DMA((2,))],
    )
    return normed, grad_q, grad_k, grad_v


def solution(mesh):
    placed = (P("ctx", "tp"), P("ctx", "tp"), P("ctx", "tp"), P("tp"), P("ctx", "tp"))
    return jax.shard_map(
        on_device,
        mesh=mesh,
        in_specs=placed,
        out_specs=(P("ctx", "tp"), P("ctx", "tp"), P("ctx", "tp"), P("ctx", "tp")),
        check_vma=False,
    )
```

```python
import functools

import jax
import jax.numpy as jnp
from jax import lax
from jax.experimental import pallas as pl
from jax.experimental.pallas import tpu as pltpu
from jax.sharding import PartitionSpec as P

HEAD = 128

epsilon = 1e-06
F32 = jnp.float32
BF16 = jnp.bfloat16

NN = (((1,), (0,)), ((), ()))
NT = (((1,), (1,)), ((), ()))
TN = (((0,), (0,)), ((), ()))


def dot(a, b, dims):
    return lax.dot_general(a, b, dims, preferred_element_type=F32)


VMEM = pl.BlockSpec(memory_space=pltpu.VMEM)
HBM = pl.BlockSpec(memory_space=pltpu.HBM)


def call(body, outs, *args, ins=None, dests=None, scratch=(), flops=1e7):
    moved = sum(a.size * a.dtype.itemsize for a in args)
    return pl.pallas_call(
        body,
        out_shape=outs,
        in_specs=ins or [VMEM] * len(args),
        out_specs=dests or jax.tree.map(lambda _: VMEM, outs),
        scratch_shapes=scratch,
        compiler_params=pltpu.CompilerParams(vmem_limit_bytes=16 * 1024 * 1024),
        cost_estimate=pl.CostEstimate(flops=int(flops), bytes_accessed=int(moved), transcendentals=0),
    )(*args)


def head(h):
    return slice(h * HEAD, (h + 1) * HEAD)


def causal_mask(tokens):
    row = lax.broadcasted_iota(jnp.int32, (tokens, tokens), 0)
    col = lax.broadcasted_iota(jnp.int32, (tokens, tokens), 1)
    return row >= col


def rows_of(scratch, parts, place):
    rows = scratch.shape[0] // parts
    return scratch.at[pl.ds(pl.multiple_of(place * rows, rows), rows), :]


def partner(i, group):
    return (group - i) % group


def give(scratch, group, outs):
    if len(outs) == 1:
        outs[0][...] = scratch[...].reshape(outs[0].shape)
        return
    place = lax.rem(lax.axis_index("ctx"), group)
    for i, out in enumerate(outs):
        out[...] = rows_of(scratch, group, lax.bitwise_xor(place, partner(i, group)))[...]


def take(ins, scratch, group):
    if len(ins) == 1:
        scratch[...] = ins[0][...].reshape(scratch.shape)
        return
    place = lax.rem(lax.axis_index("ctx"), group)
    for i, piece in enumerate(ins):
        rows_of(scratch, group, lax.bitwise_xor(place, partner(i, group)))[...] = piece[...]


def running_sums(scratch, parts, reverse):
    rows = scratch.shape[0] // parts
    running = jnp.zeros((rows, scratch.shape[1]), F32)
    for place in range(parts - 1, -1, -1) if reverse else range(parts):
        own = slice(place * rows, (place + 1) * rows)
        here = scratch[own, :]
        scratch[own, :] = running
        running = running + here
    return running


def states_body(heads, group, many, *refs):
    given, held, outs = refs[:many], refs[many : 2 * many], refs[2 * many : -2]
    state, sems = refs[-2:]
    copies = [pltpu.make_async_copy(a, b, sems.at[i]) for i, (a, b) in enumerate(zip(given, held))]
    for copy in copies:
        copy.start()
    copies[0].wait()
    copies[1].wait()
    left, right = held[0], held[1]
    for h in range(heads):
        state[head(h), :] = dot(left[:, head(h)], right[:, head(h)], TN)
    give(state, group, outs)
    for copy in copies[2:]:
        copy.wait()


def scan_body(count, reverse, arrived, sums, scratch):
    take([arrived], scratch, count)
    running_sums(scratch, count, reverse)
    give(scratch, count, [sums])


def inner_body(group, reverse, *refs):
    arrived, total, outs, sums = refs[:group], refs[group], refs[group + 1 : -1], refs[-1]
    take(arrived, sums, group)
    total[...] = running_sums(sums, group, reverse)
    give(sums, group, outs)


def add_body(group, sums, over, *outs):
    place = lax.rem(lax.axis_index("ctx"), group)
    for i, out in enumerate(outs):
        out[...] = rows_of(sums, group, lax.bitwise_xor(place, partner(i, group)))[...] + over[...]


def late_body(group, reverse, *refs):
    arrived, over, outs, sums = refs[:group], refs[group], refs[group + 1 : -1], refs[-1]
    take(arrived, sums, group)
    running_sums(sums, group, reverse)
    add_body(group, sums, over, *outs)


def pick(pieces, scratch, group):
    many = len(pieces) // 2
    if many == 0:
        take(pieces, scratch, group)
        return
    early = lax.axis_index("ctx") < group
    place = lax.rem(lax.axis_index("ctx"), group)
    for i in range(many):
        rows = rows_of(scratch, group, lax.bitwise_xor(place, partner(i, group)))
        rows[...] = jnp.where(early, pieces[i][...], pieces[many + i][...])


def scores_body(heads, factor, q, k, v, scores, attended):
    causal = causal_mask(q.shape[0])
    for h in range(heads):
        raw = dot(q[:, head(h)], k[:, head(h)], NT) * factor
        sc = jnp.where(causal, raw, 0.0).astype(BF16)
        scores[h] = sc
        attended[:, head(h)] = dot(sc, v[:, head(h)], NN)


def attend_body(heads, factor, group, q, og, gain, local, *refs):
    pieces, (attended, stats, prefix) = refs[:-3], refs[-3:]
    pick(pieces, prefix, group)
    power = 0.0
    inner = 0.0
    for h in range(heads):
        att = factor * dot(q[:, head(h)], prefix[head(h), :].astype(BF16), NN) + local[:, head(h)]
        attended[:, head(h)] = att
        weighted = og[:, head(h)].astype(F32) * gain[h : h + 1, :]
        power = power + att * att
        inner = inner + weighted * att
    stats[0:1, :] = jnp.sum(power.T, axis=0, keepdims=True)
    stats[1:2, :] = jnp.sum(inner.T, axis=0, keepdims=True)


def grad_body(heads, features, group, ways, attended, og, gain, q, *refs):
    stats, (normed, grad), outs, updates = refs[:ways], refs[ways : ways + 2], refs[ways + 2 : -1], refs[-1]
    total = stats[0][...]
    for other in stats[1:]:
        total = total + other[...]
    inv_rms = lax.rsqrt(total[0:1, :] / features + epsilon)
    bend = inv_rms * inv_rms * (total[1:2, :] / features)
    tokens = q.shape[0]
    inv_rms = jnp.broadcast_to(inv_rms, (HEAD, tokens)).T
    bend = jnp.broadcast_to(bend, (HEAD, tokens)).T
    for h in range(heads):
        att = attended[:, head(h)]
        gain_h = gain[h : h + 1, :]
        weighted = og[:, head(h)].astype(F32) * gain_h
        ga = (inv_rms * (weighted - att * bend)).astype(BF16)
        grad[:, head(h)] = ga
        updates[head(h), :] = dot(q[:, head(h)], ga, TN)
        normed[:, head(h)] = (att * inv_rms * gain_h).astype(BF16)
    give(updates, group, outs)


def local_body(heads, factor, ga, q, k, v, prefix, scores, normed, normed_out, gq, gk_part, gv_part):
    normed_out[...] = normed[...]
    causal = causal_mask(q.shape[0])
    for h in range(heads):
        gah = ga[:, head(h)]
        raw = dot(gah, v[:, head(h)], NT) * factor
        gs = jnp.where(causal, raw, 0.0).astype(BF16)
        out = factor * dot(gah, prefix[head(h), :].astype(BF16), NT)
        gq[:, head(h)] = (out + dot(gs, k[:, head(h)], NN)).astype(BF16)
        gk_part[:, head(h)] = dot(gs, q[:, head(h)], TN)
        gv_part[:, head(h)] = dot(scores[h], gah, TN)


def final_body(heads, factor, group, k, v, gk_part, gv_part, *refs):
    pieces, outs, (suffix, gk, gv, sems) = refs[:-6], refs[-6:-4], refs[-4:]
    copies = [pltpu.make_async_copy(a, b, sems.at[i]) for i, (a, b) in enumerate(zip((gk, gv), outs))]
    pick(pieces, suffix, group)
    suf = [suffix[head(h), :].astype(BF16) for h in range(heads)]
    for h in range(heads):
        gk[:, head(h)] = (factor * dot(v[:, head(h)], suf[h], NT) + gk_part[:, head(h)]).astype(BF16)
    copies[0].start()
    for h in range(heads):
        gv[:, head(h)] = (factor * dot(k[:, head(h)], suf[h], NN) + gv_part[:, head(h)]).astype(BF16)
    copies[1].start()
    for copy in copies:
        copy.wait()


def exchange(pieces, active):
    group = len(pieces)
    return [pieces[0]] + [
        lax.ppermute(
            pieces[i],
            "ctx",
            [(j, j ^ partner(i, group) if j in active else j) for j in range(2 * group)],
        )
        for i in range(1, group)
    ]


def carried_in(pieces, reverse, state):
    group = len(pieces)
    count = lax.axis_size("ctx")
    sds = jax.ShapeDtypeStruct
    if group == 1:
        arrived = lax.all_to_all(pieces[0], "ctx", 0, 0, tiled=True)
        sums = call(
            functools.partial(scan_body, count, reverse),
            sds(arrived.shape, F32), arrived, scratch=[state],
        )
        return [lax.all_to_all(sums, "ctx", 0, 0, tiled=True)]
    rows, width = pieces[0].shape
    piece = sds((rows, width), F32)
    early, late, both = range(group), range(group, count), range(count)
    first, second = (late, early) if reverse else (early, late)
    kept = [sds((group * rows, width), F32)] if reverse else []
    total, *back = call(
        functools.partial(inner_body, group, reverse),
        [piece] * (group + 1) + kept,
        *exchange(pieces, both if reverse else first),
        scratch=[] if reverse else [state],
    )
    over = lax.ppermute(total, "ctx", [(j, j ^ group) for j in both])
    ahead = exchange(back[:group], first)
    if reverse:
        back = call(functools.partial(add_body, group), [piece] * group, back[group], over)
    else:
        back = call(
            functools.partial(late_body, group, reverse),
            [piece] * group, *exchange(pieces, second), over, scratch=[state],
        )
    behind = exchange(back, second)
    return [*behind, *ahead] if reverse else [*ahead, *behind]


def from_all(part, axis):
    count = lax.axis_size(axis)
    even = count & (count - 1) == 0
    return [part] + [
        lax.ppermute(part, axis, [(i, i ^ step if even else (i + step) % count) for i in range(count)])
        for step in range(1, count)
    ]


def on_device(queries, keys, values, gain, out_grad):
    tokens, width = queries.shape
    heads = width // HEAD
    count = lax.axis_size("ctx")
    factor = (HEAD * tokens * count) ** (-0.5)
    features = width * lax.axis_size("tp")
    gains = gain.reshape(heads, HEAD)
    sds = jax.ShapeDtypeStruct
    wide = sds((tokens, width), F32)
    half = sds((tokens, width), BF16)
    state = pltpu.VMEM((width, HEAD), F32)
    if count in (4, 8):
        group = count // 2
        pieces = [sds((width // group, HEAD), F32)] * group
    else:
        group = count
        pieces = [sds((count, width // count, HEAD), F32)]

    given = (keys, values, queries, out_grad, gains)
    keys, values, queries, out_grad, gains, *states = call(
        functools.partial(states_body, heads, group, len(given)),
        (*(pltpu.VMEM(a.shape, a.dtype) for a in given), *pieces),
        *(pltpu.with_memory_space_constraint(a, pltpu.HBM) for a in given),
        ins=[HBM] * len(given),
        scratch=[state, pltpu.SemaphoreType.DMA((len(given),))],
    )
    prefix = carried_in(states, False, state)
    pairs = heads * tokens * tokens * HEAD
    scores, local = call(
        functools.partial(scores_body, heads, factor),
        (sds((heads, tokens, tokens), BF16), wide),
        queries, keys, values,
        flops=4 * pairs,
    )
    attended, stats, prefix = call(
        functools.partial(attend_body, heads, factor, group),
        (wide, sds((2, tokens), F32), sds((width, HEAD), F32)),
        queries, out_grad, gains, local, *prefix,
    )
    every = from_all(stats, "tp")
    normed, grad_attn, *updates = call(
        functools.partial(grad_body, heads, features, group, len(every)),
        (pltpu.VMEM((tokens, width), BF16), half, *pieces),
        attended, out_grad, gains, queries, *every,
        scratch=[state],
    )
    suffix = carried_in(updates, True, state)
    normed, grad_q, gk_part, gv_part = call(
        functools.partial(local_body, heads, factor),
        (half, half, wide, wide),
        grad_attn, queries, keys, values, prefix, scores, normed,
        flops=9 * pairs,
    )
    held = pltpu.VMEM((tokens, width), BF16)
    grad_k, grad_v = call(
        functools.partial(final_body, heads, factor, group),
        (half, half),
        keys, values, gk_part, gv_part, *suffix,
        dests=(HBM, HBM),
        scratch=[state, held, held, pltpu.SemaphoreType.DMA((2,))],
    )
    return normed, grad_q, grad_k, grad_v


def solution(mesh):
    placed = (P("ctx", "tp"), P("ctx", "tp"), P("ctx", "tp"), P("tp"), P("ctx", "tp"))
    return jax.shard_map(
        on_device,
        mesh=mesh,
        in_specs=placed,
        out_specs=(P("ctx", "tp"), P("ctx", "tp"), P("ctx", "tp"), P("ctx", "tp")),
        check_vma=False,
    )
```

```python
import functools

import jax
import jax.numpy as jnp
from jax import lax
from jax.experimental import pallas as pl
from jax.experimental.pallas import tpu as pltpu
from jax.sharding import PartitionSpec as P

HEAD = 128

epsilon = 1e-06
F32 = jnp.float32
BF16 = jnp.bfloat16

NN = (((1,), (0,)), ((), ()))
NT = (((1,), (1,)), ((), ()))
TN = (((0,), (0,)), ((), ()))


def dot(a, b, dims):
    return lax.dot_general(a, b, dims, preferred_element_type=F32)


VMEM = pl.BlockSpec(memory_space=pltpu.VMEM)
HBM = pl.BlockSpec(memory_space=pltpu.HBM)


def call(body, outs, *args, ins=None, dests=None, scratch=(), flops=1e7):
    moved = sum(a.size * a.dtype.itemsize for a in args)
    return pl.pallas_call(
        body,
        out_shape=outs,
        in_specs=ins or [VMEM] * len(args),
        out_specs=dests or jax.tree.map(lambda _: VMEM, outs),
        scratch_shapes=scratch,
        compiler_params=pltpu.CompilerParams(vmem_limit_bytes=16 * 1024 * 1024),
        cost_estimate=pl.CostEstimate(flops=int(flops), bytes_accessed=int(moved), transcendentals=0),
    )(*args)


def head(h):
    return slice(h * HEAD, (h + 1) * HEAD)


def causal_mask(tokens):
    row = lax.broadcasted_iota(jnp.int32, (tokens, tokens), 0)
    col = lax.broadcasted_iota(jnp.int32, (tokens, tokens), 1)
    return row >= col


def rows_of(scratch, parts, place):
    rows = scratch.shape[0] // parts
    return scratch.at[pl.ds(pl.multiple_of(place * rows, rows), rows), :]


def partner(i, group):
    return (group - i) % group


def give(scratch, group, outs):
    if len(outs) == 1:
        outs[0][...] = scratch[...].reshape(outs[0].shape)
        return
    place = lax.rem(lax.axis_index("ctx"), group)
    for i, out in enumerate(outs):
        out[...] = rows_of(scratch, group, lax.bitwise_xor(place, partner(i, group)))[...]


def take(ins, scratch, group):
    if len(ins) == 1:
        scratch[...] = ins[0][...].reshape(scratch.shape)
        return
    place = lax.rem(lax.axis_index("ctx"), group)
    for i, piece in enumerate(ins):
        rows_of(scratch, group, lax.bitwise_xor(place, partner(i, group)))[...] = piece[...]


def running_sums(scratch, parts, reverse):
    rows = scratch.shape[0] // parts
    running = jnp.zeros((rows, scratch.shape[1]), F32)
    for place in range(parts - 1, -1, -1) if reverse else range(parts):
        own = slice(place * rows, (place + 1) * rows)
        here = scratch[own, :]
        scratch[own, :] = running
        running = running + here
    return running


def states_body(heads, group, many, *refs):
    given, held, outs = refs[:many], refs[many : 2 * many], refs[2 * many : -2]
    state, sems = refs[-2:]
    copies = [pltpu.make_async_copy(a, b, sems.at[i]) for i, (a, b) in enumerate(zip(given, held))]
    for copy in copies:
        copy.start()
    copies[0].wait()
    copies[1].wait()
    left, right = held[0], held[1]
    for h in range(heads):
        state[head(h), :] = dot(left[:, head(h)], right[:, head(h)], TN)
    give(state, group, outs)
    for copy in copies[2:]:
        copy.wait()


def scan_body(count, reverse, arrived, sums, scratch):
    take([arrived], scratch, count)
    running_sums(scratch, count, reverse)
    give(scratch, count, [sums])


def inner_body(group, reverse, *refs):
    arrived, total, outs, sums = refs[:group], refs[group], refs[group + 1 : -1], refs[-1]
    take(arrived, sums, group)
    total[...] = running_sums(sums, group, reverse)
    give(sums, group, outs)


def add_body(group, sums, over, *outs):
    place = lax.rem(lax.axis_index("ctx"), group)
    for i, out in enumerate(outs):
        out[...] = rows_of(sums, group, lax.bitwise_xor(place, partner(i, group)))[...] + over[...]


def late_body(group, reverse, *refs):
    arrived, over, outs, sums = refs[:group], refs[group], refs[group + 1 : -1], refs[-1]
    take(arrived, sums, group)
    running_sums(sums, group, reverse)
    add_body(group, sums, over, *outs)


def pick(pieces, scratch, group):
    many = len(pieces) // 2
    if many == 0:
        take(pieces, scratch, group)
        return
    early = lax.axis_index("ctx") < group
    place = lax.rem(lax.axis_index("ctx"), group)
    for i in range(many):
        rows = rows_of(scratch, group, lax.bitwise_xor(place, partner(i, group)))
        rows[...] = jnp.where(early, pieces[i][...], pieces[many + i][...])


def scores_body(heads, factor, q, k, v, scores, attended):
    causal = causal_mask(q.shape[0])
    for h in range(heads):
        raw = dot(q[:, head(h)], k[:, head(h)], NT) * factor
        sc = jnp.where(causal, raw, 0.0).astype(BF16)
        scores[h] = sc
        attended[:, head(h)] = dot(sc, v[:, head(h)], NN)


def attend_body(heads, factor, group, q, og, gain, local, *refs):
    pieces, (attended, stats, prefix) = refs[:-3], refs[-3:]
    pick(pieces, prefix, group)
    power = 0.0
    inner = 0.0
    for h in range(heads):
        att = factor * dot(q[:, head(h)], prefix[head(h), :].astype(BF16), NN) + local[:, head(h)]
        attended[:, head(h)] = att
        weighted = og[:, head(h)].astype(F32) * gain[h : h + 1, :]
        power = power + att * att
        inner = inner + weighted * att
    stats[0:1, :] = jnp.sum(power.T, axis=0, keepdims=True)
    stats[1:2, :] = jnp.sum(inner.T, axis=0, keepdims=True)


def grad_body(heads, features, group, ways, attended, og, gain, q, *refs):
    stats, (normed, grad), outs, updates = refs[:ways], refs[ways : ways + 2], refs[ways + 2 : -1], refs[-1]
    total = stats[0][...]
    for other in stats[1:]:
        total = total + other[...]
    inv_rms = lax.rsqrt(total[0:1, :] / features + epsilon)
    bend = inv_rms * inv_rms * (total[1:2, :] / features)
    tokens = q.shape[0]
    inv_rms = jnp.broadcast_to(inv_rms, (HEAD, tokens)).T
    bend = jnp.broadcast_to(bend, (HEAD, tokens)).T
    for h in range(heads):
        att = attended[:, head(h)]
        gain_h = gain[h : h + 1, :]
        weighted = og[:, head(h)].astype(F32) * gain_h
        ga = (inv_rms * (weighted - att * bend)).astype(BF16)
        grad[:, head(h)] = ga
        updates[head(h), :] = dot(q[:, head(h)], ga, TN)
        normed[:, head(h)] = (att * inv_rms * gain_h).astype(BF16)
    give(updates, group, outs)


def local_body(heads, factor, ga, q, k, v, prefix, scores, normed, normed_out, gq, gk_part, gv_part):
    normed_out[...] = normed[...]
    causal = causal_mask(q.shape[0])
    for h in range(heads):
        gah = ga[:, head(h)]
        raw = dot(gah, v[:, head(h)], NT) * factor
        gs = jnp.where(causal, raw, 0.0).astype(BF16)
        out = factor * dot(gah, prefix[head(h), :].astype(BF16), NT)
        gq[:, head(h)] = (out + dot(gs, k[:, head(h)], NN)).astype(BF16)
        gk_part[:, head(h)] = dot(gs, q[:, head(h)], TN)
        gv_part[:, head(h)] = dot(scores[h], gah, TN)


def final_body(heads, factor, group, k, v, gk_part, gv_part, *refs):
    pieces, outs, (suffix, gk, gv, sems) = refs[:-6], refs[-6:-4], refs[-4:]
    copies = [pltpu.make_async_copy(a, b, sems.at[i]) for i, (a, b) in enumerate(zip((gk, gv), outs))]
    pick(pieces, suffix, group)
    suf = [suffix[head(h), :].astype(BF16) for h in range(heads)]
    for h in range(heads):
        gk[:, head(h)] = (factor * dot(v[:, head(h)], suf[h], NT) + gk_part[:, head(h)]).astype(BF16)
    copies[0].start()
    for h in range(heads):
        gv[:, head(h)] = (factor * dot(k[:, head(h)], suf[h], NN) + gv_part[:, head(h)]).astype(BF16)
    copies[1].start()
    for copy in copies:
        copy.wait()


def exchange(pieces, active):
    group = len(pieces)
    ways = lax.axis_size("tp")

    def target(j, t, step):
        return (j ^ step) * ways + t if j in active else j * ways + (t ^ 1)

    return [pieces[0]] + [
        lax.ppermute(
            pieces[i],
            ("ctx", "tp"),
            [
                (j * ways + t, target(j, t, partner(i, group)))
                for j in range(2 * group)
                for t in range(ways)
            ],
        )
        for i in range(1, group)
    ]


def carried_in(pieces, reverse, state):
    group = len(pieces)
    count = lax.axis_size("ctx")
    sds = jax.ShapeDtypeStruct
    if group == 1:
        arrived = lax.all_to_all(pieces[0], "ctx", 0, 0, tiled=True)
        sums = call(
            functools.partial(scan_body, count, reverse),
            sds(arrived.shape, F32), arrived, scratch=[state],
        )
        return [lax.all_to_all(sums, "ctx", 0, 0, tiled=True)]
    rows, width = pieces[0].shape
    piece = sds((rows, width), F32)
    early, late, both = range(group), range(group, count), range(count)
    first, second = (late, early) if reverse else (early, late)
    kept = [sds((group * rows, width), F32)] if reverse else []
    total, *back = call(
        functools.partial(inner_body, group, reverse),
        [piece] * (group + 1) + kept,
        *exchange(pieces, both if reverse else first),
        scratch=[] if reverse else [state],
    )
    over = lax.ppermute(total, "ctx", [(j, j ^ group) for j in both])
    ahead = exchange(back[:group], first)
    if reverse:
        back = call(functools.partial(add_body, group), [piece] * group, back[group], over)
    else:
        back = call(
            functools.partial(late_body, group, reverse),
            [piece] * group, *exchange(pieces, second), over, scratch=[state],
        )
    behind = exchange(back, second)
    return [*behind, *ahead] if reverse else [*ahead, *behind]


def from_all(part, axis):
    count = lax.axis_size(axis)
    even = count & (count - 1) == 0
    return [part] + [
        lax.ppermute(part, axis, [(i, i ^ step if even else (i + step) % count) for i in range(count)])
        for step in range(1, count)
    ]


def on_device(queries, keys, values, gain, out_grad):
    tokens, width = queries.shape
    heads = width // HEAD
    count = lax.axis_size("ctx")
    factor = (HEAD * tokens * count) ** (-0.5)
    features = width * lax.axis_size("tp")
    gains = gain.reshape(heads, HEAD)
    sds = jax.ShapeDtypeStruct
    wide = sds((tokens, width), F32)
    half = sds((tokens, width), BF16)
    state = pltpu.VMEM((width, HEAD), F32)
    if count in (4, 8) and lax.axis_size("tp") % 2 == 0:
        group = count // 2
        pieces = [sds((width // group, HEAD), F32)] * group
    else:
        group = count
        pieces = [sds((count, width // count, HEAD), F32)]

    given = (keys, values, queries, out_grad, gains)
    keys, values, queries, out_grad, gains, *states = call(
        functools.partial(states_body, heads, group, len(given)),
        (*(pltpu.VMEM(a.shape, a.dtype) for a in given), *pieces),
        *(pltpu.with_memory_space_constraint(a, pltpu.HBM) for a in given),
        ins=[HBM] * len(given),
        scratch=[state, pltpu.SemaphoreType.DMA((len(given),))],
    )
    prefix = carried_in(states, False, state)
    pairs = heads * tokens * tokens * HEAD
    scores, local = call(
        functools.partial(scores_body, heads, factor),
        (sds((heads, tokens, tokens), BF16), wide),
        queries, keys, values,
        flops=4 * pairs,
    )
    attended, stats, prefix = call(
        functools.partial(attend_body, heads, factor, group),
        (wide, sds((2, tokens), F32), sds((width, HEAD), F32)),
        queries, out_grad, gains, local, *prefix,
    )
    every = from_all(stats, "tp")
    normed, grad_attn, *updates = call(
        functools.partial(grad_body, heads, features, group, len(every)),
        (pltpu.VMEM((tokens, width), BF16), half, *pieces),
        attended, out_grad, gains, queries, *every,
        scratch=[state],
    )
    suffix = carried_in(updates, True, state)
    normed, grad_q, gk_part, gv_part = call(
        functools.partial(local_body, heads, factor),
        (half, half, wide, wide),
        grad_attn, queries, keys, values, prefix, scores, normed,
        flops=9 * pairs,
    )
    held = pltpu.VMEM((tokens, width), BF16)
    grad_k, grad_v = call(
        functools.partial(final_body, heads, factor, group),
        (half, half),
        keys, values, gk_part, gv_part, *suffix,
        dests=(HBM, HBM),
        scratch=[state, held, held, pltpu.SemaphoreType.DMA((2,))],
    )
    return normed, grad_q, grad_k, grad_v


def solution(mesh):
    placed = (P("ctx", "tp"), P("ctx", "tp"), P("ctx", "tp"), P("tp"), P("ctx", "tp"))
    return jax.shard_map(
        on_device,
        mesh=mesh,
        in_specs=placed,
        out_specs=(P("ctx", "tp"), P("ctx", "tp"), P("ctx", "tp"), P("ctx", "tp")),
        check_vma=False,
    )
```

```python
import functools

import jax
import jax.numpy as jnp
from jax import lax
from jax.experimental import pallas as pl
from jax.experimental.pallas import tpu as pltpu
from jax.sharding import PartitionSpec as P

HEAD = 128

epsilon = 1e-06
F32 = jnp.float32
BF16 = jnp.bfloat16

NN = (((1,), (0,)), ((), ()))
NT = (((1,), (1,)), ((), ()))
TN = (((0,), (0,)), ((), ()))


def dot(a, b, dims):
    return lax.dot_general(a, b, dims, preferred_element_type=F32)


VMEM = pl.BlockSpec(memory_space=pltpu.VMEM)
HBM = pl.BlockSpec(memory_space=pltpu.HBM)


def call(body, outs, *args, ins=None, dests=None, scratch=(), flops=1e7):
    moved = sum(a.size * a.dtype.itemsize for a in args)
    return pl.pallas_call(
        body,
        out_shape=outs,
        in_specs=ins or [VMEM] * len(args),
        out_specs=dests or jax.tree.map(lambda _: VMEM, outs),
        scratch_shapes=scratch,
        compiler_params=pltpu.CompilerParams(vmem_limit_bytes=16 * 1024 * 1024),
        cost_estimate=pl.CostEstimate(flops=int(flops), bytes_accessed=int(moved), transcendentals=0),
    )(*args)


def head(h):
    return slice(h * HEAD, (h + 1) * HEAD)


def causal_mask(tokens):
    row = lax.broadcasted_iota(jnp.int32, (tokens, tokens), 0)
    col = lax.broadcasted_iota(jnp.int32, (tokens, tokens), 1)
    return row >= col


def rows_of(scratch, parts, place):
    rows = scratch.shape[0] // parts
    return scratch.at[pl.ds(pl.multiple_of(place * rows, rows), rows), :]


def partner(i, group):
    return group - 1 - i


def give(scratch, group, outs):
    if len(outs) == 1:
        outs[0][...] = scratch[...].reshape(outs[0].shape)
        return
    place = lax.rem(lax.axis_index("ctx"), group)
    for i, out in enumerate(outs):
        out[...] = rows_of(scratch, group, lax.bitwise_xor(place, partner(i, group)))[...]


def take(ins, scratch, group):
    if len(ins) == 1:
        scratch[...] = ins[0][...].reshape(scratch.shape)
        return
    place = lax.rem(lax.axis_index("ctx"), group)
    for i, piece in enumerate(ins):
        rows_of(scratch, group, lax.bitwise_xor(place, partner(i, group)))[...] = piece[...]


def running_sums(scratch, parts, reverse):
    rows = scratch.shape[0] // parts
    running = jnp.zeros((rows, scratch.shape[1]), F32)
    for place in range(parts - 1, -1, -1) if reverse else range(parts):
        own = slice(place * rows, (place + 1) * rows)
        here = scratch[own, :]
        scratch[own, :] = running
        running = running + here
    return running


def states_body(heads, group, many, *refs):
    given, held, outs = refs[:many], refs[many : 2 * many], refs[2 * many : -2]
    state, sems = refs[-2:]
    copies = [pltpu.make_async_copy(a, b, sems.at[i]) for i, (a, b) in enumerate(zip(given, held))]
    for copy in copies:
        copy.start()
    copies[0].wait()
    copies[1].wait()
    left, right = held[0], held[1]
    for h in range(heads):
        state[head(h), :] = dot(left[:, head(h)], right[:, head(h)], TN)
    give(state, group, outs)
    for copy in copies[2:]:
        copy.wait()


def scan_body(count, reverse, arrived, sums, scratch):
    take([arrived], scratch, count)
    running_sums(scratch, count, reverse)
    give(scratch, count, [sums])


def inner_body(group, reverse, *refs):
    arrived, total, outs, sums = refs[:group], refs[group], refs[group + 1 : -1], refs[-1]
    take(arrived, sums, group)
    total[...] = running_sums(sums, group, reverse)
    give(sums, group, outs)


def add_body(group, sums, over, *outs):
    place = lax.rem(lax.axis_index("ctx"), group)
    for i, out in enumerate(outs):
        out[...] = rows_of(sums, group, lax.bitwise_xor(place, partner(i, group)))[...] + over[...]


def late_body(group, reverse, *refs):
    arrived, over, outs, sums = refs[:group], refs[group], refs[group + 1 : -1], refs[-1]
    take(arrived, sums, group)
    running_sums(sums, group, reverse)
    add_body(group, sums, over, *outs)


def pick(pieces, scratch, group):
    many = len(pieces) // 2
    if many == 0:
        take(pieces, scratch, group)
        return
    early = lax.axis_index("ctx") < group
    place = lax.rem(lax.axis_index("ctx"), group)
    for i in range(many):
        rows = rows_of(scratch, group, lax.bitwise_xor(place, partner(i, group)))
        rows[...] = jnp.where(early, pieces[i][...], pieces[many + i][...])


def scores_body(heads, factor, q, k, v, scores, attended):
    causal = causal_mask(q.shape[0])
    for h in range(heads):
        raw = dot(q[:, head(h)], k[:, head(h)], NT) * factor
        sc = jnp.where(causal, raw, 0.0).astype(BF16)
        scores[h] = sc
        attended[:, head(h)] = dot(sc, v[:, head(h)], NN)


def attend_body(heads, factor, group, q, og, gain, local, *refs):
    pieces, (attended, stats, prefix) = refs[:-3], refs[-3:]
    pick(pieces, prefix, group)
    power = 0.0
    inner = 0.0
    for h in range(heads):
        att = factor * dot(q[:, head(h)], prefix[head(h), :].astype(BF16), NN) + local[:, head(h)]
        attended[:, head(h)] = att
        weighted = og[:, head(h)].astype(F32) * gain[h : h + 1, :]
        power = power + att * att
        inner = inner + weighted * att
    stats[0:1, :] = jnp.sum(power.T, axis=0, keepdims=True)
    stats[1:2, :] = jnp.sum(inner.T, axis=0, keepdims=True)


def grad_body(heads, features, group, ways, attended, og, gain, q, *refs):
    stats, (normed, grad), outs, updates = refs[:ways], refs[ways : ways + 2], refs[ways + 2 : -1], refs[-1]
    total = stats[0][...]
    for other in stats[1:]:
        total = total + other[...]
    inv_rms = lax.rsqrt(total[0:1, :] / features + epsilon)
    bend = inv_rms * inv_rms * (total[1:2, :] / features)
    tokens = q.shape[0]
    inv_rms = jnp.broadcast_to(inv_rms, (HEAD, tokens)).T
    bend = jnp.broadcast_to(bend, (HEAD, tokens)).T
    for h in range(heads):
        att = attended[:, head(h)]
        gain_h = gain[h : h + 1, :]
        weighted = og[:, head(h)].astype(F32) * gain_h
        ga = (inv_rms * (weighted - att * bend)).astype(BF16)
        grad[:, head(h)] = ga
        updates[head(h), :] = dot(q[:, head(h)], ga, TN)
        normed[:, head(h)] = (att * inv_rms * gain_h).astype(BF16)
    give(updates, group, outs)


def local_body(heads, factor, ga, q, k, v, prefix, scores, normed, normed_out, gq, gk_part, gv_part):
    normed_out[...] = normed[...]
    causal = causal_mask(q.shape[0])
    for h in range(heads):
        gah = ga[:, head(h)]
        raw = dot(gah, v[:, head(h)], NT) * factor
        gs = jnp.where(causal, raw, 0.0).astype(BF16)
        out = factor * dot(gah, prefix[head(h), :].astype(BF16), NT)
        gq[:, head(h)] = (out + dot(gs, k[:, head(h)], NN)).astype(BF16)
        gk_part[:, head(h)] = dot(gs, q[:, head(h)], TN)
        gv_part[:, head(h)] = dot(scores[h], gah, TN)


def final_body(heads, factor, group, k, v, gk_part, gv_part, *refs):
    pieces, outs, (suffix, gk, gv, sems) = refs[:-6], refs[-6:-4], refs[-4:]
    copies = [pltpu.make_async_copy(a, b, sems.at[i]) for i, (a, b) in enumerate(zip((gk, gv), outs))]
    pick(pieces, suffix, group)
    suf = [suffix[head(h), :].astype(BF16) for h in range(heads)]
    for h in range(heads):
        gk[:, head(h)] = (factor * dot(v[:, head(h)], suf[h], NT) + gk_part[:, head(h)]).astype(BF16)
    copies[0].start()
    for h in range(heads):
        gv[:, head(h)] = (factor * dot(k[:, head(h)], suf[h], NN) + gv_part[:, head(h)]).astype(BF16)
    copies[1].start()
    for copy in copies:
        copy.wait()


def exchange(pieces, active, group):
    ways = lax.axis_size("tp")
    return [
        lax.ppermute(
            piece,
            ("ctx", "tp"),
            [
                (j * ways + t, (j ^ partner(i, group) if j in active else j) * ways + (t ^ 1))
                for j in range(2 * group)
                for t in range(ways)
            ],
        )
        for i, piece in enumerate(pieces)
    ]


def carried_in(pieces, reverse, state):
    group = len(pieces)
    count = lax.axis_size("ctx")
    sds = jax.ShapeDtypeStruct
    if group == 1:
        arrived = lax.all_to_all(pieces[0], "ctx", 0, 0, tiled=True)
        sums = call(
            functools.partial(scan_body, count, reverse),
            sds(arrived.shape, F32), arrived, scratch=[state],
        )
        return [lax.all_to_all(sums, "ctx", 0, 0, tiled=True)]
    rows, width = pieces[0].shape
    piece = sds((rows, width), F32)
    early, late, both = range(group), range(group, count), range(count)
    first, second = (late, early) if reverse else (early, late)
    arrived = exchange(pieces, both if reverse else first, group)
    kept = [sds((group * rows, width), F32)] if reverse else []
    total, *back = call(
        functools.partial(inner_body, group, reverse),
        [piece] * (group + 1) + kept,
        *arrived,
        scratch=[] if reverse else [state],
    )
    over = lax.ppermute(total, "ctx", [(j, j ^ group) for j in both])
    ahead = exchange(back[:group], first, group)
    if reverse:
        back = call(functools.partial(add_body, group), [piece] * group, back[group], over)
    else:
        back = call(
            functools.partial(late_body, group, reverse),
            [piece] * group, *exchange(pieces[:-1], second, group), arrived[-1], over, scratch=[state],
        )
    behind = exchange(back, second, group)
    return [*behind, *ahead] if reverse else [*ahead, *behind]


def from_all(part, axis):
    count = lax.axis_size(axis)
    even = count & (count - 1) == 0
    steps = [1, 3, 2] if count == 4 else range(1, count)
    return [part] + [
        lax.ppermute(part, axis, [(i, i ^ step if even else (i + step) % count) for i in range(count)])
        for step in steps
    ]


def on_device(queries, keys, values, gain, out_grad):
    tokens, width = queries.shape
    heads = width // HEAD
    count = lax.axis_size("ctx")
    factor = (HEAD * tokens * count) ** (-0.5)
    features = width * lax.axis_size("tp")
    gains = gain.reshape(heads, HEAD)
    sds = jax.ShapeDtypeStruct
    wide = sds((tokens, width), F32)
    half = sds((tokens, width), BF16)
    state = pltpu.VMEM((width, HEAD), F32)
    if count in (4, 8) and lax.axis_size("tp") % 2 == 0:
        group = count // 2
        pieces = [sds((width // group, HEAD), F32)] * group
    else:
        group = count
        pieces = [sds((count, width // count, HEAD), F32)]

    given = (keys, values, queries, out_grad, gains)
    keys, values, queries, out_grad, gains, *states = call(
        functools.partial(states_body, heads, group, len(given)),
        (*(pltpu.VMEM(a.shape, a.dtype) for a in given), *pieces),
        *(pltpu.with_memory_space_constraint(a, pltpu.HBM) for a in given),
        ins=[HBM] * len(given),
        scratch=[state, pltpu.SemaphoreType.DMA((len(given),))],
    )
    prefix = carried_in(states, False, state)
    pairs = heads * tokens * tokens * HEAD
    scores, local = call(
        functools.partial(scores_body, heads, factor),
        (sds((heads, tokens, tokens), BF16), wide),
        queries, keys, values,
        flops=4 * pairs,
    )
    attended, stats, prefix = call(
        functools.partial(attend_body, heads, factor, group),
        (wide, sds((2, tokens), F32), sds((width, HEAD), F32)),
        queries, out_grad, gains, local, *prefix,
    )
    every = from_all(stats, "tp")
    normed, grad_attn, *updates = call(
        functools.partial(grad_body, heads, features, group, len(every)),
        (pltpu.VMEM((tokens, width), BF16), half, *pieces),
        attended, out_grad, gains, queries, *every,
        scratch=[state],
    )
    suffix = carried_in(updates, True, state)
    normed, grad_q, gk_part, gv_part = call(
        functools.partial(local_body, heads, factor),
        (half, half, wide, wide),
        grad_attn, queries, keys, values, prefix, scores, normed,
        flops=9 * pairs,
    )
    held = pltpu.VMEM((tokens, width), BF16)
    grad_k, grad_v = call(
        functools.partial(final_body, heads, factor, group),
        (half, half),
        keys, values, gk_part, gv_part, *suffix,
        dests=(HBM, HBM),
        scratch=[state, held, held, pltpu.SemaphoreType.DMA((2,))],
    )
    return normed, grad_q, grad_k, grad_v


def solution(mesh):
    placed = (P("ctx", "tp"), P("ctx", "tp"), P("ctx", "tp"), P("tp"), P("ctx", "tp"))
    return jax.shard_map(
        on_device,
        mesh=mesh,
        in_specs=placed,
        out_specs=(P("ctx", "tp"), P("ctx", "tp"), P("ctx", "tp"), P("ctx", "tp")),
        check_vma=False,
    )
```

```python
import functools

import jax
import jax.numpy as jnp
from jax import lax
from jax.experimental import pallas as pl
from jax.experimental.pallas import tpu as pltpu
from jax.sharding import PartitionSpec as P

HEAD = 128

epsilon = 1e-06
F32 = jnp.float32
BF16 = jnp.bfloat16

NN = (((1,), (0,)), ((), ()))
NT = (((1,), (1,)), ((), ()))
TN = (((0,), (0,)), ((), ()))


def dot(a, b, dims):
    return lax.dot_general(a, b, dims, preferred_element_type=F32)


VMEM = pl.BlockSpec(memory_space=pltpu.VMEM)
HBM = pl.BlockSpec(memory_space=pltpu.HBM)


def call(body, outs, *args, ins=None, dests=None, scratch=(), flops=1e7):
    moved = sum(a.size * a.dtype.itemsize for a in args)
    return pl.pallas_call(
        body,
        out_shape=outs,
        in_specs=ins or [VMEM] * len(args),
        out_specs=dests or jax.tree.map(lambda _: VMEM, outs),
        scratch_shapes=scratch,
        compiler_params=pltpu.CompilerParams(vmem_limit_bytes=16 * 1024 * 1024),
        cost_estimate=pl.CostEstimate(flops=int(flops), bytes_accessed=int(moved), transcendentals=0),
    )(*args)


def head(h):
    return slice(h * HEAD, (h + 1) * HEAD)


def causal_mask(tokens):
    row = lax.broadcasted_iota(jnp.int32, (tokens, tokens), 0)
    col = lax.broadcasted_iota(jnp.int32, (tokens, tokens), 1)
    return row >= col


def rows_of(scratch, parts, place):
    rows = scratch.shape[0] // parts
    return scratch.at[pl.ds(pl.multiple_of(place * rows, rows), rows), :]


def partner(i, group):
    return group - 1 - i


def give(scratch, group, outs):
    if len(outs) == 1:
        outs[0][...] = scratch[...].reshape(outs[0].shape)
        return
    place = lax.rem(lax.axis_index("ctx"), group)
    for i, out in enumerate(outs):
        out[...] = rows_of(scratch, group, lax.bitwise_xor(place, partner(i, group)))[...]


def take(ins, scratch, group):
    if len(ins) == 1:
        scratch[...] = ins[0][...].reshape(scratch.shape)
        return
    place = lax.rem(lax.axis_index("ctx"), group)
    for i, piece in enumerate(ins):
        rows_of(scratch, group, lax.bitwise_xor(place, partner(i, group)))[...] = piece[...]


def running_sums(scratch, parts, reverse):
    rows = scratch.shape[0] // parts
    running = jnp.zeros((rows, scratch.shape[1]), F32)
    for place in range(parts - 1, -1, -1) if reverse else range(parts):
        own = slice(place * rows, (place + 1) * rows)
        here = scratch[own, :]
        scratch[own, :] = running
        running = running + here
    return running


def loads(pairs, sems):
    copies = [pltpu.make_async_copy(a, b, sems.at[i]) for i, (a, b) in enumerate(pairs)]
    for copy in copies:
        copy.start()
    return copies


def states_body(heads, group, k_hbm, v_hbm, k, v, *refs):
    outs, (state, sems) = refs[:-2], refs[-2:]
    parts = [(a.at[:, head(h)], b.at[:, head(h)]) for h in range(heads) for a, b in ((k_hbm, k), (v_hbm, v))]
    copies = loads(parts, sems)
    for h in range(heads):
        copies[2 * h].wait()
        copies[2 * h + 1].wait()
        state[head(h), :] = dot(k[:, head(h)], v[:, head(h)], TN)
    give(state, group, outs[:group])
    for i, again in enumerate(outs[group:]):
        again[...] = outs[i][...]


def scan_body(count, reverse, arrived, sums, scratch):
    take([arrived], scratch, count)
    running_sums(scratch, count, reverse)
    give(scratch, count, [sums])


def inner_body(group, reverse, *refs):
    arrived, total, outs, sums = refs[:group], refs[group], refs[group + 1 : 2 * group + 1], refs[-1]
    take(arrived, sums, group)
    total[...] = running_sums(sums, group, reverse)
    give(sums, group, outs)
    if not reverse:
        refs[-2][...] = arrived[-1][...]


def add_body(group, sums, over, *outs):
    place = lax.rem(lax.axis_index("ctx"), group)
    for i, out in enumerate(outs):
        out[...] = rows_of(sums, group, lax.bitwise_xor(place, partner(i, group)))[...] + over[...]


def late_body(group, reverse, *refs):
    arrived, over, outs, sums = refs[:group], refs[group], refs[group + 1 : -1], refs[-1]
    take(arrived, sums, group)
    running_sums(sums, group, reverse)
    add_body(group, sums, over, *outs)


def pick(pieces, scratch, group):
    many = len(pieces) // 2
    if many == 0:
        take(pieces, scratch, group)
        return
    early = lax.axis_index("ctx") < group
    place = lax.rem(lax.axis_index("ctx"), group)
    for i in range(many):
        rows = rows_of(scratch, group, lax.bitwise_xor(place, partner(i, group)))
        rows[...] = jnp.where(early, pieces[i][...], pieces[many + i][...])


def scores_body(heads, factor, k, v, q_hbm, og_hbm, gain_hbm, scores, attended, q, og, gain, sems):
    copies = loads(((q_hbm, q), (og_hbm, og), (gain_hbm, gain)), sems)
    copies[0].wait()
    causal = causal_mask(q.shape[0])
    for h in range(heads):
        raw = dot(q[:, head(h)], k[:, head(h)], NT) * factor
        sc = jnp.where(causal, raw, 0.0).astype(BF16)
        scores[h] = sc
        attended[:, head(h)] = dot(sc, v[:, head(h)], NN)
    for copy in copies[1:]:
        copy.wait()


def attend_body(heads, factor, group, q, og, gain, local, *refs):
    pieces, (attended, stats, prefix) = refs[:-3], refs[-3:]
    pick(pieces, prefix, group)
    power = 0.0
    inner = 0.0
    for h in range(heads):
        att = factor * dot(q[:, head(h)], prefix[head(h), :].astype(BF16), NN) + local[:, head(h)]
        attended[:, head(h)] = att
        weighted = og[:, head(h)].astype(F32) * gain[h : h + 1, :]
        power = power + att * att
        inner = inner + weighted * att
    stats[0:1, :] = jnp.sum(power.T, axis=0, keepdims=True)
    stats[1:2, :] = jnp.sum(inner.T, axis=0, keepdims=True)


def grad_body(heads, features, group, ways, attended, og, gain, q, *refs):
    stats, (normed, grad), outs, updates = refs[:ways], refs[ways : ways + 2], refs[ways + 2 : -1], refs[-1]
    total = stats[0][...]
    for other in stats[1:]:
        total = total + other[...]
    inv_rms = lax.rsqrt(total[0:1, :] / features + epsilon)
    bend = inv_rms * inv_rms * (total[1:2, :] / features)
    tokens = q.shape[0]
    inv_rms = jnp.broadcast_to(inv_rms, (HEAD, tokens)).T
    bend = jnp.broadcast_to(bend, (HEAD, tokens)).T
    for h in range(heads):
        att = attended[:, head(h)]
        gain_h = gain[h : h + 1, :]
        weighted = og[:, head(h)].astype(F32) * gain_h
        ga = (inv_rms * (weighted - att * bend)).astype(BF16)
        grad[:, head(h)] = ga
        updates[head(h), :] = dot(q[:, head(h)], ga, TN)
        normed[:, head(h)] = (att * inv_rms * gain_h).astype(BF16)
    give(updates, group, outs)


def local_body(heads, factor, ga, q, k, v, prefix, scores, normed, normed_out, gq, gk_part, gv_part):
    normed_out[...] = normed[...]
    causal = causal_mask(q.shape[0])
    for h in range(heads):
        gah = ga[:, head(h)]
        raw = dot(gah, v[:, head(h)], NT) * factor
        gs = jnp.where(causal, raw, 0.0).astype(BF16)
        out = factor * dot(gah, prefix[head(h), :].astype(BF16), NT)
        gq[:, head(h)] = (out + dot(gs, k[:, head(h)], NN)).astype(BF16)
        gk_part[:, head(h)] = dot(gs, q[:, head(h)], TN)
        gv_part[:, head(h)] = dot(scores[h], gah, TN)


def final_body(heads, factor, group, k, v, gk_part, gv_part, *refs):
    pieces, outs, (suffix, gk, gv, sems) = refs[:-6], refs[-6:-4], refs[-4:]
    pick(pieces, suffix, group)
    copies = []

    def send(h, held, out):
        copy = pltpu.make_async_copy(held.at[:, head(h)], out.at[:, head(h)], sems.at[len(copies)])
        copy.start()
        copies.append(copy)

    for h in range(heads):
        suf = suffix[head(h), :].astype(BF16)
        gk[:, head(h)] = (factor * dot(v[:, head(h)], suf, NT) + gk_part[:, head(h)]).astype(BF16)
        send(h, gk, outs[0])
        gv[:, head(h)] = (factor * dot(k[:, head(h)], suf, NN) + gv_part[:, head(h)]).astype(BF16)
        send(h, gv, outs[1])
    for copy in copies:
        copy.wait()


def exchange(pieces, active, group):
    ways = lax.axis_size("tp")
    return [
        lax.ppermute(
            piece,
            ("ctx", "tp"),
            [
                (j * ways + t, (j ^ partner(i, group) if j in active else j) * ways + (t ^ 1))
                for j in range(2 * group)
                for t in range(ways)
            ],
        )
        for i, piece in enumerate(pieces)
    ]


def carried_in(pieces, reverse, state):
    group = len(pieces) if reverse else (len(pieces) + 1) // 2
    pieces, again = pieces[:group], pieces[group:]
    count = lax.axis_size("ctx")
    sds = jax.ShapeDtypeStruct
    if group == 1:
        arrived = lax.all_to_all(pieces[0], "ctx", 0, 0, tiled=True)
        sums = call(
            functools.partial(scan_body, count, reverse),
            sds(arrived.shape, F32), arrived, scratch=[state],
        )
        return [lax.all_to_all(sums, "ctx", 0, 0, tiled=True)]
    rows, width = pieces[0].shape
    piece = sds((rows, width), F32)
    early, late, both = range(group), range(group, count), range(count)
    first, second = (late, early) if reverse else (early, late)
    arrived = exchange(pieces, both if reverse else first, group)
    kept = sds((group * rows, width), F32) if reverse else piece
    total, *back = call(
        functools.partial(inner_body, group, reverse),
        [piece] * (group + 1) + [kept],
        *arrived,
        scratch=[] if reverse else [state],
    )
    over = lax.ppermute(total, "ctx", [(j, j ^ group) for j in both])
    ahead = exchange(back[:group], first, group)
    if reverse:
        back = call(functools.partial(add_body, group), [piece] * group, back[group], over)
    else:
        back = call(
            functools.partial(late_body, group, reverse),
            [piece] * group, *exchange(again, second, group), back[group], over, scratch=[state],
        )
    behind = exchange(back, second, group)
    return [*behind, *ahead] if reverse else [*ahead, *behind]


def from_all(part, axis):
    count = lax.axis_size(axis)
    even = count & (count - 1) == 0
    steps = [1, 3, 2] if count == 4 else range(1, count)
    return [part] + [
        lax.ppermute(part, axis, [(i, i ^ step if even else (i + step) % count) for i in range(count)])
        for step in steps
    ]


def on_device(queries, keys, values, gain, out_grad):
    tokens, width = queries.shape
    heads = width // HEAD
    count = lax.axis_size("ctx")
    factor = (HEAD * tokens * count) ** (-0.5)
    features = width * lax.axis_size("tp")
    gains = gain.reshape(heads, HEAD)
    sds = jax.ShapeDtypeStruct
    wide = sds((tokens, width), F32)
    half = sds((tokens, width), BF16)
    state = pltpu.VMEM((width, HEAD), F32)
    if count in (4, 8) and lax.axis_size("tp") % 2 == 0:
        group = count // 2
        pieces = [sds((width // group, HEAD), F32)] * group
    else:
        group = count
        pieces = [sds((count, width // count, HEAD), F32)]

    def in_hbm(*arrays):
        return [pltpu.with_memory_space_constraint(array, pltpu.HBM) for array in arrays]

    def in_vmem(array):
        return pltpu.VMEM(array.shape, array.dtype)

    k_held, v_held, *states = call(
        functools.partial(states_body, heads, group),
        (in_vmem(keys), in_vmem(values), *pieces, *pieces[1:]),
        *in_hbm(keys, values),
        ins=[HBM, HBM],
        scratch=[state, pltpu.SemaphoreType.DMA((2 * heads,))],
    )
    prefix = carried_in(states, False, state)
    pairs = heads * tokens * tokens * HEAD
    scores, local, q_held, og_held, gain_held = call(
        functools.partial(scores_body, heads, factor),
        (
            sds((heads, tokens, tokens), BF16), wide,
            in_vmem(queries), in_vmem(out_grad), in_vmem(gains),
        ),
        k_held, v_held, *in_hbm(queries, out_grad, gains),
        ins=[VMEM, VMEM, HBM, HBM, HBM],
        scratch=[pltpu.SemaphoreType.DMA((3,))],
        flops=4 * pairs,
    )
    attended, stats, prefix = call(
        functools.partial(attend_body, heads, factor, group),
        (wide, sds((2, tokens), F32), sds((width, HEAD), F32)),
        q_held, og_held, gain_held, local, *prefix,
    )
    every = from_all(stats, "tp")
    normed, grad_attn, *updates = call(
        functools.partial(grad_body, heads, features, group, len(every)),
        (pltpu.VMEM((tokens, width), BF16), half, *pieces),
        attended, og_held, gain_held, q_held, *every,
        scratch=[state],
    )
    suffix = carried_in(updates, True, state)
    normed, grad_q, gk_part, gv_part = call(
        functools.partial(local_body, heads, factor),
        (half, half, wide, wide),
        grad_attn, q_held, k_held, v_held, prefix, scores, normed,
        flops=9 * pairs,
    )
    held = pltpu.VMEM((tokens, width), BF16)
    grad_k, grad_v = call(
        functools.partial(final_body, heads, factor, group),
        (half, half),
        k_held, v_held, gk_part, gv_part, *suffix,
        dests=(HBM, HBM),
        scratch=[state, held, held, pltpu.SemaphoreType.DMA((2 * heads,))],
    )
    return normed, grad_q, grad_k, grad_v


def solution(mesh):
    placed = (P("ctx", "tp"), P("ctx", "tp"), P("ctx", "tp"), P("tp"), P("ctx", "tp"))
    return jax.shard_map(
        on_device,
        mesh=mesh,
        in_specs=placed,
        out_specs=(P("ctx", "tp"), P("ctx", "tp"), P("ctx", "tp"), P("ctx", "tp")),
        check_vma=False,
    )
```

```python
import functools

import jax
import jax.numpy as jnp
from jax import lax
from jax.experimental import pallas as pl
from jax.experimental.pallas import tpu as pltpu
from jax.sharding import PartitionSpec as P

HEAD = 128

epsilon = 1e-06
ALONE = (0, 2)
SHARED = (1, 3)
F32 = jnp.float32
BF16 = jnp.bfloat16

NN = (((1,), (0,)), ((), ()))
NT = (((1,), (1,)), ((), ()))
TN = (((0,), (0,)), ((), ()))


def dot(a, b, dims):
    return lax.dot_general(a, b, dims, preferred_element_type=F32)


VMEM = pl.BlockSpec(memory_space=pltpu.VMEM)
HBM = pl.BlockSpec(memory_space=pltpu.HBM)


def call(body, outs, *args, ins=None, dests=None, scratch=(), flops=1e7):
    moved = sum(a.size * a.dtype.itemsize for a in args)
    return pl.pallas_call(
        body,
        out_shape=outs,
        in_specs=ins or [VMEM] * len(args),
        out_specs=dests or jax.tree.map(lambda _: VMEM, outs),
        scratch_shapes=scratch,
        compiler_params=pltpu.CompilerParams(vmem_limit_bytes=16 * 1024 * 1024),
        cost_estimate=pl.CostEstimate(flops=int(flops), bytes_accessed=int(moved), transcendentals=0),
    )(*args)


def head(h):
    return slice(h * HEAD, (h + 1) * HEAD)


def causal_mask(tokens):
    row = lax.broadcasted_iota(jnp.int32, (tokens, tokens), 0)
    col = lax.broadcasted_iota(jnp.int32, (tokens, tokens), 1)
    return row >= col


def rows_of(scratch, parts, place):
    rows = scratch.shape[0] // parts
    return scratch.at[pl.ds(pl.multiple_of(place * rows, rows), rows), :]


def partner(i, group):
    return group - 1 - i


def give(scratch, group, outs):
    if len(outs) == 1:
        outs[0][...] = scratch[...].reshape(outs[0].shape)
        return
    place = lax.rem(lax.axis_index("ctx"), group)
    for i, out in enumerate(outs):
        out[...] = rows_of(scratch, group, lax.bitwise_xor(place, partner(i, group)))[...]


def take(ins, scratch, group):
    if len(ins) == 1:
        scratch[...] = ins[0][...].reshape(scratch.shape)
        return
    place = lax.rem(lax.axis_index("ctx"), group)
    for i, piece in enumerate(ins):
        rows_of(scratch, group, lax.bitwise_xor(place, partner(i, group)))[...] = piece[...]


def running_sums(scratch, parts, reverse):
    rows = scratch.shape[0] // parts
    running = jnp.zeros((rows, scratch.shape[1]), F32)
    for place in range(parts - 1, -1, -1) if reverse else range(parts):
        own = slice(place * rows, (place + 1) * rows)
        here = scratch[own, :]
        scratch[own, :] = running
        running = running + here
    return running


def loads(pairs, sems):
    copies = [pltpu.make_async_copy(a, b, sems.at[i]) for i, (a, b) in enumerate(pairs)]
    for copy in copies:
        copy.start()
    return copies


def states_body(heads, group, k_hbm, v_hbm, k, v, *refs):
    outs, (state, sems) = refs[:-2], refs[-2:]
    for copy in loads(((k_hbm, k), (v_hbm, v)), sems):
        copy.wait()
    for h in range(heads):
        state[head(h), :] = dot(k[:, head(h)], v[:, head(h)], TN)
    give(state, group, outs[:group])
    for again, i in zip(outs[group:], ALONE):
        again[...] = outs[i][...]


def scan_body(count, reverse, arrived, sums, scratch):
    take([arrived], scratch, count)
    running_sums(scratch, count, reverse)
    give(scratch, count, [sums])


def inner_body(group, reverse, *refs):
    arrived, total, outs, sums = refs[:group], refs[group], refs[group + 1 : 2 * group + 1], refs[-1]
    take(arrived, sums, group)
    total[...] = running_sums(sums, group, reverse)
    give(sums, group, outs)
    if not reverse:
        for passed, i in zip(refs[2 * group + 1 : -1], SHARED):
            passed[...] = arrived[i][...]


def add_body(group, sums, over, *outs):
    place = lax.rem(lax.axis_index("ctx"), group)
    for i, out in enumerate(outs):
        out[...] = rows_of(sums, group, lax.bitwise_xor(place, partner(i, group)))[...] + over[...]


def late_body(group, reverse, *refs):
    arrived, over, outs, sums = refs[:group], refs[group], refs[group + 1 : -1], refs[-1]
    take(arrived, sums, group)
    running_sums(sums, group, reverse)
    add_body(group, sums, over, *outs)


def pick(pieces, scratch, group):
    many = len(pieces) // 2
    if many == 0:
        take(pieces, scratch, group)
        return
    early = lax.axis_index("ctx") < group
    place = lax.rem(lax.axis_index("ctx"), group)
    for i in range(many):
        rows = rows_of(scratch, group, lax.bitwise_xor(place, partner(i, group)))
        rows[...] = jnp.where(early, pieces[i][...], pieces[many + i][...])


def scores_body(heads, factor, k, v, q_hbm, og_hbm, gain_hbm, scores, attended, q, weighted, gain, og, sems):
    copies = loads(((q_hbm, q), (og_hbm, og), (gain_hbm, gain)), sems)
    copies[0].wait()
    causal = causal_mask(q.shape[0])
    for h in range(heads):
        raw = dot(q[:, head(h)], k[:, head(h)], NT) * factor
        sc = jnp.where(causal, raw, 0.0).astype(BF16)
        scores[h] = sc
        attended[:, head(h)] = dot(sc, v[:, head(h)], NN)
    for copy in copies[1:]:
        copy.wait()
    for h in range(heads):
        weighted[:, head(h)] = og[:, head(h)].astype(F32) * gain[h : h + 1, :]


def attend_body(heads, factor, group, q, weighted, local, *refs):
    pieces, (attended, stats, prefix) = refs[:-3], refs[-3:]
    pick(pieces, prefix, group)
    power = 0.0
    inner = 0.0
    for h in range(heads):
        att = factor * dot(q[:, head(h)], prefix[head(h), :].astype(BF16), NN) + local[:, head(h)]
        attended[:, head(h)] = att
        power = power + att * att
        inner = inner + weighted[:, head(h)] * att
    stats[0:1, :] = jnp.sum(power.T, axis=0, keepdims=True)
    stats[1:2, :] = jnp.sum(inner.T, axis=0, keepdims=True)


def grad_body(heads, features, group, ways, attended, weighted, q, *refs):
    stats, (spread, grad), outs, updates = refs[:ways], refs[ways : ways + 2], refs[ways + 2 : -1], refs[-1]
    total = stats[0][...]
    for other in stats[1:]:
        total = total + other[...]
    inv_rms = lax.rsqrt(total[0:1, :] / features + epsilon)
    bend = inv_rms * inv_rms * (total[1:2, :] / features)
    tokens = q.shape[0]
    inv_rms = jnp.broadcast_to(inv_rms, (HEAD, tokens)).T
    bend = jnp.broadcast_to(bend, (HEAD, tokens)).T
    spread[...] = inv_rms
    for h in range(heads):
        ga = (inv_rms * (weighted[:, head(h)] - attended[:, head(h)] * bend)).astype(BF16)
        grad[:, head(h)] = ga
        updates[head(h), :] = dot(q[:, head(h)], ga, TN)
    give(updates, group, outs)


def local_body(heads, factor, ga, q, k, v, prefix, scores, attended, inv_rms, gain, normed, gq, gk_part, gv_part):
    causal = causal_mask(q.shape[0])
    for h in range(heads):
        normed[:, head(h)] = (attended[:, head(h)] * inv_rms[...] * gain[h : h + 1, :]).astype(BF16)
        gah = ga[:, head(h)]
        raw = dot(gah, v[:, head(h)], NT) * factor
        gs = jnp.where(causal, raw, 0.0).astype(BF16)
        out = factor * dot(gah, prefix[head(h), :].astype(BF16), NT)
        gq[:, head(h)] = (out + dot(gs, k[:, head(h)], NN)).astype(BF16)
        gk_part[:, head(h)] = dot(gs, q[:, head(h)], TN)
        gv_part[:, head(h)] = dot(scores[h], gah, TN)


def final_body(heads, factor, group, k, v, gk_part, gv_part, *refs):
    pieces, outs, (suffix, gk, gv, sems) = refs[:-6], refs[-6:-4], refs[-4:]
    pick(pieces, suffix, group)
    copies = []

    def send(h, held, out):
        copy = pltpu.make_async_copy(held.at[:, head(h)], out.at[:, head(h)], sems.at[len(copies)])
        copy.start()
        copies.append(copy)

    for h in range(heads):
        suf = suffix[head(h), :].astype(BF16)
        gk[:, head(h)] = (factor * dot(v[:, head(h)], suf, NT) + gk_part[:, head(h)]).astype(BF16)
        send(h, gk, outs[0])
        gv[:, head(h)] = (factor * dot(k[:, head(h)], suf, NN) + gv_part[:, head(h)]).astype(BF16)
        send(h, gv, outs[1])
    for copy in copies:
        copy.wait()


def exchange(piece, i, active, group):
    ways = lax.axis_size("tp")
    pairs = [
        (j * ways + t, (j ^ partner(i, group) if j in active else j) * ways + (t ^ 1))
        for j in range(2 * group)
        for t in range(ways)
    ]
    return lax.ppermute(piece, ("ctx", "tp"), pairs)


def carried_in(pieces, reverse, state):
    again = () if reverse or len(pieces) == 1 else pieces[-len(ALONE) :]
    group = len(pieces) - len(again)
    pieces = pieces[:group]
    count = lax.axis_size("ctx")
    sds = jax.ShapeDtypeStruct
    if group == 1:
        arrived = lax.all_to_all(pieces[0], "ctx", 0, 0, tiled=True)
        sums = call(
            functools.partial(scan_body, count, reverse),
            sds(arrived.shape, F32), arrived, scratch=[state],
        )
        return [lax.all_to_all(sums, "ctx", 0, 0, tiled=True)]
    rows, width = pieces[0].shape
    piece = sds((rows, width), F32)
    early, late, both = range(group), range(group, count), range(count)
    first, second = (late, early) if reverse else (early, late)
    everyone = range(group)
    arrived = [
        exchange(pieces[i], i, both if reverse or i in SHARED else first, group) for i in everyone
    ]
    kept = [sds((group * rows, width), F32)] if reverse else [piece] * len(SHARED)
    total, *back = call(
        functools.partial(inner_body, group, reverse),
        [piece] * (group + 1) + kept,
        *arrived,
        scratch=[] if reverse else [state],
    )
    over = lax.ppermute(total, "ctx", [(j, j ^ group) for j in both])
    ahead = [exchange(back[i], i, first, group) for i in everyone]
    if reverse:
        back = call(functools.partial(add_body, group), [piece] * group, back[group], over)
    else:
        own = [exchange(part, i, second, group) for part, i in zip(again, ALONE)]
        mixed = [own[ALONE.index(i)] if i in ALONE else back[group + SHARED.index(i)] for i in everyone]
        back = call(
            functools.partial(late_body, group, reverse),
            [piece] * group, *mixed, over, scratch=[state],
        )
    behind = [exchange(back[i], i, second, group) for i in everyone]
    return [*behind, *ahead] if reverse else [*ahead, *behind]


def from_all(part, axis):
    count = lax.axis_size(axis)
    even = count & (count - 1) == 0
    steps = [1, 3, 2] if count == 4 else range(1, count)
    return [part] + [
        lax.ppermute(part, axis, [(i, i ^ step if even else (i + step) % count) for i in range(count)])
        for step in steps
    ]


def on_device(queries, keys, values, gain, out_grad):
    tokens, width = queries.shape
    heads = width // HEAD
    count = lax.axis_size("ctx")
    factor = (HEAD * tokens * count) ** (-0.5)
    features = width * lax.axis_size("tp")
    gains = gain.reshape(heads, HEAD)
    sds = jax.ShapeDtypeStruct
    wide = sds((tokens, width), F32)
    half = sds((tokens, width), BF16)
    state = pltpu.VMEM((width, HEAD), F32)
    if count == 8 and lax.axis_size("tp") % 2 == 0:
        group = count // 2
        pieces = [sds((width // group, HEAD), F32)] * group
    else:
        group = count
        pieces = [sds((count, width // count, HEAD), F32)]

    def in_hbm(*arrays):
        return [pltpu.with_memory_space_constraint(array, pltpu.HBM) for array in arrays]

    def in_vmem(array):
        return pltpu.VMEM(array.shape, array.dtype)

    k_held, v_held, *states = call(
        functools.partial(states_body, heads, group),
        (in_vmem(keys), in_vmem(values), *pieces, *(pieces[i] for i in ALONE if len(pieces) > 1)),
        *in_hbm(keys, values),
        ins=[HBM, HBM],
        scratch=[state, pltpu.SemaphoreType.DMA((2,))],
    )
    prefix = carried_in(states, False, state)
    pairs = heads * tokens * tokens * HEAD
    scores, local, q_held, weighted, gain_held = call(
        functools.partial(scores_body, heads, factor),
        (
            sds((heads, tokens, tokens), BF16), wide,
            in_vmem(queries), in_vmem(wide), in_vmem(gains),
        ),
        k_held, v_held, *in_hbm(queries, out_grad, gains),
        ins=[VMEM, VMEM, HBM, HBM, HBM],
        scratch=[in_vmem(out_grad), pltpu.SemaphoreType.DMA((3,))],
        flops=4 * pairs,
    )
    attended, stats, prefix = call(
        functools.partial(attend_body, heads, factor, group),
        (wide, sds((2, tokens), F32), sds((width, HEAD), F32)),
        q_held, weighted, local, *prefix,
    )
    every = from_all(stats, "tp")
    inv_rms, grad_attn, *updates = call(
        functools.partial(grad_body, heads, features, group, len(every)),
        (pltpu.VMEM((tokens, HEAD), F32), half, *pieces),
        attended, weighted, q_held, *every,
        scratch=[state],
    )
    suffix = carried_in(updates, True, state)
    normed, grad_q, gk_part, gv_part = call(
        functools.partial(local_body, heads, factor),
        (half, half, wide, wide),
        grad_attn, q_held, k_held, v_held, prefix, scores, attended, inv_rms, gain_held,
        flops=9 * pairs,
    )
    held = pltpu.VMEM((tokens, width), BF16)
    grad_k, grad_v = call(
        functools.partial(final_body, heads, factor, group),
        (half, half),
        k_held, v_held, gk_part, gv_part, *suffix,
        dests=(HBM, HBM),
        scratch=[state, held, held, pltpu.SemaphoreType.DMA((2 * heads,))],
    )
    return normed, grad_q, grad_k, grad_v


def solution(mesh):
    placed = (P("ctx", "tp"), P("ctx", "tp"), P("ctx", "tp"), P("tp"), P("ctx", "tp"))
    return jax.shard_map(
        on_device,
        mesh=mesh,
        in_specs=placed,
        out_specs=(P("ctx", "tp"), P("ctx", "tp"), P("ctx", "tp"), P("ctx", "tp")),
        check_vma=False,
    )
```

```python
import functools

import jax
import jax.numpy as jnp
from jax import lax
from jax.experimental import pallas as pl
from jax.experimental.pallas import tpu as pltpu
from jax.sharding import PartitionSpec as P

HEAD = 128

epsilon = 1e-06
ALONE = (0, 2)
SHARED = (1, 3)
F32 = jnp.float32
BF16 = jnp.bfloat16

NN = (((1,), (0,)), ((), ()))
NT = (((1,), (1,)), ((), ()))
TN = (((0,), (0,)), ((), ()))


def dot(a, b, dims):
    return lax.dot_general(a, b, dims, preferred_element_type=F32)


VMEM = pl.BlockSpec(memory_space=pltpu.VMEM)
HBM = pl.BlockSpec(memory_space=pltpu.HBM)


def call(body, outs, *args, ins=None, dests=None, scratch=(), flops=1e7):
    moved = sum(a.size * a.dtype.itemsize for a in args)
    return pl.pallas_call(
        body,
        out_shape=outs,
        in_specs=ins or [VMEM] * len(args),
        out_specs=dests or jax.tree.map(lambda _: VMEM, outs),
        scratch_shapes=scratch,
        compiler_params=pltpu.CompilerParams(vmem_limit_bytes=16 * 1024 * 1024),
        cost_estimate=pl.CostEstimate(flops=int(flops), bytes_accessed=int(moved), transcendentals=0),
    )(*args)


def head(h):
    return slice(h * HEAD, (h + 1) * HEAD)


def causal_mask(tokens):
    row = lax.broadcasted_iota(jnp.int32, (tokens, tokens), 0)
    col = lax.broadcasted_iota(jnp.int32, (tokens, tokens), 1)
    return row >= col


def rows_of(scratch, parts, place):
    rows = scratch.shape[0] // parts
    return scratch.at[pl.ds(pl.multiple_of(place * rows, rows), rows), :]


def partner(i, group):
    return group - 1 - i


def give(scratch, group, outs):
    if len(outs) == 1:
        outs[0][...] = scratch[...].reshape(outs[0].shape)
        return
    place = lax.rem(lax.axis_index("ctx"), group)
    for i, out in enumerate(outs):
        out[...] = rows_of(scratch, group, lax.bitwise_xor(place, partner(i, group)))[...]


def take(ins, scratch, group):
    if len(ins) == 1:
        scratch[...] = ins[0][...].reshape(scratch.shape)
        return
    place = lax.rem(lax.axis_index("ctx"), group)
    for i, piece in enumerate(ins):
        rows_of(scratch, group, lax.bitwise_xor(place, partner(i, group)))[...] = piece[...]


def running_sums(scratch, parts, reverse):
    rows = scratch.shape[0] // parts
    running = jnp.zeros((rows, scratch.shape[1]), F32)
    for place in range(parts - 1, -1, -1) if reverse else range(parts):
        own = slice(place * rows, (place + 1) * rows)
        here = scratch[own, :]
        scratch[own, :] = running
        running = running + here
    return running


def loads(pairs, sems):
    copies = [pltpu.make_async_copy(a, b, sems.at[i]) for i, (a, b) in enumerate(pairs)]
    for copy in copies:
        copy.start()
    return copies


def states_body(heads, group, k_hbm, v_hbm, k, v, *refs):
    outs, (state, sems) = refs[:-2], refs[-2:]
    for copy in loads(((k_hbm, k), (v_hbm, v)), sems):
        copy.wait()
    for h in range(heads):
        state[head(h), :] = dot(k[:, head(h)], v[:, head(h)], TN)
    give(state, group, outs[:group])
    for again, i in zip(outs[group:], ALONE):
        again[...] = outs[i][...]


def scan_body(count, reverse, arrived, sums, scratch):
    take([arrived], scratch, count)
    running_sums(scratch, count, reverse)
    give(scratch, count, [sums])


def inner_body(group, reverse, *refs):
    arrived, total, outs, sums = refs[:group], refs[group], refs[group + 1 : 2 * group + 1], refs[-1]
    take(arrived, sums, group)
    total[...] = running_sums(sums, group, reverse)
    give(sums, group, outs)
    if not reverse:
        for passed, i in zip(refs[2 * group + 1 : -1], SHARED):
            passed[...] = arrived[i][...]


def add_body(group, sums, over, *outs):
    place = lax.rem(lax.axis_index("ctx"), group)
    for i, out in enumerate(outs):
        out[...] = rows_of(sums, group, lax.bitwise_xor(place, partner(i, group)))[...] + over[...]


def late_body(group, reverse, *refs):
    arrived, over, outs, sums = refs[:group], refs[group], refs[group + 1 : -1], refs[-1]
    take(arrived, sums, group)
    running_sums(sums, group, reverse)
    add_body(group, sums, over, *outs)


def pick(pieces, scratch, group):
    many = len(pieces) // 2
    if many == 0:
        take(pieces, scratch, group)
        return
    early = lax.axis_index("ctx") < group
    place = lax.rem(lax.axis_index("ctx"), group)
    for i in range(many):
        rows = rows_of(scratch, group, lax.bitwise_xor(place, partner(i, group)))
        rows[...] = jnp.where(early, pieces[i][...], pieces[many + i][...])


def scores_body(heads, factor, k, v, q_hbm, og_hbm, gain_hbm, scores, attended, q, weighted, gain, og, sems):
    copies = loads(((q_hbm, q), (og_hbm, og), (gain_hbm, gain)), sems)
    copies[0].wait()
    causal = causal_mask(q.shape[0])
    for h in range(heads):
        raw = dot(q[:, head(h)], k[:, head(h)], NT) * factor
        sc = jnp.where(causal, raw, 0.0).astype(BF16)
        scores[h] = sc
        attended[:, head(h)] = dot(sc, v[:, head(h)], NN)
    for copy in copies[1:]:
        copy.wait()
    for h in range(heads):
        weighted[:, head(h)] = og[:, head(h)].astype(F32) * gain[h : h + 1, :]


def attend_body(heads, factor, group, q, weighted, local, *refs):
    pieces, (attended, stats, prefix) = refs[:-3], refs[-3:]
    pick(pieces, prefix, group)
    power = 0.0
    inner = 0.0
    for h in range(heads):
        att = factor * dot(q[:, head(h)], prefix[head(h), :].astype(BF16), NN) + local[:, head(h)]
        attended[:, head(h)] = att
        power = power + att * att
        inner = inner + weighted[:, head(h)] * att
    stats[0:1, :] = jnp.sum(power.T, axis=0, keepdims=True)
    stats[1:2, :] = jnp.sum(inner.T, axis=0, keepdims=True)


def grad_body(heads, features, group, ways, attended, weighted, q, *refs):
    stats, (spread, grad), outs, updates = refs[:ways], refs[ways : ways + 2], refs[ways + 2 : -1], refs[-1]
    total = stats[0][...]
    for other in stats[1:]:
        total = total + other[...]
    inv_rms = lax.rsqrt(total[0:1, :] / features + epsilon)
    bend = inv_rms * inv_rms * (total[1:2, :] / features)
    tokens = q.shape[0]
    inv_rms = jnp.broadcast_to(inv_rms, (HEAD, tokens)).T
    bend = jnp.broadcast_to(bend, (HEAD, tokens)).T
    spread[...] = inv_rms
    for h in range(heads):
        ga = (inv_rms * (weighted[:, head(h)] - attended[:, head(h)] * bend)).astype(BF16)
        grad[:, head(h)] = ga
        updates[head(h), :] = dot(q[:, head(h)], ga, TN)
    give(updates, group, outs)


def local_body(heads, factor, ga, q, k, v, prefix, scores, attended, inv_rms, gain, normed, gq, gk_part, gv_part):
    causal = causal_mask(q.shape[0])
    for h in range(heads):
        normed[:, head(h)] = (attended[:, head(h)] * inv_rms[...] * gain[h : h + 1, :]).astype(BF16)
        gah = ga[:, head(h)]
        raw = dot(gah, v[:, head(h)], NT) * factor
        gs = jnp.where(causal, raw, 0.0).astype(BF16)
        out = factor * dot(gah, prefix[head(h), :].astype(BF16), NT)
        gq[:, head(h)] = (out + dot(gs, k[:, head(h)], NN)).astype(BF16)
        gk_part[:, head(h)] = dot(gs, q[:, head(h)], TN)
        gv_part[:, head(h)] = dot(scores[h], gah, TN)


def final_body(heads, factor, group, k, v, gk_part, gv_part, *refs):
    pieces, outs, (suffix, gk, gv, sems) = refs[:-6], refs[-6:-4], refs[-4:]
    pick(pieces, suffix, group)
    copies = []

    def send(h, held, out):
        copy = pltpu.make_async_copy(held.at[:, head(h)], out.at[:, head(h)], sems.at[len(copies)])
        copy.start()
        copies.append(copy)

    for h in range(heads):
        suf = suffix[head(h), :].astype(BF16)
        gk[:, head(h)] = (factor * dot(v[:, head(h)], suf, NT) + gk_part[:, head(h)]).astype(BF16)
        send(h, gk, outs[0])
        gv[:, head(h)] = (factor * dot(k[:, head(h)], suf, NN) + gv_part[:, head(h)]).astype(BF16)
        send(h, gv, outs[1])
    for copy in copies:
        copy.wait()


def exchange(piece, i, active, group):
    ways = lax.axis_size("tp")
    pairs = [
        (j * ways + t, (j ^ partner(i, group) if j in active else j) * ways + (t ^ 1))
        for j in range(2 * group)
        for t in range(ways)
    ]
    return lax.ppermute(piece, ("ctx", "tp"), pairs)


def carried_in(pieces, reverse, state):
    again = () if reverse or len(pieces) == 1 else pieces[-len(ALONE) :]
    group = len(pieces) - len(again)
    pieces = pieces[:group]
    count = lax.axis_size("ctx")
    sds = jax.ShapeDtypeStruct
    if group == 1:
        arrived = lax.all_to_all(pieces[0], "ctx", 0, 0, tiled=True)
        sums = call(
            functools.partial(scan_body, count, reverse),
            sds(arrived.shape, F32), arrived, scratch=[state],
        )
        return [lax.all_to_all(sums, "ctx", 0, 0, tiled=True)]
    rows, width = pieces[0].shape
    piece = sds((rows, width), F32)
    early, late, both = range(group), range(group, count), range(count)
    first, second = (late, early) if reverse else (early, late)
    everyone = range(group)
    arrived = [
        exchange(pieces[i], i, both if reverse or i in SHARED else first, group) for i in everyone
    ]
    kept = [sds((group * rows, width), F32)] if reverse else [piece] * len(SHARED)
    total, *back = call(
        functools.partial(inner_body, group, reverse),
        [piece] * (group + 1) + kept,
        *arrived,
        scratch=[] if reverse else [state],
    )
    over = lax.ppermute(total, "ctx", [(j, j ^ group) for j in both])
    ahead = [exchange(back[i], i, first, group) for i in everyone]
    if reverse:
        back = call(functools.partial(add_body, group), [piece] * group, back[group], over)
    else:
        own = [exchange(part, i, second, group) for part, i in zip(again, ALONE)]
        mixed = [own[ALONE.index(i)] if i in ALONE else back[group + SHARED.index(i)] for i in everyone]
        back = call(
            functools.partial(late_body, group, reverse),
            [piece] * group, *mixed, over, scratch=[state],
        )
    behind = [exchange(back[i], i, second, group) for i in everyone]
    return [*behind, *ahead] if reverse else [*ahead, *behind]


def from_all(part, axis):
    count = lax.axis_size(axis)
    even = count & (count - 1) == 0
    return [part] + [
        lax.ppermute(part, axis, [(i, i ^ step if even else (i + step) % count) for i in range(count)])
        for step in range(1, count)
    ]


def on_device(queries, keys, values, gain, out_grad):
    tokens, width = queries.shape
    heads = width // HEAD
    count = lax.axis_size("ctx")
    factor = (HEAD * tokens * count) ** (-0.5)
    features = width * lax.axis_size("tp")
    gains = gain.reshape(heads, HEAD)
    sds = jax.ShapeDtypeStruct
    wide = sds((tokens, width), F32)
    half = sds((tokens, width), BF16)
    state = pltpu.VMEM((width, HEAD), F32)
    if count == 8 and lax.axis_size("tp") % 2 == 0:
        group = count // 2
        pieces = [sds((width // group, HEAD), F32)] * group
    else:
        group = count
        pieces = [sds((count, width // count, HEAD), F32)]

    def in_hbm(*arrays):
        return [pltpu.with_memory_space_constraint(array, pltpu.HBM) for array in arrays]

    def in_vmem(array):
        return pltpu.VMEM(array.shape, array.dtype)

    k_held, v_held, *states = call(
        functools.partial(states_body, heads, group),
        (in_vmem(keys), in_vmem(values), *pieces, *(pieces[i] for i in ALONE if len(pieces) > 1)),
        *in_hbm(keys, values),
        ins=[HBM, HBM],
        scratch=[state, pltpu.SemaphoreType.DMA((2,))],
    )
    prefix = carried_in(states, False, state)
    pairs = heads * tokens * tokens * HEAD
    scores, local, q_held, weighted, gain_held = call(
        functools.partial(scores_body, heads, factor),
        (
            sds((heads, tokens, tokens), BF16), wide,
            in_vmem(queries), in_vmem(wide), in_vmem(gains),
        ),
        k_held, v_held, *in_hbm(queries, out_grad, gains),
        ins=[VMEM, VMEM, HBM, HBM, HBM],
        scratch=[in_vmem(out_grad), pltpu.SemaphoreType.DMA((3,))],
        flops=4 * pairs,
    )
    attended, stats, prefix = call(
        functools.partial(attend_body, heads, factor, group),
        (wide, sds((2, tokens), F32), sds((width, HEAD), F32)),
        q_held, weighted, local, *prefix,
    )
    every = from_all(stats, "tp")
    inv_rms, grad_attn, *updates = call(
        functools.partial(grad_body, heads, features, group, len(every)),
        (pltpu.VMEM((tokens, HEAD), F32), half, *pieces),
        attended, weighted, q_held, *every,
        scratch=[state],
    )
    suffix = carried_in(updates, True, state)
    normed, grad_q, gk_part, gv_part = call(
        functools.partial(local_body, heads, factor),
        (half, half, wide, wide),
        grad_attn, q_held, k_held, v_held, prefix, scores, attended, inv_rms, gain_held,
        flops=9 * pairs,
    )
    held = pltpu.VMEM((tokens, width), BF16)
    grad_k, grad_v = call(
        functools.partial(final_body, heads, factor, group),
        (half, half),
        k_held, v_held, gk_part, gv_part, *suffix,
        dests=(HBM, HBM),
        scratch=[state, held, held, pltpu.SemaphoreType.DMA((2 * heads,))],
    )
    return normed, grad_q, grad_k, grad_v


def solution(mesh):
    placed = (P("ctx", "tp"), P("ctx", "tp"), P("ctx", "tp"), P("tp"), P("ctx", "tp"))
    return jax.shard_map(
        on_device,
        mesh=mesh,
        in_specs=placed,
        out_specs=(P("ctx", "tp"), P("ctx", "tp"), P("ctx", "tp"), P("ctx", "tp")),
        check_vma=False,
    )
```

```python
import functools

import jax
import jax.numpy as jnp
from jax import lax
from jax.experimental import pallas as pl
from jax.experimental.pallas import tpu as pltpu
from jax.sharding import PartitionSpec as P

HEAD = 128

epsilon = 1e-06
STEPS = (3, 1, 2, 0)
F32 = jnp.float32
BF16 = jnp.bfloat16

NN = (((1,), (0,)), ((), ()))
NT = (((1,), (1,)), ((), ()))
TN = (((0,), (0,)), ((), ()))


def dot(a, b, dims):
    return lax.dot_general(a, b, dims, preferred_element_type=F32)


VMEM = pl.BlockSpec(memory_space=pltpu.VMEM)
HBM = pl.BlockSpec(memory_space=pltpu.HBM)


def call(body, outs, *args, ins=None, dests=None, scratch=(), flops=1e7):
    moved = sum(a.size * a.dtype.itemsize for a in args)
    return pl.pallas_call(
        body,
        out_shape=outs,
        in_specs=ins or [VMEM] * len(args),
        out_specs=dests or jax.tree.map(lambda _: VMEM, outs),
        scratch_shapes=scratch,
        compiler_params=pltpu.CompilerParams(vmem_limit_bytes=16 * 1024 * 1024),
        cost_estimate=pl.CostEstimate(flops=int(flops), bytes_accessed=int(moved), transcendentals=0),
    )(*args)


def head(h):
    return slice(h * HEAD, (h + 1) * HEAD)


def causal_mask(tokens):
    row = lax.broadcasted_iota(jnp.int32, (tokens, tokens), 0)
    col = lax.broadcasted_iota(jnp.int32, (tokens, tokens), 1)
    return row >= col


def rows_of(scratch, parts, place):
    rows = scratch.shape[0] // parts
    return scratch.at[pl.ds(pl.multiple_of(place * rows, rows), rows), :]


def halves(state):
    rows = state.shape[0] // 2
    x = lax.rem(lax.axis_index("ctx"), 2)

    def part(which):
        return state[pl.ds(pl.multiple_of(which * rows, rows), rows), :]

    return part(x), part(1 - x)


def give(state, outs):
    if len(outs) == 1:
        outs[0][...] = state[...].reshape(outs[0].shape)
        return
    mine, other = halves(state)
    for out, step in zip(outs, STEPS * 2):
        out[...] = other if step % 2 else mine


def sums_in_half(arrived, late, reverse):
    first = lax.rem(lax.axis_index("ctx"), 2) == 0
    diagonal, across, along, own = (ref[...] for ref in arrived)
    outer = [jnp.where(first, along, diagonal), jnp.where(first, diagonal, along)]
    inner = [jnp.where(first, own, across), jnp.where(first, across, own)]
    blocks = inner + outer if late else outer + inner
    before = [None] * 4
    running = jnp.zeros_like(own)
    for place in range(3, -1, -1) if reverse else range(4):
        before[place] = running
        running = running + blocks[place]
    inner, outer = (before[:2], before[2:]) if late else (before[2:], before[:2])
    back = [
        jnp.where(first, outer[1], outer[0]),
        jnp.where(first, inner[1], inner[0]),
        jnp.where(first, outer[0], outer[1]),
        jnp.where(first, inner[0], inner[1]),
    ]
    return back, running


def loads(pairs, sems):
    copies = [pltpu.make_async_copy(a, b, sems.at[i]) for i, (a, b) in enumerate(pairs)]
    for copy in copies:
        copy.start()
    return copies


def states_body(heads, k_hbm, v_hbm, k, v, *refs):
    outs, (state, sems) = refs[:-2], refs[-2:]
    for copy in loads(((k_hbm, k), (v_hbm, v)), sems):
        copy.wait()
    for h in range(heads):
        state[head(h), :] = dot(k[:, head(h)], v[:, head(h)], TN)
    give(state, outs)


def scan_body(count, reverse, arrived, sums):
    running = jnp.zeros(arrived.shape[1:], F32)
    for place in range(count - 1, -1, -1) if reverse else range(count):
        sums[place] = running
        running = running + arrived[place]


def lead_body(reverse, *refs):
    arrived, total, outs, more = refs[:4], refs[4], refs[5:9], refs[9:]
    back, running = sums_in_half(arrived, reverse, reverse)
    total[...] = running
    for out, part in zip(outs, back):
        out[...] = part
    if reverse:
        for out, part in zip(more, sums_in_half(arrived, False, True)[0]):
            out[...] = part
    else:
        more[0][...] = arrived[3][...]


def late_body(*refs):
    arrived, over, outs = refs[:4], refs[4], refs[5:]
    for out, part in zip(outs, sums_in_half(arrived, True, False)[0]):
        out[...] = part + over[...]


def add_body(*refs):
    for part, out in zip(refs[:4], refs[5:]):
        out[...] = part[...] + refs[4][...]


def pick(pieces, state):
    if len(pieces) == 1:
        state[...] = pieces[0][...].reshape(state.shape)
        return
    me = lax.axis_index("ctx")
    early, first = me < 4, lax.rem(me, 2) == 0
    inner = lax.rem(lax.div(me + 2, 4), 2) == 1
    diagonal, across, along, own = (
        jnp.where(early, a[...], b[...]) for a, b in zip(pieces[:4], pieces[4:])
    )
    mine = jnp.where(inner, own, along)
    other = jnp.where(inner, across, diagonal)
    rows = state.shape[0] // 2
    state[:rows, :] = jnp.where(first, mine, other)
    state[rows:, :] = jnp.where(first, other, mine)


def scores_body(heads, factor, k, v, q_hbm, og_hbm, gain_hbm, scores, attended, q, weighted, gain, og, sems):
    copies = loads(((q_hbm, q), (og_hbm, og), (gain_hbm, gain)), sems)
    copies[0].wait()
    causal = causal_mask(q.shape[0])
    for h in range(heads):
        raw = dot(q[:, head(h)], k[:, head(h)], NT) * factor
        sc = jnp.where(causal, raw, 0.0).astype(BF16)
        scores[h] = sc
        attended[:, head(h)] = dot(sc, v[:, head(h)], NN)
    for copy in copies[1:]:
        copy.wait()
    for h in range(heads):
        weighted[:, head(h)] = og[:, head(h)].astype(F32) * gain[h : h + 1, :]


def attend_body(heads, factor, q, weighted, local, *refs):
    pieces, (attended, stats, prefix) = refs[:-3], refs[-3:]
    pick(pieces, prefix)
    power = 0.0
    inner = 0.0
    for h in range(heads):
        att = factor * dot(q[:, head(h)], prefix[head(h), :].astype(BF16), NN) + local[:, head(h)]
        attended[:, head(h)] = att
        power = power + att * att
        inner = inner + weighted[:, head(h)] * att
    stats[0:1, :] = jnp.sum(power.T, axis=0, keepdims=True)
    stats[1:2, :] = jnp.sum(inner.T, axis=0, keepdims=True)


def grad_body(heads, features, ways, attended, weighted, q, *refs):
    stats, (spread, grad), outs, updates = refs[:ways], refs[ways : ways + 2], refs[ways + 2 : -1], refs[-1]
    total = stats[0][...]
    for other in stats[1:]:
        total = total + other[...]
    inv_rms = lax.rsqrt(total[0:1, :] / features + epsilon)
    bend = inv_rms * inv_rms * (total[1:2, :] / features)
    tokens = q.shape[0]
    inv_rms = jnp.broadcast_to(inv_rms, (HEAD, tokens)).T
    bend = jnp.broadcast_to(bend, (HEAD, tokens)).T
    spread[...] = inv_rms
    for h in range(heads):
        ga = (inv_rms * (weighted[:, head(h)] - attended[:, head(h)] * bend)).astype(BF16)
        grad[:, head(h)] = ga
        updates[head(h), :] = dot(q[:, head(h)], ga, TN)
    give(updates, outs)


def local_body(heads, factor, ga, q, k, v, prefix, scores, attended, inv_rms, gain, normed, gq, gk_part, gv_part):
    causal = causal_mask(q.shape[0])
    for h in range(heads):
        normed[:, head(h)] = (attended[:, head(h)] * inv_rms[...] * gain[h : h + 1, :]).astype(BF16)
        gah = ga[:, head(h)]
        raw = dot(gah, v[:, head(h)], NT) * factor
        gs = jnp.where(causal, raw, 0.0).astype(BF16)
        out = factor * dot(gah, prefix[head(h), :].astype(BF16), NT)
        gq[:, head(h)] = (out + dot(gs, k[:, head(h)], NN)).astype(BF16)
        gk_part[:, head(h)] = dot(gs, q[:, head(h)], TN)
        gv_part[:, head(h)] = dot(scores[h], gah, TN)


def final_body(heads, factor, k, v, gk_part, gv_part, *refs):
    pieces, outs, (suffix, gk, gv, sems) = refs[:-6], refs[-6:-4], refs[-4:]
    pick(pieces, suffix)
    copies = []

    def send(h, held, out):
        copy = pltpu.make_async_copy(held.at[:, head(h)], out.at[:, head(h)], sems.at[len(copies)])
        copy.start()
        copies.append(copy)

    for h in range(heads):
        suf = suffix[head(h), :].astype(BF16)
        gk[:, head(h)] = (factor * dot(v[:, head(h)], suf, NT) + gk_part[:, head(h)]).astype(BF16)
        send(h, gk, outs[0])
        gv[:, head(h)] = (factor * dot(k[:, head(h)], suf, NN) + gv_part[:, head(h)]).astype(BF16)
        send(h, gv, outs[1])
    for copy in copies:
        copy.wait()


def exchange(pieces, halves_in, gather):
    ways = lax.axis_size("tp")

    def target(j, step):
        inner = j // 2 in (1, 2)
        if j // 4 not in halves_in or (step == 1 and not inner):
            return j
        return j ^ 2 if step == 3 and inner == gather else j ^ step

    return [
        lax.ppermute(
            piece,
            ("ctx", "tp"),
            [(j * ways + t, target(j, step) * ways + (t ^ 1)) for j in range(8) for t in range(ways)],
        )
        for piece, step in zip(pieces, STEPS)
    ]


def cross(total):
    ways = lax.axis_size("tp")
    pairs = [
        (j * ways + t, (j ^ 6) * ways + t if j // 2 in (1, 2) else j * ways + (t ^ 1))
        for j in range(8)
        for t in range(ways)
    ]
    return lax.ppermute(total, ("ctx", "tp"), pairs)


def carried_in(pieces, reverse):
    count = lax.axis_size("ctx")
    sds = jax.ShapeDtypeStruct
    if len(pieces) == 1:
        arrived = lax.all_to_all(pieces[0], "ctx", 0, 0, tiled=True)
        sums = call(functools.partial(scan_body, count, reverse), sds(arrived.shape, F32), arrived)
        return [lax.all_to_all(sums, "ctx", 0, 0, tiled=True)]
    piece = sds(pieces[0].shape, F32)
    if reverse:
        arrived = exchange(pieces, (0, 1), True)
        total, *back = call(functools.partial(lead_body, True), [piece] * 9, *arrived)
        over = cross(total)
        ahead = exchange(back[:4], (1,), False)
        back = call(add_body, [piece] * 4, *back[4:], over)
        return exchange(back, (0,), False) + ahead
    arrived = exchange(pieces[:3], (0,), True)
    own = lax.ppermute(pieces[3], "tp", [(t, t ^ 1) for t in range(lax.axis_size("tp"))])
    total, *back = call(functools.partial(lead_body, False), [piece] * 6, *arrived, own)
    over = cross(total)
    ahead = exchange(back[:4], (0,), False)
    arrived = exchange(pieces[4:7], (1,), True)
    back = call(late_body, [piece] * 4, *arrived, back[4], over)
    return ahead + exchange(back, (1,), False)


def from_all(part, axis):
    count = lax.axis_size(axis)
    even = count & (count - 1) == 0
    steps = [1, 3, 2] if count == 4 else range(1, count)
    return [part] + [
        lax.ppermute(part, axis, [(i, i ^ step if even else (i + step) % count) for i in range(count)])
        for step in steps
    ]


def on_device(queries, keys, values, gain, out_grad):
    tokens, width = queries.shape
    heads = width // HEAD
    count = lax.axis_size("ctx")
    factor = (HEAD * tokens * count) ** (-0.5)
    features = width * lax.axis_size("tp")
    gains = gain.reshape(heads, HEAD)
    sds = jax.ShapeDtypeStruct
    wide = sds((tokens, width), F32)
    half = sds((tokens, width), BF16)
    state = pltpu.VMEM((width, HEAD), F32)
    if count == 8 and lax.axis_size("tp") % 2 == 0:
        pieces = [sds((width // 2, HEAD), F32)] * 4
    else:
        pieces = [sds((count, width // count, HEAD), F32)]

    def in_hbm(*arrays):
        return [pltpu.with_memory_space_constraint(array, pltpu.HBM) for array in arrays]

    def in_vmem(array):
        return pltpu.VMEM(array.shape, array.dtype)

    k_held, v_held, *states = call(
        functools.partial(states_body, heads),
        (in_vmem(keys), in_vmem(values), *pieces, *pieces[1:]),
        *in_hbm(keys, values),
        ins=[HBM, HBM],
        scratch=[state, pltpu.SemaphoreType.DMA((2,))],
    )
    prefix = carried_in(states, False)
    pairs = heads * tokens * tokens * HEAD
    scores, local, q_held, weighted, gain_held = call(
        functools.partial(scores_body, heads, factor),
        (
            sds((heads, tokens, tokens), BF16), wide,
            in_vmem(queries), in_vmem(wide), in_vmem(gains),
        ),
        k_held, v_held, *in_hbm(queries, out_grad, gains),
        ins=[VMEM, VMEM, HBM, HBM, HBM],
        scratch=[in_vmem(out_grad), pltpu.SemaphoreType.DMA((3,))],
        flops=4 * pairs,
    )
    attended, stats, prefix = call(
        functools.partial(attend_body, heads, factor),
        (wide, sds((2, tokens), F32), sds((width, HEAD), F32)),
        q_held, weighted, local, *prefix,
    )
    every = from_all(stats, "tp")
    inv_rms, grad_attn, *updates = call(
        functools.partial(grad_body, heads, features, len(every)),
        (pltpu.VMEM((tokens, HEAD), F32), half, *pieces),
        attended, weighted, q_held, *every,
        scratch=[state],
    )
    suffix = carried_in(updates, True)
    normed, grad_q, gk_part, gv_part = call(
        functools.partial(local_body, heads, factor),
        (half, half, wide, wide),
        grad_attn, q_held, k_held, v_held, prefix, scores, attended, inv_rms, gain_held,
        flops=9 * pairs,
    )
    held = pltpu.VMEM((tokens, width), BF16)
    grad_k, grad_v = call(
        functools.partial(final_body, heads, factor),
        (half, half),
        k_held, v_held, gk_part, gv_part, *suffix,
        dests=(HBM, HBM),
        scratch=[state, held, held, pltpu.SemaphoreType.DMA((2 * heads,))],
    )
    return normed, grad_q, grad_k, grad_v


def solution(mesh):
    placed = (P("ctx", "tp"), P("ctx", "tp"), P("ctx", "tp"), P("tp"), P("ctx", "tp"))
    return jax.shard_map(
        on_device,
        mesh=mesh,
        in_specs=placed,
        out_specs=(P("ctx", "tp"), P("ctx", "tp"), P("ctx", "tp"), P("ctx", "tp")),
        check_vma=False,
    )
```

```python
import functools

import jax
import jax.numpy as jnp
from jax import lax
from jax.experimental import pallas as pl
from jax.experimental.pallas import tpu as pltpu
from jax.sharding import PartitionSpec as P

HEAD = 128

epsilon = 1e-06
STEPS = (3, 1, 2, 0)
BACK_STEPS = (3, 2, 1, 0)
F32 = jnp.float32
BF16 = jnp.bfloat16

NN = (((1,), (0,)), ((), ()))
NT = (((1,), (1,)), ((), ()))
TN = (((0,), (0,)), ((), ()))


def dot(a, b, dims):
    return lax.dot_general(a, b, dims, preferred_element_type=F32)


VMEM = pl.BlockSpec(memory_space=pltpu.VMEM)
HBM = pl.BlockSpec(memory_space=pltpu.HBM)


def call(body, outs, *args, ins=None, dests=None, scratch=(), flops=1e7):
    moved = sum(a.size * a.dtype.itemsize for a in args)
    return pl.pallas_call(
        body,
        out_shape=outs,
        in_specs=ins or [VMEM] * len(args),
        out_specs=dests or jax.tree.map(lambda _: VMEM, outs),
        scratch_shapes=scratch,
        compiler_params=pltpu.CompilerParams(vmem_limit_bytes=16 * 1024 * 1024),
        cost_estimate=pl.CostEstimate(flops=int(flops), bytes_accessed=int(moved), transcendentals=0),
    )(*args)


def head(h):
    return slice(h * HEAD, (h + 1) * HEAD)


def causal_mask(tokens):
    row = lax.broadcasted_iota(jnp.int32, (tokens, tokens), 0)
    col = lax.broadcasted_iota(jnp.int32, (tokens, tokens), 1)
    return row >= col


def rows_of(scratch, parts, place):
    rows = scratch.shape[0] // parts
    return scratch.at[pl.ds(pl.multiple_of(place * rows, rows), rows), :]


def halves(state):
    rows = state.shape[0] // 2
    x = lax.rem(lax.axis_index("ctx"), 2)

    def part(which):
        return state[pl.ds(pl.multiple_of(which * rows, rows), rows), :]

    return part(x), part(1 - x)


def give(state, outs):
    if len(outs) == 1:
        outs[0][...] = state[...].reshape(outs[0].shape)
        return
    mine, other = halves(state)
    for out, step in zip(outs, STEPS * 2):
        out[...] = other if step % 2 else mine


def quarter(state, place):
    rows = state.shape[0] // 4
    return state.at[pl.ds(pl.multiple_of(place * rows, rows), rows), :]


def give_quarters(state, outs):
    if len(outs) == 1:
        outs[0][...] = state[...].reshape(outs[0].shape)
        return
    place = lax.rem(lax.axis_index("ctx"), 4)
    for out, step in zip(outs, BACK_STEPS):
        out[...] = quarter(state, lax.bitwise_xor(place, step))[...]


def sums_in_half(arrived, late):
    first = lax.rem(lax.axis_index("ctx"), 2) == 0
    diagonal, across, along, own = (ref[...] for ref in arrived)
    outer = [jnp.where(first, along, diagonal), jnp.where(first, diagonal, along)]
    inner = [jnp.where(first, own, across), jnp.where(first, across, own)]
    before = []
    running = jnp.zeros_like(own)
    for block in inner + outer if late else outer + inner:
        before.append(running)
        running = running + block
    inner, outer = (before[:2], before[2:]) if late else (before[2:], before[:2])
    back = [
        jnp.where(first, outer[1], outer[0]),
        jnp.where(first, inner[1], inner[0]),
        jnp.where(first, outer[0], outer[1]),
        jnp.where(first, inner[0], inner[1]),
    ]
    return back, running


def loads(pairs, sems):
    copies = [pltpu.make_async_copy(a, b, sems.at[i]) for i, (a, b) in enumerate(pairs)]
    for copy in copies:
        copy.start()
    return copies


def states_body(heads, k_hbm, v_hbm, k, v, *refs):
    outs, (state, sems) = refs[:-2], refs[-2:]
    for copy in loads(((k_hbm, k), (v_hbm, v)), sems):
        copy.wait()
    for h in range(heads):
        state[head(h), :] = dot(k[:, head(h)], v[:, head(h)], TN)
    give(state, outs)


def scan_body(count, reverse, arrived, sums):
    running = jnp.zeros(arrived.shape[1:], F32)
    for place in range(count - 1, -1, -1) if reverse else range(count):
        sums[place] = running
        running = running + arrived[place]


def lead_body(*refs):
    arrived, total, outs, passed = refs[:4], refs[4], refs[5:9], refs[9]
    back, running = sums_in_half(arrived, False)
    total[...] = running
    for out, part in zip(outs, back):
        out[...] = part
    passed[...] = arrived[3][...]


def late_body(*refs):
    arrived, over, outs = refs[:4], refs[4], refs[5:]
    for out, part in zip(outs, sums_in_half(arrived, True)[0]):
        out[...] = part + over[...]


def back_lead_body(*refs):
    arrived, total, outs, sums = refs[:4], refs[4], refs[5:9], refs[9]
    place = lax.rem(lax.axis_index("ctx"), 4)
    for piece, step in zip(arrived, BACK_STEPS):
        quarter(sums, lax.bitwise_xor(place, step))[...] = piece[...]
    rows = total.shape[0]
    running = jnp.zeros(total.shape, F32)
    for block in range(3, -1, -1):
        own = slice(block * rows, (block + 1) * rows)
        here = sums[own, :]
        sums[own, :] = running
        running = running + here
    total[...] = running
    give_quarters(sums, outs)


def back_add_body(sums, over, *outs):
    give_quarters(sums, outs)
    for out in outs:
        out[...] += over[...]


def pick(pieces, state):
    if len(pieces) == 1:
        state[...] = pieces[0][...].reshape(state.shape)
        return
    me = lax.axis_index("ctx")
    early, first = me < 4, lax.rem(me, 2) == 0
    inner = lax.rem(lax.div(me + 2, 4), 2) == 1
    diagonal, across, along, own = (
        jnp.where(early, a[...], b[...]) for a, b in zip(pieces[:4], pieces[4:])
    )
    mine = jnp.where(inner, own, along)
    other = jnp.where(inner, across, diagonal)
    rows = state.shape[0] // 2
    state[:rows, :] = jnp.where(first, mine, other)
    state[rows:, :] = jnp.where(first, other, mine)


def pick_quarters(pieces, state):
    if len(pieces) == 1:
        state[...] = pieces[0][...].reshape(state.shape)
        return
    me = lax.axis_index("ctx")
    for i, step in enumerate(BACK_STEPS):
        rows = quarter(state, lax.bitwise_xor(lax.rem(me, 4), step))
        rows[...] = jnp.where(me < 4, pieces[i][...], pieces[4 + i][...])


def scores_body(heads, factor, k, v, q_hbm, og_hbm, gain_hbm, scores, attended, q, weighted, gain, og, sems):
    copies = loads(((q_hbm, q), (og_hbm, og), (gain_hbm, gain)), sems)
    copies[0].wait()
    causal = causal_mask(q.shape[0])
    for h in range(heads):
        raw = dot(q[:, head(h)], k[:, head(h)], NT) * factor
        sc = jnp.where(causal, raw, 0.0).astype(BF16)
        scores[h] = sc
        attended[:, head(h)] = dot(sc, v[:, head(h)], NN)
    for copy in copies[1:]:
        copy.wait()
    for h in range(heads):
        weighted[:, head(h)] = og[:, head(h)].astype(F32) * gain[h : h + 1, :]


def attend_body(heads, factor, q, weighted, local, *refs):
    pieces, (attended, stats, prefix) = refs[:-3], refs[-3:]
    pick(pieces, prefix)
    power = 0.0
    inner = 0.0
    for h in range(heads):
        att = factor * dot(q[:, head(h)], prefix[head(h), :].astype(BF16), NN) + local[:, head(h)]
        attended[:, head(h)] = att
        power = power + att * att
        inner = inner + weighted[:, head(h)] * att
    stats[0:1, :] = jnp.sum(power.T, axis=0, keepdims=True)
    stats[1:2, :] = jnp.sum(inner.T, axis=0, keepdims=True)


def grad_body(heads, features, ways, attended, weighted, q, *refs):
    stats, (spread, grad), outs, updates = refs[:ways], refs[ways : ways + 2], refs[ways + 2 : -1], refs[-1]
    total = stats[0][...]
    for other in stats[1:]:
        total = total + other[...]
    inv_rms = lax.rsqrt(total[0:1, :] / features + epsilon)
    bend = inv_rms * inv_rms * (total[1:2, :] / features)
    tokens = q.shape[0]
    inv_rms = jnp.broadcast_to(inv_rms, (HEAD, tokens)).T
    bend = jnp.broadcast_to(bend, (HEAD, tokens)).T
    spread[...] = inv_rms
    for h in range(heads):
        ga = (inv_rms * (weighted[:, head(h)] - attended[:, head(h)] * bend)).astype(BF16)
        grad[:, head(h)] = ga
        updates[head(h), :] = dot(q[:, head(h)], ga, TN)
    give_quarters(updates, outs)


def local_body(heads, factor, ga, q, k, v, prefix, scores, attended, inv_rms, gain, normed, gq, gk_part, gv_part):
    causal = causal_mask(q.shape[0])
    for h in range(heads):
        normed[:, head(h)] = (attended[:, head(h)] * inv_rms[...] * gain[h : h + 1, :]).astype(BF16)
        gah = ga[:, head(h)]
        raw = dot(gah, v[:, head(h)], NT) * factor
        gs = jnp.where(causal, raw, 0.0).astype(BF16)
        out = factor * dot(gah, prefix[head(h), :].astype(BF16), NT)
        gq[:, head(h)] = (out + dot(gs, k[:, head(h)], NN)).astype(BF16)
        gk_part[:, head(h)] = dot(gs, q[:, head(h)], TN)
        gv_part[:, head(h)] = dot(scores[h], gah, TN)


def final_body(heads, factor, k, v, gk_part, gv_part, *refs):
    pieces, outs, (suffix, gk, gv, sems) = refs[:-6], refs[-6:-4], refs[-4:]
    pick_quarters(pieces, suffix)
    copies = []

    def send(h, held, out):
        copy = pltpu.make_async_copy(held.at[:, head(h)], out.at[:, head(h)], sems.at[len(copies)])
        copy.start()
        copies.append(copy)

    for h in range(heads):
        suf = suffix[head(h), :].astype(BF16)
        gk[:, head(h)] = (factor * dot(v[:, head(h)], suf, NT) + gk_part[:, head(h)]).astype(BF16)
        send(h, gk, outs[0])
        gv[:, head(h)] = (factor * dot(k[:, head(h)], suf, NN) + gv_part[:, head(h)]).astype(BF16)
        send(h, gv, outs[1])
    for copy in copies:
        copy.wait()


def permuted(piece, target):
    ways = lax.axis_size("tp")
    pairs = []
    for j in range(8):
        to, swap = target(j)
        pairs += [(j * ways + t, to * ways + (t ^ swap)) for t in range(ways)]
    return lax.ppermute(piece, ("ctx", "tp"), pairs)


def exchange(pieces, half, gather):
    def target(j, step):
        inner = j // 2 in (1, 2)
        if j // 4 != half or (step == 1 and not inner):
            return j, 1
        return (j ^ 2 if step == 3 and inner == gather else j ^ step), 1

    return [
        permuted(piece, functools.partial(target, step=step)) for piece, step in zip(pieces, STEPS)
    ]


def back_exchange(pieces, halves_in):
    return [
        permuted(piece, lambda j, step=step: (j ^ step if j // 4 in halves_in else j, 1))
        for piece, step in zip(pieces, BACK_STEPS)
    ]


def over_all(pieces, reverse):
    count = lax.axis_size("ctx")
    arrived = lax.all_to_all(pieces[0], "ctx", 0, 0, tiled=True)
    sums = call(
        functools.partial(scan_body, count, reverse),
        jax.ShapeDtypeStruct(arrived.shape, F32),
        arrived,
    )
    return [lax.all_to_all(sums, "ctx", 0, 0, tiled=True)]


def earlier_sums(pieces):
    if len(pieces) == 1:
        return over_all(pieces, False)
    piece = jax.ShapeDtypeStruct(pieces[0].shape, F32)
    arrived = exchange(pieces[:3], 0, True)
    own = permuted(pieces[3], lambda j: (j, 1))
    total, *back = call(lead_body, [piece] * 6, *arrived, own)
    over = permuted(total, lambda j: (j ^ 6, 0) if j // 2 in (1, 2) else (j, 1))
    ahead = exchange(back[:4], 0, False)
    arrived = exchange(pieces[4:7], 1, True)
    back = call(late_body, [piece] * 4, *arrived, back[4], over)
    return ahead + exchange(back, 1, False)


def later_sums(pieces):
    if len(pieces) == 1:
        return over_all(pieces, True)
    rows, width = pieces[0].shape
    piece = jax.ShapeDtypeStruct((rows, width), F32)
    arrived = back_exchange(pieces, (0, 1))
    total, *back, sums = call(
        back_lead_body, [piece] * 5 + [jax.ShapeDtypeStruct((4 * rows, width), F32)], *arrived
    )
    over = permuted(total, lambda j: (j ^ 4, 0))
    ahead = back_exchange(back, (1,))
    back = call(back_add_body, [piece] * 4, sums, over)
    return back_exchange(back, (0,)) + ahead


def from_all(part, axis):
    count = lax.axis_size(axis)
    even = count & (count - 1) == 0
    steps = [1, 3, 2] if count == 4 else range(1, count)
    return [part] + [
        lax.ppermute(part, axis, [(i, i ^ step if even else (i + step) % count) for i in range(count)])
        for step in steps
    ]


def on_device(queries, keys, values, gain, out_grad):
    tokens, width = queries.shape
    heads = width // HEAD
    count = lax.axis_size("ctx")
    factor = (HEAD * tokens * count) ** (-0.5)
    features = width * lax.axis_size("tp")
    gains = gain.reshape(heads, HEAD)
    sds = jax.ShapeDtypeStruct
    wide = sds((tokens, width), F32)
    half = sds((tokens, width), BF16)
    state = pltpu.VMEM((width, HEAD), F32)
    if count == 8 and lax.axis_size("tp") % 2 == 0:
        pieces = [sds((width // 2, HEAD), F32)] * 7
        quarters = [sds((width // 4, HEAD), F32)] * 4
    else:
        pieces = quarters = [sds((count, width // count, HEAD), F32)]

    def in_hbm(*arrays):
        return [pltpu.with_memory_space_constraint(array, pltpu.HBM) for array in arrays]

    def in_vmem(array):
        return pltpu.VMEM(array.shape, array.dtype)

    k_held, v_held, *states = call(
        functools.partial(states_body, heads),
        (in_vmem(keys), in_vmem(values), *pieces),
        *in_hbm(keys, values),
        ins=[HBM, HBM],
        scratch=[state, pltpu.SemaphoreType.DMA((2,))],
    )
    prefix = earlier_sums(states)
    pairs = heads * tokens * tokens * HEAD
    scores, local, q_held, weighted, gain_held = call(
        functools.partial(scores_body, heads, factor),
        (
            sds((heads, tokens, tokens), BF16), wide,
            in_vmem(queries), in_vmem(wide), in_vmem(gains),
        ),
        k_held, v_held, *in_hbm(queries, out_grad, gains),
        ins=[VMEM, VMEM, HBM, HBM, HBM],
        scratch=[in_vmem(out_grad), pltpu.SemaphoreType.DMA((3,))],
        flops=4 * pairs,
    )
    attended, stats, prefix = call(
        functools.partial(attend_body, heads, factor),
        (wide, sds((2, tokens), F32), sds((width, HEAD), F32)),
        q_held, weighted, local, *prefix,
    )
    every = from_all(stats, "tp")
    inv_rms, grad_attn, *updates = call(
        functools.partial(grad_body, heads, features, len(every)),
        (pltpu.VMEM((tokens, HEAD), F32), half, *quarters),
        attended, weighted, q_held, *every,
        scratch=[state],
    )
    suffix = later_sums(updates)
    normed, grad_q, gk_part, gv_part = call(
        functools.partial(local_body, heads, factor),
        (half, half, wide, wide),
        grad_attn, q_held, k_held, v_held, prefix, scores, attended, inv_rms, gain_held,
        flops=9 * pairs,
    )
    held = pltpu.VMEM((tokens, width), BF16)
    grad_k, grad_v = call(
        functools.partial(final_body, heads, factor),
        (half, half),
        k_held, v_held, gk_part, gv_part, *suffix,
        dests=(HBM, HBM),
        scratch=[state, held, held, pltpu.SemaphoreType.DMA((2 * heads,))],
    )
    return normed, grad_q, grad_k, grad_v


def solution(mesh):
    placed = (P("ctx", "tp"), P("ctx", "tp"), P("ctx", "tp"), P("tp"), P("ctx", "tp"))
    return jax.shard_map(
        on_device,
        mesh=mesh,
        in_specs=placed,
        out_specs=(P("ctx", "tp"), P("ctx", "tp"), P("ctx", "tp"), P("ctx", "tp")),
        check_vma=False,
    )
```

```python
import functools

import jax
import jax.numpy as jnp
from jax import lax
from jax.experimental import pallas as pl
from jax.experimental.pallas import tpu as pltpu
from jax.sharding import PartitionSpec as P

HEAD = 128

epsilon = 1e-06
ALONE = (0, 2)
SHARED = (1, 3)
F32 = jnp.float32
BF16 = jnp.bfloat16

NN = (((1,), (0,)), ((), ()))
NT = (((1,), (1,)), ((), ()))
TN = (((0,), (0,)), ((), ()))


def dot(a, b, dims):
    return lax.dot_general(a, b, dims, preferred_element_type=F32)


VMEM = pl.BlockSpec(memory_space=pltpu.VMEM)
HBM = pl.BlockSpec(memory_space=pltpu.HBM)


def call(body, outs, *args, ins=None, dests=None, scratch=(), flops=1e7):
    moved = sum(a.size * a.dtype.itemsize for a in args)
    return pl.pallas_call(
        body,
        out_shape=outs,
        in_specs=ins or [VMEM] * len(args),
        out_specs=dests or jax.tree.map(lambda _: VMEM, outs),
        scratch_shapes=scratch,
        compiler_params=pltpu.CompilerParams(vmem_limit_bytes=16 * 1024 * 1024),
        cost_estimate=pl.CostEstimate(flops=int(flops), bytes_accessed=int(moved), transcendentals=0),
    )(*args)


def head(h):
    return slice(h * HEAD, (h + 1) * HEAD)


def causal_mask(tokens):
    row = lax.broadcasted_iota(jnp.int32, (tokens, tokens), 0)
    col = lax.broadcasted_iota(jnp.int32, (tokens, tokens), 1)
    return row >= col


def rows_of(scratch, parts, place):
    rows = scratch.shape[0] // parts
    return scratch.at[pl.ds(pl.multiple_of(place * rows, rows), rows), :]


def partner(i, group):
    return group - 1 - i


def give(scratch, group, outs):
    if len(outs) == 1:
        outs[0][...] = scratch[...].reshape(outs[0].shape)
        return
    place = lax.rem(lax.axis_index("ctx"), group)
    for i, out in enumerate(outs):
        out[...] = rows_of(scratch, group, lax.bitwise_xor(place, partner(i, group)))[...]


def take(ins, scratch, group):
    if len(ins) == 1:
        scratch[...] = ins[0][...].reshape(scratch.shape).astype(scratch.dtype)
        return
    place = lax.rem(lax.axis_index("ctx"), group)
    for i, piece in enumerate(ins):
        rows_of(scratch, group, lax.bitwise_xor(place, partner(i, group)))[...] = piece[...]


def running_sums(scratch, parts, reverse):
    rows = scratch.shape[0] // parts
    running = jnp.zeros((rows, scratch.shape[1]), F32)
    for place in range(parts - 1, -1, -1) if reverse else range(parts):
        own = slice(place * rows, (place + 1) * rows)
        here = scratch[own, :]
        scratch[own, :] = running
        running = running + here
    return running


def loads(pairs, sems):
    copies = [pltpu.make_async_copy(a, b, sems.at[i]) for i, (a, b) in enumerate(pairs)]
    for copy in copies:
        copy.start()
    return copies


def states_body(heads, group, k_hbm, v_hbm, k, v, *refs):
    outs, (state, sems) = refs[:-2], refs[-2:]
    for copy in loads(((k_hbm, k), (v_hbm, v)), sems):
        copy.wait()
    for h in range(heads):
        state[head(h), :] = dot(k[:, head(h)], v[:, head(h)], TN)
    give(state, group, outs[:group])
    for again, i in zip(outs[group:], ALONE):
        again[...] = outs[i][...]


def scan_body(count, reverse, arrived, sums, scratch):
    take([arrived], scratch, count)
    running_sums(scratch, count, reverse)
    give(scratch, count, [sums])


def inner_body(group, reverse, *refs):
    arrived, total, outs, sums = refs[:group], refs[group], refs[group + 1 : 2 * group + 1], refs[-1]
    take(arrived, sums, group)
    total[...] = running_sums(sums, group, reverse)
    give(sums, group, outs)
    if not reverse:
        for passed, i in zip(refs[2 * group + 1 : -1], SHARED):
            passed[...] = arrived[i][...]


def add_body(group, sums, over, *outs):
    place = lax.rem(lax.axis_index("ctx"), group)
    for i, out in enumerate(outs):
        out[...] = rows_of(sums, group, lax.bitwise_xor(place, partner(i, group)))[...] + over[...]


def late_body(group, reverse, *refs):
    arrived, over, outs, sums = refs[:group], refs[group], refs[group + 1 : -1], refs[-1]
    take(arrived, sums, group)
    running_sums(sums, group, reverse)
    add_body(group, sums, over, *outs)


def pick(pieces, scratch, group):
    many = len(pieces) // 2
    if many == 0:
        take(pieces, scratch, group)
        return
    early = lax.axis_index("ctx") < group
    place = lax.rem(lax.axis_index("ctx"), group)
    for i in range(many):
        rows = rows_of(scratch, group, lax.bitwise_xor(place, partner(i, group)))
        rows[...] = jnp.where(early, pieces[i][...], pieces[many + i][...]).astype(scratch.dtype)


def scores_body(heads, factor, k, v, q_hbm, og_hbm, gain_hbm, scores, attended, q, weighted, gain, og, sems):
    copies = loads(((q_hbm, q), (og_hbm, og), (gain_hbm, gain)), sems)
    copies[0].wait()
    causal = causal_mask(q.shape[0])
    for h in range(heads):
        raw = dot(q[:, head(h)], k[:, head(h)], NT) * factor
        sc = jnp.where(causal, raw, 0.0).astype(BF16)
        scores[h] = sc
        attended[:, head(h)] = dot(sc, v[:, head(h)], NN)
    for copy in copies[1:]:
        copy.wait()
    for h in range(heads):
        weighted[:, head(h)] = og[:, head(h)].astype(F32) * gain[h : h + 1, :]


def attend_body(heads, factor, group, q, weighted, local, *refs):
    pieces, (attended, stats, prefix) = refs[:-3], refs[-3:]
    pick(pieces, prefix, group)
    power = 0.0
    inner = 0.0
    for h in range(heads):
        att = factor * dot(q[:, head(h)], prefix[head(h), :], NN) + local[:, head(h)]
        attended[:, head(h)] = att
        power = power + att * att
        inner = inner + weighted[:, head(h)] * att
    lane = lax.broadcasted_iota(jnp.int32, power.shape, 1)
    power = jnp.sum(power, axis=1, keepdims=True)
    inner = jnp.sum(inner, axis=1, keepdims=True)
    stats[...] = jnp.where(lane == 0, power, inner)[:, :8].T[:2, :]


def grad_body(heads, features, group, ways, attended, weighted, q, *refs):
    stats, (spread, grad), outs, updates = refs[:ways], refs[ways : ways + 2], refs[ways + 2 : -1], refs[-1]
    total = stats[0][...]
    for other in stats[1:]:
        total = total + other[...]
    inv_rms = lax.rsqrt(total[0:1, :] / features + epsilon)
    bend = inv_rms * inv_rms * (total[1:2, :] / features)
    row = lax.broadcasted_iota(jnp.int32, (8, q.shape[0]), 0)
    columns = jnp.where(row == 0, inv_rms, bend).T
    inv_rms = jnp.broadcast_to(columns[:, 0:1], (q.shape[0], HEAD))
    bend = jnp.broadcast_to(columns[:, 1:2], (q.shape[0], HEAD))
    spread[...] = inv_rms
    for h in range(heads):
        ga = (inv_rms * (weighted[:, head(h)] - attended[:, head(h)] * bend)).astype(BF16)
        grad[:, head(h)] = ga
        updates[head(h), :] = dot(q[:, head(h)], ga, TN)
    give(updates, group, outs)


def local_body(heads, factor, ga, q, k, v, prefix, scores, attended, inv_rms, gain, normed, gq, gk_part, gv_part):
    causal = causal_mask(q.shape[0])
    for h in range(heads):
        normed[:, head(h)] = (attended[:, head(h)] * inv_rms[...] * gain[h : h + 1, :]).astype(BF16)
        gah = ga[:, head(h)]
        raw = dot(gah, v[:, head(h)], NT) * factor
        gs = jnp.where(causal, raw, 0.0).astype(BF16)
        out = factor * dot(gah, prefix[head(h), :], NT)
        gq[:, head(h)] = (out + dot(gs, k[:, head(h)], NN)).astype(BF16)
        gk_part[:, head(h)] = dot(gs, q[:, head(h)], TN)
        gv_part[:, head(h)] = dot(scores[h], gah, TN)


def final_body(heads, factor, group, k, v, gk_part, gv_part, *refs):
    pieces, outs, (suffix, gk, gv, sems) = refs[:-6], refs[-6:-4], refs[-4:]
    pick(pieces, suffix, group)
    copies = []

    def send(h, held, out):
        copy = pltpu.make_async_copy(held.at[:, head(h)], out.at[:, head(h)], sems.at[len(copies)])
        copy.start()
        copies.append(copy)

    for h in range(heads):
        suf = suffix[head(h), :]
        gk[:, head(h)] = (factor * dot(v[:, head(h)], suf, NT) + gk_part[:, head(h)]).astype(BF16)
        send(h, gk, outs[0])
        gv[:, head(h)] = (factor * dot(k[:, head(h)], suf, NN) + gv_part[:, head(h)]).astype(BF16)
        send(h, gv, outs[1])
    for copy in copies:
        copy.wait()


def exchange(piece, i, active, group):
    ways = lax.axis_size("tp")
    pairs = [
        (j * ways + t, (j ^ partner(i, group) if j in active else j) * ways + (t ^ 1))
        for j in range(2 * group)
        for t in range(ways)
    ]
    return lax.ppermute(piece, ("ctx", "tp"), pairs)


def carried_in(pieces, reverse, state):
    again = () if reverse or len(pieces) == 1 else pieces[-len(ALONE) :]
    group = len(pieces) - len(again)
    pieces = pieces[:group]
    count = lax.axis_size("ctx")
    sds = jax.ShapeDtypeStruct
    if group == 1:
        arrived = lax.all_to_all(pieces[0], "ctx", 0, 0, tiled=True)
        sums = call(
            functools.partial(scan_body, count, reverse),
            sds(arrived.shape, F32), arrived, scratch=[state],
        )
        return [lax.all_to_all(sums, "ctx", 0, 0, tiled=True)]
    rows, width = pieces[0].shape
    piece = sds((rows, width), F32)
    early, late, both = range(group), range(group, count), range(count)
    first, second = (late, early) if reverse else (early, late)
    everyone = range(group)
    arrived = [
        exchange(pieces[i], i, both if reverse or i in SHARED else first, group) for i in everyone
    ]
    kept = [sds((group * rows, width), F32)] if reverse else [piece] * len(SHARED)
    total, *back = call(
        functools.partial(inner_body, group, reverse),
        [piece] * (group + 1) + kept,
        *arrived,
        scratch=[] if reverse else [state],
    )
    over = lax.ppermute(total, "ctx", [(j, j ^ group) for j in both])
    ahead = [exchange(back[i], i, first, group) for i in everyone]
    if reverse:
        back = call(functools.partial(add_body, group), [piece] * group, back[group], over)
    else:
        own = [exchange(part, i, second, group) for part, i in zip(again, ALONE)]
        mixed = [own[ALONE.index(i)] if i in ALONE else back[group + SHARED.index(i)] for i in everyone]
        back = call(
            functools.partial(late_body, group, reverse),
            [piece] * group, *mixed, over, scratch=[state],
        )
    behind = [exchange(back[i], i, second, group) for i in everyone]
    return [*behind, *ahead] if reverse else [*ahead, *behind]


def from_all(part, axis):
    count = lax.axis_size(axis)
    even = count & (count - 1) == 0
    steps = [1, 3, 2] if count == 4 else range(1, count)
    return [part] + [
        lax.ppermute(part, axis, [(i, i ^ step if even else (i + step) % count) for i in range(count)])
        for step in steps
    ]


def on_device(queries, keys, values, gain, out_grad):
    tokens, width = queries.shape
    heads = width // HEAD
    count = lax.axis_size("ctx")
    factor = (HEAD * tokens * count) ** (-0.5)
    features = width * lax.axis_size("tp")
    gains = gain.reshape(heads, HEAD)
    sds = jax.ShapeDtypeStruct
    wide = sds((tokens, width), F32)
    half = sds((tokens, width), BF16)
    state = pltpu.VMEM((width, HEAD), F32)
    if count == 8 and lax.axis_size("tp") % 2 == 0:
        group = count // 2
        pieces = [sds((width // group, HEAD), F32)] * group
    else:
        group = count
        pieces = [sds((count, width // count, HEAD), F32)]

    def in_hbm(*arrays):
        return [pltpu.with_memory_space_constraint(array, pltpu.HBM) for array in arrays]

    def in_vmem(array):
        return pltpu.VMEM(array.shape, array.dtype)

    k_held, v_held, *states = call(
        functools.partial(states_body, heads, group),
        (in_vmem(keys), in_vmem(values), *pieces, *(pieces[i] for i in ALONE if len(pieces) > 1)),
        *in_hbm(keys, values),
        ins=[HBM, HBM],
        scratch=[state, pltpu.SemaphoreType.DMA((2,))],
    )
    prefix = carried_in(states, False, state)
    pairs = heads * tokens * tokens * HEAD
    scores, local, q_held, weighted, gain_held = call(
        functools.partial(scores_body, heads, factor),
        (
            sds((heads, tokens, tokens), BF16), wide,
            in_vmem(queries), in_vmem(wide), in_vmem(gains),
        ),
        k_held, v_held, *in_hbm(queries, out_grad, gains),
        ins=[VMEM, VMEM, HBM, HBM, HBM],
        scratch=[in_vmem(out_grad), pltpu.SemaphoreType.DMA((3,))],
        flops=4 * pairs,
    )
    attended, stats, prefix = call(
        functools.partial(attend_body, heads, factor, group),
        (wide, sds((2, tokens), F32), sds((width, HEAD), BF16)),
        q_held, weighted, local, *prefix,
    )
    every = from_all(stats, "tp")
    inv_rms, grad_attn, *updates = call(
        functools.partial(grad_body, heads, features, group, len(every)),
        (pltpu.VMEM((tokens, HEAD), F32), half, *pieces),
        attended, weighted, q_held, *every,
        scratch=[state],
    )
    suffix = carried_in(updates, True, state)
    normed, grad_q, gk_part, gv_part = call(
        functools.partial(local_body, heads, factor),
        (half, half, wide, wide),
        grad_attn, q_held, k_held, v_held, prefix, scores, attended, inv_rms, gain_held,
        flops=9 * pairs,
    )
    held = pltpu.VMEM((tokens, width), BF16)
    grad_k, grad_v = call(
        functools.partial(final_body, heads, factor, group),
        (half, half),
        k_held, v_held, gk_part, gv_part, *suffix,
        dests=(HBM, HBM),
        scratch=[pltpu.VMEM((width, HEAD), BF16), held, held, pltpu.SemaphoreType.DMA((2 * heads,))],
    )
    return normed, grad_q, grad_k, grad_v


def solution(mesh):
    placed = (P("ctx", "tp"), P("ctx", "tp"), P("ctx", "tp"), P("tp"), P("ctx", "tp"))
    return jax.shard_map(
        on_device,
        mesh=mesh,
        in_specs=placed,
        out_specs=(P("ctx", "tp"), P("ctx", "tp"), P("ctx", "tp"), P("ctx", "tp")),
        check_vma=False,
    )
```

```python
import functools

import jax
import jax.numpy as jnp
from jax import lax
from jax.experimental import pallas as pl
from jax.experimental.pallas import tpu as pltpu
from jax.sharding import PartitionSpec as P

HEAD = 128

epsilon = 1e-06
ALONE = (0, 2)
SHARED = (1, 3)
F32 = jnp.float32
BF16 = jnp.bfloat16

NN = (((1,), (0,)), ((), ()))
NT = (((1,), (1,)), ((), ()))
TN = (((0,), (0,)), ((), ()))


def dot(a, b, dims):
    return lax.dot_general(a, b, dims, preferred_element_type=F32)


def exact(a, b, dims):
    return lax.dot_general(
        a, b, dims, precision=lax.Precision.HIGHEST, preferred_element_type=F32
    )


VMEM = pl.BlockSpec(memory_space=pltpu.VMEM)
HBM = pl.BlockSpec(memory_space=pltpu.HBM)


def call(body, outs, *args, ins=None, dests=None, scratch=(), flops=1e7):
    moved = sum(a.size * a.dtype.itemsize for a in args)
    return pl.pallas_call(
        body,
        out_shape=outs,
        in_specs=ins or [VMEM] * len(args),
        out_specs=dests or jax.tree.map(lambda _: VMEM, outs),
        scratch_shapes=scratch,
        compiler_params=pltpu.CompilerParams(vmem_limit_bytes=16 * 1024 * 1024),
        cost_estimate=pl.CostEstimate(flops=int(flops), bytes_accessed=int(moved), transcendentals=0),
    )(*args)


def head(h):
    return slice(h * HEAD, (h + 1) * HEAD)


def causal_mask(tokens):
    row = lax.broadcasted_iota(jnp.int32, (tokens, tokens), 0)
    col = lax.broadcasted_iota(jnp.int32, (tokens, tokens), 1)
    return row >= col


def rows_of(scratch, parts, place):
    rows = scratch.shape[0] // parts
    return scratch.at[pl.ds(pl.multiple_of(place * rows, rows), rows), :]


def partner(i, group):
    return group - 1 - i


def give(scratch, group, outs):
    if len(outs) == 1:
        outs[0][...] = scratch[...].reshape(outs[0].shape)
        return
    place = lax.rem(lax.axis_index("ctx"), group)
    for i, out in enumerate(outs):
        out[...] = rows_of(scratch, group, lax.bitwise_xor(place, partner(i, group)))[...]


def take(ins, scratch, group):
    if len(ins) == 1:
        scratch[...] = ins[0][...].reshape(scratch.shape)
        return
    place = lax.rem(lax.axis_index("ctx"), group)
    for i, piece in enumerate(ins):
        rows_of(scratch, group, lax.bitwise_xor(place, partner(i, group)))[...] = piece[...]


def running_sums(scratch, parts, reverse):
    rows = scratch.shape[0] // parts
    running = jnp.zeros((rows, scratch.shape[1]), F32)
    for place in range(parts - 1, -1, -1) if reverse else range(parts):
        own = slice(place * rows, (place + 1) * rows)
        here = scratch[own, :]
        scratch[own, :] = running
        running = running + here
    return running


def loads(pairs, sems):
    copies = [pltpu.make_async_copy(a, b, sems.at[i]) for i, (a, b) in enumerate(pairs)]
    for copy in copies:
        copy.start()
    return copies


def states_body(heads, group, k_hbm, v_hbm, k, v, *refs):
    outs, (state, sems) = refs[:-2], refs[-2:]
    for copy in loads(((k_hbm, k), (v_hbm, v)), sems):
        copy.wait()
    for h in range(heads):
        state[head(h), :] = dot(k[:, head(h)], v[:, head(h)], TN)
    give(state, group, outs[:group])
    for again, i in zip(outs[group:], ALONE):
        again[...] = outs[i][...]


def scan_body(count, reverse, arrived, sums, scratch):
    take([arrived], scratch, count)
    running_sums(scratch, count, reverse)
    give(scratch, count, [sums])


def inner_body(group, reverse, *refs):
    arrived, total, outs, sums = refs[:group], refs[group], refs[group + 1 : 2 * group + 1], refs[-1]
    take(arrived, sums, group)
    total[...] = running_sums(sums, group, reverse)
    give(sums, group, outs)
    if not reverse:
        for passed, i in zip(refs[2 * group + 1 : -1], SHARED):
            passed[...] = arrived[i][...]


def add_body(group, sums, over, *outs):
    place = lax.rem(lax.axis_index("ctx"), group)
    for i, out in enumerate(outs):
        out[...] = rows_of(sums, group, lax.bitwise_xor(place, partner(i, group)))[...] + over[...]


def late_body(group, reverse, *refs):
    arrived, over, outs, sums = refs[:group], refs[group], refs[group + 1 : -1], refs[-1]
    take(arrived, sums, group)
    running_sums(sums, group, reverse)
    add_body(group, sums, over, *outs)


def pick(pieces, scratch, group):
    many = len(pieces) // 2
    if many == 0:
        take(pieces, scratch, group)
        return
    early = lax.axis_index("ctx") < group
    place = lax.rem(lax.axis_index("ctx"), group)
    for i in range(many):
        rows = rows_of(scratch, group, lax.bitwise_xor(place, partner(i, group)))
        rows[...] = jnp.where(early, pieces[i][...], pieces[many + i][...])


def scores_body(heads, factor, k, v, q_hbm, og_hbm, gain_hbm, scores, attended, q, weighted, gain, og, sems):
    copies = loads(((q_hbm, q), (og_hbm, og), (gain_hbm, gain)), sems)
    copies[0].wait()
    causal = causal_mask(q.shape[0])
    for h in range(heads):
        raw = dot(q[:, head(h)], k[:, head(h)], NT) * factor
        sc = jnp.where(causal, raw, 0.0).astype(BF16)
        scores[h] = sc
        attended[:, head(h)] = dot(sc, v[:, head(h)], NN)
    for copy in copies[1:]:
        copy.wait()
    for h in range(heads):
        weighted[:, head(h)] = og[:, head(h)].astype(F32) * gain[h : h + 1, :]


def attend_body(heads, factor, group, q, weighted, local, *refs):
    pieces, (attended, stats, prefix) = refs[:-3], refs[-3:]
    pick(pieces, prefix, group)
    power = 0.0
    inner = 0.0
    for h in range(heads):
        att = factor * dot(q[:, head(h)], prefix[head(h), :].astype(BF16), NN) + local[:, head(h)]
        attended[:, head(h)] = att
        power = power + att * att
        inner = inner + weighted[:, head(h)] * att
    ones = jnp.ones((8, HEAD), F32)
    stats[0:1, :] = exact(ones, power, NT)[0:1, :]
    stats[1:2, :] = exact(ones, inner, NT)[0:1, :]


def grad_body(heads, features, group, ways, attended, weighted, q, *refs):
    stats, (spread, grad), outs, updates = refs[:ways], refs[ways : ways + 2], refs[ways + 2 : -1], refs[-1]
    total = stats[0][...]
    for other in stats[1:]:
        total = total + other[...]
    inv_rms = lax.rsqrt(total[0:1, :] / features + epsilon)
    bend = inv_rms * inv_rms * (total[1:2, :] / features)
    row = lax.broadcasted_iota(jnp.int32, (8, q.shape[0]), 0)
    both = jnp.where(row == 0, inv_rms, jnp.where(row == 1, bend, 0.0))
    row = lax.broadcasted_iota(jnp.int32, (8, HEAD), 0)
    inv_rms = exact(both, jnp.where(row == 0, 1.0, 0.0), TN)
    bend = exact(both, jnp.where(row == 1, 1.0, 0.0), TN)
    spread[...] = inv_rms
    for h in range(heads):
        ga = (inv_rms * (weighted[:, head(h)] - attended[:, head(h)] * bend)).astype(BF16)
        grad[:, head(h)] = ga
        updates[head(h), :] = dot(q[:, head(h)], ga, TN)
    give(updates, group, outs)


def local_body(heads, factor, ga, q, k, v, prefix, scores, attended, inv_rms, gain, normed, gq, gk_part, gv_part):
    causal = causal_mask(q.shape[0])
    for h in range(heads):
        normed[:, head(h)] = (attended[:, head(h)] * inv_rms[...] * gain[h : h + 1, :]).astype(BF16)
        gah = ga[:, head(h)]
        raw = dot(gah, v[:, head(h)], NT) * factor
        gs = jnp.where(causal, raw, 0.0).astype(BF16)
        out = factor * dot(gah, prefix[head(h), :].astype(BF16), NT)
        gq[:, head(h)] = (out + dot(gs, k[:, head(h)], NN)).astype(BF16)
        gk_part[:, head(h)] = dot(gs, q[:, head(h)], TN)
        gv_part[:, head(h)] = dot(scores[h], gah, TN)


def final_body(heads, factor, group, k, v, gk_part, gv_part, *refs):
    pieces, outs, (suffix, gk, gv, sems) = refs[:-6], refs[-6:-4], refs[-4:]
    pick(pieces, suffix, group)
    copies = []

    def send(h, held, out):
        copy = pltpu.make_async_copy(held.at[:, head(h)], out.at[:, head(h)], sems.at[len(copies)])
        copy.start()
        copies.append(copy)

    for h in range(heads):
        suf = suffix[head(h), :].astype(BF16)
        gk[:, head(h)] = (factor * dot(v[:, head(h)], suf, NT) + gk_part[:, head(h)]).astype(BF16)
        send(h, gk, outs[0])
        gv[:, head(h)] = (factor * dot(k[:, head(h)], suf, NN) + gv_part[:, head(h)]).astype(BF16)
        send(h, gv, outs[1])
    for copy in copies:
        copy.wait()


def exchange(piece, i, active, group):
    ways = lax.axis_size("tp")
    pairs = [
        (j * ways + t, (j ^ partner(i, group) if j in active else j) * ways + (t ^ 1))
        for j in range(2 * group)
        for t in range(ways)
    ]
    return lax.ppermute(piece, ("ctx", "tp"), pairs)


def carried_in(pieces, reverse, state):
    again = () if reverse or len(pieces) == 1 else pieces[-len(ALONE) :]
    group = len(pieces) - len(again)
    pieces = pieces[:group]
    count = lax.axis_size("ctx")
    sds = jax.ShapeDtypeStruct
    if group == 1:
        arrived = lax.all_to_all(pieces[0], "ctx", 0, 0, tiled=True)
        sums = call(
            functools.partial(scan_body, count, reverse),
            sds(arrived.shape, F32), arrived, scratch=[state],
        )
        return [lax.all_to_all(sums, "ctx", 0, 0, tiled=True)]
    rows, width = pieces[0].shape
    piece = sds((rows, width), F32)
    early, late, both = range(group), range(group, count), range(count)
    first, second = (late, early) if reverse else (early, late)
    everyone = range(group)
    arrived = [
        exchange(pieces[i], i, both if reverse or i in SHARED else first, group) for i in everyone
    ]
    kept = [sds((group * rows, width), F32)] if reverse else [piece] * len(SHARED)
    total, *back = call(
        functools.partial(inner_body, group, reverse),
        [piece] * (group + 1) + kept,
        *arrived,
        scratch=[] if reverse else [state],
    )
    over = lax.ppermute(total, "ctx", [(j, j ^ group) for j in both])
    ahead = [exchange(back[i], i, first, group) for i in everyone]
    if reverse:
        back = call(functools.partial(add_body, group), [piece] * group, back[group], over)
    else:
        own = [exchange(part, i, second, group) for part, i in zip(again, ALONE)]
        mixed = [own[ALONE.index(i)] if i in ALONE else back[group + SHARED.index(i)] for i in everyone]
        back = call(
            functools.partial(late_body, group, reverse),
            [piece] * group, *mixed, over, scratch=[state],
        )
    behind = [exchange(back[i], i, second, group) for i in everyone]
    return [*behind, *ahead] if reverse else [*ahead, *behind]


def from_all(part, axis):
    count = lax.axis_size(axis)
    even = count & (count - 1) == 0
    steps = [1, 3, 2] if count == 4 else range(1, count)
    return [part] + [
        lax.ppermute(part, axis, [(i, i ^ step if even else (i + step) % count) for i in range(count)])
        for step in steps
    ]


def on_device(queries, keys, values, gain, out_grad):
    tokens, width = queries.shape
    heads = width // HEAD
    count = lax.axis_size("ctx")
    factor = (HEAD * tokens * count) ** (-0.5)
    features = width * lax.axis_size("tp")
    gains = gain.reshape(heads, HEAD)
    sds = jax.ShapeDtypeStruct
    wide = sds((tokens, width), F32)
    half = sds((tokens, width), BF16)
    state = pltpu.VMEM((width, HEAD), F32)
    if count == 8 and lax.axis_size("tp") % 2 == 0:
        group = count // 2
        pieces = [sds((width // group, HEAD), F32)] * group
    else:
        group = count
        pieces = [sds((count, width // count, HEAD), F32)]

    def in_hbm(*arrays):
        return [pltpu.with_memory_space_constraint(array, pltpu.HBM) for array in arrays]

    def in_vmem(array):
        return pltpu.VMEM(array.shape, array.dtype)

    k_held, v_held, *states = call(
        functools.partial(states_body, heads, group),
        (in_vmem(keys), in_vmem(values), *pieces, *(pieces[i] for i in ALONE if len(pieces) > 1)),
        *in_hbm(keys, values),
        ins=[HBM, HBM],
        scratch=[state, pltpu.SemaphoreType.DMA((2,))],
    )
    prefix = carried_in(states, False, state)
    pairs = heads * tokens * tokens * HEAD
    scores, local, q_held, weighted, gain_held = call(
        functools.partial(scores_body, heads, factor),
        (
            sds((heads, tokens, tokens), BF16), wide,
            in_vmem(queries), in_vmem(wide), in_vmem(gains),
        ),
        k_held, v_held, *in_hbm(queries, out_grad, gains),
        ins=[VMEM, VMEM, HBM, HBM, HBM],
        scratch=[in_vmem(out_grad), pltpu.SemaphoreType.DMA((3,))],
        flops=4 * pairs,
    )
    attended, stats, prefix = call(
        functools.partial(attend_body, heads, factor, group),
        (wide, sds((2, tokens), F32), sds((width, HEAD), F32)),
        q_held, weighted, local, *prefix,
    )
    every = from_all(stats, "tp")
    inv_rms, grad_attn, *updates = call(
        functools.partial(grad_body, heads, features, group, len(every)),
        (pltpu.VMEM((tokens, HEAD), F32), half, *pieces),
        attended, weighted, q_held, *every,
        scratch=[state],
    )
    suffix = carried_in(updates, True, state)
    normed, grad_q, gk_part, gv_part = call(
        functools.partial(local_body, heads, factor),
        (half, half, wide, wide),
        grad_attn, q_held, k_held, v_held, prefix, scores, attended, inv_rms, gain_held,
        flops=9 * pairs,
    )
    held = pltpu.VMEM((tokens, width), BF16)
    grad_k, grad_v = call(
        functools.partial(final_body, heads, factor, group),
        (half, half),
        k_held, v_held, gk_part, gv_part, *suffix,
        dests=(HBM, HBM),
        scratch=[state, held, held, pltpu.SemaphoreType.DMA((2 * heads,))],
    )
    return normed, grad_q, grad_k, grad_v


def solution(mesh):
    placed = (P("ctx", "tp"), P("ctx", "tp"), P("ctx", "tp"), P("tp"), P("ctx", "tp"))
    return jax.shard_map(
        on_device,
        mesh=mesh,
        in_specs=placed,
        out_specs=(P("ctx", "tp"), P("ctx", "tp"), P("ctx", "tp"), P("ctx", "tp")),
        check_vma=False,
    )
```

```python
import functools

import jax
import jax.numpy as jnp
from jax import lax
from jax.experimental import pallas as pl
from jax.experimental.pallas import tpu as pltpu
from jax.sharding import PartitionSpec as P

HEAD = 128

epsilon = 1e-06
GATHER_STEPS = (2, 3, 1, 0)
STEPS = (3, 1, 2, 0)
BACK_STEPS = (3, 2, 1, 0)
F32 = jnp.float32
BF16 = jnp.bfloat16

NN = (((1,), (0,)), ((), ()))
NT = (((1,), (1,)), ((), ()))
TN = (((0,), (0,)), ((), ()))


def dot(a, b, dims):
    return lax.dot_general(a, b, dims, preferred_element_type=F32)


VMEM = pl.BlockSpec(memory_space=pltpu.VMEM)
HBM = pl.BlockSpec(memory_space=pltpu.HBM)


def call(body, outs, *args, ins=None, dests=None, scratch=(), flops=1e7):
    moved = sum(a.size * a.dtype.itemsize for a in args)
    return pl.pallas_call(
        body,
        out_shape=outs,
        in_specs=ins or [VMEM] * len(args),
        out_specs=dests or jax.tree.map(lambda _: VMEM, outs),
        scratch_shapes=scratch,
        compiler_params=pltpu.CompilerParams(vmem_limit_bytes=16 * 1024 * 1024),
        cost_estimate=pl.CostEstimate(flops=int(flops), bytes_accessed=int(moved), transcendentals=0),
    )(*args)


def head(h):
    return slice(h * HEAD, (h + 1) * HEAD)


def causal_mask(tokens):
    row = lax.broadcasted_iota(jnp.int32, (tokens, tokens), 0)
    col = lax.broadcasted_iota(jnp.int32, (tokens, tokens), 1)
    return row >= col


def rows_of(scratch, parts, place):
    rows = scratch.shape[0] // parts
    return scratch.at[pl.ds(pl.multiple_of(place * rows, rows), rows), :]


def halves(state):
    rows = state.shape[0] // 2
    x = lax.rem(lax.axis_index("ctx"), 2)

    def part(which):
        return state[pl.ds(pl.multiple_of(which * rows, rows), rows), :]

    return part(x), part(1 - x)


def give(state, outs):
    if len(outs) == 1:
        outs[0][...] = state[...].reshape(outs[0].shape)
        return
    mine, other = halves(state)
    for out, step in zip(outs, GATHER_STEPS * 2):
        out[...] = other if step % 2 else mine


def quarter(state, place):
    rows = state.shape[0] // 4
    return state.at[pl.ds(pl.multiple_of(place * rows, rows), rows), :]


def give_quarters(state, outs):
    if len(outs) == 1:
        outs[0][...] = state[...].reshape(outs[0].shape)
        return
    place = lax.rem(lax.axis_index("ctx"), 4)
    for out, step in zip(outs, BACK_STEPS):
        out[...] = quarter(state, lax.bitwise_xor(place, step))[...]


def sums_in_half(arrived, late):
    first = lax.rem(lax.axis_index("ctx"), 2) == 0
    along, diagonal, across, own = (ref[...] for ref in arrived)
    outer = [jnp.where(first, along, diagonal), jnp.where(first, diagonal, along)]
    inner = [jnp.where(first, own, across), jnp.where(first, across, own)]
    before = []
    running = jnp.zeros_like(own)
    for block in inner + outer if late else outer + inner:
        before.append(running)
        running = running + block
    inner, outer = (before[:2], before[2:]) if late else (before[2:], before[:2])
    back = [
        jnp.where(first, outer[1], outer[0]),
        jnp.where(first, inner[1], inner[0]),
        jnp.where(first, outer[0], outer[1]),
        jnp.where(first, inner[0], inner[1]),
    ]
    return back, running


def loads(pairs, sems):
    copies = [pltpu.make_async_copy(a, b, sems.at[i]) for i, (a, b) in enumerate(pairs)]
    for copy in copies:
        copy.start()
    return copies


def states_body(heads, k_hbm, v_hbm, k, v, *refs):
    outs, (state, sems) = refs[:-2], refs[-2:]
    for copy in loads(((k_hbm, k), (v_hbm, v)), sems):
        copy.wait()
    for h in range(heads):
        state[head(h), :] = dot(k[:, head(h)], v[:, head(h)], TN)
    give(state, outs)


def scan_body(count, reverse, arrived, sums):
    running = jnp.zeros(arrived.shape[1:], F32)
    for place in range(count - 1, -1, -1) if reverse else range(count):
        sums[place] = running
        running = running + arrived[place]


def lead_body(*refs):
    arrived, total, outs, passed = refs[:4], refs[4], refs[5:9], refs[9]
    back, running = sums_in_half(arrived, False)
    total[...] = running
    for out, part in zip(outs, back):
        out[...] = part
    passed[...] = arrived[3][...]


def late_body(*refs):
    arrived, over, outs = refs[:4], refs[4], refs[5:]
    for out, part in zip(outs, sums_in_half(arrived, True)[0]):
        out[...] = part + over[...]


def back_lead_body(*refs):
    arrived, total, outs, sums = refs[:4], refs[4], refs[5:9], refs[9]
    place = lax.rem(lax.axis_index("ctx"), 4)
    for piece, step in zip(arrived, BACK_STEPS):
        quarter(sums, lax.bitwise_xor(place, step))[...] = piece[...]
    rows = total.shape[0]
    running = jnp.zeros(total.shape, F32)
    for block in range(3, -1, -1):
        own = slice(block * rows, (block + 1) * rows)
        here = sums[own, :]
        sums[own, :] = running
        running = running + here
    total[...] = running
    give_quarters(sums, outs)


def back_add_body(sums, over, *outs):
    give_quarters(sums, outs)
    for out in outs:
        out[...] += over[...]


def pick(pieces, state):
    if len(pieces) == 1:
        state[...] = pieces[0][...].reshape(state.shape)
        return
    me = lax.axis_index("ctx")
    early, first = me < 4, lax.rem(me, 2) == 0
    inner = lax.rem(lax.div(me + 2, 4), 2) == 1
    diagonal, across, along, own = (
        jnp.where(early, a[...], b[...]) for a, b in zip(pieces[:4], pieces[4:])
    )
    mine = jnp.where(inner, own, along)
    other = jnp.where(inner, across, diagonal)
    rows = state.shape[0] // 2
    state[:rows, :] = jnp.where(first, mine, other)
    state[rows:, :] = jnp.where(first, other, mine)


def pick_quarters(pieces, state):
    if len(pieces) == 1:
        state[...] = pieces[0][...].reshape(state.shape)
        return
    me = lax.axis_index("ctx")
    for i, step in enumerate(BACK_STEPS):
        rows = quarter(state, lax.bitwise_xor(lax.rem(me, 4), step))
        rows[...] = jnp.where(me < 4, pieces[i][...], pieces[4 + i][...])


def scores_body(heads, factor, k, v, q_hbm, og_hbm, gain_hbm, scores, attended, q, weighted, gain, og, sems):
    copies = loads(((q_hbm, q), (og_hbm, og), (gain_hbm, gain)), sems)
    copies[0].wait()
    causal = causal_mask(q.shape[0])
    for h in range(heads):
        raw = dot(q[:, head(h)], k[:, head(h)], NT) * factor
        sc = jnp.where(causal, raw, 0.0).astype(BF16)
        scores[h] = sc
        attended[:, head(h)] = dot(sc, v[:, head(h)], NN)
    for copy in copies[1:]:
        copy.wait()
    for h in range(heads):
        weighted[:, head(h)] = og[:, head(h)].astype(F32) * gain[h : h + 1, :]


def attend_body(heads, factor, q, weighted, local, *refs):
    pieces, (attended, stats, prefix) = refs[:-3], refs[-3:]
    pick(pieces, prefix)
    power = 0.0
    inner = 0.0
    for h in range(heads):
        att = factor * dot(q[:, head(h)], prefix[head(h), :].astype(BF16), NN) + local[:, head(h)]
        attended[:, head(h)] = att
        power = power + att * att
        inner = inner + weighted[:, head(h)] * att
    stats[0:1, :] = jnp.sum(power.T, axis=0, keepdims=True)
    stats[1:2, :] = jnp.sum(inner.T, axis=0, keepdims=True)


def grad_body(heads, features, ways, attended, weighted, q, *refs):
    stats, (spread, grad), outs, updates = refs[:ways], refs[ways : ways + 2], refs[ways + 2 : -1], refs[-1]
    total = stats[0][...]
    for other in stats[1:]:
        total = total + other[...]
    inv_rms = lax.rsqrt(total[0:1, :] / features + epsilon)
    bend = inv_rms * inv_rms * (total[1:2, :] / features)
    tokens = q.shape[0]
    inv_rms = jnp.broadcast_to(inv_rms, (HEAD, tokens)).T
    bend = jnp.broadcast_to(bend, (HEAD, tokens)).T
    spread[...] = inv_rms
    for h in range(heads):
        ga = (inv_rms * (weighted[:, head(h)] - attended[:, head(h)] * bend)).astype(BF16)
        grad[:, head(h)] = ga
        updates[head(h), :] = dot(q[:, head(h)], ga, TN)
    give_quarters(updates, outs)


def local_body(heads, factor, ga, q, k, v, prefix, scores, attended, inv_rms, gain, normed, gq, gk_part, gv_part):
    causal = causal_mask(q.shape[0])
    for h in range(heads):
        normed[:, head(h)] = (attended[:, head(h)] * inv_rms[...] * gain[h : h + 1, :]).astype(BF16)
        gah = ga[:, head(h)]
        raw = dot(gah, v[:, head(h)], NT) * factor
        gs = jnp.where(causal, raw, 0.0).astype(BF16)
        out = factor * dot(gah, prefix[head(h), :].astype(BF16), NT)
        gq[:, head(h)] = (out + dot(gs, k[:, head(h)], NN)).astype(BF16)
        gk_part[:, head(h)] = dot(gs, q[:, head(h)], TN)
        gv_part[:, head(h)] = dot(scores[h], gah, TN)


def final_body(heads, factor, k, v, gk_part, gv_part, *refs):
    pieces, outs, (suffix, gk, gv, sems) = refs[:-6], refs[-6:-4], refs[-4:]
    pick_quarters(pieces, suffix)
    copies = []

    def send(h, held, out):
        copy = pltpu.make_async_copy(held.at[:, head(h)], out.at[:, head(h)], sems.at[len(copies)])
        copy.start()
        copies.append(copy)

    for h in range(heads):
        suf = suffix[head(h), :].astype(BF16)
        gk[:, head(h)] = (factor * dot(v[:, head(h)], suf, NT) + gk_part[:, head(h)]).astype(BF16)
        send(h, gk, outs[0])
        gv[:, head(h)] = (factor * dot(k[:, head(h)], suf, NN) + gv_part[:, head(h)]).astype(BF16)
        send(h, gv, outs[1])
    for copy in copies:
        copy.wait()


def permuted(piece, target):
    ways = lax.axis_size("tp")
    pairs = []
    for j in range(8):
        to, swap = target(j)
        pairs += [(j * ways + t, to * ways + (t ^ swap)) for t in range(ways)]
    return lax.ppermute(piece, ("ctx", "tp"), pairs)


def exchange(pieces, half, gather):
    def target(j, step):
        inner = j // 2 in (1, 2)
        if j // 4 != half or (step == 1 and not inner):
            return j, 1
        return (j ^ 2 if step == 3 and inner == gather else j ^ step), 1

    return [
        permuted(piece, functools.partial(target, step=step))
        for piece, step in zip(pieces, GATHER_STEPS if gather else STEPS)
    ]


def back_exchange(pieces, halves_in):
    return [
        permuted(piece, lambda j, step=step: (j ^ step if j // 4 in halves_in else j, 1))
        for piece, step in zip(pieces, BACK_STEPS)
    ]


def over_all(pieces, reverse):
    count = lax.axis_size("ctx")
    arrived = lax.all_to_all(pieces[0], "ctx", 0, 0, tiled=True)
    sums = call(
        functools.partial(scan_body, count, reverse),
        jax.ShapeDtypeStruct(arrived.shape, F32),
        arrived,
    )
    return [lax.all_to_all(sums, "ctx", 0, 0, tiled=True)]


def earlier_sums(pieces):
    if len(pieces) == 1:
        return over_all(pieces, False)
    piece = jax.ShapeDtypeStruct(pieces[0].shape, F32)
    arrived = exchange(pieces[:3], 0, True)
    own = permuted(pieces[3], lambda j: (j, 1))
    total, *back = call(lead_body, [piece] * 6, *arrived, own)
    over = permuted(total, lambda j: (j ^ 6, 0) if j // 2 in (1, 2) else (j, 1))
    ahead = exchange(back[:4], 0, False)
    arrived = exchange(pieces[4:7], 1, True)
    back = call(late_body, [piece] * 4, *arrived, back[4], over)
    return ahead + exchange(back, 1, False)


def later_sums(pieces):
    if len(pieces) == 1:
        return over_all(pieces, True)
    rows, width = pieces[0].shape
    piece = jax.ShapeDtypeStruct((rows, width), F32)
    arrived = back_exchange(pieces, (0, 1))
    total, *back, sums = call(
        back_lead_body, [piece] * 5 + [jax.ShapeDtypeStruct((4 * rows, width), F32)], *arrived
    )
    over = permuted(total, lambda j: (j ^ 4, 0))
    ahead = back_exchange(back, (1,))
    back = call(back_add_body, [piece] * 4, sums, over)
    return back_exchange(back, (0,)) + ahead


def from_all(part, axis):
    count = lax.axis_size(axis)
    even = count & (count - 1) == 0
    steps = [1, 3, 2] if count == 4 else range(1, count)
    return [part] + [
        lax.ppermute(part, axis, [(i, i ^ step if even else (i + step) % count) for i in range(count)])
        for step in steps
    ]


def on_device(queries, keys, values, gain, out_grad):
    tokens, width = queries.shape
    heads = width // HEAD
    count = lax.axis_size("ctx")
    factor = (HEAD * tokens * count) ** (-0.5)
    features = width * lax.axis_size("tp")
    gains = gain.reshape(heads, HEAD)
    sds = jax.ShapeDtypeStruct
    wide = sds((tokens, width), F32)
    half = sds((tokens, width), BF16)
    state = pltpu.VMEM((width, HEAD), F32)
    if count == 8 and lax.axis_size("tp") % 2 == 0:
        pieces = [sds((width // 2, HEAD), F32)] * 7
        quarters = [sds((width // 4, HEAD), F32)] * 4
    else:
        pieces = quarters = [sds((count, width // count, HEAD), F32)]

    def in_hbm(*arrays):
        return [pltpu.with_memory_space_constraint(array, pltpu.HBM) for array in arrays]

    def in_vmem(array):
        return pltpu.VMEM(array.shape, array.dtype)

    k_held, v_held, *states = call(
        functools.partial(states_body, heads),
        (in_vmem(keys), in_vmem(values), *pieces),
        *in_hbm(keys, values),
        ins=[HBM, HBM],
        scratch=[state, pltpu.SemaphoreType.DMA((2,))],
    )
    prefix = earlier_sums(states)
    pairs = heads * tokens * tokens * HEAD
    scores, local, q_held, weighted, gain_held = call(
        functools.partial(scores_body, heads, factor),
        (
            sds((heads, tokens, tokens), BF16), wide,
            in_vmem(queries), in_vmem(wide), in_vmem(gains),
        ),
        k_held, v_held, *in_hbm(queries, out_grad, gains),
        ins=[VMEM, VMEM, HBM, HBM, HBM],
        scratch=[in_vmem(out_grad), pltpu.SemaphoreType.DMA((3,))],
        flops=4 * pairs,
    )
    attended, stats, prefix = call(
        functools.partial(attend_body, heads, factor),
        (wide, sds((2, tokens), F32), sds((width, HEAD), F32)),
        q_held, weighted, local, *prefix,
    )
    every = from_all(stats, "tp")
    inv_rms, grad_attn, *updates = call(
        functools.partial(grad_body, heads, features, len(every)),
        (pltpu.VMEM((tokens, HEAD), F32), half, *quarters),
        attended, weighted, q_held, *every,
        scratch=[state],
    )
    suffix = later_sums(updates)
    normed, grad_q, gk_part, gv_part = call(
        functools.partial(local_body, heads, factor),
        (half, half, wide, wide),
        grad_attn, q_held, k_held, v_held, prefix, scores, attended, inv_rms, gain_held,
        flops=9 * pairs,
    )
    held = pltpu.VMEM((tokens, width), BF16)
    grad_k, grad_v = call(
        functools.partial(final_body, heads, factor),
        (half, half),
        k_held, v_held, gk_part, gv_part, *suffix,
        dests=(HBM, HBM),
        scratch=[state, held, held, pltpu.SemaphoreType.DMA((2 * heads,))],
    )
    return normed, grad_q, grad_k, grad_v


def solution(mesh):
    placed = (P("ctx", "tp"), P("ctx", "tp"), P("ctx", "tp"), P("tp"), P("ctx", "tp"))
    return jax.shard_map(
        on_device,
        mesh=mesh,
        in_specs=placed,
        out_specs=(P("ctx", "tp"), P("ctx", "tp"), P("ctx", "tp"), P("ctx", "tp")),
        check_vma=False,
    )
```

```python
import functools

import jax
import jax.numpy as jnp
from jax import lax
from jax.experimental import pallas as pl
from jax.experimental.pallas import tpu as pltpu
from jax.sharding import PartitionSpec as P

HEAD = 128

epsilon = 1e-06
ALONE = (0, 2)
SHARED = (1, 3)
F32 = jnp.float32
BF16 = jnp.bfloat16

NN = (((1,), (0,)), ((), ()))
NT = (((1,), (1,)), ((), ()))
TN = (((0,), (0,)), ((), ()))


def dot(a, b, dims):
    return lax.dot_general(a, b, dims, preferred_element_type=F32)


VMEM = pl.BlockSpec(memory_space=pltpu.VMEM)
HBM = pl.BlockSpec(memory_space=pltpu.HBM)


def call(body, outs, *args, ins=None, dests=None, scratch=(), flops=1e7):
    moved = sum(a.size * a.dtype.itemsize for a in args)
    return pl.pallas_call(
        body,
        out_shape=outs,
        in_specs=ins or [VMEM] * len(args),
        out_specs=dests or jax.tree.map(lambda _: VMEM, outs),
        scratch_shapes=scratch,
        compiler_params=pltpu.CompilerParams(vmem_limit_bytes=16 * 1024 * 1024),
        cost_estimate=pl.CostEstimate(flops=int(flops), bytes_accessed=int(moved), transcendentals=0),
    )(*args)


def head(h):
    return slice(h * HEAD, (h + 1) * HEAD)


def causal_mask(tokens):
    row = lax.broadcasted_iota(jnp.int32, (tokens, tokens), 0)
    col = lax.broadcasted_iota(jnp.int32, (tokens, tokens), 1)
    return row >= col


def rows_of(scratch, parts, place):
    rows = scratch.shape[0] // parts
    return scratch.at[pl.ds(pl.multiple_of(place * rows, rows), rows), :]


def step_of(i, odd):
    return (3, 2 - odd, 1 + odd, 0)[i]


def give(scratch, group, outs):
    if len(outs) == 1:
        outs[0][...] = scratch[...].reshape(outs[0].shape)
        return
    place = lax.rem(lax.axis_index("ctx"), group)
    odd = lax.rem(lax.axis_index("tp"), 2)
    for i, out in enumerate(outs):
        out[...] = rows_of(scratch, group, lax.bitwise_xor(place, step_of(i, odd)))[...]


def take(ins, scratch, group):
    if len(ins) == 1:
        scratch[...] = ins[0][...].reshape(scratch.shape)
        return
    place = lax.rem(lax.axis_index("ctx"), group)
    odd = 1 - lax.rem(lax.axis_index("tp"), 2)
    for i, piece in enumerate(ins):
        rows_of(scratch, group, lax.bitwise_xor(place, step_of(i, odd)))[...] = piece[...]


def running_sums(scratch, parts, reverse):
    rows = scratch.shape[0] // parts
    running = jnp.zeros((rows, scratch.shape[1]), F32)
    for place in range(parts - 1, -1, -1) if reverse else range(parts):
        own = slice(place * rows, (place + 1) * rows)
        here = scratch[own, :]
        scratch[own, :] = running
        running = running + here
    return running


def loads(pairs, sems):
    copies = [pltpu.make_async_copy(a, b, sems.at[i]) for i, (a, b) in enumerate(pairs)]
    for copy in copies:
        copy.start()
    return copies


def states_body(heads, group, k_hbm, v_hbm, k, v, *refs):
    outs, (state, sems) = refs[:-2], refs[-2:]
    for copy in loads(((k_hbm, k), (v_hbm, v)), sems):
        copy.wait()
    for h in range(heads):
        state[head(h), :] = dot(k[:, head(h)], v[:, head(h)], TN)
    give(state, group, outs[:group])
    for again, i in zip(outs[group:], ALONE):
        again[...] = outs[i][...]


def scan_body(count, reverse, arrived, sums, scratch):
    take([arrived], scratch, count)
    running_sums(scratch, count, reverse)
    give(scratch, count, [sums])


def inner_body(group, reverse, *refs):
    arrived, total, outs, sums = refs[:group], refs[group], refs[group + 1 : 2 * group + 1], refs[-1]
    take(arrived, sums, group)
    total[...] = running_sums(sums, group, reverse)
    give(sums, group, outs)
    if not reverse:
        for passed, i in zip(refs[2 * group + 1 : -1], SHARED):
            passed[...] = arrived[i][...]


def add_body(group, sums, over, *outs):
    place = lax.rem(lax.axis_index("ctx"), group)
    odd = lax.rem(lax.axis_index("tp"), 2)
    for i, out in enumerate(outs):
        out[...] = rows_of(sums, group, lax.bitwise_xor(place, step_of(i, odd)))[...] + over[...]


def late_body(group, reverse, *refs):
    arrived, over, outs, sums = refs[:group], refs[group], refs[group + 1 : -1], refs[-1]
    take(arrived, sums, group)
    running_sums(sums, group, reverse)
    add_body(group, sums, over, *outs)


def pick(pieces, scratch, group):
    many = len(pieces) // 2
    if many == 0:
        take(pieces, scratch, group)
        return
    early = lax.axis_index("ctx") < group
    place = lax.rem(lax.axis_index("ctx"), group)
    odd = 1 - lax.rem(lax.axis_index("tp"), 2)
    for i in range(many):
        rows = rows_of(scratch, group, lax.bitwise_xor(place, step_of(i, odd)))
        rows[...] = jnp.where(early, pieces[i][...], pieces[many + i][...])


def scores_body(heads, factor, k, v, q_hbm, og_hbm, gain_hbm, scores, attended, q, weighted, gain, og, sems):
    copies = loads(((q_hbm, q), (og_hbm, og), (gain_hbm, gain)), sems)
    copies[0].wait()
    causal = causal_mask(q.shape[0])
    for h in range(heads):
        raw = dot(q[:, head(h)], k[:, head(h)], NT) * factor
        sc = jnp.where(causal, raw, 0.0).astype(BF16)
        scores[h] = sc
        attended[:, head(h)] = dot(sc, v[:, head(h)], NN)
    for copy in copies[1:]:
        copy.wait()
    for h in range(heads):
        weighted[:, head(h)] = og[:, head(h)].astype(F32) * gain[h : h + 1, :]


def attend_body(heads, factor, group, q, weighted, local, *refs):
    pieces, (attended, stats, prefix) = refs[:-3], refs[-3:]
    pick(pieces, prefix, group)
    power = 0.0
    inner = 0.0
    for h in range(heads):
        att = factor * dot(q[:, head(h)], prefix[head(h), :].astype(BF16), NN) + local[:, head(h)]
        attended[:, head(h)] = att
        power = power + att * att
        inner = inner + weighted[:, head(h)] * att
    stats[0:1, :] = jnp.sum(power.T, axis=0, keepdims=True)
    stats[1:2, :] = jnp.sum(inner.T, axis=0, keepdims=True)


def grad_body(heads, features, group, ways, attended, weighted, q, *refs):
    stats, (spread, grad), outs, updates = refs[:ways], refs[ways : ways + 2], refs[ways + 2 : -1], refs[-1]
    total = stats[0][...]
    for other in stats[1:]:
        total = total + other[...]
    inv_rms = lax.rsqrt(total[0:1, :] / features + epsilon)
    bend = inv_rms * inv_rms * (total[1:2, :] / features)
    tokens = q.shape[0]
    inv_rms = jnp.broadcast_to(inv_rms, (HEAD, tokens)).T
    bend = jnp.broadcast_to(bend, (HEAD, tokens)).T
    spread[...] = inv_rms
    for h in range(heads):
        ga = (inv_rms * (weighted[:, head(h)] - attended[:, head(h)] * bend)).astype(BF16)
        grad[:, head(h)] = ga
        updates[head(h), :] = dot(q[:, head(h)], ga, TN)
    give(updates, group, outs)


def local_body(heads, factor, ga, q, k, v, prefix, scores, attended, inv_rms, gain, normed, gq, gk_part, gv_part):
    causal = causal_mask(q.shape[0])
    for h in range(heads):
        normed[:, head(h)] = (attended[:, head(h)] * inv_rms[...] * gain[h : h + 1, :]).astype(BF16)
        gah = ga[:, head(h)]
        raw = dot(gah, v[:, head(h)], NT) * factor
        gs = jnp.where(causal, raw, 0.0).astype(BF16)
        out = factor * dot(gah, prefix[head(h), :].astype(BF16), NT)
        gq[:, head(h)] = (out + dot(gs, k[:, head(h)], NN)).astype(BF16)
        gk_part[:, head(h)] = dot(gs, q[:, head(h)], TN)
        gv_part[:, head(h)] = dot(scores[h], gah, TN)


def final_body(heads, factor, group, k, v, gk_part, gv_part, *refs):
    pieces, outs, (suffix, gk, gv, sems) = refs[:-6], refs[-6:-4], refs[-4:]
    pick(pieces, suffix, group)
    copies = []

    def send(h, held, out):
        copy = pltpu.make_async_copy(held.at[:, head(h)], out.at[:, head(h)], sems.at[len(copies)])
        copy.start()
        copies.append(copy)

    for h in range(heads):
        suf = suffix[head(h), :].astype(BF16)
        gk[:, head(h)] = (factor * dot(v[:, head(h)], suf, NT) + gk_part[:, head(h)]).astype(BF16)
        send(h, gk, outs[0])
        gv[:, head(h)] = (factor * dot(k[:, head(h)], suf, NN) + gv_part[:, head(h)]).astype(BF16)
        send(h, gv, outs[1])
    for copy in copies:
        copy.wait()


def exchange(piece, i, active, group):
    ways = lax.axis_size("tp")
    pairs = [
        (j * ways + t, (j ^ step_of(i, t % 2) if j in active else j) * ways + (t ^ 1))
        for j in range(2 * group)
        for t in range(ways)
    ]
    return lax.ppermute(piece, ("ctx", "tp"), pairs)


def carried_in(pieces, reverse, state):
    again = () if reverse or len(pieces) == 1 else pieces[-len(ALONE) :]
    group = len(pieces) - len(again)
    pieces = pieces[:group]
    count = lax.axis_size("ctx")
    sds = jax.ShapeDtypeStruct
    if group == 1:
        arrived = lax.all_to_all(pieces[0], "ctx", 0, 0, tiled=True)
        sums = call(
            functools.partial(scan_body, count, reverse),
            sds(arrived.shape, F32), arrived, scratch=[state],
        )
        return [lax.all_to_all(sums, "ctx", 0, 0, tiled=True)]
    rows, width = pieces[0].shape
    piece = sds((rows, width), F32)
    early, late, both = range(group), range(group, count), range(count)
    first, second = (late, early) if reverse else (early, late)
    everyone = range(group)
    arrived = [
        exchange(pieces[i], i, both if reverse or i in SHARED else first, group) for i in everyone
    ]
    kept = [sds((group * rows, width), F32)] if reverse else [piece] * len(SHARED)
    total, *back = call(
        functools.partial(inner_body, group, reverse),
        [piece] * (group + 1) + kept,
        *arrived,
        scratch=[] if reverse else [state],
    )
    over = lax.ppermute(total, "ctx", [(j, j ^ group) for j in both])
    ahead = [exchange(back[i], i, first, group) for i in everyone]
    if reverse:
        back = call(functools.partial(add_body, group), [piece] * group, back[group], over)
    else:
        own = [exchange(part, i, second, group) for part, i in zip(again, ALONE)]
        mixed = [own[ALONE.index(i)] if i in ALONE else back[group + SHARED.index(i)] for i in everyone]
        back = call(
            functools.partial(late_body, group, reverse),
            [piece] * group, *mixed, over, scratch=[state],
        )
    behind = [exchange(back[i], i, second, group) for i in everyone]
    return [*behind, *ahead] if reverse else [*ahead, *behind]


def from_all(part, axis):
    count = lax.axis_size(axis)
    even = count & (count - 1) == 0
    steps = [1, 3, 2] if count == 4 else range(1, count)
    return [part] + [
        lax.ppermute(part, axis, [(i, i ^ step if even else (i + step) % count) for i in range(count)])
        for step in steps
    ]


def on_device(queries, keys, values, gain, out_grad):
    tokens, width = queries.shape
    heads = width // HEAD
    count = lax.axis_size("ctx")
    factor = (HEAD * tokens * count) ** (-0.5)
    features = width * lax.axis_size("tp")
    gains = gain.reshape(heads, HEAD)
    sds = jax.ShapeDtypeStruct
    wide = sds((tokens, width), F32)
    half = sds((tokens, width), BF16)
    state = pltpu.VMEM((width, HEAD), F32)
    if count == 8 and lax.axis_size("tp") % 2 == 0:
        group = count // 2
        pieces = [sds((width // group, HEAD), F32)] * group
    else:
        group = count
        pieces = [sds((count, width // count, HEAD), F32)]

    def in_hbm(*arrays):
        return [pltpu.with_memory_space_constraint(array, pltpu.HBM) for array in arrays]

    def in_vmem(array):
        return pltpu.VMEM(array.shape, array.dtype)

    k_held, v_held, *states = call(
        functools.partial(states_body, heads, group),
        (in_vmem(keys), in_vmem(values), *pieces, *(pieces[i] for i in ALONE if len(pieces) > 1)),
        *in_hbm(keys, values),
        ins=[HBM, HBM],
        scratch=[state, pltpu.SemaphoreType.DMA((2,))],
    )
    prefix = carried_in(states, False, state)
    pairs = heads * tokens * tokens * HEAD
    scores, local, q_held, weighted, gain_held = call(
        functools.partial(scores_body, heads, factor),
        (
            sds((heads, tokens, tokens), BF16), wide,
            in_vmem(queries), in_vmem(wide), in_vmem(gains),
        ),
        k_held, v_held, *in_hbm(queries, out_grad, gains),
        ins=[VMEM, VMEM, HBM, HBM, HBM],
        scratch=[in_vmem(out_grad), pltpu.SemaphoreType.DMA((3,))],
        flops=4 * pairs,
    )
    attended, stats, prefix = call(
        functools.partial(attend_body, heads, factor, group),
        (wide, sds((2, tokens), F32), sds((width, HEAD), F32)),
        q_held, weighted, local, *prefix,
    )
    every = from_all(stats, "tp")
    inv_rms, grad_attn, *updates = call(
        functools.partial(grad_body, heads, features, group, len(every)),
        (pltpu.VMEM((tokens, HEAD), F32), half, *pieces),
        attended, weighted, q_held, *every,
        scratch=[state],
    )
    suffix = carried_in(updates, True, state)
    normed, grad_q, gk_part, gv_part = call(
        functools.partial(local_body, heads, factor),
        (half, half, wide, wide),
        grad_attn, q_held, k_held, v_held, prefix, scores, attended, inv_rms, gain_held,
        flops=9 * pairs,
    )
    held = pltpu.VMEM((tokens, width), BF16)
    grad_k, grad_v = call(
        functools.partial(final_body, heads, factor, group),
        (half, half),
        k_held, v_held, gk_part, gv_part, *suffix,
        dests=(HBM, HBM),
        scratch=[state, held, held, pltpu.SemaphoreType.DMA((2 * heads,))],
    )
    return normed, grad_q, grad_k, grad_v


def solution(mesh):
    placed = (P("ctx", "tp"), P("ctx", "tp"), P("ctx", "tp"), P("tp"), P("ctx", "tp"))
    return jax.shard_map(
        on_device,
        mesh=mesh,
        in_specs=placed,
        out_specs=(P("ctx", "tp"), P("ctx", "tp"), P("ctx", "tp"), P("ctx", "tp")),
        check_vma=False,
    )
```

```python
import functools

import jax
import jax.numpy as jnp
from jax import lax
from jax.experimental import pallas as pl
from jax.experimental.pallas import tpu as pltpu
from jax.sharding import PartitionSpec as P

HEAD = 128

epsilon = 1e-06
ALONE = (0, 1, 2)
SHARED = (3,)
F32 = jnp.float32
BF16 = jnp.bfloat16

NN = (((1,), (0,)), ((), ()))
NT = (((1,), (1,)), ((), ()))
TN = (((0,), (0,)), ((), ()))


def dot(a, b, dims):
    return lax.dot_general(a, b, dims, preferred_element_type=F32)


VMEM = pl.BlockSpec(memory_space=pltpu.VMEM)
HBM = pl.BlockSpec(memory_space=pltpu.HBM)


def call(body, outs, *args, ins=None, dests=None, scratch=(), flops=1e7):
    moved = sum(a.size * a.dtype.itemsize for a in args)
    return pl.pallas_call(
        body,
        out_shape=outs,
        in_specs=ins or [VMEM] * len(args),
        out_specs=dests or jax.tree.map(lambda _: VMEM, outs),
        scratch_shapes=scratch,
        compiler_params=pltpu.CompilerParams(vmem_limit_bytes=16 * 1024 * 1024),
        cost_estimate=pl.CostEstimate(flops=int(flops), bytes_accessed=int(moved), transcendentals=0),
    )(*args)


def head(h):
    return slice(h * HEAD, (h + 1) * HEAD)


def causal_mask(tokens):
    row = lax.broadcasted_iota(jnp.int32, (tokens, tokens), 0)
    col = lax.broadcasted_iota(jnp.int32, (tokens, tokens), 1)
    return row >= col


def rows_of(scratch, parts, place):
    rows = scratch.shape[0] // parts
    return scratch.at[pl.ds(pl.multiple_of(place * rows, rows), rows), :]


def step_of(i, odd):
    return (3, 2 - odd, 1 + odd, 0)[i]


def give(scratch, group, outs):
    if len(outs) == 1:
        outs[0][...] = scratch[...].reshape(outs[0].shape)
        return
    place = lax.rem(lax.axis_index("ctx"), group)
    odd = lax.rem(lax.axis_index("tp"), 2)
    for i, out in enumerate(outs):
        out[...] = rows_of(scratch, group, lax.bitwise_xor(place, step_of(i, odd)))[...]


def take(ins, scratch, group):
    if len(ins) == 1:
        scratch[...] = ins[0][...].reshape(scratch.shape)
        return
    place = lax.rem(lax.axis_index("ctx"), group)
    odd = 1 - lax.rem(lax.axis_index("tp"), 2)
    for i, piece in enumerate(ins):
        rows_of(scratch, group, lax.bitwise_xor(place, step_of(i, odd)))[...] = piece[...]


def running_sums(scratch, parts, reverse):
    rows = scratch.shape[0] // parts
    running = jnp.zeros((rows, scratch.shape[1]), F32)
    for place in range(parts - 1, -1, -1) if reverse else range(parts):
        own = slice(place * rows, (place + 1) * rows)
        here = scratch[own, :]
        scratch[own, :] = running
        running = running + here
    return running


def loads(pairs, sems):
    copies = [pltpu.make_async_copy(a, b, sems.at[i]) for i, (a, b) in enumerate(pairs)]
    for copy in copies:
        copy.start()
    return copies


def states_body(heads, group, k_hbm, v_hbm, k, v, *refs):
    outs, (state, sems) = refs[:-2], refs[-2:]
    for copy in loads(((k_hbm, k), (v_hbm, v)), sems):
        copy.wait()
    for h in range(heads):
        state[head(h), :] = dot(k[:, head(h)], v[:, head(h)], TN)
    give(state, group, outs[:group])
    for again, i in zip(outs[group:], ALONE):
        again[...] = outs[i][...]


def scan_body(count, reverse, arrived, sums, scratch):
    take([arrived], scratch, count)
    running_sums(scratch, count, reverse)
    give(scratch, count, [sums])


def inner_body(group, reverse, *refs):
    arrived, total, outs, sums = refs[:group], refs[group], refs[group + 1 : 2 * group + 1], refs[-1]
    take(arrived, sums, group)
    total[...] = running_sums(sums, group, reverse)
    give(sums, group, outs)
    if not reverse:
        for passed, i in zip(refs[2 * group + 1 : -1], SHARED):
            passed[...] = arrived[i][...]


def add_body(group, sums, over, *outs):
    place = lax.rem(lax.axis_index("ctx"), group)
    odd = lax.rem(lax.axis_index("tp"), 2)
    for i, out in enumerate(outs):
        out[...] = rows_of(sums, group, lax.bitwise_xor(place, step_of(i, odd)))[...] + over[...]


def late_body(group, reverse, *refs):
    arrived, over, outs, sums = refs[:group], refs[group], refs[group + 1 : -1], refs[-1]
    take(arrived, sums, group)
    running_sums(sums, group, reverse)
    add_body(group, sums, over, *outs)


def pick(pieces, scratch, group):
    many = len(pieces) // 2
    if many == 0:
        take(pieces, scratch, group)
        return
    early = lax.axis_index("ctx") < group
    place = lax.rem(lax.axis_index("ctx"), group)
    odd = 1 - lax.rem(lax.axis_index("tp"), 2)
    for i in range(many):
        rows = rows_of(scratch, group, lax.bitwise_xor(place, step_of(i, odd)))
        rows[...] = jnp.where(early, pieces[i][...], pieces[many + i][...])


def scores_body(heads, factor, k, v, q_hbm, og_hbm, gain_hbm, scores, attended, q, weighted, gain, og, sems):
    copies = loads(((q_hbm, q), (og_hbm, og), (gain_hbm, gain)), sems)
    copies[0].wait()
    causal = causal_mask(q.shape[0])
    for h in range(heads):
        raw = dot(q[:, head(h)], k[:, head(h)], NT) * factor
        sc = jnp.where(causal, raw, 0.0).astype(BF16)
        scores[h] = sc
        attended[:, head(h)] = dot(sc, v[:, head(h)], NN)
    for copy in copies[1:]:
        copy.wait()
    for h in range(heads):
        weighted[:, head(h)] = og[:, head(h)].astype(F32) * gain[h : h + 1, :]


def attend_body(heads, factor, group, q, weighted, local, *refs):
    pieces, (attended, stats, prefix) = refs[:-3], refs[-3:]
    pick(pieces, prefix, group)
    power = 0.0
    inner = 0.0
    for h in range(heads):
        att = factor * dot(q[:, head(h)], prefix[head(h), :].astype(BF16), NN) + local[:, head(h)]
        attended[:, head(h)] = att
        power = power + att * att
        inner = inner + weighted[:, head(h)] * att
    stats[0:1, :] = jnp.sum(power.T, axis=0, keepdims=True)
    stats[1:2, :] = jnp.sum(inner.T, axis=0, keepdims=True)


def grad_body(heads, features, group, ways, attended, weighted, q, *refs):
    stats, (spread, grad), outs, updates = refs[:ways], refs[ways : ways + 2], refs[ways + 2 : -1], refs[-1]
    total = stats[0][...]
    for other in stats[1:]:
        total = total + other[...]
    inv_rms = lax.rsqrt(total[0:1, :] / features + epsilon)
    bend = inv_rms * inv_rms * (total[1:2, :] / features)
    tokens = q.shape[0]
    inv_rms = jnp.broadcast_to(inv_rms, (HEAD, tokens)).T
    bend = jnp.broadcast_to(bend, (HEAD, tokens)).T
    spread[...] = inv_rms
    for h in range(heads):
        ga = (inv_rms * (weighted[:, head(h)] - attended[:, head(h)] * bend)).astype(BF16)
        grad[:, head(h)] = ga
        updates[head(h), :] = dot(q[:, head(h)], ga, TN)
    give(updates, group, outs)


def local_body(heads, factor, ga, q, k, v, prefix, scores, attended, inv_rms, gain, normed, gq, gk_part, gv_part):
    causal = causal_mask(q.shape[0])
    for h in range(heads):
        normed[:, head(h)] = (attended[:, head(h)] * inv_rms[...] * gain[h : h + 1, :]).astype(BF16)
        gah = ga[:, head(h)]
        raw = dot(gah, v[:, head(h)], NT) * factor
        gs = jnp.where(causal, raw, 0.0).astype(BF16)
        out = factor * dot(gah, prefix[head(h), :].astype(BF16), NT)
        gq[:, head(h)] = (out + dot(gs, k[:, head(h)], NN)).astype(BF16)
        gk_part[:, head(h)] = dot(gs, q[:, head(h)], TN)
        gv_part[:, head(h)] = dot(scores[h], gah, TN)


def final_body(heads, factor, group, k, v, gk_part, gv_part, *refs):
    pieces, outs, (suffix, gk, gv, sems) = refs[:-6], refs[-6:-4], refs[-4:]
    pick(pieces, suffix, group)
    copies = []

    def send(h, held, out):
        copy = pltpu.make_async_copy(held.at[:, head(h)], out.at[:, head(h)], sems.at[len(copies)])
        copy.start()
        copies.append(copy)

    for h in range(heads):
        suf = suffix[head(h), :].astype(BF16)
        gk[:, head(h)] = (factor * dot(v[:, head(h)], suf, NT) + gk_part[:, head(h)]).astype(BF16)
        send(h, gk, outs[0])
        gv[:, head(h)] = (factor * dot(k[:, head(h)], suf, NN) + gv_part[:, head(h)]).astype(BF16)
        send(h, gv, outs[1])
    for copy in copies:
        copy.wait()


def exchange(piece, i, active, group):
    ways = lax.axis_size("tp")
    pairs = [
        (j * ways + t, (j ^ step_of(i, t % 2) if j in active else j) * ways + (t ^ 1))
        for j in range(2 * group)
        for t in range(ways)
    ]
    return lax.ppermute(piece, ("ctx", "tp"), pairs)


def carried_in(pieces, reverse, state):
    again = () if reverse or len(pieces) == 1 else pieces[-len(ALONE) :]
    group = len(pieces) - len(again)
    pieces = pieces[:group]
    count = lax.axis_size("ctx")
    sds = jax.ShapeDtypeStruct
    if group == 1:
        arrived = lax.all_to_all(pieces[0], "ctx", 0, 0, tiled=True)
        sums = call(
            functools.partial(scan_body, count, reverse),
            sds(arrived.shape, F32), arrived, scratch=[state],
        )
        return [lax.all_to_all(sums, "ctx", 0, 0, tiled=True)]
    rows, width = pieces[0].shape
    piece = sds((rows, width), F32)
    early, late, both = range(group), range(group, count), range(count)
    first, second = (late, early) if reverse else (early, late)
    everyone = range(group)
    arrived = [
        exchange(pieces[i], i, both if reverse or i in SHARED else first, group) for i in everyone
    ]
    kept = [sds((group * rows, width), F32)] if reverse else [piece] * len(SHARED)
    total, *back = call(
        functools.partial(inner_body, group, reverse),
        [piece] * (group + 1) + kept,
        *arrived,
        scratch=[] if reverse else [state],
    )
    over = lax.ppermute(total, "ctx", [(j, j ^ group) for j in both])
    ahead = [exchange(back[i], i, first, group) for i in everyone]
    if reverse:
        back = call(functools.partial(add_body, group), [piece] * group, back[group], over)
    else:
        own = [exchange(part, i, second, group) for part, i in zip(again, ALONE)]
        mixed = [own[ALONE.index(i)] if i in ALONE else back[group + SHARED.index(i)] for i in everyone]
        back = call(
            functools.partial(late_body, group, reverse),
            [piece] * group, *mixed, over, scratch=[state],
        )
    behind = [exchange(back[i], i, second, group) for i in everyone]
    return [*behind, *ahead] if reverse else [*ahead, *behind]


def from_all(part, axis):
    count = lax.axis_size(axis)
    even = count & (count - 1) == 0
    steps = [1, 3, 2] if count == 4 else range(1, count)
    return [part] + [
        lax.ppermute(part, axis, [(i, i ^ step if even else (i + step) % count) for i in range(count)])
        for step in steps
    ]


def on_device(queries, keys, values, gain, out_grad):
    tokens, width = queries.shape
    heads = width // HEAD
    count = lax.axis_size("ctx")
    factor = (HEAD * tokens * count) ** (-0.5)
    features = width * lax.axis_size("tp")
    gains = gain.reshape(heads, HEAD)
    sds = jax.ShapeDtypeStruct
    wide = sds((tokens, width), F32)
    half = sds((tokens, width), BF16)
    state = pltpu.VMEM((width, HEAD), F32)
    if count == 8 and lax.axis_size("tp") % 2 == 0:
        group = count // 2
        pieces = [sds((width // group, HEAD), F32)] * group
    else:
        group = count
        pieces = [sds((count, width // count, HEAD), F32)]

    def in_hbm(*arrays):
        return [pltpu.with_memory_space_constraint(array, pltpu.HBM) for array in arrays]

    def in_vmem(array):
        return pltpu.VMEM(array.shape, array.dtype)

    k_held, v_held, *states = call(
        functools.partial(states_body, heads, group),
        (in_vmem(keys), in_vmem(values), *pieces, *(pieces[i] for i in ALONE if len(pieces) > 1)),
        *in_hbm(keys, values),
        ins=[HBM, HBM],
        scratch=[state, pltpu.SemaphoreType.DMA((2,))],
    )
    prefix = carried_in(states, False, state)
    pairs = heads * tokens * tokens * HEAD
    scores, local, q_held, weighted, gain_held = call(
        functools.partial(scores_body, heads, factor),
        (
            sds((heads, tokens, tokens), BF16), wide,
            in_vmem(queries), in_vmem(wide), in_vmem(gains),
        ),
        k_held, v_held, *in_hbm(queries, out_grad, gains),
        ins=[VMEM, VMEM, HBM, HBM, HBM],
        scratch=[in_vmem(out_grad), pltpu.SemaphoreType.DMA((3,))],
        flops=4 * pairs,
    )
    attended, stats, prefix = call(
        functools.partial(attend_body, heads, factor, group),
        (wide, sds((2, tokens), F32), sds((width, HEAD), F32)),
        q_held, weighted, local, *prefix,
    )
    every = from_all(stats, "tp")
    inv_rms, grad_attn, *updates = call(
        functools.partial(grad_body, heads, features, group, len(every)),
        (pltpu.VMEM((tokens, HEAD), F32), half, *pieces),
        attended, weighted, q_held, *every,
        scratch=[state],
    )
    suffix = carried_in(updates, True, state)
    normed, grad_q, gk_part, gv_part = call(
        functools.partial(local_body, heads, factor),
        (half, half, wide, wide),
        grad_attn, q_held, k_held, v_held, prefix, scores, attended, inv_rms, gain_held,
        flops=9 * pairs,
    )
    held = pltpu.VMEM((tokens, width), BF16)
    grad_k, grad_v = call(
        functools.partial(final_body, heads, factor, group),
        (half, half),
        k_held, v_held, gk_part, gv_part, *suffix,
        dests=(HBM, HBM),
        scratch=[state, held, held, pltpu.SemaphoreType.DMA((2 * heads,))],
    )
    return normed, grad_q, grad_k, grad_v


def solution(mesh):
    placed = (P("ctx", "tp"), P("ctx", "tp"), P("ctx", "tp"), P("tp"), P("ctx", "tp"))
    return jax.shard_map(
        on_device,
        mesh=mesh,
        in_specs=placed,
        out_specs=(P("ctx", "tp"), P("ctx", "tp"), P("ctx", "tp"), P("ctx", "tp")),
        check_vma=False,
    )
```

```python
import functools

import jax
import jax.numpy as jnp
from jax import lax
from jax.experimental import pallas as pl
from jax.experimental.pallas import tpu as pltpu
from jax.sharding import PartitionSpec as P

HEAD = 128

epsilon = 1e-06
LOADS = 4
ALONE = (0, 2)
SHARED = (1, 3)
F32 = jnp.float32
BF16 = jnp.bfloat16

NN = (((1,), (0,)), ((), ()))
NT = (((1,), (1,)), ((), ()))
TN = (((0,), (0,)), ((), ()))


def dot(a, b, dims):
    return lax.dot_general(a, b, dims, preferred_element_type=F32)


VMEM = pl.BlockSpec(memory_space=pltpu.VMEM)
HBM = pl.BlockSpec(memory_space=pltpu.HBM)


def call(body, outs, *args, ins=None, dests=None, scratch=(), flops=1e7):
    moved = sum(a.size * a.dtype.itemsize for a in args)
    return pl.pallas_call(
        body,
        out_shape=outs,
        in_specs=ins or [VMEM] * len(args),
        out_specs=dests or jax.tree.map(lambda _: VMEM, outs),
        scratch_shapes=scratch,
        compiler_params=pltpu.CompilerParams(vmem_limit_bytes=16 * 1024 * 1024),
        cost_estimate=pl.CostEstimate(flops=int(flops), bytes_accessed=int(moved), transcendentals=0),
    )(*args)


def head(h):
    return slice(h * HEAD, (h + 1) * HEAD)


def causal_mask(tokens):
    row = lax.broadcasted_iota(jnp.int32, (tokens, tokens), 0)
    col = lax.broadcasted_iota(jnp.int32, (tokens, tokens), 1)
    return row >= col


def rows_of(scratch, parts, place):
    rows = scratch.shape[0] // parts
    return scratch.at[pl.ds(pl.multiple_of(place * rows, rows), rows), :]


def partner(i, group):
    return group - 1 - i


def give(scratch, group, outs):
    if len(outs) == 1:
        outs[0][...] = scratch[...].reshape(outs[0].shape)
        return
    place = lax.rem(lax.axis_index("ctx"), group)
    for i, out in enumerate(outs):
        out[...] = rows_of(scratch, group, lax.bitwise_xor(place, partner(i, group)))[...]


def take(ins, scratch, group):
    if len(ins) == 1:
        scratch[...] = ins[0][...].reshape(scratch.shape)
        return
    place = lax.rem(lax.axis_index("ctx"), group)
    for i, piece in enumerate(ins):
        rows_of(scratch, group, lax.bitwise_xor(place, partner(i, group)))[...] = piece[...]


def running_sums(scratch, parts, reverse):
    rows = scratch.shape[0] // parts
    running = jnp.zeros((rows, scratch.shape[1]), F32)
    for place in range(parts - 1, -1, -1) if reverse else range(parts):
        own = slice(place * rows, (place + 1) * rows)
        here = scratch[own, :]
        scratch[own, :] = running
        running = running + here
    return running


def loads(pairs, sems):
    copies = [pltpu.make_async_copy(a, b, sems.at[i]) for i, (a, b) in enumerate(pairs)]
    for copy in copies:
        copy.start()
    return copies


def states_body(heads, group, k_hbm, v_hbm, k, v, *refs):
    outs, (state, sems) = refs[:-2], refs[-2:]
    rows = k.shape[0] // LOADS
    blocks = [slice(i * rows, (i + 1) * rows) for i in range(LOADS)]
    for copy in loads([(a.at[r, :], b.at[r, :]) for r in blocks for a, b in ((k_hbm, k), (v_hbm, v))], sems):
        copy.wait()
    for h in range(heads):
        state[head(h), :] = dot(k[:, head(h)], v[:, head(h)], TN)
    give(state, group, outs[:group])
    for again, i in zip(outs[group:], ALONE):
        again[...] = outs[i][...]


def scan_body(count, reverse, arrived, sums, scratch):
    take([arrived], scratch, count)
    running_sums(scratch, count, reverse)
    give(scratch, count, [sums])


def inner_body(group, reverse, *refs):
    arrived, total, outs, sums = refs[:group], refs[group], refs[group + 1 : 2 * group + 1], refs[-1]
    take(arrived, sums, group)
    total[...] = running_sums(sums, group, reverse)
    give(sums, group, outs)
    if not reverse:
        for passed, i in zip(refs[2 * group + 1 : -1], SHARED):
            passed[...] = arrived[i][...]


def add_body(group, sums, over, *outs):
    place = lax.rem(lax.axis_index("ctx"), group)
    for i, out in enumerate(outs):
        out[...] = rows_of(sums, group, lax.bitwise_xor(place, partner(i, group)))[...] + over[...]


def late_body(group, reverse, *refs):
    arrived, over, outs, sums = refs[:group], refs[group], refs[group + 1 : -1], refs[-1]
    take(arrived, sums, group)
    running_sums(sums, group, reverse)
    add_body(group, sums, over, *outs)


def pick(pieces, scratch, group):
    many = len(pieces) // 2
    if many == 0:
        take(pieces, scratch, group)
        return
    early = lax.axis_index("ctx") < group
    place = lax.rem(lax.axis_index("ctx"), group)
    for i in range(many):
        rows = rows_of(scratch, group, lax.bitwise_xor(place, partner(i, group)))
        rows[...] = jnp.where(early, pieces[i][...], pieces[many + i][...])


def scores_body(heads, factor, k, v, q_hbm, og_hbm, gain_hbm, scores, attended, q, weighted, gain, og, sems):
    copies = loads(((q_hbm, q), (og_hbm, og), (gain_hbm, gain)), sems)
    copies[0].wait()
    causal = causal_mask(q.shape[0])
    for h in range(heads):
        raw = dot(q[:, head(h)], k[:, head(h)], NT) * factor
        sc = jnp.where(causal, raw, 0.0).astype(BF16)
        scores[h] = sc
        attended[:, head(h)] = dot(sc, v[:, head(h)], NN)
    for copy in copies[1:]:
        copy.wait()
    for h in range(heads):
        weighted[:, head(h)] = og[:, head(h)].astype(F32) * gain[h : h + 1, :]


def attend_body(heads, factor, group, q, weighted, local, *refs):
    pieces, (attended, stats, prefix) = refs[:-3], refs[-3:]
    pick(pieces, prefix, group)
    power = 0.0
    inner = 0.0
    for h in range(heads):
        att = factor * dot(q[:, head(h)], prefix[head(h), :].astype(BF16), NN) + local[:, head(h)]
        attended[:, head(h)] = att
        power = power + att * att
        inner = inner + weighted[:, head(h)] * att
    stats[0:1, :] = jnp.sum(power.T, axis=0, keepdims=True)
    stats[1:2, :] = jnp.sum(inner.T, axis=0, keepdims=True)


def grad_body(heads, features, group, ways, attended, weighted, q, *refs):
    stats, (spread, grad), outs, updates = refs[:ways], refs[ways : ways + 2], refs[ways + 2 : -1], refs[-1]
    total = stats[0][...]
    for other in stats[1:]:
        total = total + other[...]
    inv_rms = lax.rsqrt(total[0:1, :] / features + epsilon)
    bend = inv_rms * inv_rms * (total[1:2, :] / features)
    tokens = q.shape[0]
    inv_rms = jnp.broadcast_to(inv_rms, (HEAD, tokens)).T
    bend = jnp.broadcast_to(bend, (HEAD, tokens)).T
    spread[...] = inv_rms
    for h in range(heads):
        ga = (inv_rms * (weighted[:, head(h)] - attended[:, head(h)] * bend)).astype(BF16)
        grad[:, head(h)] = ga
        updates[head(h), :] = dot(q[:, head(h)], ga, TN)
    give(updates, group, outs)


def local_body(heads, factor, ga, q, k, v, prefix, scores, attended, inv_rms, gain, normed, gq, gk_part, gv_part):
    causal = causal_mask(q.shape[0])
    for h in range(heads):
        normed[:, head(h)] = (attended[:, head(h)] * inv_rms[...] * gain[h : h + 1, :]).astype(BF16)
        gah = ga[:, head(h)]
        raw = dot(gah, v[:, head(h)], NT) * factor
        gs = jnp.where(causal, raw, 0.0).astype(BF16)
        out = factor * dot(gah, prefix[head(h), :].astype(BF16), NT)
        gq[:, head(h)] = (out + dot(gs, k[:, head(h)], NN)).astype(BF16)
        gk_part[:, head(h)] = dot(gs, q[:, head(h)], TN)
        gv_part[:, head(h)] = dot(scores[h], gah, TN)


def final_body(heads, factor, group, k, v, gk_part, gv_part, *refs):
    pieces, outs, (suffix, gk, gv, sems) = refs[:-6], refs[-6:-4], refs[-4:]
    pick(pieces, suffix, group)
    suf = [suffix[head(h), :].astype(BF16) for h in range(heads)]
    rows = k.shape[0] // 2
    copies = []
    for block in range(2):
        own = slice(block * rows, (block + 1) * rows)
        for held, out, left, part, dims in ((gk, outs[0], v, gk_part, NT), (gv, outs[1], k, gv_part, NN)):
            for h in range(heads):
                held[own, head(h)] = (
                    factor * dot(left[own, head(h)], suf[h], dims) + part[own, head(h)]
                ).astype(BF16)
            copy = pltpu.make_async_copy(held.at[own, :], out.at[own, :], sems.at[len(copies)])
            copy.start()
            copies.append(copy)
    for copy in copies:
        copy.wait()


def exchange(piece, i, active, group):
    ways = lax.axis_size("tp")
    pairs = [
        (j * ways + t, (j ^ partner(i, group) if j in active else j) * ways + (t ^ 1))
        for j in range(2 * group)
        for t in range(ways)
    ]
    return lax.ppermute(piece, ("ctx", "tp"), pairs)


def carried_in(pieces, reverse, state):
    again = () if reverse or len(pieces) == 1 else pieces[-len(ALONE) :]
    group = len(pieces) - len(again)
    pieces = pieces[:group]
    count = lax.axis_size("ctx")
    sds = jax.ShapeDtypeStruct
    if group == 1:
        arrived = lax.all_to_all(pieces[0], "ctx", 0, 0, tiled=True)
        sums = call(
            functools.partial(scan_body, count, reverse),
            sds(arrived.shape, F32), arrived, scratch=[state],
        )
        return [lax.all_to_all(sums, "ctx", 0, 0, tiled=True)]
    rows, width = pieces[0].shape
    piece = sds((rows, width), F32)
    early, late, both = range(group), range(group, count), range(count)
    first, second = (late, early) if reverse else (early, late)
    everyone = range(group)
    arrived = [
        exchange(pieces[i], i, both if reverse or i in SHARED else first, group) for i in everyone
    ]
    kept = [sds((group * rows, width), F32)] if reverse else [piece] * len(SHARED)
    total, *back = call(
        functools.partial(inner_body, group, reverse),
        [piece] * (group + 1) + kept,
        *arrived,
        scratch=[] if reverse else [state],
    )
    over = lax.ppermute(total, "ctx", [(j, j ^ group) for j in both])
    ahead = [exchange(back[i], i, first, group) for i in everyone]
    if reverse:
        back = call(functools.partial(add_body, group), [piece] * group, back[group], over)
    else:
        own = [exchange(part, i, second, group) for part, i in zip(again, ALONE)]
        mixed = [own[ALONE.index(i)] if i in ALONE else back[group + SHARED.index(i)] for i in everyone]
        back = call(
            functools.partial(late_body, group, reverse),
            [piece] * group, *mixed, over, scratch=[state],
        )
    behind = [exchange(back[i], i, second, group) for i in everyone]
    return [*behind, *ahead] if reverse else [*ahead, *behind]


def from_all(part, axis):
    count = lax.axis_size(axis)
    even = count & (count - 1) == 0
    steps = [1, 3, 2] if count == 4 else range(1, count)
    return [part] + [
        lax.ppermute(part, axis, [(i, i ^ step if even else (i + step) % count) for i in range(count)])
        for step in steps
    ]


def on_device(queries, keys, values, gain, out_grad):
    tokens, width = queries.shape
    heads = width // HEAD
    count = lax.axis_size("ctx")
    factor = (HEAD * tokens * count) ** (-0.5)
    features = width * lax.axis_size("tp")
    gains = gain.reshape(heads, HEAD)
    sds = jax.ShapeDtypeStruct
    wide = sds((tokens, width), F32)
    half = sds((tokens, width), BF16)
    state = pltpu.VMEM((width, HEAD), F32)
    if count == 8 and lax.axis_size("tp") % 2 == 0:
        group = count // 2
        pieces = [sds((width // group, HEAD), F32)] * group
    else:
        group = count
        pieces = [sds((count, width // count, HEAD), F32)]

    def in_hbm(*arrays):
        return [pltpu.with_memory_space_constraint(array, pltpu.HBM) for array in arrays]

    def in_vmem(array):
        return pltpu.VMEM(array.shape, array.dtype)

    k_held, v_held, *states = call(
        functools.partial(states_body, heads, group),
        (in_vmem(keys), in_vmem(values), *pieces, *(pieces[i] for i in ALONE if len(pieces) > 1)),
        *in_hbm(keys, values),
        ins=[HBM, HBM],
        scratch=[state, pltpu.SemaphoreType.DMA((2 * LOADS,))],
    )
    prefix = carried_in(states, False, state)
    pairs = heads * tokens * tokens * HEAD
    scores, local, q_held, weighted, gain_held = call(
        functools.partial(scores_body, heads, factor),
        (
            sds((heads, tokens, tokens), BF16), wide,
            in_vmem(queries), in_vmem(wide), in_vmem(gains),
        ),
        k_held, v_held, *in_hbm(queries, out_grad, gains),
        ins=[VMEM, VMEM, HBM, HBM, HBM],
        scratch=[in_vmem(out_grad), pltpu.SemaphoreType.DMA((3,))],
        flops=4 * pairs,
    )
    attended, stats, prefix = call(
        functools.partial(attend_body, heads, factor, group),
        (wide, sds((2, tokens), F32), sds((width, HEAD), F32)),
        q_held, weighted, local, *prefix,
    )
    every = from_all(stats, "tp")
    inv_rms, grad_attn, *updates = call(
        functools.partial(grad_body, heads, features, group, len(every)),
        (pltpu.VMEM((tokens, HEAD), F32), half, *pieces),
        attended, weighted, q_held, *every,
        scratch=[state],
    )
    suffix = carried_in(updates, True, state)
    normed, grad_q, gk_part, gv_part = call(
        functools.partial(local_body, heads, factor),
        (half, half, wide, wide),
        grad_attn, q_held, k_held, v_held, prefix, scores, attended, inv_rms, gain_held,
        flops=9 * pairs,
    )
    held = pltpu.VMEM((tokens, width), BF16)
    grad_k, grad_v = call(
        functools.partial(final_body, heads, factor, group),
        (half, half),
        k_held, v_held, gk_part, gv_part, *suffix,
        dests=(HBM, HBM),
        scratch=[state, held, held, pltpu.SemaphoreType.DMA((4,))],
    )
    return normed, grad_q, grad_k, grad_v


def solution(mesh):
    placed = (P("ctx", "tp"), P("ctx", "tp"), P("ctx", "tp"), P("tp"), P("ctx", "tp"))
    return jax.shard_map(
        on_device,
        mesh=mesh,
        in_specs=placed,
        out_specs=(P("ctx", "tp"), P("ctx", "tp"), P("ctx", "tp"), P("ctx", "tp")),
        check_vma=False,
    )
```

```python
import functools

import jax
import jax.numpy as jnp
from jax import lax
from jax.experimental import pallas as pl
from jax.experimental.pallas import tpu as pltpu
from jax.sharding import PartitionSpec as P

HEAD = 128

epsilon = 1e-06
LOADS = 4
ALONE = (0, 2)
SHARED = (1, 3)
F32 = jnp.float32
BF16 = jnp.bfloat16

NN = (((1,), (0,)), ((), ()))
NT = (((1,), (1,)), ((), ()))
TN = (((0,), (0,)), ((), ()))


def dot(a, b, dims):
    return lax.dot_general(a, b, dims, preferred_element_type=F32)


VMEM = pl.BlockSpec(memory_space=pltpu.VMEM)
HBM = pl.BlockSpec(memory_space=pltpu.HBM)


def call(body, outs, *args, ins=None, dests=None, scratch=(), flops=1e7):
    moved = sum(a.size * a.dtype.itemsize for a in args)
    return pl.pallas_call(
        body,
        out_shape=outs,
        in_specs=ins or [VMEM] * len(args),
        out_specs=dests or jax.tree.map(lambda _: VMEM, outs),
        scratch_shapes=scratch,
        compiler_params=pltpu.CompilerParams(vmem_limit_bytes=16 * 1024 * 1024),
        cost_estimate=pl.CostEstimate(flops=int(flops), bytes_accessed=int(moved), transcendentals=0),
    )(*args)


def head(h):
    return slice(h * HEAD, (h + 1) * HEAD)


def causal_mask(tokens):
    row = lax.broadcasted_iota(jnp.int32, (tokens, tokens), 0)
    col = lax.broadcasted_iota(jnp.int32, (tokens, tokens), 1)
    return row >= col


def rows_of(scratch, parts, place):
    rows = scratch.shape[0] // parts
    return scratch.at[pl.ds(pl.multiple_of(place * rows, rows), rows), :]


def partner(i, group):
    return group - 1 - i


def give(scratch, group, outs):
    if len(outs) == 1:
        outs[0][...] = scratch[...].reshape(outs[0].shape)
        return
    place = lax.rem(lax.axis_index("ctx"), group)
    for i, out in enumerate(outs):
        out[...] = rows_of(scratch, group, lax.bitwise_xor(place, partner(i, group)))[...]


def take(ins, scratch, group):
    if len(ins) == 1:
        scratch[...] = ins[0][...].reshape(scratch.shape)
        return
    place = lax.rem(lax.axis_index("ctx"), group)
    for i, piece in enumerate(ins):
        rows_of(scratch, group, lax.bitwise_xor(place, partner(i, group)))[...] = piece[...]


def running_sums(scratch, parts, reverse):
    rows = scratch.shape[0] // parts
    running = jnp.zeros((rows, scratch.shape[1]), F32)
    for place in range(parts - 1, -1, -1) if reverse else range(parts):
        own = slice(place * rows, (place + 1) * rows)
        here = scratch[own, :]
        scratch[own, :] = running
        running = running + here
    return running


def loads(pairs, sems):
    copies = [pltpu.make_async_copy(a, b, sems.at[i]) for i, (a, b) in enumerate(pairs)]
    for copy in copies:
        copy.start()
    return copies


def states_body(heads, group, k_hbm, v_hbm, k, v, *refs):
    outs, (state, sems) = refs[:-2], refs[-2:]
    rows = k.shape[0] // LOADS
    blocks = [slice(i * rows, (i + 1) * rows) for i in range(LOADS)]
    for copy in loads([(a.at[r, :], b.at[r, :]) for r in blocks for a, b in ((k_hbm, k), (v_hbm, v))], sems):
        copy.wait()
    for h in range(heads):
        state[head(h), :] = dot(k[:, head(h)], v[:, head(h)], TN)
    give(state, group, outs[:group])
    for again, i in zip(outs[group:], ALONE):
        again[...] = outs[i][...]


def scan_body(count, reverse, arrived, sums, scratch):
    take([arrived], scratch, count)
    running_sums(scratch, count, reverse)
    give(scratch, count, [sums])


def inner_body(group, reverse, *refs):
    arrived, total, outs, sums = refs[:group], refs[group], refs[group + 1 : 2 * group + 1], refs[-1]
    take(arrived, sums, group)
    total[...] = running_sums(sums, group, reverse)
    give(sums, group, outs)
    if not reverse:
        for passed, i in zip(refs[2 * group + 1 : -1], SHARED):
            passed[...] = arrived[i][...]


def add_body(group, sums, over, *outs):
    place = lax.rem(lax.axis_index("ctx"), group)
    for i, out in enumerate(outs):
        out[...] = rows_of(sums, group, lax.bitwise_xor(place, partner(i, group)))[...] + over[...]


def late_body(group, reverse, *refs):
    arrived, over, outs, sums = refs[:group], refs[group], refs[group + 1 : -1], refs[-1]
    take(arrived, sums, group)
    running_sums(sums, group, reverse)
    add_body(group, sums, over, *outs)


def pick(pieces, scratch, group):
    many = len(pieces) // 2
    if many == 0:
        take(pieces, scratch, group)
        return
    early = lax.axis_index("ctx") < group
    place = lax.rem(lax.axis_index("ctx"), group)
    for i in range(many):
        rows = rows_of(scratch, group, lax.bitwise_xor(place, partner(i, group)))
        rows[...] = jnp.where(early, pieces[i][...], pieces[many + i][...])


def scores_body(heads, factor, k, v, q_hbm, og_hbm, gain_hbm, scores, attended, q, q_turned, weighted, gain, og, sems):
    copies = loads(((q_hbm, q), (og_hbm, og), (gain_hbm, gain)), sems)
    copies[0].wait()
    q_turned[...] = q[...].T
    causal = causal_mask(q.shape[0])
    for h in range(heads):
        raw = dot(q[:, head(h)], k[:, head(h)], NT) * factor
        sc = jnp.where(causal, raw, 0.0).astype(BF16)
        scores[h] = sc
        attended[:, head(h)] = dot(sc, v[:, head(h)], NN)
    for copy in copies[1:]:
        copy.wait()
    for h in range(heads):
        weighted[:, head(h)] = og[:, head(h)].astype(F32) * gain[h : h + 1, :]


def attend_body(heads, factor, group, q, weighted, local, *refs):
    pieces, (attended, stats, prefix) = refs[:-3], refs[-3:]
    pick(pieces, prefix, group)
    power = 0.0
    inner = 0.0
    for h in range(heads):
        att = factor * dot(q[:, head(h)], prefix[head(h), :].astype(BF16), NN) + local[:, head(h)]
        attended[:, head(h)] = att
        power = power + att * att
        inner = inner + weighted[:, head(h)] * att
    stats[0:1, :] = jnp.sum(power.T, axis=0, keepdims=True)
    stats[1:2, :] = jnp.sum(inner.T, axis=0, keepdims=True)


def grad_body(heads, features, group, ways, attended, weighted, q_turned, *refs):
    stats, (spread, grad), outs, updates = refs[:ways], refs[ways : ways + 2], refs[ways + 2 : -1], refs[-1]
    total = stats[0][...]
    for other in stats[1:]:
        total = total + other[...]
    inv_rms = lax.rsqrt(total[0:1, :] / features + epsilon)
    bend = inv_rms * inv_rms * (total[1:2, :] / features)
    tokens = q_turned.shape[1]
    inv_rms = jnp.broadcast_to(inv_rms, (HEAD, tokens)).T
    bend = jnp.broadcast_to(bend, (HEAD, tokens)).T
    spread[...] = inv_rms
    for h in range(heads):
        ga = (inv_rms * (weighted[:, head(h)] - attended[:, head(h)] * bend)).astype(BF16)
        grad[:, head(h)] = ga
        updates[head(h), :] = dot(q_turned[head(h), :], ga, NN)
    give(updates, group, outs)


def local_body(heads, factor, ga, q, k, v, prefix, scores, attended, inv_rms, gain, normed, gq, gk_part, gv_part):
    causal = causal_mask(q.shape[0])
    for h in range(heads):
        normed[:, head(h)] = (attended[:, head(h)] * inv_rms[...] * gain[h : h + 1, :]).astype(BF16)
        gah = ga[:, head(h)]
        raw = dot(gah, v[:, head(h)], NT) * factor
        gs = jnp.where(causal, raw, 0.0).astype(BF16)
        out = factor * dot(gah, prefix[head(h), :].astype(BF16), NT)
        gq[:, head(h)] = (out + dot(gs, k[:, head(h)], NN)).astype(BF16)
        gk_part[:, head(h)] = dot(gs, q[:, head(h)], TN)
        gv_part[:, head(h)] = dot(scores[h], gah, TN)


def final_body(heads, factor, group, k, v, gk_part, gv_part, *refs):
    pieces, outs, (suffix, gk, gv, sems) = refs[:-6], refs[-6:-4], refs[-4:]
    pick(pieces, suffix, group)
    copies = []

    def send(h, held, out):
        copy = pltpu.make_async_copy(held.at[:, head(h)], out.at[:, head(h)], sems.at[len(copies)])
        copy.start()
        copies.append(copy)

    for h in range(heads):
        suf = suffix[head(h), :].astype(BF16)
        gk[:, head(h)] = (factor * dot(v[:, head(h)], suf, NT) + gk_part[:, head(h)]).astype(BF16)
        send(h, gk, outs[0])
        gv[:, head(h)] = (factor * dot(k[:, head(h)], suf, NN) + gv_part[:, head(h)]).astype(BF16)
        send(h, gv, outs[1])
    for copy in copies:
        copy.wait()


def exchange(piece, i, active, group):
    ways = lax.axis_size("tp")
    pairs = [
        (j * ways + t, (j ^ partner(i, group) if j in active else j) * ways + (t ^ 1))
        for j in range(2 * group)
        for t in range(ways)
    ]
    return lax.ppermute(piece, ("ctx", "tp"), pairs)


def carried_in(pieces, reverse, state):
    again = () if reverse or len(pieces) == 1 else pieces[-len(ALONE) :]
    group = len(pieces) - len(again)
    pieces = pieces[:group]
    count = lax.axis_size("ctx")
    sds = jax.ShapeDtypeStruct
    if group == 1:
        arrived = lax.all_to_all(pieces[0], "ctx", 0, 0, tiled=True)
        sums = call(
            functools.partial(scan_body, count, reverse),
            sds(arrived.shape, F32), arrived, scratch=[state],
        )
        return [lax.all_to_all(sums, "ctx", 0, 0, tiled=True)]
    rows, width = pieces[0].shape
    piece = sds((rows, width), F32)
    early, late, both = range(group), range(group, count), range(count)
    first, second = (late, early) if reverse else (early, late)
    everyone = range(group)
    arrived = [
        exchange(pieces[i], i, both if reverse or i in SHARED else first, group) for i in everyone
    ]
    kept = [sds((group * rows, width), F32)] if reverse else [piece] * len(SHARED)
    total, *back = call(
        functools.partial(inner_body, group, reverse),
        [piece] * (group + 1) + kept,
        *arrived,
        scratch=[] if reverse else [state],
    )
    over = lax.ppermute(total, "ctx", [(j, j ^ group) for j in both])
    ahead = [exchange(back[i], i, first, group) for i in everyone]
    if reverse:
        back = call(functools.partial(add_body, group), [piece] * group, back[group], over)
    else:
        own = [exchange(part, i, second, group) for part, i in zip(again, ALONE)]
        mixed = [own[ALONE.index(i)] if i in ALONE else back[group + SHARED.index(i)] for i in everyone]
        back = call(
            functools.partial(late_body, group, reverse),
            [piece] * group, *mixed, over, scratch=[state],
        )
    behind = [exchange(back[i], i, second, group) for i in everyone]
    return [*behind, *ahead] if reverse else [*ahead, *behind]


def from_all(part, axis):
    count = lax.axis_size(axis)
    even = count & (count - 1) == 0
    steps = [1, 3, 2] if count == 4 else range(1, count)
    return [part] + [
        lax.ppermute(part, axis, [(i, i ^ step if even else (i + step) % count) for i in range(count)])
        for step in steps
    ]


def on_device(queries, keys, values, gain, out_grad):
    tokens, width = queries.shape
    heads = width // HEAD
    count = lax.axis_size("ctx")
    factor = (HEAD * tokens * count) ** (-0.5)
    features = width * lax.axis_size("tp")
    gains = gain.reshape(heads, HEAD)
    sds = jax.ShapeDtypeStruct
    wide = sds((tokens, width), F32)
    half = sds((tokens, width), BF16)
    state = pltpu.VMEM((width, HEAD), F32)
    if count == 8 and lax.axis_size("tp") % 2 == 0:
        group = count // 2
        pieces = [sds((width // group, HEAD), F32)] * group
    else:
        group = count
        pieces = [sds((count, width // count, HEAD), F32)]

    def in_hbm(*arrays):
        return [pltpu.with_memory_space_constraint(array, pltpu.HBM) for array in arrays]

    def in_vmem(array):
        return pltpu.VMEM(array.shape, array.dtype)

    k_held, v_held, *states = call(
        functools.partial(states_body, heads, group),
        (in_vmem(keys), in_vmem(values), *pieces, *(pieces[i] for i in ALONE if len(pieces) > 1)),
        *in_hbm(keys, values),
        ins=[HBM, HBM],
        scratch=[state, pltpu.SemaphoreType.DMA((2 * LOADS,))],
    )
    prefix = carried_in(states, False, state)
    pairs = heads * tokens * tokens * HEAD
    scores, local, q_held, q_turned, weighted, gain_held = call(
        functools.partial(scores_body, heads, factor),
        (
            sds((heads, tokens, tokens), BF16), wide,
            in_vmem(queries), pltpu.VMEM((width, tokens), BF16), in_vmem(wide), in_vmem(gains),
        ),
        k_held, v_held, *in_hbm(queries, out_grad, gains),
        ins=[VMEM, VMEM, HBM, HBM, HBM],
        scratch=[in_vmem(out_grad), pltpu.SemaphoreType.DMA((3,))],
        flops=4 * pairs,
    )
    attended, stats, prefix = call(
        functools.partial(attend_body, heads, factor, group),
        (wide, sds((2, tokens), F32), sds((width, HEAD), F32)),
        q_held, weighted, local, *prefix,
    )
    every = from_all(stats, "tp")
    inv_rms, grad_attn, *updates = call(
        functools.partial(grad_body, heads, features, group, len(every)),
        (pltpu.VMEM((tokens, HEAD), F32), half, *pieces),
        attended, weighted, q_turned, *every,
        scratch=[state],
    )
    suffix = carried_in(updates, True, state)
    normed, grad_q, gk_part, gv_part = call(
        functools.partial(local_body, heads, factor),
        (half, half, wide, wide),
        grad_attn, q_held, k_held, v_held, prefix, scores, attended, inv_rms, gain_held,
        flops=9 * pairs,
    )
    held = pltpu.VMEM((tokens, width), BF16)
    grad_k, grad_v = call(
        functools.partial(final_body, heads, factor, group),
        (half, half),
        k_held, v_held, gk_part, gv_part, *suffix,
        dests=(HBM, HBM),
        scratch=[state, held, held, pltpu.SemaphoreType.DMA((2 * heads,))],
    )
    return normed, grad_q, grad_k, grad_v


def solution(mesh):
    placed = (P("ctx", "tp"), P("ctx", "tp"), P("ctx", "tp"), P("tp"), P("ctx", "tp"))
    return jax.shard_map(
        on_device,
        mesh=mesh,
        in_specs=placed,
        out_specs=(P("ctx", "tp"), P("ctx", "tp"), P("ctx", "tp"), P("ctx", "tp")),
        check_vma=False,
    )
```

```python
import functools

import jax
import jax.numpy as jnp
from jax import lax
from jax.experimental import pallas as pl
from jax.experimental.pallas import tpu as pltpu
from jax.sharding import PartitionSpec as P

HEAD = 128

epsilon = 1e-06
LOADS = 4
ALONE = (0, 2)
SHARED = (1, 3)
F32 = jnp.float32
BF16 = jnp.bfloat16

NN = (((1,), (0,)), ((), ()))
NT = (((1,), (1,)), ((), ()))
TN = (((0,), (0,)), ((), ()))


def dot(a, b, dims):
    return lax.dot_general(a, b, dims, preferred_element_type=F32)


VMEM = pl.BlockSpec(memory_space=pltpu.VMEM)
HBM = pl.BlockSpec(memory_space=pltpu.HBM)


def call(body, outs, *args, ins=None, dests=None, scratch=(), flops=1e7):
    moved = sum(a.size * a.dtype.itemsize for a in args)
    return pl.pallas_call(
        body,
        out_shape=outs,
        in_specs=ins or [VMEM] * len(args),
        out_specs=dests or jax.tree.map(lambda _: VMEM, outs),
        scratch_shapes=scratch,
        compiler_params=pltpu.CompilerParams(vmem_limit_bytes=16 * 1024 * 1024),
        cost_estimate=pl.CostEstimate(flops=int(flops), bytes_accessed=int(moved), transcendentals=0),
    )(*args)


def head(h):
    return slice(h * HEAD, (h + 1) * HEAD)


def causal_mask(tokens):
    row = lax.broadcasted_iota(jnp.int32, (tokens, tokens), 0)
    col = lax.broadcasted_iota(jnp.int32, (tokens, tokens), 1)
    return row >= col


def rows_of(scratch, parts, place):
    rows = scratch.shape[0] // parts
    return scratch.at[pl.ds(pl.multiple_of(place * rows, rows), rows), :]


def step_of(i, odd):
    return (3 - odd, 2 + odd, 1, 0)[i]


def give(scratch, group, outs, odd=0):
    if len(outs) == 1:
        outs[0][...] = scratch[...].reshape(outs[0].shape)
        return
    place = lax.rem(lax.axis_index("ctx"), group)
    for i, out in enumerate(outs):
        out[...] = rows_of(scratch, group, lax.bitwise_xor(place, step_of(i, odd)))[...]


def take(ins, scratch, group):
    if len(ins) == 1:
        scratch[...] = ins[0][...].reshape(scratch.shape)
        return
    place = lax.rem(lax.axis_index("ctx"), group)
    for i, piece in enumerate(ins):
        rows_of(scratch, group, lax.bitwise_xor(place, step_of(i, 0)))[...] = piece[...]


def running_sums(scratch, parts, reverse):
    rows = scratch.shape[0] // parts
    running = jnp.zeros((rows, scratch.shape[1]), F32)
    for place in range(parts - 1, -1, -1) if reverse else range(parts):
        own = slice(place * rows, (place + 1) * rows)
        here = scratch[own, :]
        scratch[own, :] = running
        running = running + here
    return running


def loads(pairs, sems):
    copies = [pltpu.make_async_copy(a, b, sems.at[i]) for i, (a, b) in enumerate(pairs)]
    for copy in copies:
        copy.start()
    return copies


def states_body(heads, group, k_hbm, v_hbm, k, v, *refs):
    outs, (state, sems) = refs[:-2], refs[-2:]
    rows = k.shape[0] // LOADS
    blocks = [slice(i * rows, (i + 1) * rows) for i in range(LOADS)]
    for copy in loads([(a.at[r, :], b.at[r, :]) for r in blocks for a, b in ((k_hbm, k), (v_hbm, v))], sems):
        copy.wait()
    for h in range(heads):
        state[head(h), :] = dot(k[:, head(h)], v[:, head(h)], TN)
    give(state, group, outs[:group])
    for again, i in zip(outs[group:], ALONE):
        again[...] = outs[i][...]


def scan_body(count, reverse, arrived, sums, scratch):
    take([arrived], scratch, count)
    running_sums(scratch, count, reverse)
    give(scratch, count, [sums])


def inner_body(group, reverse, *refs):
    arrived, total, outs, sums = refs[:group], refs[group], refs[group + 1 : 2 * group + 1], refs[-1]
    take(arrived, sums, group)
    total[...] = running_sums(sums, group, reverse)
    give(sums, group, outs, lax.rem(lax.axis_index("tp"), 2))
    if not reverse:
        for passed, i in zip(refs[2 * group + 1 : -1], SHARED):
            passed[...] = arrived[i][...]


def add_body(group, sums, over, *outs):
    place = lax.rem(lax.axis_index("ctx"), group)
    odd = lax.rem(lax.axis_index("tp"), 2)
    for i, out in enumerate(outs):
        out[...] = rows_of(sums, group, lax.bitwise_xor(place, step_of(i, odd)))[...] + over[...]


def late_body(group, reverse, *refs):
    arrived, over, outs, sums = refs[:group], refs[group], refs[group + 1 : -1], refs[-1]
    take(arrived, sums, group)
    running_sums(sums, group, reverse)
    add_body(group, sums, over, *outs)


def pick(pieces, scratch, group):
    many = len(pieces) // 2
    if many == 0:
        take(pieces, scratch, group)
        return
    early = lax.axis_index("ctx") < group
    place = lax.rem(lax.axis_index("ctx"), group)
    sent_by_odd = 1 - lax.rem(lax.axis_index("tp"), 2)
    for i in range(many):
        rows = rows_of(scratch, group, lax.bitwise_xor(place, step_of(i, sent_by_odd)))
        rows[...] = jnp.where(early, pieces[i][...], pieces[many + i][...])


def scores_body(heads, factor, k, v, q_hbm, og_hbm, gain_hbm, scores, attended, q, q_turned, weighted, gain, og, sems):
    copies = loads(((q_hbm, q), (og_hbm, og), (gain_hbm, gain)), sems)
    copies[0].wait()
    q_turned[...] = q[...].T
    causal = causal_mask(q.shape[0])
    for h in range(heads):
        raw = dot(q[:, head(h)], k[:, head(h)], NT) * factor
        sc = jnp.where(causal, raw, 0.0).astype(BF16)
        scores[h] = sc
        attended[:, head(h)] = dot(sc, v[:, head(h)], NN)
    for copy in copies[1:]:
        copy.wait()
    for h in range(heads):
        weighted[:, head(h)] = og[:, head(h)].astype(F32) * gain[h : h + 1, :]


def attend_body(heads, factor, group, q, weighted, local, *refs):
    pieces, (attended, stats, prefix) = refs[:-3], refs[-3:]
    pick(pieces, prefix, group)
    power = 0.0
    inner = 0.0
    for h in range(heads):
        att = factor * dot(q[:, head(h)], prefix[head(h), :].astype(BF16), NN) + local[:, head(h)]
        attended[:, head(h)] = att
        power = power + att * att
        inner = inner + weighted[:, head(h)] * att
    stats[0:1, :] = jnp.sum(power.T, axis=0, keepdims=True)
    stats[1:2, :] = jnp.sum(inner.T, axis=0, keepdims=True)


def grad_body(heads, features, group, ways, attended, weighted, q_turned, *refs):
    stats, (spread, grad), outs, updates = refs[:ways], refs[ways : ways + 2], refs[ways + 2 : -1], refs[-1]
    total = stats[0][...]
    for other in stats[1:]:
        total = total + other[...]
    inv_rms = lax.rsqrt(total[0:1, :] / features + epsilon)
    bend = inv_rms * inv_rms * (total[1:2, :] / features)
    tokens = q_turned.shape[1]
    inv_rms = jnp.broadcast_to(inv_rms, (HEAD, tokens)).T
    bend = jnp.broadcast_to(bend, (HEAD, tokens)).T
    spread[...] = inv_rms
    for h in range(heads):
        ga = (inv_rms * (weighted[:, head(h)] - attended[:, head(h)] * bend)).astype(BF16)
        grad[:, head(h)] = ga
        updates[head(h), :] = dot(q_turned[head(h), :], ga, NN)
    give(updates, group, outs)


def local_body(heads, factor, ga, q, k, v, prefix, scores, attended, inv_rms, gain, normed, gq, gk_part, gv_part):
    causal = causal_mask(q.shape[0])
    for h in range(heads):
        normed[:, head(h)] = (attended[:, head(h)] * inv_rms[...] * gain[h : h + 1, :]).astype(BF16)
        gah = ga[:, head(h)]
        raw = dot(gah, v[:, head(h)], NT) * factor
        gs = jnp.where(causal, raw, 0.0).astype(BF16)
        out = factor * dot(gah, prefix[head(h), :].astype(BF16), NT)
        gq[:, head(h)] = (out + dot(gs, k[:, head(h)], NN)).astype(BF16)
        gk_part[:, head(h)] = dot(gs, q[:, head(h)], TN)
        gv_part[:, head(h)] = dot(scores[h], gah, TN)


def final_body(heads, factor, group, k, v, gk_part, gv_part, *refs):
    pieces, outs, (suffix, gk, gv, sems) = refs[:-6], refs[-6:-4], refs[-4:]
    pick(pieces, suffix, group)
    copies = []

    def send(h, held, out):
        copy = pltpu.make_async_copy(held.at[:, head(h)], out.at[:, head(h)], sems.at[len(copies)])
        copy.start()
        copies.append(copy)

    for h in range(heads):
        suf = suffix[head(h), :].astype(BF16)
        gk[:, head(h)] = (factor * dot(v[:, head(h)], suf, NT) + gk_part[:, head(h)]).astype(BF16)
        send(h, gk, outs[0])
        gv[:, head(h)] = (factor * dot(k[:, head(h)], suf, NN) + gv_part[:, head(h)]).astype(BF16)
        send(h, gv, outs[1])
    for copy in copies:
        copy.wait()


def exchange(piece, i, active, back=False):
    ways = lax.axis_size("tp")
    pairs = [
        (j * ways + t, (j ^ step_of(i, t % 2 if back else 0) if j in active else j) * ways + (t ^ 1))
        for j in range(lax.axis_size("ctx"))
        for t in range(ways)
    ]
    return lax.ppermute(piece, ("ctx", "tp"), pairs)


def carried_in(pieces, reverse, state):
    again = () if reverse or len(pieces) == 1 else pieces[-len(ALONE) :]
    group = len(pieces) - len(again)
    pieces = pieces[:group]
    count = lax.axis_size("ctx")
    sds = jax.ShapeDtypeStruct
    if group == 1:
        arrived = lax.all_to_all(pieces[0], "ctx", 0, 0, tiled=True)
        sums = call(
            functools.partial(scan_body, count, reverse),
            sds(arrived.shape, F32), arrived, scratch=[state],
        )
        return [lax.all_to_all(sums, "ctx", 0, 0, tiled=True)]
    rows, width = pieces[0].shape
    piece = sds((rows, width), F32)
    early, late, both = range(group), range(group, count), range(count)
    first, second = (late, early) if reverse else (early, late)
    everyone = range(group)
    arrived = [
        exchange(pieces[i], i, both if reverse or i in SHARED else first) for i in everyone
    ]
    kept = [sds((group * rows, width), F32)] if reverse else [piece] * len(SHARED)
    total, *back = call(
        functools.partial(inner_body, group, reverse),
        [piece] * (group + 1) + kept,
        *arrived,
        scratch=[] if reverse else [state],
    )
    over = lax.ppermute(total, "ctx", [(j, j ^ group) for j in both])
    ahead = [exchange(back[i], i, first, True) for i in everyone]
    if reverse:
        back = call(functools.partial(add_body, group), [piece] * group, back[group], over)
    else:
        own = [exchange(part, i, second) for part, i in zip(again, ALONE)]
        mixed = [own[ALONE.index(i)] if i in ALONE else back[group + SHARED.index(i)] for i in everyone]
        back = call(
            functools.partial(late_body, group, reverse),
            [piece] * group, *mixed, over, scratch=[state],
        )
    behind = [exchange(back[i], i, second, True) for i in everyone]
    return [*behind, *ahead] if reverse else [*ahead, *behind]


def from_all(part, axis):
    count = lax.axis_size(axis)
    even = count & (count - 1) == 0
    steps = [1, 3, 2] if count == 4 else range(1, count)
    return [part] + [
        lax.ppermute(part, axis, [(i, i ^ step if even else (i + step) % count) for i in range(count)])
        for step in steps
    ]


def on_device(queries, keys, values, gain, out_grad):
    tokens, width = queries.shape
    heads = width // HEAD
    count = lax.axis_size("ctx")
    factor = (HEAD * tokens * count) ** (-0.5)
    features = width * lax.axis_size("tp")
    gains = gain.reshape(heads, HEAD)
    sds = jax.ShapeDtypeStruct
    wide = sds((tokens, width), F32)
    half = sds((tokens, width), BF16)
    state = pltpu.VMEM((width, HEAD), F32)
    if count == 8 and lax.axis_size("tp") % 2 == 0:
        group = count // 2
        pieces = [sds((width // group, HEAD), F32)] * group
    else:
        group = count
        pieces = [sds((count, width // count, HEAD), F32)]

    def in_hbm(*arrays):
        return [pltpu.with_memory_space_constraint(array, pltpu.HBM) for array in arrays]

    def in_vmem(array):
        return pltpu.VMEM(array.shape, array.dtype)

    k_held, v_held, *states = call(
        functools.partial(states_body, heads, group),
        (in_vmem(keys), in_vmem(values), *pieces, *(pieces[i] for i in ALONE if len(pieces) > 1)),
        *in_hbm(keys, values),
        ins=[HBM, HBM],
        scratch=[state, pltpu.SemaphoreType.DMA((2 * LOADS,))],
    )
    prefix = carried_in(states, False, state)
    pairs = heads * tokens * tokens * HEAD
    scores, local, q_held, q_turned, weighted, gain_held = call(
        functools.partial(scores_body, heads, factor),
        (
            sds((heads, tokens, tokens), BF16), wide,
            in_vmem(queries), pltpu.VMEM((width, tokens), BF16), in_vmem(wide), in_vmem(gains),
        ),
        k_held, v_held, *in_hbm(queries, out_grad, gains),
        ins=[VMEM, VMEM, HBM, HBM, HBM],
        scratch=[in_vmem(out_grad), pltpu.SemaphoreType.DMA((3,))],
        flops=4 * pairs,
    )
    attended, stats, prefix = call(
        functools.partial(attend_body, heads, factor, group),
        (wide, sds((2, tokens), F32), sds((width, HEAD), F32)),
        q_held, weighted, local, *prefix,
    )
    every = from_all(stats, "tp")
    inv_rms, grad_attn, *updates = call(
        functools.partial(grad_body, heads, features, group, len(every)),
        (pltpu.VMEM((tokens, HEAD), F32), half, *pieces),
        attended, weighted, q_turned, *every,
        scratch=[state],
    )
    suffix = carried_in(updates, True, state)
    normed, grad_q, gk_part, gv_part = call(
        functools.partial(local_body, heads, factor),
        (half, half, wide, wide),
        grad_attn, q_held, k_held, v_held, prefix, scores, attended, inv_rms, gain_held,
        flops=9 * pairs,
    )
    held = pltpu.VMEM((tokens, width), BF16)
    grad_k, grad_v = call(
        functools.partial(final_body, heads, factor, group),
        (half, half),
        k_held, v_held, gk_part, gv_part, *suffix,
        dests=(HBM, HBM),
        scratch=[state, held, held, pltpu.SemaphoreType.DMA((2 * heads,))],
    )
    return normed, grad_q, grad_k, grad_v


def solution(mesh):
    placed = (P("ctx", "tp"), P("ctx", "tp"), P("ctx", "tp"), P("tp"), P("ctx", "tp"))
    return jax.shard_map(
        on_device,
        mesh=mesh,
        in_specs=placed,
        out_specs=(P("ctx", "tp"), P("ctx", "tp"), P("ctx", "tp"), P("ctx", "tp")),
        check_vma=False,
    )
```

```python
import functools

import jax
import jax.numpy as jnp
from jax import lax
from jax.experimental import pallas as pl
from jax.experimental.pallas import tpu as pltpu
from jax.sharding import PartitionSpec as P

HEAD = 128

epsilon = 1e-06
LOADS = 4
FIRST, BACK, HAND = 0, 1, 2
ALONE = (0, 2)
SHARED = (1, 3)
F32 = jnp.float32
BF16 = jnp.bfloat16

NN = (((1,), (0,)), ((), ()))
NT = (((1,), (1,)), ((), ()))
TN = (((0,), (0,)), ((), ()))


def dot(a, b, dims):
    return lax.dot_general(a, b, dims, preferred_element_type=F32)


VMEM = pl.BlockSpec(memory_space=pltpu.VMEM)
HBM = pl.BlockSpec(memory_space=pltpu.HBM)


def call(body, outs, *args, ins=None, dests=None, scratch=(), flops=1e7):
    moved = sum(a.size * a.dtype.itemsize for a in args)
    return pl.pallas_call(
        body,
        out_shape=outs,
        in_specs=ins or [VMEM] * len(args),
        out_specs=dests or jax.tree.map(lambda _: VMEM, outs),
        scratch_shapes=scratch,
        compiler_params=pltpu.CompilerParams(vmem_limit_bytes=16 * 1024 * 1024),
        cost_estimate=pl.CostEstimate(flops=int(flops), bytes_accessed=int(moved), transcendentals=0),
    )(*args)


def head(h):
    return slice(h * HEAD, (h + 1) * HEAD)


def causal_mask(tokens):
    row = lax.broadcasted_iota(jnp.int32, (tokens, tokens), 0)
    col = lax.broadcasted_iota(jnp.int32, (tokens, tokens), 1)
    return row >= col


def rows_of(scratch, parts, place):
    rows = scratch.shape[0] // parts
    return scratch.at[pl.ds(pl.multiple_of(place * rows, rows), rows), :]


def step_of(i, odd, order):
    return (
        (3, 2, 1, 0),
        (3, 2 - odd, 1 + odd, 0),
        (3 - 2 * odd, 2 + odd, 1 + odd, 0),
    )[order][i]


def give(scratch, group, outs, order=0):
    if len(outs) == 1:
        outs[0][...] = scratch[...].reshape(outs[0].shape)
        return
    place = lax.rem(lax.axis_index("ctx"), group)
    odd = lax.rem(lax.axis_index("tp"), 2)
    for i, out in enumerate(outs):
        out[...] = rows_of(scratch, group, lax.bitwise_xor(place, step_of(i, odd, order)))[...]


def take(ins, scratch, group, order=0):
    if len(ins) == 1:
        scratch[...] = ins[0][...].reshape(scratch.shape)
        return
    place = lax.rem(lax.axis_index("ctx"), group)
    sent_by_odd = 1 - lax.rem(lax.axis_index("tp"), 2)
    for i, piece in enumerate(ins):
        rows_of(scratch, group, lax.bitwise_xor(place, step_of(i, sent_by_odd, order)))[...] = piece[...]


def running_sums(scratch, parts, reverse):
    rows = scratch.shape[0] // parts
    running = jnp.zeros((rows, scratch.shape[1]), F32)
    for place in range(parts - 1, -1, -1) if reverse else range(parts):
        own = slice(place * rows, (place + 1) * rows)
        here = scratch[own, :]
        scratch[own, :] = running
        running = running + here
    return running


def loads(pairs, sems):
    copies = [pltpu.make_async_copy(a, b, sems.at[i]) for i, (a, b) in enumerate(pairs)]
    for copy in copies:
        copy.start()
    return copies


def states_body(heads, group, k_hbm, v_hbm, k, v, *refs):
    outs, (state, sems) = refs[:-2], refs[-2:]
    rows = k.shape[0] // LOADS
    blocks = [slice(i * rows, (i + 1) * rows) for i in range(LOADS)]
    for copy in loads([(a.at[r, :], b.at[r, :]) for r in blocks for a, b in ((k_hbm, k), (v_hbm, v))], sems):
        copy.wait()
    for h in range(heads):
        state[head(h), :] = dot(k[:, head(h)], v[:, head(h)], TN)
    give(state, group, outs[:group], FIRST)
    for again, i in zip(outs[group:], ALONE):
        again[...] = outs[i][...]


def scan_body(count, reverse, arrived, sums, scratch):
    take([arrived], scratch, count)
    running_sums(scratch, count, reverse)
    give(scratch, count, [sums])


def inner_body(group, reverse, *refs):
    arrived, total, outs, sums = refs[:group], refs[group], refs[group + 1 : 2 * group + 1], refs[-1]
    take(arrived, sums, group, BACK if reverse else FIRST)
    total[...] = running_sums(sums, group, reverse)
    give(sums, group, outs, HAND)
    if not reverse:
        for passed, i in zip(refs[2 * group + 1 : -1], SHARED):
            passed[...] = arrived[i][...]


def add_body(group, sums, over, *outs):
    place = lax.rem(lax.axis_index("ctx"), group)
    odd = lax.rem(lax.axis_index("tp"), 2)
    for i, out in enumerate(outs):
        out[...] = rows_of(sums, group, lax.bitwise_xor(place, step_of(i, odd, HAND)))[...] + over[...]


def late_body(group, reverse, *refs):
    arrived, over, outs, sums = refs[:group], refs[group], refs[group + 1 : -1], refs[-1]
    take(arrived, sums, group)
    running_sums(sums, group, reverse)
    add_body(group, sums, over, *outs)


def pick(pieces, scratch, group):
    many = len(pieces) // 2
    if many == 0:
        take(pieces, scratch, group)
        return
    early = lax.axis_index("ctx") < group
    place = lax.rem(lax.axis_index("ctx"), group)
    sent_by_odd = 1 - lax.rem(lax.axis_index("tp"), 2)
    for i in range(many):
        rows = rows_of(scratch, group, lax.bitwise_xor(place, step_of(i, sent_by_odd, HAND)))
        rows[...] = jnp.where(early, pieces[i][...], pieces[many + i][...])


def scores_body(heads, factor, k, v, q_hbm, og_hbm, gain_hbm, scores, attended, q, q_turned, weighted, gain, og, sems):
    copies = loads(((q_hbm, q), (og_hbm, og), (gain_hbm, gain)), sems)
    copies[0].wait()
    q_turned[...] = q[...].T
    causal = causal_mask(q.shape[0])
    for h in range(heads):
        raw = dot(q[:, head(h)], k[:, head(h)], NT) * factor
        sc = jnp.where(causal, raw, 0.0).astype(BF16)
        scores[h] = sc
        attended[:, head(h)] = dot(sc, v[:, head(h)], NN)
    for copy in copies[1:]:
        copy.wait()
    for h in range(heads):
        weighted[:, head(h)] = og[:, head(h)].astype(F32) * gain[h : h + 1, :]


def attend_body(heads, factor, group, q, weighted, local, *refs):
    pieces, (attended, stats, prefix) = refs[:-3], refs[-3:]
    pick(pieces, prefix, group)
    power = 0.0
    inner = 0.0
    for h in range(heads):
        att = factor * dot(q[:, head(h)], prefix[head(h), :].astype(BF16), NN) + local[:, head(h)]
        attended[:, head(h)] = att
        power = power + att * att
        inner = inner + weighted[:, head(h)] * att
    stats[0:1, :] = jnp.sum(power.T, axis=0, keepdims=True)
    stats[1:2, :] = jnp.sum(inner.T, axis=0, keepdims=True)


def grad_body(heads, features, group, ways, attended, weighted, q_turned, *refs):
    stats, (spread, grad), outs, updates = refs[:ways], refs[ways : ways + 2], refs[ways + 2 : -1], refs[-1]
    total = stats[0][...]
    for other in stats[1:]:
        total = total + other[...]
    inv_rms = lax.rsqrt(total[0:1, :] / features + epsilon)
    bend = inv_rms * inv_rms * (total[1:2, :] / features)
    tokens = q_turned.shape[1]
    inv_rms = jnp.broadcast_to(inv_rms, (HEAD, tokens)).T
    bend = jnp.broadcast_to(bend, (HEAD, tokens)).T
    spread[...] = inv_rms
    for h in range(heads):
        ga = (inv_rms * (weighted[:, head(h)] - attended[:, head(h)] * bend)).astype(BF16)
        grad[:, head(h)] = ga
        updates[head(h), :] = dot(q_turned[head(h), :], ga, NN)
    give(updates, group, outs, BACK)


def local_body(heads, factor, ga, q, k, v, prefix, scores, attended, inv_rms, gain, normed, gq, gk_part, gv_part):
    causal = causal_mask(q.shape[0])
    for h in range(heads):
        normed[:, head(h)] = (attended[:, head(h)] * inv_rms[...] * gain[h : h + 1, :]).astype(BF16)
        gah = ga[:, head(h)]
        raw = dot(gah, v[:, head(h)], NT) * factor
        gs = jnp.where(causal, raw, 0.0).astype(BF16)
        out = factor * dot(gah, prefix[head(h), :].astype(BF16), NT)
        gq[:, head(h)] = (out + dot(gs, k[:, head(h)], NN)).astype(BF16)
        gk_part[:, head(h)] = dot(gs, q[:, head(h)], TN)
        gv_part[:, head(h)] = dot(scores[h], gah, TN)


def final_body(heads, factor, group, k, v, gk_part, gv_part, *refs):
    pieces, outs, (suffix, gk, gv, sems) = refs[:-6], refs[-6:-4], refs[-4:]
    pick(pieces, suffix, group)
    copies = []

    def send(h, held, out):
        copy = pltpu.make_async_copy(held.at[:, head(h)], out.at[:, head(h)], sems.at[len(copies)])
        copy.start()
        copies.append(copy)

    for h in range(heads):
        suf = suffix[head(h), :].astype(BF16)
        gk[:, head(h)] = (factor * dot(v[:, head(h)], suf, NT) + gk_part[:, head(h)]).astype(BF16)
        send(h, gk, outs[0])
        gv[:, head(h)] = (factor * dot(k[:, head(h)], suf, NN) + gv_part[:, head(h)]).astype(BF16)
        send(h, gv, outs[1])
    for copy in copies:
        copy.wait()


def exchange(piece, i, active, order):
    ways = lax.axis_size("tp")
    pairs = [
        (j * ways + t, (j ^ step_of(i, t % 2, order) if j in active else j) * ways + (t ^ 1))
        for j in range(lax.axis_size("ctx"))
        for t in range(ways)
    ]
    return lax.ppermute(piece, ("ctx", "tp"), pairs)


def carried_in(pieces, reverse, state):
    again = () if reverse or len(pieces) == 1 else pieces[-len(ALONE) :]
    group = len(pieces) - len(again)
    pieces = pieces[:group]
    count = lax.axis_size("ctx")
    sds = jax.ShapeDtypeStruct
    if group == 1:
        arrived = lax.all_to_all(pieces[0], "ctx", 0, 0, tiled=True)
        sums = call(
            functools.partial(scan_body, count, reverse),
            sds(arrived.shape, F32), arrived, scratch=[state],
        )
        return [lax.all_to_all(sums, "ctx", 0, 0, tiled=True)]
    rows, width = pieces[0].shape
    piece = sds((rows, width), F32)
    early, late, both = range(group), range(group, count), range(count)
    first, second = (late, early) if reverse else (early, late)
    everyone = range(group)
    arrived = [
        exchange(pieces[i], i, both if reverse or i in SHARED else first, BACK if reverse else FIRST)
        for i in everyone
    ]
    kept = [sds((group * rows, width), F32)] if reverse else [piece] * len(SHARED)
    total, *back = call(
        functools.partial(inner_body, group, reverse),
        [piece] * (group + 1) + kept,
        *arrived,
        scratch=[] if reverse else [state],
    )
    over = lax.ppermute(total, "ctx", [(j, j ^ group) for j in both])
    ahead = [exchange(back[i], i, first, HAND) for i in everyone]
    if reverse:
        back = call(functools.partial(add_body, group), [piece] * group, back[group], over)
    else:
        own = [exchange(part, i, second, FIRST) for part, i in zip(again, ALONE)]
        mixed = [own[ALONE.index(i)] if i in ALONE else back[group + SHARED.index(i)] for i in everyone]
        back = call(
            functools.partial(late_body, group, reverse),
            [piece] * group, *mixed, over, scratch=[state],
        )
    behind = [exchange(back[i], i, second, HAND) for i in everyone]
    return [*behind, *ahead] if reverse else [*ahead, *behind]


def from_all(part, axis):
    count = lax.axis_size(axis)
    even = count & (count - 1) == 0
    steps = [1, 3, 2] if count == 4 else range(1, count)
    return [part] + [
        lax.ppermute(part, axis, [(i, i ^ step if even else (i + step) % count) for i in range(count)])
        for step in steps
    ]


def on_device(queries, keys, values, gain, out_grad):
    tokens, width = queries.shape
    heads = width // HEAD
    count = lax.axis_size("ctx")
    factor = (HEAD * tokens * count) ** (-0.5)
    features = width * lax.axis_size("tp")
    gains = gain.reshape(heads, HEAD)
    sds = jax.ShapeDtypeStruct
    wide = sds((tokens, width), F32)
    half = sds((tokens, width), BF16)
    state = pltpu.VMEM((width, HEAD), F32)
    if count == 8 and lax.axis_size("tp") % 2 == 0:
        group = count // 2
        pieces = [sds((width // group, HEAD), F32)] * group
    else:
        group = count
        pieces = [sds((count, width // count, HEAD), F32)]

    def in_hbm(*arrays):
        return [pltpu.with_memory_space_constraint(array, pltpu.HBM) for array in arrays]

    def in_vmem(array):
        return pltpu.VMEM(array.shape, array.dtype)

    k_held, v_held, *states = call(
        functools.partial(states_body, heads, group),
        (in_vmem(keys), in_vmem(values), *pieces, *(pieces[i] for i in ALONE if len(pieces) > 1)),
        *in_hbm(keys, values),
        ins=[HBM, HBM],
        scratch=[state, pltpu.SemaphoreType.DMA((2 * LOADS,))],
    )
    prefix = carried_in(states, False, state)
    pairs = heads * tokens * tokens * HEAD
    scores, local, q_held, q_turned, weighted, gain_held = call(
        functools.partial(scores_body, heads, factor),
        (
            sds((heads, tokens, tokens), BF16), wide,
            in_vmem(queries), pltpu.VMEM((width, tokens), BF16), in_vmem(wide), in_vmem(gains),
        ),
        k_held, v_held, *in_hbm(queries, out_grad, gains),
        ins=[VMEM, VMEM, HBM, HBM, HBM],
        scratch=[in_vmem(out_grad), pltpu.SemaphoreType.DMA((3,))],
        flops=4 * pairs,
    )
    attended, stats, prefix = call(
        functools.partial(attend_body, heads, factor, group),
        (wide, sds((2, tokens), F32), sds((width, HEAD), F32)),
        q_held, weighted, local, *prefix,
    )
    every = from_all(stats, "tp")
    inv_rms, grad_attn, *updates = call(
        functools.partial(grad_body, heads, features, group, len(every)),
        (pltpu.VMEM((tokens, HEAD), F32), half, *pieces),
        attended, weighted, q_turned, *every,
        scratch=[state],
    )
    suffix = carried_in(updates, True, state)
    normed, grad_q, gk_part, gv_part = call(
        functools.partial(local_body, heads, factor),
        (half, half, wide, wide),
        grad_attn, q_held, k_held, v_held, prefix, scores, attended, inv_rms, gain_held,
        flops=9 * pairs,
    )
    held = pltpu.VMEM((tokens, width), BF16)
    grad_k, grad_v = call(
        functools.partial(final_body, heads, factor, group),
        (half, half),
        k_held, v_held, gk_part, gv_part, *suffix,
        dests=(HBM, HBM),
        scratch=[state, held, held, pltpu.SemaphoreType.DMA((2 * heads,))],
    )
    return normed, grad_q, grad_k, grad_v


def solution(mesh):
    placed = (P("ctx", "tp"), P("ctx", "tp"), P("ctx", "tp"), P("tp"), P("ctx", "tp"))
    return jax.shard_map(
        on_device,
        mesh=mesh,
        in_specs=placed,
        out_specs=(P("ctx", "tp"), P("ctx", "tp"), P("ctx", "tp"), P("ctx", "tp")),
        check_vma=False,
    )
```

```python
import functools

import jax
import jax.numpy as jnp
from jax import lax
from jax.experimental import pallas as pl
from jax.experimental.pallas import tpu as pltpu
from jax.sharding import PartitionSpec as P

HEAD = 128

epsilon = 1e-06
LOADS = 4
FIRST, BACK, HAND, HAND_BACK = 0, 1, 2, 3
ALONE = (0, 2)
SHARED = (1, 3)
F32 = jnp.float32
BF16 = jnp.bfloat16

NN = (((1,), (0,)), ((), ()))
NT = (((1,), (1,)), ((), ()))
TN = (((0,), (0,)), ((), ()))


def dot(a, b, dims):
    return lax.dot_general(a, b, dims, preferred_element_type=F32)


VMEM = pl.BlockSpec(memory_space=pltpu.VMEM)
HBM = pl.BlockSpec(memory_space=pltpu.HBM)


def call(body, outs, *args, ins=None, dests=None, scratch=(), flops=1e7):
    moved = sum(a.size * a.dtype.itemsize for a in args)
    return pl.pallas_call(
        body,
        out_shape=outs,
        in_specs=ins or [VMEM] * len(args),
        out_specs=dests or jax.tree.map(lambda _: VMEM, outs),
        scratch_shapes=scratch,
        compiler_params=pltpu.CompilerParams(vmem_limit_bytes=16 * 1024 * 1024),
        cost_estimate=pl.CostEstimate(flops=int(flops), bytes_accessed=int(moved), transcendentals=0),
    )(*args)


def head(h):
    return slice(h * HEAD, (h + 1) * HEAD)


def causal_mask(tokens):
    row = lax.broadcasted_iota(jnp.int32, (tokens, tokens), 0)
    col = lax.broadcasted_iota(jnp.int32, (tokens, tokens), 1)
    return row >= col


def rows_of(scratch, parts, place):
    rows = scratch.shape[0] // parts
    return scratch.at[pl.ds(pl.multiple_of(place * rows, rows), rows), :]


def step_of(i, odd, order):
    return (
        (3, 2, 1, 0),
        (3, 2 - odd, 1 + odd, 0),
        (3 - odd, 2 + odd, 1, 0),
        (3 - 2 * odd, 2 + odd, 1 + odd, 0),
    )[order][i]


def give(scratch, group, outs, order=0):
    if len(outs) == 1:
        outs[0][...] = scratch[...].reshape(outs[0].shape)
        return
    place = lax.rem(lax.axis_index("ctx"), group)
    odd = lax.rem(lax.axis_index("tp"), 2)
    for i, out in enumerate(outs):
        out[...] = rows_of(scratch, group, lax.bitwise_xor(place, step_of(i, odd, order)))[...]


def take(ins, scratch, group, order=0):
    if len(ins) == 1:
        scratch[...] = ins[0][...].reshape(scratch.shape)
        return
    place = lax.rem(lax.axis_index("ctx"), group)
    sent_by_odd = 1 - lax.rem(lax.axis_index("tp"), 2)
    for i, piece in enumerate(ins):
        rows_of(scratch, group, lax.bitwise_xor(place, step_of(i, sent_by_odd, order)))[...] = piece[...]


def running_sums(scratch, parts, reverse):
    rows = scratch.shape[0] // parts
    running = jnp.zeros((rows, scratch.shape[1]), F32)
    for place in range(parts - 1, -1, -1) if reverse else range(parts):
        own = slice(place * rows, (place + 1) * rows)
        here = scratch[own, :]
        scratch[own, :] = running
        running = running + here
    return running


def loads(pairs, sems):
    copies = [pltpu.make_async_copy(a, b, sems.at[i]) for i, (a, b) in enumerate(pairs)]
    for copy in copies:
        copy.start()
    return copies


def states_body(heads, group, k_hbm, v_hbm, k, v, *refs):
    outs, (state, sems) = refs[:-2], refs[-2:]
    rows = k.shape[0] // LOADS
    blocks = [slice(i * rows, (i + 1) * rows) for i in range(LOADS)]
    for copy in loads([(a.at[r, :], b.at[r, :]) for r in blocks for a, b in ((k_hbm, k), (v_hbm, v))], sems):
        copy.wait()
    for h in range(heads):
        state[head(h), :] = dot(k[:, head(h)], v[:, head(h)], TN)
    give(state, group, outs[:group], FIRST)
    for again, i in zip(outs[group:], ALONE):
        again[...] = outs[i][...]


def scan_body(count, reverse, arrived, sums, scratch):
    take([arrived], scratch, count)
    running_sums(scratch, count, reverse)
    give(scratch, count, [sums])


def inner_body(group, reverse, *refs):
    arrived, total, outs, sums = refs[:group], refs[group], refs[group + 1 : 2 * group + 1], refs[-1]
    take(arrived, sums, group, BACK if reverse else FIRST)
    total[...] = running_sums(sums, group, reverse)
    give(sums, group, outs, HAND_BACK if reverse else HAND)
    if not reverse:
        for passed, i in zip(refs[2 * group + 1 : -1], SHARED):
            passed[...] = arrived[i][...]


def add_body(group, order, sums, over, *outs):
    place = lax.rem(lax.axis_index("ctx"), group)
    odd = lax.rem(lax.axis_index("tp"), 2)
    for i, out in enumerate(outs):
        out[...] = rows_of(sums, group, lax.bitwise_xor(place, step_of(i, odd, order)))[...] + over[...]


def late_body(group, reverse, *refs):
    arrived, over, outs, sums = refs[:group], refs[group], refs[group + 1 : -1], refs[-1]
    take(arrived, sums, group)
    running_sums(sums, group, reverse)
    add_body(group, HAND, sums, over, *outs)


def pick(pieces, scratch, group, order):
    many = len(pieces) // 2
    if many == 0:
        take(pieces, scratch, group)
        return
    early = lax.axis_index("ctx") < group
    place = lax.rem(lax.axis_index("ctx"), group)
    sent_by_odd = 1 - lax.rem(lax.axis_index("tp"), 2)
    for i in range(many):
        rows = rows_of(scratch, group, lax.bitwise_xor(place, step_of(i, sent_by_odd, order)))
        rows[...] = jnp.where(early, pieces[i][...], pieces[many + i][...])


def scores_body(heads, factor, k, v, q_hbm, og_hbm, gain_hbm, scores, attended, q, q_turned, weighted, gain, og, sems):
    copies = loads(((q_hbm, q), (og_hbm, og), (gain_hbm, gain)), sems)
    copies[0].wait()
    q_turned[...] = q[...].T
    causal = causal_mask(q.shape[0])
    for h in range(heads):
        raw = dot(q[:, head(h)], k[:, head(h)], NT) * factor
        sc = jnp.where(causal, raw, 0.0).astype(BF16)
        scores[h] = sc
        attended[:, head(h)] = dot(sc, v[:, head(h)], NN)
    for copy in copies[1:]:
        copy.wait()
    for h in range(heads):
        weighted[:, head(h)] = og[:, head(h)].astype(F32) * gain[h : h + 1, :]


def attend_body(heads, factor, group, q, weighted, local, *refs):
    pieces, (attended, stats, prefix) = refs[:-3], refs[-3:]
    pick(pieces, prefix, group, HAND)
    power = 0.0
    inner = 0.0
    for h in range(heads):
        att = factor * dot(q[:, head(h)], prefix[head(h), :].astype(BF16), NN) + local[:, head(h)]
        attended[:, head(h)] = att
        power = power + att * att
        inner = inner + weighted[:, head(h)] * att
    stats[0:1, :] = jnp.sum(power.T, axis=0, keepdims=True)
    stats[1:2, :] = jnp.sum(inner.T, axis=0, keepdims=True)


def grad_body(heads, features, group, ways, attended, weighted, q_turned, *refs):
    stats, (spread, grad), outs, updates = refs[:ways], refs[ways : ways + 2], refs[ways + 2 : -1], refs[-1]
    total = stats[0][...]
    for other in stats[1:]:
        total = total + other[...]
    inv_rms = lax.rsqrt(total[0:1, :] / features + epsilon)
    bend = inv_rms * inv_rms * (total[1:2, :] / features)
    tokens = q_turned.shape[1]
    inv_rms = jnp.broadcast_to(inv_rms, (HEAD, tokens)).T
    bend = jnp.broadcast_to(bend, (HEAD, tokens)).T
    spread[...] = inv_rms
    for h in range(heads):
        ga = (inv_rms * (weighted[:, head(h)] - attended[:, head(h)] * bend)).astype(BF16)
        grad[:, head(h)] = ga
        updates[head(h), :] = dot(q_turned[head(h), :], ga, NN)
    give(updates, group, outs, BACK)


def local_body(heads, factor, ga, q, k, v, prefix, scores, attended, inv_rms, gain, normed, gq, gk_part, gv_part):
    causal = causal_mask(q.shape[0])
    for h in range(heads):
        normed[:, head(h)] = (attended[:, head(h)] * inv_rms[...] * gain[h : h + 1, :]).astype(BF16)
        gah = ga[:, head(h)]
        raw = dot(gah, v[:, head(h)], NT) * factor
        gs = jnp.where(causal, raw, 0.0).astype(BF16)
        out = factor * dot(gah, prefix[head(h), :].astype(BF16), NT)
        gq[:, head(h)] = (out + dot(gs, k[:, head(h)], NN)).astype(BF16)
        gk_part[:, head(h)] = dot(gs, q[:, head(h)], TN)
        gv_part[:, head(h)] = dot(scores[h], gah, TN)


def final_body(heads, factor, group, k, v, gk_part, gv_part, *refs):
    pieces, outs, (suffix, gk, gv, sems) = refs[:-6], refs[-6:-4], refs[-4:]
    pick(pieces, suffix, group, HAND_BACK)
    copies = []

    def send(h, held, out):
        copy = pltpu.make_async_copy(held.at[:, head(h)], out.at[:, head(h)], sems.at[len(copies)])
        copy.start()
        copies.append(copy)

    for h in range(heads):
        suf = suffix[head(h), :].astype(BF16)
        gk[:, head(h)] = (factor * dot(v[:, head(h)], suf, NT) + gk_part[:, head(h)]).astype(BF16)
        send(h, gk, outs[0])
        gv[:, head(h)] = (factor * dot(k[:, head(h)], suf, NN) + gv_part[:, head(h)]).astype(BF16)
        send(h, gv, outs[1])
    for copy in copies:
        copy.wait()


def exchange(piece, i, active, order):
    ways = lax.axis_size("tp")
    pairs = [
        (j * ways + t, (j ^ step_of(i, t % 2, order) if j in active else j) * ways + (t ^ 1))
        for j in range(lax.axis_size("ctx"))
        for t in range(ways)
    ]
    return lax.ppermute(piece, ("ctx", "tp"), pairs)


def carried_in(pieces, reverse, state):
    again = () if reverse or len(pieces) == 1 else pieces[-len(ALONE) :]
    group = len(pieces) - len(again)
    pieces = pieces[:group]
    count = lax.axis_size("ctx")
    sds = jax.ShapeDtypeStruct
    if group == 1:
        arrived = lax.all_to_all(pieces[0], "ctx", 0, 0, tiled=True)
        sums = call(
            functools.partial(scan_body, count, reverse),
            sds(arrived.shape, F32), arrived, scratch=[state],
        )
        return [lax.all_to_all(sums, "ctx", 0, 0, tiled=True)]
    rows, width = pieces[0].shape
    piece = sds((rows, width), F32)
    early, late, both = range(group), range(group, count), range(count)
    first, second = (late, early) if reverse else (early, late)
    everyone = range(group)
    hand = HAND_BACK if reverse else HAND
    arrived = [
        exchange(pieces[i], i, both if reverse or i in SHARED else first, BACK if reverse else FIRST)
        for i in everyone
    ]
    kept = [sds((group * rows, width), F32)] if reverse else [piece] * len(SHARED)
    total, *back = call(
        functools.partial(inner_body, group, reverse),
        [piece] * (group + 1) + kept,
        *arrived,
        scratch=[] if reverse else [state],
    )
    over = lax.ppermute(total, "ctx", [(j, j ^ group) for j in both])
    ahead = [exchange(back[i], i, first, hand) for i in everyone]
    if reverse:
        back = call(functools.partial(add_body, group, HAND_BACK), [piece] * group, back[group], over)
    else:
        own = [exchange(part, i, second, FIRST) for part, i in zip(again, ALONE)]
        mixed = [own[ALONE.index(i)] if i in ALONE else back[group + SHARED.index(i)] for i in everyone]
        back = call(
            functools.partial(late_body, group, reverse),
            [piece] * group, *mixed, over, scratch=[state],
        )
    behind = [exchange(back[i], i, second, hand) for i in everyone]
    return [*behind, *ahead] if reverse else [*ahead, *behind]


def from_all(part, axis):
    count = lax.axis_size(axis)
    even = count & (count - 1) == 0
    steps = [1, 3, 2] if count == 4 else range(1, count)
    return [part] + [
        lax.ppermute(part, axis, [(i, i ^ step if even else (i + step) % count) for i in range(count)])
        for step in steps
    ]


def on_device(queries, keys, values, gain, out_grad):
    tokens, width = queries.shape
    heads = width // HEAD
    count = lax.axis_size("ctx")
    factor = (HEAD * tokens * count) ** (-0.5)
    features = width * lax.axis_size("tp")
    gains = gain.reshape(heads, HEAD)
    sds = jax.ShapeDtypeStruct
    wide = sds((tokens, width), F32)
    half = sds((tokens, width), BF16)
    state = pltpu.VMEM((width, HEAD), F32)
    if count == 8 and lax.axis_size("tp") % 2 == 0:
        group = count // 2
        pieces = [sds((width // group, HEAD), F32)] * group
    else:
        group = count
        pieces = [sds((count, width // count, HEAD), F32)]

    def in_hbm(*arrays):
        return [pltpu.with_memory_space_constraint(array, pltpu.HBM) for array in arrays]

    def in_vmem(array):
        return pltpu.VMEM(array.shape, array.dtype)

    k_held, v_held, *states = call(
        functools.partial(states_body, heads, group),
        (in_vmem(keys), in_vmem(values), *pieces, *(pieces[i] for i in ALONE if len(pieces) > 1)),
        *in_hbm(keys, values),
        ins=[HBM, HBM],
        scratch=[state, pltpu.SemaphoreType.DMA((2 * LOADS,))],
    )
    prefix = carried_in(states, False, state)
    pairs = heads * tokens * tokens * HEAD
    scores, local, q_held, q_turned, weighted, gain_held = call(
        functools.partial(scores_body, heads, factor),
        (
            sds((heads, tokens, tokens), BF16), wide,
            in_vmem(queries), pltpu.VMEM((width, tokens), BF16), in_vmem(wide), in_vmem(gains),
        ),
        k_held, v_held, *in_hbm(queries, out_grad, gains),
        ins=[VMEM, VMEM, HBM, HBM, HBM],
        scratch=[in_vmem(out_grad), pltpu.SemaphoreType.DMA((3,))],
        flops=4 * pairs,
    )
    attended, stats, prefix = call(
        functools.partial(attend_body, heads, factor, group),
        (wide, sds((2, tokens), F32), sds((width, HEAD), F32)),
        q_held, weighted, local, *prefix,
    )
    every = from_all(stats, "tp")
    inv_rms, grad_attn, *updates = call(
        functools.partial(grad_body, heads, features, group, len(every)),
        (pltpu.VMEM((tokens, HEAD), F32), half, *pieces),
        attended, weighted, q_turned, *every,
        scratch=[state],
    )
    suffix = carried_in(updates, True, state)
    normed, grad_q, gk_part, gv_part = call(
        functools.partial(local_body, heads, factor),
        (half, half, wide, wide),
        grad_attn, q_held, k_held, v_held, prefix, scores, attended, inv_rms, gain_held,
        flops=9 * pairs,
    )
    held = pltpu.VMEM((tokens, width), BF16)
    grad_k, grad_v = call(
        functools.partial(final_body, heads, factor, group),
        (half, half),
        k_held, v_held, gk_part, gv_part, *suffix,
        dests=(HBM, HBM),
        scratch=[state, held, held, pltpu.SemaphoreType.DMA((2 * heads,))],
    )
    return normed, grad_q, grad_k, grad_v


def solution(mesh):
    placed = (P("ctx", "tp"), P("ctx", "tp"), P("ctx", "tp"), P("tp"), P("ctx", "tp"))
    return jax.shard_map(
        on_device,
        mesh=mesh,
        in_specs=placed,
        out_specs=(P("ctx", "tp"), P("ctx", "tp"), P("ctx", "tp"), P("ctx", "tp")),
        check_vma=False,
    )
```

```python
import functools

import jax
import jax.numpy as jnp
from jax import lax
from jax.experimental import pallas as pl
from jax.experimental.pallas import tpu as pltpu
from jax.sharding import PartitionSpec as P

HEAD = 128

epsilon = 1e-06
LOADS = 4
FIRST, BACK, HAND = 0, 1, 2
ALONE = (0, 2)
SHARED = (1, 3)
F32 = jnp.float32
BF16 = jnp.bfloat16

NN = (((1,), (0,)), ((), ()))
NT = (((1,), (1,)), ((), ()))
TN = (((0,), (0,)), ((), ()))


def dot(a, b, dims):
    return lax.dot_general(a, b, dims, preferred_element_type=F32)


VMEM = pl.BlockSpec(memory_space=pltpu.VMEM)
HBM = pl.BlockSpec(memory_space=pltpu.HBM)


def call(body, outs, *args, ins=None, dests=None, scratch=(), flops=1e7):
    moved = sum(a.size * a.dtype.itemsize for a in args)
    return pl.pallas_call(
        body,
        out_shape=outs,
        in_specs=ins or [VMEM] * len(args),
        out_specs=dests or jax.tree.map(lambda _: VMEM, outs),
        scratch_shapes=scratch,
        compiler_params=pltpu.CompilerParams(vmem_limit_bytes=16 * 1024 * 1024),
        cost_estimate=pl.CostEstimate(flops=int(flops), bytes_accessed=int(moved), transcendentals=0),
    )(*args)


def head(h):
    return slice(h * HEAD, (h + 1) * HEAD)


def causal_mask(tokens):
    row = lax.broadcasted_iota(jnp.int32, (tokens, tokens), 0)
    col = lax.broadcasted_iota(jnp.int32, (tokens, tokens), 1)
    return row >= col


def rows_of(scratch, parts, place):
    rows = scratch.shape[0] // parts
    return scratch.at[pl.ds(pl.multiple_of(place * rows, rows), rows), :]


def step_of(i, odd, order):
    return (
        (3, 2, 1, 0),
        (3, 2 - odd, 1 + odd, 0),
        (3 - odd, 1 + 2 * odd, 2 - odd, 0),
    )[order][i]


def give(scratch, group, outs, order=0):
    if len(outs) == 1:
        outs[0][...] = scratch[...].reshape(outs[0].shape)
        return
    place = lax.rem(lax.axis_index("ctx"), group)
    odd = lax.rem(lax.axis_index("tp"), 2)
    for i, out in enumerate(outs):
        out[...] = rows_of(scratch, group, lax.bitwise_xor(place, step_of(i, odd, order)))[...]


def take(ins, scratch, group, order=0):
    if len(ins) == 1:
        scratch[...] = ins[0][...].reshape(scratch.shape)
        return
    place = lax.rem(lax.axis_index("ctx"), group)
    sent_by_odd = 1 - lax.rem(lax.axis_index("tp"), 2)
    for i, piece in enumerate(ins):
        rows_of(scratch, group, lax.bitwise_xor(place, step_of(i, sent_by_odd, order)))[...] = piece[...]


def running_sums(scratch, parts, reverse):
    rows = scratch.shape[0] // parts
    running = jnp.zeros((rows, scratch.shape[1]), F32)
    for place in range(parts - 1, -1, -1) if reverse else range(parts):
        own = slice(place * rows, (place + 1) * rows)
        here = scratch[own, :]
        scratch[own, :] = running
        running = running + here
    return running


def loads(pairs, sems):
    copies = [pltpu.make_async_copy(a, b, sems.at[i]) for i, (a, b) in enumerate(pairs)]
    for copy in copies:
        copy.start()
    return copies


def states_body(heads, group, k_hbm, v_hbm, k, v, *refs):
    outs, (state, sems) = refs[:-2], refs[-2:]
    rows = k.shape[0] // LOADS
    blocks = [slice(i * rows, (i + 1) * rows) for i in range(LOADS)]
    for copy in loads([(a.at[r, :], b.at[r, :]) for r in blocks for a, b in ((k_hbm, k), (v_hbm, v))], sems):
        copy.wait()
    for h in range(heads):
        state[head(h), :] = dot(k[:, head(h)], v[:, head(h)], TN)
    give(state, group, outs[:group], FIRST)
    for again, i in zip(outs[group:], ALONE):
        again[...] = outs[i][...]


def scan_body(count, reverse, arrived, sums, scratch):
    take([arrived], scratch, count)
    running_sums(scratch, count, reverse)
    give(scratch, count, [sums])


def inner_body(group, reverse, *refs):
    arrived, total, outs, sums = refs[:group], refs[group], refs[group + 1 : 2 * group + 1], refs[-1]
    take(arrived, sums, group, BACK if reverse else FIRST)
    total[...] = running_sums(sums, group, reverse)
    give(sums, group, outs, HAND)
    if not reverse:
        for passed, i in zip(refs[2 * group + 1 : -1], SHARED):
            passed[...] = arrived[i][...]


def add_body(group, sums, over, *outs):
    place = lax.rem(lax.axis_index("ctx"), group)
    odd = lax.rem(lax.axis_index("tp"), 2)
    for i, out in enumerate(outs):
        out[...] = rows_of(sums, group, lax.bitwise_xor(place, step_of(i, odd, HAND)))[...] + over[...]


def late_body(group, reverse, *refs):
    arrived, over, outs, sums = refs[:group], refs[group], refs[group + 1 : -1], refs[-1]
    take(arrived, sums, group)
    running_sums(sums, group, reverse)
    add_body(group, sums, over, *outs)


def pick(pieces, scratch, group):
    many = len(pieces) // 2
    if many == 0:
        take(pieces, scratch, group)
        return
    early = lax.axis_index("ctx") < group
    place = lax.rem(lax.axis_index("ctx"), group)
    sent_by_odd = 1 - lax.rem(lax.axis_index("tp"), 2)
    for i in range(many):
        rows = rows_of(scratch, group, lax.bitwise_xor(place, step_of(i, sent_by_odd, HAND)))
        rows[...] = jnp.where(early, pieces[i][...], pieces[many + i][...])


def scores_body(heads, factor, k, v, q_hbm, og_hbm, gain_hbm, scores, attended, q, q_turned, weighted, gain, og, sems):
    copies = loads(((q_hbm, q), (og_hbm, og), (gain_hbm, gain)), sems)
    copies[0].wait()
    q_turned[...] = q[...].T
    causal = causal_mask(q.shape[0])
    for h in range(heads):
        raw = dot(q[:, head(h)], k[:, head(h)], NT) * factor
        sc = jnp.where(causal, raw, 0.0).astype(BF16)
        scores[h] = sc
        attended[:, head(h)] = dot(sc, v[:, head(h)], NN)
    for copy in copies[1:]:
        copy.wait()
    for h in range(heads):
        weighted[:, head(h)] = og[:, head(h)].astype(F32) * gain[h : h + 1, :]


def attend_body(heads, factor, group, q, weighted, local, *refs):
    pieces, (attended, stats, prefix) = refs[:-3], refs[-3:]
    pick(pieces, prefix, group)
    power = 0.0
    inner = 0.0
    for h in range(heads):
        att = factor * dot(q[:, head(h)], prefix[head(h), :].astype(BF16), NN) + local[:, head(h)]
        attended[:, head(h)] = att
        power = power + att * att
        inner = inner + weighted[:, head(h)] * att
    stats[0:1, :] = jnp.sum(power.T, axis=0, keepdims=True)
    stats[1:2, :] = jnp.sum(inner.T, axis=0, keepdims=True)


def grad_body(heads, features, group, ways, attended, weighted, q_turned, *refs):
    stats, (spread, grad), outs, updates = refs[:ways], refs[ways : ways + 2], refs[ways + 2 : -1], refs[-1]
    total = stats[0][...]
    for other in stats[1:]:
        total = total + other[...]
    inv_rms = lax.rsqrt(total[0:1, :] / features + epsilon)
    bend = inv_rms * inv_rms * (total[1:2, :] / features)
    tokens = q_turned.shape[1]
    inv_rms = jnp.broadcast_to(inv_rms, (HEAD, tokens)).T
    bend = jnp.broadcast_to(bend, (HEAD, tokens)).T
    spread[...] = inv_rms
    for h in range(heads):
        ga = (inv_rms * (weighted[:, head(h)] - attended[:, head(h)] * bend)).astype(BF16)
        grad[:, head(h)] = ga
        updates[head(h), :] = dot(q_turned[head(h), :], ga, NN)
    give(updates, group, outs, BACK)


def local_body(heads, factor, ga, q, k, v, prefix, scores, attended, inv_rms, gain, normed, gq, gk_part, gv_part):
    causal = causal_mask(q.shape[0])
    for h in range(heads):
        normed[:, head(h)] = (attended[:, head(h)] * inv_rms[...] * gain[h : h + 1, :]).astype(BF16)
        gah = ga[:, head(h)]
        raw = dot(gah, v[:, head(h)], NT) * factor
        gs = jnp.where(causal, raw, 0.0).astype(BF16)
        out = factor * dot(gah, prefix[head(h), :].astype(BF16), NT)
        gq[:, head(h)] = (out + dot(gs, k[:, head(h)], NN)).astype(BF16)
        gk_part[:, head(h)] = dot(gs, q[:, head(h)], TN)
        gv_part[:, head(h)] = dot(scores[h], gah, TN)


def final_body(heads, factor, group, k, v, gk_part, gv_part, *refs):
    pieces, outs, (suffix, gk, gv, sems) = refs[:-6], refs[-6:-4], refs[-4:]
    pick(pieces, suffix, group)
    copies = []

    def send(h, held, out):
        copy = pltpu.make_async_copy(held.at[:, head(h)], out.at[:, head(h)], sems.at[len(copies)])
        copy.start()
        copies.append(copy)

    for h in range(heads):
        suf = suffix[head(h), :].astype(BF16)
        gk[:, head(h)] = (factor * dot(v[:, head(h)], suf, NT) + gk_part[:, head(h)]).astype(BF16)
        send(h, gk, outs[0])
        gv[:, head(h)] = (factor * dot(k[:, head(h)], suf, NN) + gv_part[:, head(h)]).astype(BF16)
        send(h, gv, outs[1])
    for copy in copies:
        copy.wait()


def exchange(piece, i, active, order):
    ways = lax.axis_size("tp")
    pairs = [
        (j * ways + t, (j ^ step_of(i, t % 2, order) if j in active else j) * ways + (t ^ 1))
        for j in range(lax.axis_size("ctx"))
        for t in range(ways)
    ]
    return lax.ppermute(piece, ("ctx", "tp"), pairs)


def carried_in(pieces, reverse, state):
    again = () if reverse or len(pieces) == 1 else pieces[-len(ALONE) :]
    group = len(pieces) - len(again)
    pieces = pieces[:group]
    count = lax.axis_size("ctx")
    sds = jax.ShapeDtypeStruct
    if group == 1:
        arrived = lax.all_to_all(pieces[0], "ctx", 0, 0, tiled=True)
        sums = call(
            functools.partial(scan_body, count, reverse),
            sds(arrived.shape, F32), arrived, scratch=[state],
        )
        return [lax.all_to_all(sums, "ctx", 0, 0, tiled=True)]
    rows, width = pieces[0].shape
    piece = sds((rows, width), F32)
    early, late, both = range(group), range(group, count), range(count)
    first, second = (late, early) if reverse else (early, late)
    everyone = range(group)
    arrived = [
        exchange(pieces[i], i, both if reverse or i in SHARED else first, BACK if reverse else FIRST)
        for i in everyone
    ]
    kept = [sds((group * rows, width), F32)] if reverse else [piece] * len(SHARED)
    total, *back = call(
        functools.partial(inner_body, group, reverse),
        [piece] * (group + 1) + kept,
        *arrived,
        scratch=[] if reverse else [state],
    )
    over = lax.ppermute(total, "ctx", [(j, j ^ group) for j in both])
    ahead = [exchange(back[i], i, first, HAND) for i in everyone]
    if reverse:
        back = call(functools.partial(add_body, group), [piece] * group, back[group], over)
    else:
        own = [exchange(part, i, second, FIRST) for part, i in zip(again, ALONE)]
        mixed = [own[ALONE.index(i)] if i in ALONE else back[group + SHARED.index(i)] for i in everyone]
        back = call(
            functools.partial(late_body, group, reverse),
            [piece] * group, *mixed, over, scratch=[state],
        )
    behind = [exchange(back[i], i, second, HAND) for i in everyone]
    return [*behind, *ahead] if reverse else [*ahead, *behind]


def from_all(part, axis):
    count = lax.axis_size(axis)
    even = count & (count - 1) == 0
    steps = [1, 3, 2] if count == 4 else range(1, count)
    return [part] + [
        lax.ppermute(part, axis, [(i, i ^ step if even else (i + step) % count) for i in range(count)])
        for step in steps
    ]


def on_device(queries, keys, values, gain, out_grad):
    tokens, width = queries.shape
    heads = width // HEAD
    count = lax.axis_size("ctx")
    factor = (HEAD * tokens * count) ** (-0.5)
    features = width * lax.axis_size("tp")
    gains = gain.reshape(heads, HEAD)
    sds = jax.ShapeDtypeStruct
    wide = sds((tokens, width), F32)
    half = sds((tokens, width), BF16)
    state = pltpu.VMEM((width, HEAD), F32)
    if count == 8 and lax.axis_size("tp") % 2 == 0:
        group = count // 2
        pieces = [sds((width // group, HEAD), F32)] * group
    else:
        group = count
        pieces = [sds((count, width // count, HEAD), F32)]

    def in_hbm(*arrays):
        return [pltpu.with_memory_space_constraint(array, pltpu.HBM) for array in arrays]

    def in_vmem(array):
        return pltpu.VMEM(array.shape, array.dtype)

    k_held, v_held, *states = call(
        functools.partial(states_body, heads, group),
        (in_vmem(keys), in_vmem(values), *pieces, *(pieces[i] for i in ALONE if len(pieces) > 1)),
        *in_hbm(keys, values),
        ins=[HBM, HBM],
        scratch=[state, pltpu.SemaphoreType.DMA((2 * LOADS,))],
    )
    prefix = carried_in(states, False, state)
    pairs = heads * tokens * tokens * HEAD
    scores, local, q_held, q_turned, weighted, gain_held = call(
        functools.partial(scores_body, heads, factor),
        (
            sds((heads, tokens, tokens), BF16), wide,
            in_vmem(queries), pltpu.VMEM((width, tokens), BF16), in_vmem(wide), in_vmem(gains),
        ),
        k_held, v_held, *in_hbm(queries, out_grad, gains),
        ins=[VMEM, VMEM, HBM, HBM, HBM],
        scratch=[in_vmem(out_grad), pltpu.SemaphoreType.DMA((3,))],
        flops=4 * pairs,
    )
    attended, stats, prefix = call(
        functools.partial(attend_body, heads, factor, group),
        (wide, sds((2, tokens), F32), sds((width, HEAD), F32)),
        q_held, weighted, local, *prefix,
    )
    every = from_all(stats, "tp")
    inv_rms, grad_attn, *updates = call(
        functools.partial(grad_body, heads, features, group, len(every)),
        (pltpu.VMEM((tokens, HEAD), F32), half, *pieces),
        attended, weighted, q_turned, *every,
        scratch=[state],
    )
    suffix = carried_in(updates, True, state)
    normed, grad_q, gk_part, gv_part = call(
        functools.partial(local_body, heads, factor),
        (half, half, wide, wide),
        grad_attn, q_held, k_held, v_held, prefix, scores, attended, inv_rms, gain_held,
        flops=9 * pairs,
    )
    held = pltpu.VMEM((tokens, width), BF16)
    grad_k, grad_v = call(
        functools.partial(final_body, heads, factor, group),
        (half, half),
        k_held, v_held, gk_part, gv_part, *suffix,
        dests=(HBM, HBM),
        scratch=[state, held, held, pltpu.SemaphoreType.DMA((2 * heads,))],
    )
    return normed, grad_q, grad_k, grad_v


def solution(mesh):
    placed = (P("ctx", "tp"), P("ctx", "tp"), P("ctx", "tp"), P("tp"), P("ctx", "tp"))
    return jax.shard_map(
        on_device,
        mesh=mesh,
        in_specs=placed,
        out_specs=(P("ctx", "tp"), P("ctx", "tp"), P("ctx", "tp"), P("ctx", "tp")),
        check_vma=False,
    )
```

```python
import functools

import jax
import jax.numpy as jnp
from jax import lax
from jax.experimental import pallas as pl
from jax.experimental.pallas import tpu as pltpu
from jax.sharding import PartitionSpec as P

HEAD = 128

epsilon = 1e-06
LOADS = 4
FIRST, BACK, HAND = 0, 1, 2
ALONE = (0, 2)
SHARED = (1, 3)
F32 = jnp.float32
BF16 = jnp.bfloat16

NN = (((1,), (0,)), ((), ()))
NT = (((1,), (1,)), ((), ()))
TN = (((0,), (0,)), ((), ()))


def dot(a, b, dims):
    return lax.dot_general(a, b, dims, preferred_element_type=F32)


VMEM = pl.BlockSpec(memory_space=pltpu.VMEM)
HBM = pl.BlockSpec(memory_space=pltpu.HBM)


def call(body, outs, *args, ins=None, dests=None, scratch=(), flops=1e7):
    moved = sum(a.size * a.dtype.itemsize for a in args)
    return pl.pallas_call(
        body,
        out_shape=outs,
        in_specs=ins or [VMEM] * len(args),
        out_specs=dests or jax.tree.map(lambda _: VMEM, outs),
        scratch_shapes=scratch,
        compiler_params=pltpu.CompilerParams(vmem_limit_bytes=16 * 1024 * 1024),
        cost_estimate=pl.CostEstimate(flops=int(flops), bytes_accessed=int(moved), transcendentals=0),
    )(*args)


def head(h):
    return slice(h * HEAD, (h + 1) * HEAD)


def causal_mask(tokens):
    row = lax.broadcasted_iota(jnp.int32, (tokens, tokens), 0)
    col = lax.broadcasted_iota(jnp.int32, (tokens, tokens), 1)
    return row >= col


def rows_of(scratch, parts, place):
    rows = scratch.shape[0] // parts
    return scratch.at[pl.ds(pl.multiple_of(place * rows, rows), rows), :]


def step_of(i, odd, order):
    return (
        (3, 2, 1, 0),
        (3, 2 - odd, 1 + odd, 0),
        (3 - odd, 2 + odd, 1, 0),
    )[order][i]


def give(scratch, group, outs, order=0):
    if len(outs) == 1:
        outs[0][...] = scratch[...].reshape(outs[0].shape)
        return
    place = lax.rem(lax.axis_index("ctx"), group)
    odd = lax.rem(lax.axis_index("tp"), 2)
    for i, out in enumerate(outs):
        out[...] = rows_of(scratch, group, lax.bitwise_xor(place, step_of(i, odd, order)))[...]


def take(ins, scratch, group, order=0):
    if len(ins) == 1:
        scratch[...] = ins[0][...].reshape(scratch.shape)
        return
    place = lax.rem(lax.axis_index("ctx"), group)
    sent_by_odd = 1 - lax.rem(lax.axis_index("tp"), 2)
    for i, piece in enumerate(ins):
        rows_of(scratch, group, lax.bitwise_xor(place, step_of(i, sent_by_odd, order)))[...] = piece[...]


def running_sums(scratch, parts, reverse):
    rows = scratch.shape[0] // parts
    running = jnp.zeros((rows, scratch.shape[1]), F32)
    for place in range(parts - 1, -1, -1) if reverse else range(parts):
        own = slice(place * rows, (place + 1) * rows)
        here = scratch[own, :]
        scratch[own, :] = running
        running = running + here
    return running


def loads(pairs, sems):
    copies = [pltpu.make_async_copy(a, b, sems.at[i]) for i, (a, b) in enumerate(pairs)]
    for copy in copies:
        copy.start()
    return copies


def states_body(heads, group, k_hbm, v_hbm, k, v, *refs):
    outs, (state, sems) = refs[:-2], refs[-2:]
    rows = k.shape[0] // LOADS
    blocks = [slice(i * rows, (i + 1) * rows) for i in range(LOADS)]
    for copy in loads([(a.at[r, :], b.at[r, :]) for r in blocks for a, b in ((k_hbm, k), (v_hbm, v))], sems):
        copy.wait()
    for h in range(heads):
        state[head(h), :] = dot(k[:, head(h)], v[:, head(h)], TN)
    give(state, group, outs[:group], FIRST)
    for again, i in zip(outs[group:], ALONE):
        again[...] = outs[i][...]


def scan_body(count, reverse, arrived, sums, scratch):
    take([arrived], scratch, count)
    running_sums(scratch, count, reverse)
    give(scratch, count, [sums])


def inner_body(group, reverse, *refs):
    arrived, total, outs, sums = refs[:group], refs[group], refs[group + 1 : 2 * group + 1], refs[-1]
    take(arrived, sums, group, BACK if reverse else FIRST)
    total[...] = running_sums(sums, group, reverse)
    give(sums, group, outs, HAND)
    if not reverse:
        for passed, i in zip(refs[2 * group + 1 : -1], SHARED):
            passed[...] = arrived[i][...]


def add_body(group, sums, over, *outs):
    place = lax.rem(lax.axis_index("ctx"), group)
    odd = lax.rem(lax.axis_index("tp"), 2)
    for i, out in enumerate(outs):
        out[...] = rows_of(sums, group, lax.bitwise_xor(place, step_of(i, odd, HAND)))[...] + over[...]


def late_body(group, reverse, *refs):
    arrived, over, outs, sums = refs[:group], refs[group], refs[group + 1 : -1], refs[-1]
    take(arrived, sums, group)
    running_sums(sums, group, reverse)
    add_body(group, sums, over, *outs)


def pick(pieces, scratch, group):
    many = len(pieces) // 2
    if many == 0:
        take(pieces, scratch, group)
        return
    early = lax.axis_index("ctx") < group
    place = lax.rem(lax.axis_index("ctx"), group)
    sent_by_odd = 1 - lax.rem(lax.axis_index("tp"), 2)
    for i in range(many):
        rows = rows_of(scratch, group, lax.bitwise_xor(place, step_of(i, sent_by_odd, HAND)))
        rows[...] = jnp.where(early, pieces[i][...], pieces[many + i][...])


def scores_body(heads, factor, k, v, q_hbm, og_hbm, gain_hbm, scores, attended, q, q_turned, weighted, gain, og, sems):
    copies = loads(((q_hbm, q), (og_hbm, og), (gain_hbm, gain)), sems)
    copies[0].wait()
    q_turned[...] = q[...].T
    causal = causal_mask(q.shape[0])
    for h in range(heads):
        raw = dot(q[:, head(h)], k[:, head(h)], NT) * factor
        sc = jnp.where(causal, raw, 0.0).astype(BF16)
        scores[h] = sc
        attended[:, head(h)] = dot(sc, v[:, head(h)], NN)
    for copy in copies[1:]:
        copy.wait()
    for h in range(heads):
        weighted[:, head(h)] = og[:, head(h)].astype(F32) * gain[h : h + 1, :]


def attend_body(heads, factor, group, q, weighted, local, *refs):
    pieces, (attended, stats, prefix) = refs[:-3], refs[-3:]
    pick(pieces, prefix, group)
    power = 0.0
    inner = 0.0
    for h in range(heads):
        att = factor * dot(q[:, head(h)], prefix[head(h), :].astype(BF16), NN) + local[:, head(h)]
        attended[:, head(h)] = att
        power = power + att * att
        inner = inner + weighted[:, head(h)] * att
    stats[0:1, :] = jnp.sum(power.T, axis=0, keepdims=True)
    stats[1:2, :] = jnp.sum(inner.T, axis=0, keepdims=True)


def grad_body(heads, features, group, ways, attended, weighted, q_turned, *refs):
    stats, (spread, grad), outs, updates = refs[:ways], refs[ways : ways + 2], refs[ways + 2 : -1], refs[-1]
    total = stats[0][...]
    for other in stats[1:]:
        total = total + other[...]
    inv_rms = lax.rsqrt(total[0:1, :] / features + epsilon)
    bend = inv_rms * inv_rms * (total[1:2, :] / features)
    tokens = q_turned.shape[1]
    inv_rms = jnp.broadcast_to(inv_rms, (HEAD, tokens)).T
    bend = jnp.broadcast_to(bend, (HEAD, tokens)).T
    spread[...] = inv_rms
    for h in range(heads):
        ga = (inv_rms * (weighted[:, head(h)] - attended[:, head(h)] * bend)).astype(BF16)
        grad[:, head(h)] = ga
        updates[head(h), :] = dot(q_turned[head(h), :], ga, NN)
    give(updates, group, outs, BACK)


def local_body(heads, factor, ga, q, k, v, prefix, scores, attended, inv_rms, gain, normed, gq, gk_part, gv_part):
    causal = causal_mask(q.shape[0])
    for h in range(heads):
        normed[:, head(h)] = (attended[:, head(h)] * inv_rms[...] * gain[h : h + 1, :]).astype(BF16)
        gah = ga[:, head(h)]
        raw = dot(gah, v[:, head(h)], NT) * factor
        gs = jnp.where(causal, raw, 0.0).astype(BF16)
        out = factor * dot(gah, prefix[head(h), :].astype(BF16), NT)
        gq[:, head(h)] = (out + dot(gs, k[:, head(h)], NN)).astype(BF16)
        gk_part[:, head(h)] = dot(gs, q[:, head(h)], TN)
        gv_part[:, head(h)] = dot(scores[h], gah, TN)


def final_body(heads, factor, group, k, v, gk_part, gv_part, *refs):
    pieces, outs, (suffix, gk, gv, sems) = refs[:-6], refs[-6:-4], refs[-4:]
    pick(pieces, suffix, group)
    copies = []

    def send(h, held, out):
        copy = pltpu.make_async_copy(held.at[:, head(h)], out.at[:, head(h)], sems.at[len(copies)])
        copy.start()
        copies.append(copy)

    for h in range(heads):
        suf = suffix[head(h), :].astype(BF16)
        gk[:, head(h)] = (factor * dot(v[:, head(h)], suf, NT) + gk_part[:, head(h)]).astype(BF16)
        send(h, gk, outs[0])
        gv[:, head(h)] = (factor * dot(k[:, head(h)], suf, NN) + gv_part[:, head(h)]).astype(BF16)
        send(h, gv, outs[1])
    for copy in copies:
        copy.wait()


def exchange(piece, i, active, order):
    ways = lax.axis_size("tp")
    pairs = [
        (j * ways + t, (j ^ step_of(i, t % 2, order) if j in active else j) * ways + (t ^ 1))
        for j in range(lax.axis_size("ctx"))
        for t in range(ways)
    ]
    return lax.ppermute(piece, ("ctx", "tp"), pairs)


def carried_in(pieces, reverse, state):
    again = () if reverse or len(pieces) == 1 else pieces[-len(ALONE) :]
    group = len(pieces) - len(again)
    pieces = pieces[:group]
    count = lax.axis_size("ctx")
    sds = jax.ShapeDtypeStruct
    if group == 1:
        arrived = lax.all_to_all(pieces[0], "ctx", 0, 0, tiled=True)
        sums = call(
            functools.partial(scan_body, count, reverse),
            sds(arrived.shape, F32), arrived, scratch=[state],
        )
        return [lax.all_to_all(sums, "ctx", 0, 0, tiled=True)]
    rows, width = pieces[0].shape
    piece = sds((rows, width), F32)
    early, late, both = range(group), range(group, count), range(count)
    first, second = (late, early) if reverse else (early, late)
    everyone = range(group)
    arrived = [
        exchange(pieces[i], i, both if reverse or i in SHARED else first, BACK if reverse else FIRST)
        for i in everyone
    ]
    kept = [sds((group * rows, width), F32)] if reverse else [piece] * len(SHARED)
    total, *back = call(
        functools.partial(inner_body, group, reverse),
        [piece] * (group + 1) + kept,
        *arrived,
        scratch=[] if reverse else [state],
    )
    over = lax.ppermute(total, "ctx", [(j, j ^ group) for j in both])
    ahead = [exchange(back[i], i, first, HAND) for i in everyone]
    if reverse:
        back = call(functools.partial(add_body, group), [piece] * group, back[group], over)
    else:
        own = [exchange(part, i, second, FIRST) for part, i in zip(again, ALONE)]
        mixed = [own[ALONE.index(i)] if i in ALONE else back[group + SHARED.index(i)] for i in everyone]
        back = call(
            functools.partial(late_body, group, reverse),
            [piece] * group, *mixed, over, scratch=[state],
        )
    behind = [exchange(back[i], i, second, HAND) for i in everyone]
    return [*behind, *ahead] if reverse else [*ahead, *behind]


def from_all(part, axis):
    count = lax.axis_size(axis)
    even = count & (count - 1) == 0
    steps = [1, 3, 2] if count == 4 else range(1, count)
    return [part] + [
        lax.ppermute(part, axis, [(i, i ^ step if even else (i + step) % count) for i in range(count)])
        for step in steps
    ]


def on_device(queries, keys, values, gain, out_grad):
    tokens, width = queries.shape
    heads = width // HEAD
    count = lax.axis_size("ctx")
    factor = (HEAD * tokens * count) ** (-0.5)
    features = width * lax.axis_size("tp")
    gains = gain.reshape(heads, HEAD)
    sds = jax.ShapeDtypeStruct
    wide = sds((tokens, width), F32)
    half = sds((tokens, width), BF16)
    state = pltpu.VMEM((width, HEAD), F32)
    if count == 8 and lax.axis_size("tp") % 2 == 0:
        group = count // 2
        pieces = [sds((width // group, HEAD), F32)] * group
    else:
        group = count
        pieces = [sds((count, width // count, HEAD), F32)]

    def in_hbm(*arrays):
        return [pltpu.with_memory_space_constraint(array, pltpu.HBM) for array in arrays]

    def in_vmem(array):
        return pltpu.VMEM(array.shape, array.dtype)

    k_held, v_held, *states = call(
        functools.partial(states_body, heads, group),
        (in_vmem(keys), in_vmem(values), *pieces, *(pieces[i] for i in ALONE if len(pieces) > 1)),
        *in_hbm(keys, values),
        ins=[HBM, HBM],
        scratch=[state, pltpu.SemaphoreType.DMA((2 * LOADS,))],
    )
    prefix = carried_in(states, False, state)
    pairs = heads * tokens * tokens * HEAD
    scores, local, q_held, q_turned, weighted, gain_held = call(
        functools.partial(scores_body, heads, factor),
        (
            sds((heads, tokens, tokens), BF16), wide,
            in_vmem(queries), pltpu.VMEM((width, tokens), BF16), in_vmem(wide), in_vmem(gains),
        ),
        k_held, v_held, *in_hbm(queries, out_grad, gains),
        ins=[VMEM, VMEM, HBM, HBM, HBM],
        scratch=[in_vmem(out_grad), pltpu.SemaphoreType.DMA((3,))],
        flops=4 * pairs,
    )
    attended, stats, prefix = call(
        functools.partial(attend_body, heads, factor, group),
        (wide, sds((2, tokens), F32), sds((width, HEAD), F32)),
        q_held, weighted, local, *prefix,
    )
    every = from_all(stats, "tp")
    inv_rms, grad_attn, *updates = call(
        functools.partial(grad_body, heads, features, group, len(every)),
        (pltpu.VMEM((tokens, HEAD), F32), half, *pieces),
        attended, weighted, q_turned, *every,
        scratch=[state],
    )
    suffix = carried_in(updates, True, state)
    normed, grad_q, gk_part, gv_part = call(
        functools.partial(local_body, heads, factor),
        (half, half, wide, wide),
        grad_attn, q_held, k_held, v_held, prefix, scores, attended, inv_rms, gain_held,
        flops=9 * pairs,
    )
    held = pltpu.VMEM((tokens, width), BF16)
    grad_k, grad_v = call(
        functools.partial(final_body, heads, factor, group),
        (half, half),
        k_held, v_held, gk_part, gv_part, *suffix,
        dests=(HBM, HBM),
        scratch=[state, held, held, pltpu.SemaphoreType.DMA((2 * heads,))],
    )
    return normed, grad_q, grad_k, grad_v


def solution(mesh):
    placed = (P("ctx", "tp"), P("ctx", "tp"), P("ctx", "tp"), P("tp"), P("ctx", "tp"))
    return jax.shard_map(
        on_device,
        mesh=mesh,
        in_specs=placed,
        out_specs=(P("ctx", "tp"), P("ctx", "tp"), P("ctx", "tp"), P("ctx", "tp")),
        check_vma=False,
    )
```

```python
import functools

import jax
import jax.numpy as jnp
from jax import lax
from jax.experimental import pallas as pl
from jax.experimental.pallas import tpu as pltpu
from jax.sharding import PartitionSpec as P

HEAD = 128

epsilon = 1e-06
LOADS = 4
FIRST, BACK, HAND = 0, 1, 2
ALONE = (0, 2)
SHARED = (1, 3)
F32 = jnp.float32
BF16 = jnp.bfloat16

NN = (((1,), (0,)), ((), ()))
NT = (((1,), (1,)), ((), ()))
TN = (((0,), (0,)), ((), ()))


def dot(a, b, dims):
    return lax.dot_general(a, b, dims, preferred_element_type=F32)


VMEM = pl.BlockSpec(memory_space=pltpu.VMEM)
HBM = pl.BlockSpec(memory_space=pltpu.HBM)


def call(body, outs, *args, ins=None, dests=None, scratch=(), flops=1e7):
    moved = sum(a.size * a.dtype.itemsize for a in args)
    return pl.pallas_call(
        body,
        out_shape=outs,
        in_specs=ins or [VMEM] * len(args),
        out_specs=dests or jax.tree.map(lambda _: VMEM, outs),
        scratch_shapes=scratch,
        compiler_params=pltpu.CompilerParams(vmem_limit_bytes=16 * 1024 * 1024),
        cost_estimate=pl.CostEstimate(flops=int(flops), bytes_accessed=int(moved), transcendentals=0),
    )(*args)


def head(h):
    return slice(h * HEAD, (h + 1) * HEAD)


def causal_mask(tokens):
    row = lax.broadcasted_iota(jnp.int32, (tokens, tokens), 0)
    col = lax.broadcasted_iota(jnp.int32, (tokens, tokens), 1)
    return row >= col


def rows_of(scratch, parts, place):
    rows = scratch.shape[0] // parts
    return scratch.at[pl.ds(pl.multiple_of(place * rows, rows), rows), :]


def step_of(i, odd, order):
    return (
        (3, 2, 1, 0),
        (3, 2, 1, 0),
        (3 - 2 * odd, 2 + odd, 1 + odd, 0),
    )[order][i]


def give(scratch, group, outs, order=0):
    if len(outs) == 1:
        outs[0][...] = scratch[...].reshape(outs[0].shape)
        return
    place = lax.rem(lax.axis_index("ctx"), group)
    odd = lax.rem(lax.axis_index("tp"), 2)
    for i, out in enumerate(outs):
        out[...] = rows_of(scratch, group, lax.bitwise_xor(place, step_of(i, odd, order)))[...]


def take(ins, scratch, group, order=0):
    if len(ins) == 1:
        scratch[...] = ins[0][...].reshape(scratch.shape)
        return
    place = lax.rem(lax.axis_index("ctx"), group)
    sent_by_odd = 1 - lax.rem(lax.axis_index("tp"), 2)
    for i, piece in enumerate(ins):
        rows_of(scratch, group, lax.bitwise_xor(place, step_of(i, sent_by_odd, order)))[...] = piece[...]


def running_sums(scratch, parts, reverse):
    rows = scratch.shape[0] // parts
    running = jnp.zeros((rows, scratch.shape[1]), F32)
    for place in range(parts - 1, -1, -1) if reverse else range(parts):
        own = slice(place * rows, (place + 1) * rows)
        here = scratch[own, :]
        scratch[own, :] = running
        running = running + here
    return running


def loads(pairs, sems):
    copies = [pltpu.make_async_copy(a, b, sems.at[i]) for i, (a, b) in enumerate(pairs)]
    for copy in copies:
        copy.start()
    return copies


def states_body(heads, group, k_hbm, v_hbm, k, v, *refs):
    outs, (state, sems) = refs[:-2], refs[-2:]
    rows = k.shape[0] // LOADS
    blocks = [slice(i * rows, (i + 1) * rows) for i in range(LOADS)]
    for copy in loads([(a.at[r, :], b.at[r, :]) for r in blocks for a, b in ((k_hbm, k), (v_hbm, v))], sems):
        copy.wait()
    for h in range(heads):
        state[head(h), :] = dot(k[:, head(h)], v[:, head(h)], TN)
    give(state, group, outs[:group], FIRST)
    for again, i in zip(outs[group:], ALONE):
        again[...] = outs[i][...]


def scan_body(count, reverse, arrived, sums, scratch):
    take([arrived], scratch, count)
    running_sums(scratch, count, reverse)
    give(scratch, count, [sums])


def inner_body(group, reverse, *refs):
    arrived, total, outs, sums = refs[:group], refs[group], refs[group + 1 : 2 * group + 1], refs[-1]
    take(arrived, sums, group, BACK if reverse else FIRST)
    total[...] = running_sums(sums, group, reverse)
    give(sums, group, outs, HAND)
    if not reverse:
        for passed, i in zip(refs[2 * group + 1 : -1], SHARED):
            passed[...] = arrived[i][...]


def add_body(group, sums, over, *outs):
    place = lax.rem(lax.axis_index("ctx"), group)
    odd = lax.rem(lax.axis_index("tp"), 2)
    for i, out in enumerate(outs):
        out[...] = rows_of(sums, group, lax.bitwise_xor(place, step_of(i, odd, HAND)))[...] + over[...]


def late_body(group, reverse, *refs):
    arrived, over, outs, sums = refs[:group], refs[group], refs[group + 1 : -1], refs[-1]
    take(arrived, sums, group)
    running_sums(sums, group, reverse)
    add_body(group, sums, over, *outs)


def pick(pieces, scratch, group):
    many = len(pieces) // 2
    if many == 0:
        take(pieces, scratch, group)
        return
    early = lax.axis_index("ctx") < group
    place = lax.rem(lax.axis_index("ctx"), group)
    sent_by_odd = 1 - lax.rem(lax.axis_index("tp"), 2)
    for i in range(many):
        rows = rows_of(scratch, group, lax.bitwise_xor(place, step_of(i, sent_by_odd, HAND)))
        rows[...] = jnp.where(early, pieces[i][...], pieces[many + i][...])


def scores_body(heads, factor, k, v, q_hbm, og_hbm, gain_hbm, scores, attended, q, q_turned, weighted, gain, og, sems):
    copies = loads(((q_hbm, q), (og_hbm, og), (gain_hbm, gain)), sems)
    copies[0].wait()
    q_turned[...] = q[...].T
    causal = causal_mask(q.shape[0])
    for h in range(heads):
        raw = dot(q[:, head(h)], k[:, head(h)], NT) * factor
        sc = jnp.where(causal, raw, 0.0).astype(BF16)
        scores[h] = sc
        attended[:, head(h)] = dot(sc, v[:, head(h)], NN)
    for copy in copies[1:]:
        copy.wait()
    for h in range(heads):
        weighted[:, head(h)] = og[:, head(h)].astype(F32) * gain[h : h + 1, :]


def attend_body(heads, factor, group, q, weighted, local, *refs):
    pieces, (attended, stats, prefix) = refs[:-3], refs[-3:]
    pick(pieces, prefix, group)
    power = 0.0
    inner = 0.0
    for h in range(heads):
        att = factor * dot(q[:, head(h)], prefix[head(h), :].astype(BF16), NN) + local[:, head(h)]
        attended[:, head(h)] = att
        power = power + att * att
        inner = inner + weighted[:, head(h)] * att
    stats[0:1, :] = jnp.sum(power.T, axis=0, keepdims=True)
    stats[1:2, :] = jnp.sum(inner.T, axis=0, keepdims=True)


def grad_body(heads, features, group, ways, attended, weighted, q_turned, *refs):
    stats, (spread, grad), outs, updates = refs[:ways], refs[ways : ways + 2], refs[ways + 2 : -1], refs[-1]
    total = stats[0][...]
    for other in stats[1:]:
        total = total + other[...]
    inv_rms = lax.rsqrt(total[0:1, :] / features + epsilon)
    bend = inv_rms * inv_rms * (total[1:2, :] / features)
    tokens = q_turned.shape[1]
    inv_rms = jnp.broadcast_to(inv_rms, (HEAD, tokens)).T
    bend = jnp.broadcast_to(bend, (HEAD, tokens)).T
    spread[...] = inv_rms
    for h in range(heads):
        ga = (inv_rms * (weighted[:, head(h)] - attended[:, head(h)] * bend)).astype(BF16)
        grad[:, head(h)] = ga
        updates[head(h), :] = dot(q_turned[head(h), :], ga, NN)
    give(updates, group, outs, BACK)


def local_body(heads, factor, ga, q, k, v, prefix, scores, attended, inv_rms, gain, normed, gq, gk_part, gv_part):
    causal = causal_mask(q.shape[0])
    for h in range(heads):
        normed[:, head(h)] = (attended[:, head(h)] * inv_rms[...] * gain[h : h + 1, :]).astype(BF16)
        gah = ga[:, head(h)]
        raw = dot(gah, v[:, head(h)], NT) * factor
        gs = jnp.where(causal, raw, 0.0).astype(BF16)
        out = factor * dot(gah, prefix[head(h), :].astype(BF16), NT)
        gq[:, head(h)] = (out + dot(gs, k[:, head(h)], NN)).astype(BF16)
        gk_part[:, head(h)] = dot(gs, q[:, head(h)], TN)
        gv_part[:, head(h)] = dot(scores[h], gah, TN)


def final_body(heads, factor, group, k, v, gk_part, gv_part, *refs):
    pieces, outs, (suffix, gk, gv, sems) = refs[:-6], refs[-6:-4], refs[-4:]
    pick(pieces, suffix, group)
    copies = []

    def send(h, held, out):
        copy = pltpu.make_async_copy(held.at[:, head(h)], out.at[:, head(h)], sems.at[len(copies)])
        copy.start()
        copies.append(copy)

    for h in range(heads):
        suf = suffix[head(h), :].astype(BF16)
        gk[:, head(h)] = (factor * dot(v[:, head(h)], suf, NT) + gk_part[:, head(h)]).astype(BF16)
        send(h, gk, outs[0])
        gv[:, head(h)] = (factor * dot(k[:, head(h)], suf, NN) + gv_part[:, head(h)]).astype(BF16)
        send(h, gv, outs[1])
    for copy in copies:
        copy.wait()


def exchange(piece, i, active, order):
    ways = lax.axis_size("tp")
    pairs = [
        (j * ways + t, (j ^ step_of(i, t % 2, order) if j in active else j) * ways + (t ^ 1))
        for j in range(lax.axis_size("ctx"))
        for t in range(ways)
    ]
    return lax.ppermute(piece, ("ctx", "tp"), pairs)


def carried_in(pieces, reverse, state):
    again = () if reverse or len(pieces) == 1 else pieces[-len(ALONE) :]
    group = len(pieces) - len(again)
    pieces = pieces[:group]
    count = lax.axis_size("ctx")
    sds = jax.ShapeDtypeStruct
    if group == 1:
        arrived = lax.all_to_all(pieces[0], "ctx", 0, 0, tiled=True)
        sums = call(
            functools.partial(scan_body, count, reverse),
            sds(arrived.shape, F32), arrived, scratch=[state],
        )
        return [lax.all_to_all(sums, "ctx", 0, 0, tiled=True)]
    rows, width = pieces[0].shape
    piece = sds((rows, width), F32)
    early, late, both = range(group), range(group, count), range(count)
    first, second = (late, early) if reverse else (early, late)
    everyone = range(group)
    arrived = [
        exchange(pieces[i], i, both if reverse or i in SHARED else first, BACK if reverse else FIRST)
        for i in everyone
    ]
    kept = [sds((group * rows, width), F32)] if reverse else [piece] * len(SHARED)
    total, *back = call(
        functools.partial(inner_body, group, reverse),
        [piece] * (group + 1) + kept,
        *arrived,
        scratch=[] if reverse else [state],
    )
    over = lax.ppermute(total, "ctx", [(j, j ^ group) for j in both])
    ahead = [exchange(back[i], i, first, HAND) for i in everyone]
    if reverse:
        back = call(functools.partial(add_body, group), [piece] * group, back[group], over)
    else:
        own = [exchange(part, i, second, FIRST) for part, i in zip(again, ALONE)]
        mixed = [own[ALONE.index(i)] if i in ALONE else back[group + SHARED.index(i)] for i in everyone]
        back = call(
            functools.partial(late_body, group, reverse),
            [piece] * group, *mixed, over, scratch=[state],
        )
    behind = [exchange(back[i], i, second, HAND) for i in everyone]
    return [*behind, *ahead] if reverse else [*ahead, *behind]


def from_all(part, axis):
    count = lax.axis_size(axis)
    even = count & (count - 1) == 0
    steps = [1, 3, 2] if count == 4 else range(1, count)
    return [part] + [
        lax.ppermute(part, axis, [(i, i ^ step if even else (i + step) % count) for i in range(count)])
        for step in steps
    ]


def on_device(queries, keys, values, gain, out_grad):
    tokens, width = queries.shape
    heads = width // HEAD
    count = lax.axis_size("ctx")
    factor = (HEAD * tokens * count) ** (-0.5)
    features = width * lax.axis_size("tp")
    gains = gain.reshape(heads, HEAD)
    sds = jax.ShapeDtypeStruct
    wide = sds((tokens, width), F32)
    half = sds((tokens, width), BF16)
    state = pltpu.VMEM((width, HEAD), F32)
    if count == 8 and lax.axis_size("tp") % 2 == 0:
        group = count // 2
        pieces = [sds((width // group, HEAD), F32)] * group
    else:
        group = count
        pieces = [sds((count, width // count, HEAD), F32)]

    def in_hbm(*arrays):
        return [pltpu.with_memory_space_constraint(array, pltpu.HBM) for array in arrays]

    def in_vmem(array):
        return pltpu.VMEM(array.shape, array.dtype)

    k_held, v_held, *states = call(
        functools.partial(states_body, heads, group),
        (in_vmem(keys), in_vmem(values), *pieces, *(pieces[i] for i in ALONE if len(pieces) > 1)),
        *in_hbm(keys, values),
        ins=[HBM, HBM],
        scratch=[state, pltpu.SemaphoreType.DMA((2 * LOADS,))],
    )
    prefix = carried_in(states, False, state)
    pairs = heads * tokens * tokens * HEAD
    scores, local, q_held, q_turned, weighted, gain_held = call(
        functools.partial(scores_body, heads, factor),
        (
            sds((heads, tokens, tokens), BF16), wide,
            in_vmem(queries), pltpu.VMEM((width, tokens), BF16), in_vmem(wide), in_vmem(gains),
        ),
        k_held, v_held, *in_hbm(queries, out_grad, gains),
        ins=[VMEM, VMEM, HBM, HBM, HBM],
        scratch=[in_vmem(out_grad), pltpu.SemaphoreType.DMA((3,))],
        flops=4 * pairs,
    )
    attended, stats, prefix = call(
        functools.partial(attend_body, heads, factor, group),
        (wide, sds((2, tokens), F32), sds((width, HEAD), F32)),
        q_held, weighted, local, *prefix,
    )
    every = from_all(stats, "tp")
    inv_rms, grad_attn, *updates = call(
        functools.partial(grad_body, heads, features, group, len(every)),
        (pltpu.VMEM((tokens, HEAD), F32), half, *pieces),
        attended, weighted, q_turned, *every,
        scratch=[state],
    )
    suffix = carried_in(updates, True, state)
    normed, grad_q, gk_part, gv_part = call(
        functools.partial(local_body, heads, factor),
        (half, half, wide, wide),
        grad_attn, q_held, k_held, v_held, prefix, scores, attended, inv_rms, gain_held,
        flops=9 * pairs,
    )
    held = pltpu.VMEM((tokens, width), BF16)
    grad_k, grad_v = call(
        functools.partial(final_body, heads, factor, group),
        (half, half),
        k_held, v_held, gk_part, gv_part, *suffix,
        dests=(HBM, HBM),
        scratch=[state, held, held, pltpu.SemaphoreType.DMA((2 * heads,))],
    )
    return normed, grad_q, grad_k, grad_v


def solution(mesh):
    placed = (P("ctx", "tp"), P("ctx", "tp"), P("ctx", "tp"), P("tp"), P("ctx", "tp"))
    return jax.shard_map(
        on_device,
        mesh=mesh,
        in_specs=placed,
        out_specs=(P("ctx", "tp"), P("ctx", "tp"), P("ctx", "tp"), P("ctx", "tp")),
        check_vma=False,
    )
```

```python
import functools

import jax
import jax.numpy as jnp
from jax import lax
from jax.experimental import pallas as pl
from jax.experimental.pallas import tpu as pltpu
from jax.sharding import PartitionSpec as P

HEAD = 128

epsilon = 1e-06
LOADS = 4
FIRST, BACK, HAND = 0, 1, 2
ALONE = (0, 2)
SHARED = (1, 3)
F32 = jnp.float32
BF16 = jnp.bfloat16

NN = (((1,), (0,)), ((), ()))
NT = (((1,), (1,)), ((), ()))
TN = (((0,), (0,)), ((), ()))


def dot(a, b, dims):
    return lax.dot_general(a, b, dims, preferred_element_type=F32)


VMEM = pl.BlockSpec(memory_space=pltpu.VMEM)
HBM = pl.BlockSpec(memory_space=pltpu.HBM)


def call(body, outs, *args, ins=None, dests=None, scratch=(), flops=1e7):
    moved = sum(a.size * a.dtype.itemsize for a in args)
    return pl.pallas_call(
        body,
        out_shape=outs,
        in_specs=ins or [VMEM] * len(args),
        out_specs=dests or jax.tree.map(lambda _: VMEM, outs),
        scratch_shapes=scratch,
        compiler_params=pltpu.CompilerParams(vmem_limit_bytes=16 * 1024 * 1024),
        cost_estimate=pl.CostEstimate(flops=int(flops), bytes_accessed=int(moved), transcendentals=0),
    )(*args)


def head(h):
    return slice(h * HEAD, (h + 1) * HEAD)


def causal_mask(tokens):
    row = lax.broadcasted_iota(jnp.int32, (tokens, tokens), 0)
    col = lax.broadcasted_iota(jnp.int32, (tokens, tokens), 1)
    return row >= col


def rows_of(scratch, parts, place):
    rows = scratch.shape[0] // parts
    return scratch.at[pl.ds(pl.multiple_of(place * rows, rows), rows), :]


def step_of(i, odd, order):
    return (
        (3, 2, 1, 0),
        (3, 2, 1, 0),
        (3 - odd, 1 + 2 * odd, 2 - odd, 0),
    )[order][i]


def give(scratch, group, outs, order=0):
    if len(outs) == 1:
        outs[0][...] = scratch[...].reshape(outs[0].shape)
        return
    place = lax.rem(lax.axis_index("ctx"), group)
    odd = lax.rem(lax.axis_index("tp"), 2)
    for i, out in enumerate(outs):
        out[...] = rows_of(scratch, group, lax.bitwise_xor(place, step_of(i, odd, order)))[...]


def take(ins, scratch, group, order=0):
    if len(ins) == 1:
        scratch[...] = ins[0][...].reshape(scratch.shape)
        return
    place = lax.rem(lax.axis_index("ctx"), group)
    sent_by_odd = 1 - lax.rem(lax.axis_index("tp"), 2)
    for i, piece in enumerate(ins):
        rows_of(scratch, group, lax.bitwise_xor(place, step_of(i, sent_by_odd, order)))[...] = piece[...]


def running_sums(scratch, parts, reverse):
    rows = scratch.shape[0] // parts
    running = jnp.zeros((rows, scratch.shape[1]), F32)
    for place in range(parts - 1, -1, -1) if reverse else range(parts):
        own = slice(place * rows, (place + 1) * rows)
        here = scratch[own, :]
        scratch[own, :] = running
        running = running + here
    return running


def loads(pairs, sems):
    copies = [pltpu.make_async_copy(a, b, sems.at[i]) for i, (a, b) in enumerate(pairs)]
    for copy in copies:
        copy.start()
    return copies


def states_body(heads, group, k_hbm, v_hbm, k, v, *refs):
    outs, (state, sems) = refs[:-2], refs[-2:]
    rows = k.shape[0] // LOADS
    blocks = [slice(i * rows, (i + 1) * rows) for i in range(LOADS)]
    for copy in loads([(a.at[r, :], b.at[r, :]) for r in blocks for a, b in ((k_hbm, k), (v_hbm, v))], sems):
        copy.wait()
    for h in range(heads):
        state[head(h), :] = dot(k[:, head(h)], v[:, head(h)], TN)
    give(state, group, outs[:group], FIRST)
    for again, i in zip(outs[group:], ALONE):
        again[...] = outs[i][...]


def scan_body(count, reverse, arrived, sums, scratch):
    take([arrived], scratch, count)
    running_sums(scratch, count, reverse)
    give(scratch, count, [sums])


def inner_body(group, reverse, *refs):
    arrived, total, outs, sums = refs[:group], refs[group], refs[group + 1 : 2 * group + 1], refs[-1]
    take(arrived, sums, group, BACK if reverse else FIRST)
    total[...] = running_sums(sums, group, reverse)
    give(sums, group, outs, HAND)
    if not reverse:
        for passed, i in zip(refs[2 * group + 1 : -1], SHARED):
            passed[...] = arrived[i][...]


def add_body(group, sums, over, *outs):
    place = lax.rem(lax.axis_index("ctx"), group)
    odd = lax.rem(lax.axis_index("tp"), 2)
    for i, out in enumerate(outs):
        out[...] = rows_of(sums, group, lax.bitwise_xor(place, step_of(i, odd, HAND)))[...] + over[...]


def late_body(group, reverse, *refs):
    arrived, over, outs, sums = refs[:group], refs[group], refs[group + 1 : -1], refs[-1]
    take(arrived, sums, group)
    running_sums(sums, group, reverse)
    add_body(group, sums, over, *outs)


def pick(pieces, scratch, group):
    many = len(pieces) // 2
    if many == 0:
        take(pieces, scratch, group)
        return
    early = lax.axis_index("ctx") < group
    place = lax.rem(lax.axis_index("ctx"), group)
    sent_by_odd = 1 - lax.rem(lax.axis_index("tp"), 2)
    for i in range(many):
        rows = rows_of(scratch, group, lax.bitwise_xor(place, step_of(i, sent_by_odd, HAND)))
        rows[...] = jnp.where(early, pieces[i][...], pieces[many + i][...])


def scores_body(heads, factor, k, v, q_hbm, og_hbm, gain_hbm, scores, attended, q, q_turned, weighted, gain, og, sems):
    copies = loads(((q_hbm, q), (og_hbm, og), (gain_hbm, gain)), sems)
    copies[0].wait()
    q_turned[...] = q[...].T
    causal = causal_mask(q.shape[0])
    for h in range(heads):
        raw = dot(q[:, head(h)], k[:, head(h)], NT) * factor
        sc = jnp.where(causal, raw, 0.0).astype(BF16)
        scores[h] = sc
        attended[:, head(h)] = dot(sc, v[:, head(h)], NN)
    for copy in copies[1:]:
        copy.wait()
    for h in range(heads):
        weighted[:, head(h)] = og[:, head(h)].astype(F32) * gain[h : h + 1, :]


def attend_body(heads, factor, group, q, weighted, local, *refs):
    pieces, (attended, stats, prefix) = refs[:-3], refs[-3:]
    pick(pieces, prefix, group)
    power = 0.0
    inner = 0.0
    for h in range(heads):
        att = factor * dot(q[:, head(h)], prefix[head(h), :].astype(BF16), NN) + local[:, head(h)]
        attended[:, head(h)] = att
        power = power + att * att
        inner = inner + weighted[:, head(h)] * att
    stats[0:1, :] = jnp.sum(power.T, axis=0, keepdims=True)
    stats[1:2, :] = jnp.sum(inner.T, axis=0, keepdims=True)


def grad_body(heads, features, group, ways, attended, weighted, q_turned, *refs):
    stats, (spread, grad), outs, updates = refs[:ways], refs[ways : ways + 2], refs[ways + 2 : -1], refs[-1]
    total = stats[0][...]
    for other in stats[1:]:
        total = total + other[...]
    inv_rms = lax.rsqrt(total[0:1, :] / features + epsilon)
    bend = inv_rms * inv_rms * (total[1:2, :] / features)
    tokens = q_turned.shape[1]
    inv_rms = jnp.broadcast_to(inv_rms, (HEAD, tokens)).T
    bend = jnp.broadcast_to(bend, (HEAD, tokens)).T
    spread[...] = inv_rms
    for h in range(heads):
        ga = (inv_rms * (weighted[:, head(h)] - attended[:, head(h)] * bend)).astype(BF16)
        grad[:, head(h)] = ga
        updates[head(h), :] = dot(q_turned[head(h), :], ga, NN)
    give(updates, group, outs, BACK)


def local_body(heads, factor, ga, q, k, v, prefix, scores, attended, inv_rms, gain, normed, gq, gk_part, gv_part):
    causal = causal_mask(q.shape[0])
    for h in range(heads):
        normed[:, head(h)] = (attended[:, head(h)] * inv_rms[...] * gain[h : h + 1, :]).astype(BF16)
        gah = ga[:, head(h)]
        raw = dot(gah, v[:, head(h)], NT) * factor
        gs = jnp.where(causal, raw, 0.0).astype(BF16)
        out = factor * dot(gah, prefix[head(h), :].astype(BF16), NT)
        gq[:, head(h)] = (out + dot(gs, k[:, head(h)], NN)).astype(BF16)
        gk_part[:, head(h)] = dot(gs, q[:, head(h)], TN)
        gv_part[:, head(h)] = dot(scores[h], gah, TN)


def final_body(heads, factor, group, k, v, gk_part, gv_part, *refs):
    pieces, outs, (suffix, gk, gv, sems) = refs[:-6], refs[-6:-4], refs[-4:]
    pick(pieces, suffix, group)
    copies = []

    def send(h, held, out):
        copy = pltpu.make_async_copy(held.at[:, head(h)], out.at[:, head(h)], sems.at[len(copies)])
        copy.start()
        copies.append(copy)

    for h in range(heads):
        suf = suffix[head(h), :].astype(BF16)
        gk[:, head(h)] = (factor * dot(v[:, head(h)], suf, NT) + gk_part[:, head(h)]).astype(BF16)
        send(h, gk, outs[0])
        gv[:, head(h)] = (factor * dot(k[:, head(h)], suf, NN) + gv_part[:, head(h)]).astype(BF16)
        send(h, gv, outs[1])
    for copy in copies:
        copy.wait()


def exchange(piece, i, active, order):
    ways = lax.axis_size("tp")
    pairs = [
        (j * ways + t, (j ^ step_of(i, t % 2, order) if j in active else j) * ways + (t ^ 1))
        for j in range(lax.axis_size("ctx"))
        for t in range(ways)
    ]
    return lax.ppermute(piece, ("ctx", "tp"), pairs)


def carried_in(pieces, reverse, state):
    again = () if reverse or len(pieces) == 1 else pieces[-len(ALONE) :]
    group = len(pieces) - len(again)
    pieces = pieces[:group]
    count = lax.axis_size("ctx")
    sds = jax.ShapeDtypeStruct
    if group == 1:
        arrived = lax.all_to_all(pieces[0], "ctx", 0, 0, tiled=True)
        sums = call(
            functools.partial(scan_body, count, reverse),
            sds(arrived.shape, F32), arrived, scratch=[state],
        )
        return [lax.all_to_all(sums, "ctx", 0, 0, tiled=True)]
    rows, width = pieces[0].shape
    piece = sds((rows, width), F32)
    early, late, both = range(group), range(group, count), range(count)
    first, second = (late, early) if reverse else (early, late)
    everyone = range(group)
    arrived = [
        exchange(pieces[i], i, both if reverse or i in SHARED else first, BACK if reverse else FIRST)
        for i in everyone
    ]
    kept = [sds((group * rows, width), F32)] if reverse else [piece] * len(SHARED)
    total, *back = call(
        functools.partial(inner_body, group, reverse),
        [piece] * (group + 1) + kept,
        *arrived,
        scratch=[] if reverse else [state],
    )
    over = lax.ppermute(total, "ctx", [(j, j ^ group) for j in both])
    ahead = [exchange(back[i], i, first, HAND) for i in everyone]
    if reverse:
        back = call(functools.partial(add_body, group), [piece] * group, back[group], over)
    else:
        own = [exchange(part, i, second, FIRST) for part, i in zip(again, ALONE)]
        mixed = [own[ALONE.index(i)] if i in ALONE else back[group + SHARED.index(i)] for i in everyone]
        back = call(
            functools.partial(late_body, group, reverse),
            [piece] * group, *mixed, over, scratch=[state],
        )
    behind = [exchange(back[i], i, second, HAND) for i in everyone]
    return [*behind, *ahead] if reverse else [*ahead, *behind]


def from_all(part, axis):
    count = lax.axis_size(axis)
    even = count & (count - 1) == 0
    steps = [1, 3, 2] if count == 4 else range(1, count)
    return [part] + [
        lax.ppermute(part, axis, [(i, i ^ step if even else (i + step) % count) for i in range(count)])
        for step in steps
    ]


def on_device(queries, keys, values, gain, out_grad):
    tokens, width = queries.shape
    heads = width // HEAD
    count = lax.axis_size("ctx")
    factor = (HEAD * tokens * count) ** (-0.5)
    features = width * lax.axis_size("tp")
    gains = gain.reshape(heads, HEAD)
    sds = jax.ShapeDtypeStruct
    wide = sds((tokens, width), F32)
    half = sds((tokens, width), BF16)
    state = pltpu.VMEM((width, HEAD), F32)
    if count == 8 and lax.axis_size("tp") % 2 == 0:
        group = count // 2
        pieces = [sds((width // group, HEAD), F32)] * group
    else:
        group = count
        pieces = [sds((count, width // count, HEAD), F32)]

    def in_hbm(*arrays):
        return [pltpu.with_memory_space_constraint(array, pltpu.HBM) for array in arrays]

    def in_vmem(array):
        return pltpu.VMEM(array.shape, array.dtype)

    k_held, v_held, *states = call(
        functools.partial(states_body, heads, group),
        (in_vmem(keys), in_vmem(values), *pieces, *(pieces[i] for i in ALONE if len(pieces) > 1)),
        *in_hbm(keys, values),
        ins=[HBM, HBM],
        scratch=[state, pltpu.SemaphoreType.DMA((2 * LOADS,))],
    )
    prefix = carried_in(states, False, state)
    pairs = heads * tokens * tokens * HEAD
    scores, local, q_held, q_turned, weighted, gain_held = call(
        functools.partial(scores_body, heads, factor),
        (
            sds((heads, tokens, tokens), BF16), wide,
            in_vmem(queries), pltpu.VMEM((width, tokens), BF16), in_vmem(wide), in_vmem(gains),
        ),
        k_held, v_held, *in_hbm(queries, out_grad, gains),
        ins=[VMEM, VMEM, HBM, HBM, HBM],
        scratch=[in_vmem(out_grad), pltpu.SemaphoreType.DMA((3,))],
        flops=4 * pairs,
    )
    attended, stats, prefix = call(
        functools.partial(attend_body, heads, factor, group),
        (wide, sds((2, tokens), F32), sds((width, HEAD), F32)),
        q_held, weighted, local, *prefix,
    )
    every = from_all(stats, "tp")
    inv_rms, grad_attn, *updates = call(
        functools.partial(grad_body, heads, features, group, len(every)),
        (pltpu.VMEM((tokens, HEAD), F32), half, *pieces),
        attended, weighted, q_turned, *every,
        scratch=[state],
    )
    suffix = carried_in(updates, True, state)
    normed, grad_q, gk_part, gv_part = call(
        functools.partial(local_body, heads, factor),
        (half, half, wide, wide),
        grad_attn, q_held, k_held, v_held, prefix, scores, attended, inv_rms, gain_held,
        flops=9 * pairs,
    )
    held = pltpu.VMEM((tokens, width), BF16)
    grad_k, grad_v = call(
        functools.partial(final_body, heads, factor, group),
        (half, half),
        k_held, v_held, gk_part, gv_part, *suffix,
        dests=(HBM, HBM),
        scratch=[state, held, held, pltpu.SemaphoreType.DMA((2 * heads,))],
    )
    return normed, grad_q, grad_k, grad_v


def solution(mesh):
    placed = (P("ctx", "tp"), P("ctx", "tp"), P("ctx", "tp"), P("tp"), P("ctx", "tp"))
    return jax.shard_map(
        on_device,
        mesh=mesh,
        in_specs=placed,
        out_specs=(P("ctx", "tp"), P("ctx", "tp"), P("ctx", "tp"), P("ctx", "tp")),
        check_vma=False,
    )
```

```python
import functools

import jax
import jax.numpy as jnp
from jax import lax
from jax.experimental import pallas as pl
from jax.experimental.pallas import tpu as pltpu
from jax.sharding import PartitionSpec as P

HEAD = 128

epsilon = 1e-06
LOADS = 4
FIRST, BACK, HAND = 0, 1, 2
ALONE = (0, 2)
SHARED = (1, 3)
F32 = jnp.float32
BF16 = jnp.bfloat16

NN = (((1,), (0,)), ((), ()))
NT = (((1,), (1,)), ((), ()))
TN = (((0,), (0,)), ((), ()))


def dot(a, b, dims):
    return lax.dot_general(a, b, dims, preferred_element_type=F32)


VMEM = pl.BlockSpec(memory_space=pltpu.VMEM)
HBM = pl.BlockSpec(memory_space=pltpu.HBM)


def call(body, outs, *args, ins=None, dests=None, scratch=(), flops=1e7):
    moved = sum(a.size * a.dtype.itemsize for a in args)
    return pl.pallas_call(
        body,
        out_shape=outs,
        in_specs=ins or [VMEM] * len(args),
        out_specs=dests or jax.tree.map(lambda _: VMEM, outs),
        scratch_shapes=scratch,
        compiler_params=pltpu.CompilerParams(vmem_limit_bytes=16 * 1024 * 1024),
        cost_estimate=pl.CostEstimate(flops=int(flops), bytes_accessed=int(moved), transcendentals=0),
    )(*args)


def head(h):
    return slice(h * HEAD, (h + 1) * HEAD)


def causal_mask(tokens):
    row = lax.broadcasted_iota(jnp.int32, (tokens, tokens), 0)
    col = lax.broadcasted_iota(jnp.int32, (tokens, tokens), 1)
    return row >= col


def rows_of(scratch, parts, place):
    rows = scratch.shape[0] // parts
    return scratch.at[pl.ds(pl.multiple_of(place * rows, rows), rows), :]


def step_of(i, odd, order):
    return (
        (3, 1, 2, 0),
        (3, 2, 1, 0),
        (3 - odd, 1 + 2 * odd, 2 - odd, 0),
    )[order][i]


def give(scratch, group, outs, order=0):
    if len(outs) == 1:
        outs[0][...] = scratch[...].reshape(outs[0].shape)
        return
    place = lax.rem(lax.axis_index("ctx"), group)
    odd = lax.rem(lax.axis_index("tp"), 2)
    for i, out in enumerate(outs):
        out[...] = rows_of(scratch, group, lax.bitwise_xor(place, step_of(i, odd, order)))[...]


def take(ins, scratch, group, order=0):
    if len(ins) == 1:
        scratch[...] = ins[0][...].reshape(scratch.shape)
        return
    place = lax.rem(lax.axis_index("ctx"), group)
    sent_by_odd = 1 - lax.rem(lax.axis_index("tp"), 2)
    for i, piece in enumerate(ins):
        rows_of(scratch, group, lax.bitwise_xor(place, step_of(i, sent_by_odd, order)))[...] = piece[...]


def running_sums(scratch, parts, reverse):
    rows = scratch.shape[0] // parts
    running = jnp.zeros((rows, scratch.shape[1]), F32)
    for place in range(parts - 1, -1, -1) if reverse else range(parts):
        own = slice(place * rows, (place + 1) * rows)
        here = scratch[own, :]
        scratch[own, :] = running
        running = running + here
    return running


def loads(pairs, sems):
    copies = [pltpu.make_async_copy(a, b, sems.at[i]) for i, (a, b) in enumerate(pairs)]
    for copy in copies:
        copy.start()
    return copies


def states_body(heads, group, k_hbm, v_hbm, k, v, *refs):
    outs, (state, sems) = refs[:-2], refs[-2:]
    rows = k.shape[0] // LOADS
    blocks = [slice(i * rows, (i + 1) * rows) for i in range(LOADS)]
    for copy in loads([(a.at[r, :], b.at[r, :]) for r in blocks for a, b in ((k_hbm, k), (v_hbm, v))], sems):
        copy.wait()
    for h in range(heads):
        state[head(h), :] = dot(k[:, head(h)], v[:, head(h)], TN)
    give(state, group, outs[:group], FIRST)
    for again, i in zip(outs[group:], ALONE):
        again[...] = outs[i][...]


def scan_body(count, reverse, arrived, sums, scratch):
    take([arrived], scratch, count)
    running_sums(scratch, count, reverse)
    give(scratch, count, [sums])


def inner_body(group, reverse, *refs):
    arrived, total, outs, sums = refs[:group], refs[group], refs[group + 1 : 2 * group + 1], refs[-1]
    take(arrived, sums, group, BACK if reverse else FIRST)
    total[...] = running_sums(sums, group, reverse)
    give(sums, group, outs, HAND)
    if not reverse:
        for passed, i in zip(refs[2 * group + 1 : -1], SHARED):
            passed[...] = arrived[i][...]


def add_body(group, sums, over, *outs):
    place = lax.rem(lax.axis_index("ctx"), group)
    odd = lax.rem(lax.axis_index("tp"), 2)
    for i, out in enumerate(outs):
        out[...] = rows_of(sums, group, lax.bitwise_xor(place, step_of(i, odd, HAND)))[...] + over[...]


def late_body(group, reverse, *refs):
    arrived, over, outs, sums = refs[:group], refs[group], refs[group + 1 : -1], refs[-1]
    take(arrived, sums, group)
    running_sums(sums, group, reverse)
    add_body(group, sums, over, *outs)


def pick(pieces, scratch, group):
    many = len(pieces) // 2
    if many == 0:
        take(pieces, scratch, group)
        return
    early = lax.axis_index("ctx") < group
    place = lax.rem(lax.axis_index("ctx"), group)
    sent_by_odd = 1 - lax.rem(lax.axis_index("tp"), 2)
    for i in range(many):
        rows = rows_of(scratch, group, lax.bitwise_xor(place, step_of(i, sent_by_odd, HAND)))
        rows[...] = jnp.where(early, pieces[i][...], pieces[many + i][...])


def scores_body(heads, factor, k, v, q_hbm, og_hbm, gain_hbm, scores, attended, q, q_turned, weighted, gain, og, sems):
    copies = loads(((q_hbm, q), (og_hbm, og), (gain_hbm, gain)), sems)
    copies[0].wait()
    q_turned[...] = q[...].T
    causal = causal_mask(q.shape[0])
    for h in range(heads):
        raw = dot(q[:, head(h)], k[:, head(h)], NT) * factor
        sc = jnp.where(causal, raw, 0.0).astype(BF16)
        scores[h] = sc
        attended[:, head(h)] = dot(sc, v[:, head(h)], NN)
    for copy in copies[1:]:
        copy.wait()
    for h in range(heads):
        weighted[:, head(h)] = og[:, head(h)].astype(F32) * gain[h : h + 1, :]


def attend_body(heads, factor, group, q, weighted, local, *refs):
    pieces, (attended, stats, prefix) = refs[:-3], refs[-3:]
    pick(pieces, prefix, group)
    power = 0.0
    inner = 0.0
    for h in range(heads):
        att = factor * dot(q[:, head(h)], prefix[head(h), :].astype(BF16), NN) + local[:, head(h)]
        attended[:, head(h)] = att
        power = power + att * att
        inner = inner + weighted[:, head(h)] * att
    stats[0:1, :] = jnp.sum(power.T, axis=0, keepdims=True)
    stats[1:2, :] = jnp.sum(inner.T, axis=0, keepdims=True)


def grad_body(heads, features, group, ways, attended, weighted, q_turned, *refs):
    stats, (spread, grad), outs, updates = refs[:ways], refs[ways : ways + 2], refs[ways + 2 : -1], refs[-1]
    total = stats[0][...]
    for other in stats[1:]:
        total = total + other[...]
    inv_rms = lax.rsqrt(total[0:1, :] / features + epsilon)
    bend = inv_rms * inv_rms * (total[1:2, :] / features)
    tokens = q_turned.shape[1]
    inv_rms = jnp.broadcast_to(inv_rms, (HEAD, tokens)).T
    bend = jnp.broadcast_to(bend, (HEAD, tokens)).T
    spread[...] = inv_rms
    for h in range(heads):
        ga = (inv_rms * (weighted[:, head(h)] - attended[:, head(h)] * bend)).astype(BF16)
        grad[:, head(h)] = ga
        updates[head(h), :] = dot(q_turned[head(h), :], ga, NN)
    give(updates, group, outs, BACK)


def local_body(heads, factor, ga, q, k, v, prefix, scores, attended, inv_rms, gain, normed, gq, gk_part, gv_part):
    causal = causal_mask(q.shape[0])
    for h in range(heads):
        normed[:, head(h)] = (attended[:, head(h)] * inv_rms[...] * gain[h : h + 1, :]).astype(BF16)
        gah = ga[:, head(h)]
        raw = dot(gah, v[:, head(h)], NT) * factor
        gs = jnp.where(causal, raw, 0.0).astype(BF16)
        out = factor * dot(gah, prefix[head(h), :].astype(BF16), NT)
        gq[:, head(h)] = (out + dot(gs, k[:, head(h)], NN)).astype(BF16)
        gk_part[:, head(h)] = dot(gs, q[:, head(h)], TN)
        gv_part[:, head(h)] = dot(scores[h], gah, TN)


def final_body(heads, factor, group, k, v, gk_part, gv_part, *refs):
    pieces, outs, (suffix, gk, gv, sems) = refs[:-6], refs[-6:-4], refs[-4:]
    pick(pieces, suffix, group)
    copies = []

    def send(h, held, out):
        copy = pltpu.make_async_copy(held.at[:, head(h)], out.at[:, head(h)], sems.at[len(copies)])
        copy.start()
        copies.append(copy)

    for h in range(heads):
        suf = suffix[head(h), :].astype(BF16)
        gk[:, head(h)] = (factor * dot(v[:, head(h)], suf, NT) + gk_part[:, head(h)]).astype(BF16)
        send(h, gk, outs[0])
        gv[:, head(h)] = (factor * dot(k[:, head(h)], suf, NN) + gv_part[:, head(h)]).astype(BF16)
        send(h, gv, outs[1])
    for copy in copies:
        copy.wait()


def exchange(piece, i, active, order):
    ways = lax.axis_size("tp")
    pairs = [
        (j * ways + t, (j ^ step_of(i, t % 2, order) if j in active else j) * ways + (t ^ 1))
        for j in range(lax.axis_size("ctx"))
        for t in range(ways)
    ]
    return lax.ppermute(piece, ("ctx", "tp"), pairs)


def carried_in(pieces, reverse, state):
    again = () if reverse or len(pieces) == 1 else pieces[-len(ALONE) :]
    group = len(pieces) - len(again)
    pieces = pieces[:group]
    count = lax.axis_size("ctx")
    sds = jax.ShapeDtypeStruct
    if group == 1:
        arrived = lax.all_to_all(pieces[0], "ctx", 0, 0, tiled=True)
        sums = call(
            functools.partial(scan_body, count, reverse),
            sds(arrived.shape, F32), arrived, scratch=[state],
        )
        return [lax.all_to_all(sums, "ctx", 0, 0, tiled=True)]
    rows, width = pieces[0].shape
    piece = sds((rows, width), F32)
    early, late, both = range(group), range(group, count), range(count)
    first, second = (late, early) if reverse else (early, late)
    everyone = range(group)
    arrived = [
        exchange(pieces[i], i, both if reverse or i in SHARED else first, BACK if reverse else FIRST)
        for i in everyone
    ]
    kept = [sds((group * rows, width), F32)] if reverse else [piece] * len(SHARED)
    total, *back = call(
        functools.partial(inner_body, group, reverse),
        [piece] * (group + 1) + kept,
        *arrived,
        scratch=[] if reverse else [state],
    )
    over = lax.ppermute(total, "ctx", [(j, j ^ group) for j in both])
    ahead = [exchange(back[i], i, first, HAND) for i in everyone]
    if reverse:
        back = call(functools.partial(add_body, group), [piece] * group, back[group], over)
    else:
        own = [exchange(part, i, second, FIRST) for part, i in zip(again, ALONE)]
        mixed = [own[ALONE.index(i)] if i in ALONE else back[group + SHARED.index(i)] for i in everyone]
        back = call(
            functools.partial(late_body, group, reverse),
            [piece] * group, *mixed, over, scratch=[state],
        )
    behind = [exchange(back[i], i, second, HAND) for i in everyone]
    return [*behind, *ahead] if reverse else [*ahead, *behind]


def from_all(part, axis):
    count = lax.axis_size(axis)
    even = count & (count - 1) == 0
    steps = [1, 3, 2] if count == 4 else range(1, count)
    return [part] + [
        lax.ppermute(part, axis, [(i, i ^ step if even else (i + step) % count) for i in range(count)])
        for step in steps
    ]


def on_device(queries, keys, values, gain, out_grad):
    tokens, width = queries.shape
    heads = width // HEAD
    count = lax.axis_size("ctx")
    factor = (HEAD * tokens * count) ** (-0.5)
    features = width * lax.axis_size("tp")
    gains = gain.reshape(heads, HEAD)
    sds = jax.ShapeDtypeStruct
    wide = sds((tokens, width), F32)
    half = sds((tokens, width), BF16)
    state = pltpu.VMEM((width, HEAD), F32)
    if count == 8 and lax.axis_size("tp") % 2 == 0:
        group = count // 2
        pieces = [sds((width // group, HEAD), F32)] * group
    else:
        group = count
        pieces = [sds((count, width // count, HEAD), F32)]

    def in_hbm(*arrays):
        return [pltpu.with_memory_space_constraint(array, pltpu.HBM) for array in arrays]

    def in_vmem(array):
        return pltpu.VMEM(array.shape, array.dtype)

    k_held, v_held, *states = call(
        functools.partial(states_body, heads, group),
        (in_vmem(keys), in_vmem(values), *pieces, *(pieces[i] for i in ALONE if len(pieces) > 1)),
        *in_hbm(keys, values),
        ins=[HBM, HBM],
        scratch=[state, pltpu.SemaphoreType.DMA((2 * LOADS,))],
    )
    prefix = carried_in(states, False, state)
    pairs = heads * tokens * tokens * HEAD
    scores, local, q_held, q_turned, weighted, gain_held = call(
        functools.partial(scores_body, heads, factor),
        (
            sds((heads, tokens, tokens), BF16), wide,
            in_vmem(queries), pltpu.VMEM((width, tokens), BF16), in_vmem(wide), in_vmem(gains),
        ),
        k_held, v_held, *in_hbm(queries, out_grad, gains),
        ins=[VMEM, VMEM, HBM, HBM, HBM],
        scratch=[in_vmem(out_grad), pltpu.SemaphoreType.DMA((3,))],
        flops=4 * pairs,
    )
    attended, stats, prefix = call(
        functools.partial(attend_body, heads, factor, group),
        (wide, sds((2, tokens), F32), sds((width, HEAD), F32)),
        q_held, weighted, local, *prefix,
    )
    every = from_all(stats, "tp")
    inv_rms, grad_attn, *updates = call(
        functools.partial(grad_body, heads, features, group, len(every)),
        (pltpu.VMEM((tokens, HEAD), F32), half, *pieces),
        attended, weighted, q_turned, *every,
        scratch=[state],
    )
    suffix = carried_in(updates, True, state)
    normed, grad_q, gk_part, gv_part = call(
        functools.partial(local_body, heads, factor),
        (half, half, wide, wide),
        grad_attn, q_held, k_held, v_held, prefix, scores, attended, inv_rms, gain_held,
        flops=9 * pairs,
    )
    held = pltpu.VMEM((tokens, width), BF16)
    grad_k, grad_v = call(
        functools.partial(final_body, heads, factor, group),
        (half, half),
        k_held, v_held, gk_part, gv_part, *suffix,
        dests=(HBM, HBM),
        scratch=[state, held, held, pltpu.SemaphoreType.DMA((2 * heads,))],
    )
    return normed, grad_q, grad_k, grad_v


def solution(mesh):
    placed = (P("ctx", "tp"), P("ctx", "tp"), P("ctx", "tp"), P("tp"), P("ctx", "tp"))
    return jax.shard_map(
        on_device,
        mesh=mesh,
        in_specs=placed,
        out_specs=(P("ctx", "tp"), P("ctx", "tp"), P("ctx", "tp"), P("ctx", "tp")),
        check_vma=False,
    )
```

```python
import functools

import jax
import jax.numpy as jnp
from jax import lax
from jax.experimental import pallas as pl
from jax.experimental.pallas import tpu as pltpu
from jax.sharding import PartitionSpec as P

HEAD = 128

epsilon = 1e-06
LOADS = 4
FIRST, BACK, HAND = 0, 1, 2
ALONE = (0, 1, 2)
SHARED = (3,)
F32 = jnp.float32
BF16 = jnp.bfloat16

NN = (((1,), (0,)), ((), ()))
NT = (((1,), (1,)), ((), ()))
TN = (((0,), (0,)), ((), ()))


def dot(a, b, dims):
    return lax.dot_general(a, b, dims, preferred_element_type=F32)


VMEM = pl.BlockSpec(memory_space=pltpu.VMEM)
HBM = pl.BlockSpec(memory_space=pltpu.HBM)


def call(body, outs, *args, ins=None, dests=None, scratch=(), flops=1e7):
    moved = sum(a.size * a.dtype.itemsize for a in args)
    return pl.pallas_call(
        body,
        out_shape=outs,
        in_specs=ins or [VMEM] * len(args),
        out_specs=dests or jax.tree.map(lambda _: VMEM, outs),
        scratch_shapes=scratch,
        compiler_params=pltpu.CompilerParams(vmem_limit_bytes=16 * 1024 * 1024),
        cost_estimate=pl.CostEstimate(flops=int(flops), bytes_accessed=int(moved), transcendentals=0),
    )(*args)


def head(h):
    return slice(h * HEAD, (h + 1) * HEAD)


def causal_mask(tokens):
    row = lax.broadcasted_iota(jnp.int32, (tokens, tokens), 0)
    col = lax.broadcasted_iota(jnp.int32, (tokens, tokens), 1)
    return row >= col


def rows_of(scratch, parts, place):
    rows = scratch.shape[0] // parts
    return scratch.at[pl.ds(pl.multiple_of(place * rows, rows), rows), :]


def step_of(i, odd, order):
    return (
        (3, 2, 1, 0),
        (3, 2, 1, 0),
        (3 - odd, 1 + 2 * odd, 2 - odd, 0),
    )[order][i]


def give(scratch, group, outs, order=0):
    if len(outs) == 1:
        outs[0][...] = scratch[...].reshape(outs[0].shape)
        return
    place = lax.rem(lax.axis_index("ctx"), group)
    odd = lax.rem(lax.axis_index("tp"), 2)
    for i, out in enumerate(outs):
        out[...] = rows_of(scratch, group, lax.bitwise_xor(place, step_of(i, odd, order)))[...]


def take(ins, scratch, group, order=0):
    if len(ins) == 1:
        scratch[...] = ins[0][...].reshape(scratch.shape)
        return
    place = lax.rem(lax.axis_index("ctx"), group)
    sent_by_odd = 1 - lax.rem(lax.axis_index("tp"), 2)
    for i, piece in enumerate(ins):
        rows_of(scratch, group, lax.bitwise_xor(place, step_of(i, sent_by_odd, order)))[...] = piece[...]


def running_sums(scratch, parts, reverse):
    rows = scratch.shape[0] // parts
    running = jnp.zeros((rows, scratch.shape[1]), F32)
    for place in range(parts - 1, -1, -1) if reverse else range(parts):
        own = slice(place * rows, (place + 1) * rows)
        here = scratch[own, :]
        scratch[own, :] = running
        running = running + here
    return running


def loads(pairs, sems):
    copies = [pltpu.make_async_copy(a, b, sems.at[i]) for i, (a, b) in enumerate(pairs)]
    for copy in copies:
        copy.start()
    return copies


def states_body(heads, group, k_hbm, v_hbm, k, v, *refs):
    outs, (state, sems) = refs[:-2], refs[-2:]
    rows = k.shape[0] // LOADS
    blocks = [slice(i * rows, (i + 1) * rows) for i in range(LOADS)]
    for copy in loads([(a.at[r, :], b.at[r, :]) for r in blocks for a, b in ((k_hbm, k), (v_hbm, v))], sems):
        copy.wait()
    for h in range(heads):
        state[head(h), :] = dot(k[:, head(h)], v[:, head(h)], TN)
    give(state, group, outs[:group], FIRST)
    for again, i in zip(outs[group:], ALONE):
        again[...] = outs[i][...]


def scan_body(count, reverse, arrived, sums, scratch):
    take([arrived], scratch, count)
    running_sums(scratch, count, reverse)
    give(scratch, count, [sums])


def inner_body(group, reverse, *refs):
    arrived, total, outs, sums = refs[:group], refs[group], refs[group + 1 : 2 * group + 1], refs[-1]
    take(arrived, sums, group, BACK if reverse else FIRST)
    total[...] = running_sums(sums, group, reverse)
    give(sums, group, outs, HAND)
    if not reverse:
        for passed, i in zip(refs[2 * group + 1 : -1], SHARED):
            passed[...] = arrived[i][...]


def add_body(group, sums, over, *outs):
    place = lax.rem(lax.axis_index("ctx"), group)
    odd = lax.rem(lax.axis_index("tp"), 2)
    for i, out in enumerate(outs):
        out[...] = rows_of(sums, group, lax.bitwise_xor(place, step_of(i, odd, HAND)))[...] + over[...]


def late_body(group, reverse, *refs):
    arrived, over, outs, sums = refs[:group], refs[group], refs[group + 1 : -1], refs[-1]
    take(arrived, sums, group)
    running_sums(sums, group, reverse)
    add_body(group, sums, over, *outs)


def pick(pieces, scratch, group):
    many = len(pieces) // 2
    if many == 0:
        take(pieces, scratch, group)
        return
    early = lax.axis_index("ctx") < group
    place = lax.rem(lax.axis_index("ctx"), group)
    sent_by_odd = 1 - lax.rem(lax.axis_index("tp"), 2)
    for i in range(many):
        rows = rows_of(scratch, group, lax.bitwise_xor(place, step_of(i, sent_by_odd, HAND)))
        rows[...] = jnp.where(early, pieces[i][...], pieces[many + i][...])


def scores_body(heads, factor, k, v, q_hbm, og_hbm, gain_hbm, scores, attended, q, q_turned, weighted, gain, og, sems):
    copies = loads(((q_hbm, q), (og_hbm, og), (gain_hbm, gain)), sems)
    copies[0].wait()
    q_turned[...] = q[...].T
    causal = causal_mask(q.shape[0])
    for h in range(heads):
        raw = dot(q[:, head(h)], k[:, head(h)], NT) * factor
        sc = jnp.where(causal, raw, 0.0).astype(BF16)
        scores[h] = sc
        attended[:, head(h)] = dot(sc, v[:, head(h)], NN)
    for copy in copies[1:]:
        copy.wait()
    for h in range(heads):
        weighted[:, head(h)] = og[:, head(h)].astype(F32) * gain[h : h + 1, :]


def attend_body(heads, factor, group, q, weighted, local, *refs):
    pieces, (attended, stats, prefix) = refs[:-3], refs[-3:]
    pick(pieces, prefix, group)
    power = 0.0
    inner = 0.0
    for h in range(heads):
        att = factor * dot(q[:, head(h)], prefix[head(h), :].astype(BF16), NN) + local[:, head(h)]
        attended[:, head(h)] = att
        power = power + att * att
        inner = inner + weighted[:, head(h)] * att
    stats[0:1, :] = jnp.sum(power.T, axis=0, keepdims=True)
    stats[1:2, :] = jnp.sum(inner.T, axis=0, keepdims=True)


def grad_body(heads, features, group, ways, attended, weighted, q_turned, *refs):
    stats, (spread, grad), outs, updates = refs[:ways], refs[ways : ways + 2], refs[ways + 2 : -1], refs[-1]
    total = stats[0][...]
    for other in stats[1:]:
        total = total + other[...]
    inv_rms = lax.rsqrt(total[0:1, :] / features + epsilon)
    bend = inv_rms * inv_rms * (total[1:2, :] / features)
    tokens = q_turned.shape[1]
    inv_rms = jnp.broadcast_to(inv_rms, (HEAD, tokens)).T
    bend = jnp.broadcast_to(bend, (HEAD, tokens)).T
    spread[...] = inv_rms
    for h in range(heads):
        ga = (inv_rms * (weighted[:, head(h)] - attended[:, head(h)] * bend)).astype(BF16)
        grad[:, head(h)] = ga
        updates[head(h), :] = dot(q_turned[head(h), :], ga, NN)
    give(updates, group, outs, BACK)


def local_body(heads, factor, ga, q, k, v, prefix, scores, attended, inv_rms, gain, normed, gq, gk_part, gv_part):
    causal = causal_mask(q.shape[0])
    for h in range(heads):
        normed[:, head(h)] = (attended[:, head(h)] * inv_rms[...] * gain[h : h + 1, :]).astype(BF16)
        gah = ga[:, head(h)]
        raw = dot(gah, v[:, head(h)], NT) * factor
        gs = jnp.where(causal, raw, 0.0).astype(BF16)
        out = factor * dot(gah, prefix[head(h), :].astype(BF16), NT)
        gq[:, head(h)] = (out + dot(gs, k[:, head(h)], NN)).astype(BF16)
        gk_part[:, head(h)] = dot(gs, q[:, head(h)], TN)
        gv_part[:, head(h)] = dot(scores[h], gah, TN)


def final_body(heads, factor, group, k, v, gk_part, gv_part, *refs):
    pieces, outs, (suffix, gk, gv, sems) = refs[:-6], refs[-6:-4], refs[-4:]
    pick(pieces, suffix, group)
    copies = []

    def send(h, held, out):
        copy = pltpu.make_async_copy(held.at[:, head(h)], out.at[:, head(h)], sems.at[len(copies)])
        copy.start()
        copies.append(copy)

    for h in range(heads):
        suf = suffix[head(h), :].astype(BF16)
        gk[:, head(h)] = (factor * dot(v[:, head(h)], suf, NT) + gk_part[:, head(h)]).astype(BF16)
        send(h, gk, outs[0])
        gv[:, head(h)] = (factor * dot(k[:, head(h)], suf, NN) + gv_part[:, head(h)]).astype(BF16)
        send(h, gv, outs[1])
    for copy in copies:
        copy.wait()


def exchange(piece, i, active, order):
    ways = lax.axis_size("tp")
    pairs = [
        (j * ways + t, (j ^ step_of(i, t % 2, order) if j in active else j) * ways + (t ^ 1))
        for j in range(lax.axis_size("ctx"))
        for t in range(ways)
    ]
    return lax.ppermute(piece, ("ctx", "tp"), pairs)


def carried_in(pieces, reverse, state):
    again = () if reverse or len(pieces) == 1 else pieces[-len(ALONE) :]
    group = len(pieces) - len(again)
    pieces = pieces[:group]
    count = lax.axis_size("ctx")
    sds = jax.ShapeDtypeStruct
    if group == 1:
        arrived = lax.all_to_all(pieces[0], "ctx", 0, 0, tiled=True)
        sums = call(
            functools.partial(scan_body, count, reverse),
            sds(arrived.shape, F32), arrived, scratch=[state],
        )
        return [lax.all_to_all(sums, "ctx", 0, 0, tiled=True)]
    rows, width = pieces[0].shape
    piece = sds((rows, width), F32)
    early, late, both = range(group), range(group, count), range(count)
    first, second = (late, early) if reverse else (early, late)
    everyone = range(group)
    arrived = [
        exchange(pieces[i], i, both if reverse or i in SHARED else first, BACK if reverse else FIRST)
        for i in everyone
    ]
    kept = [sds((group * rows, width), F32)] if reverse else [piece] * len(SHARED)
    total, *back = call(
        functools.partial(inner_body, group, reverse),
        [piece] * (group + 1) + kept,
        *arrived,
        scratch=[] if reverse else [state],
    )
    over = lax.ppermute(total, "ctx", [(j, j ^ group) for j in both])
    ahead = [exchange(back[i], i, first, HAND) for i in everyone]
    if reverse:
        back = call(functools.partial(add_body, group), [piece] * group, back[group], over)
    else:
        own = [exchange(part, i, second, FIRST) for part, i in zip(again, ALONE)]
        mixed = [own[ALONE.index(i)] if i in ALONE else back[group + SHARED.index(i)] for i in everyone]
        back = call(
            functools.partial(late_body, group, reverse),
            [piece] * group, *mixed, over, scratch=[state],
        )
    behind = [exchange(back[i], i, second, HAND) for i in everyone]
    return [*behind, *ahead] if reverse else [*ahead, *behind]


def from_all(part, axis):
    count = lax.axis_size(axis)
    even = count & (count - 1) == 0
    steps = [1, 3, 2] if count == 4 else range(1, count)
    return [part] + [
        lax.ppermute(part, axis, [(i, i ^ step if even else (i + step) % count) for i in range(count)])
        for step in steps
    ]


def on_device(queries, keys, values, gain, out_grad):
    tokens, width = queries.shape
    heads = width // HEAD
    count = lax.axis_size("ctx")
    factor = (HEAD * tokens * count) ** (-0.5)
    features = width * lax.axis_size("tp")
    gains = gain.reshape(heads, HEAD)
    sds = jax.ShapeDtypeStruct
    wide = sds((tokens, width), F32)
    half = sds((tokens, width), BF16)
    state = pltpu.VMEM((width, HEAD), F32)
    if count == 8 and lax.axis_size("tp") % 2 == 0:
        group = count // 2
        pieces = [sds((width // group, HEAD), F32)] * group
    else:
        group = count
        pieces = [sds((count, width // count, HEAD), F32)]

    def in_hbm(*arrays):
        return [pltpu.with_memory_space_constraint(array, pltpu.HBM) for array in arrays]

    def in_vmem(array):
        return pltpu.VMEM(array.shape, array.dtype)

    k_held, v_held, *states = call(
        functools.partial(states_body, heads, group),
        (in_vmem(keys), in_vmem(values), *pieces, *(pieces[i] for i in ALONE if len(pieces) > 1)),
        *in_hbm(keys, values),
        ins=[HBM, HBM],
        scratch=[state, pltpu.SemaphoreType.DMA((2 * LOADS,))],
    )
    prefix = carried_in(states, False, state)
    pairs = heads * tokens * tokens * HEAD
    scores, local, q_held, q_turned, weighted, gain_held = call(
        functools.partial(scores_body, heads, factor),
        (
            sds((heads, tokens, tokens), BF16), wide,
            in_vmem(queries), pltpu.VMEM((width, tokens), BF16), in_vmem(wide), in_vmem(gains),
        ),
        k_held, v_held, *in_hbm(queries, out_grad, gains),
        ins=[VMEM, VMEM, HBM, HBM, HBM],
        scratch=[in_vmem(out_grad), pltpu.SemaphoreType.DMA((3,))],
        flops=4 * pairs,
    )
    attended, stats, prefix = call(
        functools.partial(attend_body, heads, factor, group),
        (wide, sds((2, tokens), F32), sds((width, HEAD), F32)),
        q_held, weighted, local, *prefix,
    )
    every = from_all(stats, "tp")
    inv_rms, grad_attn, *updates = call(
        functools.partial(grad_body, heads, features, group, len(every)),
        (pltpu.VMEM((tokens, HEAD), F32), half, *pieces),
        attended, weighted, q_turned, *every,
        scratch=[state],
    )
    suffix = carried_in(updates, True, state)
    normed, grad_q, gk_part, gv_part = call(
        functools.partial(local_body, heads, factor),
        (half, half, wide, wide),
        grad_attn, q_held, k_held, v_held, prefix, scores, attended, inv_rms, gain_held,
        flops=9 * pairs,
    )
    held = pltpu.VMEM((tokens, width), BF16)
    grad_k, grad_v = call(
        functools.partial(final_body, heads, factor, group),
        (half, half),
        k_held, v_held, gk_part, gv_part, *suffix,
        dests=(HBM, HBM),
        scratch=[state, held, held, pltpu.SemaphoreType.DMA((2 * heads,))],
    )
    return normed, grad_q, grad_k, grad_v


def solution(mesh):
    placed = (P("ctx", "tp"), P("ctx", "tp"), P("ctx", "tp"), P("tp"), P("ctx", "tp"))
    return jax.shard_map(
        on_device,
        mesh=mesh,
        in_specs=placed,
        out_specs=(P("ctx", "tp"), P("ctx", "tp"), P("ctx", "tp"), P("ctx", "tp")),
        check_vma=False,
    )
```

```python
import functools

import jax
import jax.numpy as jnp
from jax import lax
from jax.experimental import pallas as pl
from jax.experimental.pallas import tpu as pltpu
from jax.sharding import PartitionSpec as P

HEAD = 128

epsilon = 1e-06
LOADS = 4
FIRST, BACK, HAND = 0, 1, 2
ALONE = (0, 2)
SHARED = (1, 3)
F32 = jnp.float32
BF16 = jnp.bfloat16

NN = (((1,), (0,)), ((), ()))
NT = (((1,), (1,)), ((), ()))
TN = (((0,), (0,)), ((), ()))


def dot(a, b, dims):
    return lax.dot_general(a, b, dims, preferred_element_type=F32)


VMEM = pl.BlockSpec(memory_space=pltpu.VMEM)
HBM = pl.BlockSpec(memory_space=pltpu.HBM)


def call(body, outs, *args, ins=None, dests=None, scratch=(), flops=1e7):
    moved = sum(a.size * a.dtype.itemsize for a in args)
    return pl.pallas_call(
        body,
        out_shape=outs,
        in_specs=ins or [VMEM] * len(args),
        out_specs=dests or jax.tree.map(lambda _: VMEM, outs),
        scratch_shapes=scratch,
        compiler_params=pltpu.CompilerParams(vmem_limit_bytes=16 * 1024 * 1024),
        cost_estimate=pl.CostEstimate(flops=int(flops), bytes_accessed=int(moved), transcendentals=0),
    )(*args)


def head(h):
    return slice(h * HEAD, (h + 1) * HEAD)


def causal_mask(tokens):
    row = lax.broadcasted_iota(jnp.int32, (tokens, tokens), 0)
    col = lax.broadcasted_iota(jnp.int32, (tokens, tokens), 1)
    return row >= col


def rows_of(scratch, parts, place):
    rows = scratch.shape[0] // parts
    return scratch.at[pl.ds(pl.multiple_of(place * rows, rows), rows), :]


def step_of(i, odd, order):
    return (
        (3, 2, 1, 0),
        (3, 1, 2, 0),
        (3 - odd, 1 + 2 * odd, 2 - odd, 0),
    )[order][i]


def give(scratch, group, outs, order=0):
    if len(outs) == 1:
        outs[0][...] = scratch[...].reshape(outs[0].shape)
        return
    place = lax.rem(lax.axis_index("ctx"), group)
    odd = lax.rem(lax.axis_index("tp"), 2)
    for i, out in enumerate(outs):
        out[...] = rows_of(scratch, group, lax.bitwise_xor(place, step_of(i, odd, order)))[...]


def take(ins, scratch, group, order=0):
    if len(ins) == 1:
        scratch[...] = ins[0][...].reshape(scratch.shape)
        return
    place = lax.rem(lax.axis_index("ctx"), group)
    sent_by_odd = 1 - lax.rem(lax.axis_index("tp"), 2)
    for i, piece in enumerate(ins):
        rows_of(scratch, group, lax.bitwise_xor(place, step_of(i, sent_by_odd, order)))[...] = piece[...]


def running_sums(scratch, parts, reverse):
    rows = scratch.shape[0] // parts
    running = jnp.zeros((rows, scratch.shape[1]), F32)
    for place in range(parts - 1, -1, -1) if reverse else range(parts):
        own = slice(place * rows, (place + 1) * rows)
        here = scratch[own, :]
        scratch[own, :] = running
        running = running + here
    return running


def loads(pairs, sems):
    copies = [pltpu.make_async_copy(a, b, sems.at[i]) for i, (a, b) in enumerate(pairs)]
    for copy in copies:
        copy.start()
    return copies


def states_body(heads, group, k_hbm, v_hbm, k, v, *refs):
    outs, (state, sems) = refs[:-2], refs[-2:]
    rows = k.shape[0] // LOADS
    blocks = [slice(i * rows, (i + 1) * rows) for i in range(LOADS)]
    for copy in loads([(a.at[r, :], b.at[r, :]) for r in blocks for a, b in ((k_hbm, k), (v_hbm, v))], sems):
        copy.wait()
    for h in range(heads):
        state[head(h), :] = dot(k[:, head(h)], v[:, head(h)], TN)
    give(state, group, outs[:group], FIRST)
    for again, i in zip(outs[group:], ALONE):
        again[...] = outs[i][...]


def scan_body(count, reverse, arrived, sums, scratch):
    take([arrived], scratch, count)
    running_sums(scratch, count, reverse)
    give(scratch, count, [sums])


def inner_body(group, reverse, *refs):
    arrived, total, outs, sums = refs[:group], refs[group], refs[group + 1 : 2 * group + 1], refs[-1]
    take(arrived, sums, group, BACK if reverse else FIRST)
    total[...] = running_sums(sums, group, reverse)
    give(sums, group, outs, HAND)
    if not reverse:
        for passed, i in zip(refs[2 * group + 1 : -1], SHARED):
            passed[...] = arrived[i][...]


def add_body(group, sums, over, *outs):
    place = lax.rem(lax.axis_index("ctx"), group)
    odd = lax.rem(lax.axis_index("tp"), 2)
    for i, out in enumerate(outs):
        out[...] = rows_of(sums, group, lax.bitwise_xor(place, step_of(i, odd, HAND)))[...] + over[...]


def late_body(group, reverse, *refs):
    arrived, over, outs, sums = refs[:group], refs[group], refs[group + 1 : -1], refs[-1]
    take(arrived, sums, group)
    running_sums(sums, group, reverse)
    add_body(group, sums, over, *outs)


def pick(pieces, scratch, group):
    many = len(pieces) // 2
    if many == 0:
        take(pieces, scratch, group)
        return
    early = lax.axis_index("ctx") < group
    place = lax.rem(lax.axis_index("ctx"), group)
    sent_by_odd = 1 - lax.rem(lax.axis_index("tp"), 2)
    for i in range(many):
        rows = rows_of(scratch, group, lax.bitwise_xor(place, step_of(i, sent_by_odd, HAND)))
        rows[...] = jnp.where(early, pieces[i][...], pieces[many + i][...])


def scores_body(heads, factor, k, v, q_hbm, og_hbm, gain_hbm, scores, attended, q, q_turned, weighted, gain, og, sems):
    copies = loads(((q_hbm, q), (og_hbm, og), (gain_hbm, gain)), sems)
    copies[0].wait()
    q_turned[...] = q[...].T
    causal = causal_mask(q.shape[0])
    for h in range(heads):
        raw = dot(q[:, head(h)], k[:, head(h)], NT) * factor
        sc = jnp.where(causal, raw, 0.0).astype(BF16)
        scores[h] = sc
        attended[:, head(h)] = dot(sc, v[:, head(h)], NN)
    for copy in copies[1:]:
        copy.wait()
    for h in range(heads):
        weighted[:, head(h)] = og[:, head(h)].astype(F32) * gain[h : h + 1, :]


def attend_body(heads, factor, group, q, weighted, local, *refs):
    pieces, (attended, stats, prefix) = refs[:-3], refs[-3:]
    pick(pieces, prefix, group)
    power = 0.0
    inner = 0.0
    for h in range(heads):
        att = factor * dot(q[:, head(h)], prefix[head(h), :].astype(BF16), NN) + local[:, head(h)]
        attended[:, head(h)] = att
        power = power + att * att
        inner = inner + weighted[:, head(h)] * att
    stats[0:1, :] = jnp.sum(power.T, axis=0, keepdims=True)
    stats[1:2, :] = jnp.sum(inner.T, axis=0, keepdims=True)


def grad_body(heads, features, group, ways, attended, weighted, q_turned, *refs):
    stats, (spread, grad), outs, updates = refs[:ways], refs[ways : ways + 2], refs[ways + 2 : -1], refs[-1]
    total = stats[0][...]
    for other in stats[1:]:
        total = total + other[...]
    inv_rms = lax.rsqrt(total[0:1, :] / features + epsilon)
    bend = inv_rms * inv_rms * (total[1:2, :] / features)
    tokens = q_turned.shape[1]
    inv_rms = jnp.broadcast_to(inv_rms, (HEAD, tokens)).T
    bend = jnp.broadcast_to(bend, (HEAD, tokens)).T
    spread[...] = inv_rms
    for h in range(heads):
        ga = (inv_rms * (weighted[:, head(h)] - attended[:, head(h)] * bend)).astype(BF16)
        grad[:, head(h)] = ga
        updates[head(h), :] = dot(q_turned[head(h), :], ga, NN)
    give(updates, group, outs, BACK)


def local_body(heads, factor, ga, q, k, v, prefix, scores, attended, inv_rms, gain, normed, gq, gk_part, gv_part):
    causal = causal_mask(q.shape[0])
    for h in range(heads):
        normed[:, head(h)] = (attended[:, head(h)] * inv_rms[...] * gain[h : h + 1, :]).astype(BF16)
        gah = ga[:, head(h)]
        raw = dot(gah, v[:, head(h)], NT) * factor
        gs = jnp.where(causal, raw, 0.0).astype(BF16)
        out = factor * dot(gah, prefix[head(h), :].astype(BF16), NT)
        gq[:, head(h)] = (out + dot(gs, k[:, head(h)], NN)).astype(BF16)
        gk_part[:, head(h)] = dot(gs, q[:, head(h)], TN)
        gv_part[:, head(h)] = dot(scores[h], gah, TN)


def final_body(heads, factor, group, k, v, gk_part, gv_part, *refs):
    pieces, outs, (suffix, gk, gv, sems) = refs[:-6], refs[-6:-4], refs[-4:]
    pick(pieces, suffix, group)
    copies = []

    def send(h, held, out):
        copy = pltpu.make_async_copy(held.at[:, head(h)], out.at[:, head(h)], sems.at[len(copies)])
        copy.start()
        copies.append(copy)

    for h in range(heads):
        suf = suffix[head(h), :].astype(BF16)
        gk[:, head(h)] = (factor * dot(v[:, head(h)], suf, NT) + gk_part[:, head(h)]).astype(BF16)
        send(h, gk, outs[0])
        gv[:, head(h)] = (factor * dot(k[:, head(h)], suf, NN) + gv_part[:, head(h)]).astype(BF16)
        send(h, gv, outs[1])
    for copy in copies:
        copy.wait()


def exchange(piece, i, active, order):
    ways = lax.axis_size("tp")
    pairs = [
        (j * ways + t, (j ^ step_of(i, t % 2, order) if j in active else j) * ways + (t ^ 1))
        for j in range(lax.axis_size("ctx"))
        for t in range(ways)
    ]
    return lax.ppermute(piece, ("ctx", "tp"), pairs)


def carried_in(pieces, reverse, state):
    again = () if reverse or len(pieces) == 1 else pieces[-len(ALONE) :]
    group = len(pieces) - len(again)
    pieces = pieces[:group]
    count = lax.axis_size("ctx")
    sds = jax.ShapeDtypeStruct
    if group == 1:
        arrived = lax.all_to_all(pieces[0], "ctx", 0, 0, tiled=True)
        sums = call(
            functools.partial(scan_body, count, reverse),
            sds(arrived.shape, F32), arrived, scratch=[state],
        )
        return [lax.all_to_all(sums, "ctx", 0, 0, tiled=True)]
    rows, width = pieces[0].shape
    piece = sds((rows, width), F32)
    early, late, both = range(group), range(group, count), range(count)
    first, second = (late, early) if reverse else (early, late)
    everyone = range(group)
    arrived = [
        exchange(pieces[i], i, both if reverse or i in SHARED else first, BACK if reverse else FIRST)
        for i in everyone
    ]
    kept = [sds((group * rows, width), F32)] if reverse else [piece] * len(SHARED)
    total, *back = call(
        functools.partial(inner_body, group, reverse),
        [piece] * (group + 1) + kept,
        *arrived,
        scratch=[] if reverse else [state],
    )
    over = lax.ppermute(total, "ctx", [(j, j ^ group) for j in both])
    ahead = [exchange(back[i], i, first, HAND) for i in everyone]
    if reverse:
        back = call(functools.partial(add_body, group), [piece] * group, back[group], over)
    else:
        own = [exchange(part, i, second, FIRST) for part, i in zip(again, ALONE)]
        mixed = [own[ALONE.index(i)] if i in ALONE else back[group + SHARED.index(i)] for i in everyone]
        back = call(
            functools.partial(late_body, group, reverse),
            [piece] * group, *mixed, over, scratch=[state],
        )
    behind = [exchange(back[i], i, second, HAND) for i in everyone]
    return [*behind, *ahead] if reverse else [*ahead, *behind]


def from_all(part, axis):
    count = lax.axis_size(axis)
    even = count & (count - 1) == 0
    steps = [1, 3, 2] if count == 4 else range(1, count)
    return [part] + [
        lax.ppermute(part, axis, [(i, i ^ step if even else (i + step) % count) for i in range(count)])
        for step in steps
    ]


def on_device(queries, keys, values, gain, out_grad):
    tokens, width = queries.shape
    heads = width // HEAD
    count = lax.axis_size("ctx")
    factor = (HEAD * tokens * count) ** (-0.5)
    features = width * lax.axis_size("tp")
    gains = gain.reshape(heads, HEAD)
    sds = jax.ShapeDtypeStruct
    wide = sds((tokens, width), F32)
    half = sds((tokens, width), BF16)
    state = pltpu.VMEM((width, HEAD), F32)
    if count == 8 and lax.axis_size("tp") % 2 == 0:
        group = count // 2
        pieces = [sds((width // group, HEAD), F32)] * group
    else:
        group = count
        pieces = [sds((count, width // count, HEAD), F32)]

    def in_hbm(*arrays):
        return [pltpu.with_memory_space_constraint(array, pltpu.HBM) for array in arrays]

    def in_vmem(array):
        return pltpu.VMEM(array.shape, array.dtype)

    k_held, v_held, *states = call(
        functools.partial(states_body, heads, group),
        (in_vmem(keys), in_vmem(values), *pieces, *(pieces[i] for i in ALONE if len(pieces) > 1)),
        *in_hbm(keys, values),
        ins=[HBM, HBM],
        scratch=[state, pltpu.SemaphoreType.DMA((2 * LOADS,))],
    )
    prefix = carried_in(states, False, state)
    pairs = heads * tokens * tokens * HEAD
    scores, local, q_held, q_turned, weighted, gain_held = call(
        functools.partial(scores_body, heads, factor),
        (
            sds((heads, tokens, tokens), BF16), wide,
            in_vmem(queries), pltpu.VMEM((width, tokens), BF16), in_vmem(wide), in_vmem(gains),
        ),
        k_held, v_held, *in_hbm(queries, out_grad, gains),
        ins=[VMEM, VMEM, HBM, HBM, HBM],
        scratch=[in_vmem(out_grad), pltpu.SemaphoreType.DMA((3,))],
        flops=4 * pairs,
    )
    attended, stats, prefix = call(
        functools.partial(attend_body, heads, factor, group),
        (wide, sds((2, tokens), F32), sds((width, HEAD), F32)),
        q_held, weighted, local, *prefix,
    )
    every = from_all(stats, "tp")
    inv_rms, grad_attn, *updates = call(
        functools.partial(grad_body, heads, features, group, len(every)),
        (pltpu.VMEM((tokens, HEAD), F32), half, *pieces),
        attended, weighted, q_turned, *every,
        scratch=[state],
    )
    suffix = carried_in(updates, True, state)
    normed, grad_q, gk_part, gv_part = call(
        functools.partial(local_body, heads, factor),
        (half, half, wide, wide),
        grad_attn, q_held, k_held, v_held, prefix, scores, attended, inv_rms, gain_held,
        flops=9 * pairs,
    )
    held = pltpu.VMEM((tokens, width), BF16)
    grad_k, grad_v = call(
        functools.partial(final_body, heads, factor, group),
        (half, half),
        k_held, v_held, gk_part, gv_part, *suffix,
        dests=(HBM, HBM),
        scratch=[state, held, held, pltpu.SemaphoreType.DMA((2 * heads,))],
    )
    return normed, grad_q, grad_k, grad_v


def solution(mesh):
    placed = (P("ctx", "tp"), P("ctx", "tp"), P("ctx", "tp"), P("tp"), P("ctx", "tp"))
    return jax.shard_map(
        on_device,
        mesh=mesh,
        in_specs=placed,
        out_specs=(P("ctx", "tp"), P("ctx", "tp"), P("ctx", "tp"), P("ctx", "tp")),
        check_vma=False,
    )
```
